32 devices in a mesh: batch: 8 (over z, y), band: 4 (over x, core).
Axes of the slice: x: 2, y: 2, z: 4, core: 2. Of those that a mesh axis runs over, the one named last changes fastest.
Arguments:
- tokens: bfloat16 [24, 256, 768], P('batch', 'band'), may hold values from -32 to 32
- cotangent: bfloat16 [24, 256, 768], P('batch', 'band'), may hold values from -17 to 17
- visible: int32 [24, 256], P('batch', 'band'), may hold values from 0 to 1, as said below
- first_gain: float32 [768], replicated, may hold values from 0.1 to 1.9
- first_bias: float32 [768], replicated, may hold values from -3 to 3
- qkv_weight: bfloat16 [768, 2304], replicated, may hold values from -0.21875 to 0.21875
- qv_bias: float32 [2, 768], replicated, may hold values from -3 to 3
- proj_weight: bfloat16 [768, 768], replicated, may hold values from -0.625 to 0.625
- proj_bias: float32 [768], replicated, may hold values from -2 to 2
- attn_scale: float32 [768], replicated, may hold values from 0.5 to 2
- second_gain: float32 [768], replicated, may hold values from 0.1 to 1.9
- second_bias: float32 [768], replicated, may hold values from -3 to 3
- expand_weight: bfloat16 [768, 3072], replicated, may hold values from -0.21875 to 0.21875
- expand_bias: float32 [3072], replicated, may hold values from -3 to 3
- reduce_weight: bfloat16 [3072, 768], replicated, may hold values from -0.109375 to 0.109375
- reduce_bias: float32 [768], replicated, may hold values from -2 to 2
- mlp_scale: float32 [768], replicated, may hold values from 0.5 to 2
Outputs:
- layer_out: bfloat16 [24, 256, 768], P('batch', 'band')
- grad_tokens: bfloat16 [24, 256, 768], P('batch', 'band')
- grad_first_gain: float32 [768], P(('batch', 'band'))
- grad_first_bias: float32 [768], P(('batch', 'band'))
- grad_qkv_weight: float32 [768, 2304], P(('batch', 'band'))
- grad_qv_bias: float32 [2, 768], P(None, ('batch', 'band'))
- grad_proj_weight: float32 [768, 768], P(('batch', 'band'))
- grad_proj_bias: float32 [768], P(('batch', 'band'))
- grad_attn_scale: float32 [768], P(('batch', 'band'))
- grad_second_gain: float32 [768], P(('batch', 'band'))
- grad_second_bias: float32 [768], P(('batch', 'band'))
- grad_expand_weight: float32 [768, 3072], P(('batch', 'band'))
- grad_expand_bias: float32 [3072], P(('batch', 'band'))
- grad_reduce_weight: float32 [3072, 768], P(('batch', 'band'))
- grad_reduce_bias: float32 [768], P(('batch', 'band'))
- grad_mlp_scale: float32 [768], P(('batch', 'band'))
The draws below stay inside these ranges and needn't reach their ends.
Inputs may be any that keep to these rules, and one draw needn't show every extreme that they name: Patch (r, c) of the 14 x 14 grid sits in slot r * 16 + c; in all other slots (columns from 14 on, rows from 14 on) visible is 0; tokens and cotangent there may hold any values. Each image has 78 to 137 visible patches, and in every draw some image has exactly 78 and some exactly 137.
All inputs are finite; a program needn't handle non-finite values.
Results may differ from the reference program's by a relative error of at most 0.012.
Values may be sent and summed in bfloat16 or wider, within the bound.
No kernel may reach another device: no remote copies, remote signals or barrier semaphores. Data moves between devices by JAX's collectives and lax.ppermute only.
A program may use at most 192 MiB of HBM per device.

```python
import math
import jax
import jax.numpy as jnp
from jax import lax

H = 12
HD = 64
FF = 3072
GRID = 14
ROW_SLOTS = 16
D = 768
POS = 256
IMAGES = 24
VIS_LO = 78
VIS_HI = 137


def draw_tokens(key, part):
    key = jax.random.fold_in(key, 3)
    subkeys = jax.random.split(key, 3)
    base_field = jnp.clip(jax.random.normal(subkeys[0], (IMAGES, POS, D)), -6.0, 6.0)
    row_scale = jnp.exp(jax.random.uniform(subkeys[1], (IMAGES, POS, 1), minval=-1.15, maxval=1.15))
    columns = jnp.exp(jax.random.uniform(subkeys[2], (1, 1, D), minval=-0.5, maxval=0.5))
    return (base_field * row_scale * columns).astype(jnp.bfloat16)


def draw_cotangent(key, part):
    key = jax.random.fold_in(key, 7)
    subkeys = jax.random.split(key, 2)
    base_field = jnp.clip(jax.random.normal(subkeys[0], (IMAGES, POS, D)), -6.0, 6.0)
    image_scale = jnp.exp(jax.random.uniform(subkeys[1], (IMAGES, 1, 1), minval=-1.0, maxval=1.0))
    return (base_field * image_scale).astype(jnp.bfloat16)


def draw_visible(key, part):
    key = jax.random.fold_in(key, 5)
    subkeys = jax.random.split(key, 4)
    counts = jax.random.randint(subkeys[0], (IMAGES,), VIS_LO, VIS_HI + 1)
    first_pick = jax.random.randint(subkeys[1], (), 0, IMAGES)
    offset = jax.random.randint(subkeys[2], (), 1, IMAGES)
    second_pick = (first_pick + offset) % IMAGES
    counts = counts.at[first_pick].set(VIS_HI).at[second_pick].set(VIS_LO)
    patches = GRID * GRID
    rank_scores = jax.random.randint(subkeys[3], (IMAGES, patches), 0, 1 << 20) * patches + jnp.arange(patches, dtype=jnp.int32)[None, :]
    sort_order = jnp.argsort(rank_scores, axis=1)
    patch_rank = jnp.argsort(sort_order, axis=1)
    patch_drawn = (patch_rank < counts[:, None]).astype(jnp.int32).reshape(IMAGES, GRID, GRID)
    row_count = POS // ROW_SLOTS
    padded = jnp.pad(patch_drawn, ((0, 0), (0, row_count - GRID), (0, ROW_SLOTS - GRID)))
    return padded.reshape(IMAGES, POS)


def gaussian(own_key, dims, deviation, most, kind=jnp.bfloat16):
    return jnp.clip(deviation * jax.random.normal(own_key, dims, jnp.float32), -most, most).astype(kind)


def setup_inputs(seed: int = 0) -> dict:
    streams_of = jax.random.split(jax.random.key(seed), 18)
    tokens = draw_tokens(jax.random.fold_in(streams_of[17], 71), 0)
    cotangent = draw_cotangent(jax.random.fold_in(streams_of[17], 71), 0)
    visible = draw_visible(jax.random.fold_in(streams_of[17], 71), 0)
    first_gain = jnp.clip(1.0 + 0.18 * jax.random.normal(streams_of[3], (D,), jnp.float32), 0.1, 1.9)
    first_bias = gaussian(streams_of[4], (D,), 0.5, 3.0, jnp.float32)
    qkv_weight = gaussian(streams_of[5], (D, 3 * D), D ** -0.5, 0.21875)
    qv_bias = gaussian(streams_of[6], (2, D), 0.5, 3.0, jnp.float32)
    proj_weight = gaussian(streams_of[7], (D, D), (D // 8) ** -0.5, 0.625)
    proj_bias = gaussian(streams_of[8], (D,), 0.3, 2.0, jnp.float32)
    attn_scale = jnp.clip(jnp.exp(jax.random.uniform(streams_of[9], (D,), jnp.float32, math.log(0.5), math.log(2.0))), 0.5, 2.0)
    second_gain = jnp.clip(1.0 + 0.18 * jax.random.normal(streams_of[10], (D,), jnp.float32), 0.1, 1.9)
    second_bias = gaussian(streams_of[11], (D,), 0.5, 3.0, jnp.float32)
    expand_weight = gaussian(streams_of[12], (D, FF), D ** -0.5, 0.21875)
    expand_bias = gaussian(streams_of[13], (FF,), 0.5, 3.0, jnp.float32)
    reduce_weight = gaussian(streams_of[14], (FF, D), FF ** -0.5, 0.109375)
    reduce_bias = gaussian(streams_of[15], (D,), 0.3, 2.0, jnp.float32)
    mlp_scale = jnp.clip(jnp.exp(jax.random.uniform(streams_of[16], (D,), jnp.float32, math.log(0.5), math.log(2.0))), 0.5, 2.0)
    return dict(tokens=tokens, cotangent=cotangent, visible=visible, first_gain=first_gain, first_bias=first_bias, qkv_weight=qkv_weight, qv_bias=qv_bias, proj_weight=proj_weight, proj_bias=proj_bias, attn_scale=attn_scale, second_gain=second_gain, second_bias=second_bias, expand_weight=expand_weight, expand_bias=expand_bias, reduce_weight=reduce_weight, reduce_bias=reduce_bias, mlp_scale=mlp_scale)


@jax.custom_vjp
def low(v):
    return lax.optimization_barrier(v.astype(jnp.bfloat16)).astype(jnp.float32)

@jax.custom_vjp
def low_back(v):
    return v

def low_keep(v):
    return (low(v), None)

def low_pass(kept, grad):
    return (grad,)

def back_keep(v):
    return (v, None)

def back_low(kept, grad):
    return (low(grad),)
low.defvjp(low_keep, low_pass)
low_back.defvjp(back_keep, back_low)
NORM_EPS = 1e-06

def layer_norm(values, norm_gain, norm_shift):
    center = values - lax.optimization_barrier(jnp.mean(values, axis=-1, keepdims=True))
    spread = lax.optimization_barrier(jnp.mean(center * center, axis=-1, keepdims=True))
    return center * lax.rsqrt(spread + NORM_EPS) * norm_gain + norm_shift

def matmul(left_side, right_side):
    return jnp.einsum('bsd,de->bse', left_side, right_side, precision=lax.Precision.HIGHEST)

def block(params, tokens, shown_mask):
    first_gain, first_bias, qkv_weight, qv_bias, proj_weight, proj_bias, attn_scale, second_gain, second_bias, expand_weight, expand_bias, reduce_weight, reduce_bias, mlp_scale = params
    block_count = tokens.shape[0]
    normed = low(layer_norm(tokens, first_gain, first_bias))
    zero_part = jnp.zeros_like(qv_bias[0])
    packed = matmul(normed, qkv_weight) + jnp.concatenate([qv_bias[0], zero_part, qv_bias[1]])
    packed = low(low_back(packed))
    unpacked = packed.reshape(block_count, POS, 3, H, HD)
    queries = unpacked[:, :, 0]
    key_rows = unpacked[:, :, 1]
    value_rows = unpacked[:, :, 2]
    score_scale = 1.0 / math.sqrt(HD)
    scores = low_back(jnp.einsum('bqhe,bkhe->bhqk', queries, key_rows, precision=lax.Precision.HIGHEST) * score_scale)
    scores = jnp.where(shown_mask[:, None, None, :] > 0, scores, -1e+30)
    row_top = lax.optimization_barrier(jnp.max(scores, axis=-1, keepdims=True))
    raised = jnp.exp(scores - row_top)
    attn_prob = raised / lax.optimization_barrier(jnp.sum(raised, axis=-1, keepdims=True))
    mixed_rows = jnp.einsum('bhqk,bkhe->bqhe', low(attn_prob), value_rows, precision=lax.Precision.HIGHEST)
    mixed_rows = low(low_back(mixed_rows.reshape(block_count, POS, D)))
    branch_one = low_back(matmul(mixed_rows, proj_weight) + proj_bias)
    residual = tokens + attn_scale * branch_one
    normed_two = low(layer_norm(residual, second_gain, second_bias))
    hidden = low_back(matmul(normed_two, expand_weight) + expand_bias)
    activated = low(jax.nn.gelu(hidden, approximate=False))
    branch_two = low_back(matmul(activated, reduce_weight) + reduce_bias)
    return shown_mask[..., None] * (residual + mlp_scale * branch_two)

def reference(tokens, cotangent, visible, first_gain, first_bias, qkv_weight, qv_bias, proj_weight, proj_bias, attn_scale, second_gain, second_bias, expand_weight, expand_bias, reduce_weight, reduce_bias, mlp_scale):
    params = (first_gain, first_bias, qkv_weight.astype(jnp.float32), qv_bias, proj_weight.astype(jnp.float32), proj_bias, attn_scale, second_gain, second_bias, expand_weight.astype(jnp.float32), expand_bias, reduce_weight.astype(jnp.float32), reduce_bias, mlp_scale)
    group_size = math.gcd(IMAGES, 16)
    rounds = IMAGES // group_size
    token_blocks = tokens.astype(jnp.float32).reshape(rounds, group_size, POS, D)
    cot_blocks = cotangent.astype(jnp.float32).reshape(rounds, group_size, POS, D)
    mask_blocks = visible.astype(jnp.float32).reshape(rounds, group_size, POS)

    def advance(totals, block_item):
        token_part, cot_part, mask_part = block_item
        result, pull_back = jax.vjp(lambda weights_in, tokens_in: block(weights_in, tokens_in, mask_part), params, token_part)
        param_grads, token_grads = pull_back(cot_part)
        totals = jax.tree.map(lambda left_side, right_side: left_side + right_side, totals, param_grads)
        return (totals, (result.astype(jnp.bfloat16), token_grads.astype(jnp.bfloat16)))
    zero_grads = jax.tree.map(jnp.zeros_like, params)
    grads, (out_blocks, back_blocks) = lax.scan(advance, zero_grads, (token_blocks, cot_blocks, mask_blocks))
    return (out_blocks.reshape(IMAGES, POS, D), back_blocks.reshape(IMAGES, POS, D), grads[0], grads[1], grads[2], grads[3], grads[4], grads[5], grads[6], grads[7], grads[8], grads[9], grads[10], grads[11], grads[12], grads[13])
```

```python
import functools
import math

import jax
import jax.numpy as jnp
from jax import lax
from jax.experimental import pallas as pl
from jax.experimental.pallas import tpu as pltpu
from jax.sharding import PartitionSpec as P

HD = 64
NORM_EPS = 1e-06
PACK = 144
SLOTS = 256
BAND = 64
IMGS = 3
ROWS = IMGS * PACK
D = 768
HALF = D // 2
FF = 3072
FH = FF // 2
SMALL = 128
MIB = 1024 * 1024
F32 = jnp.float32
BF = jnp.bfloat16
ANY = pl.BlockSpec(memory_space=pl.ANY)
VM = pl.BlockSpec(memory_space=pltpu.VMEM)


def dot(a, b):
    return jnp.dot(a, b, preferred_element_type=F32)


def dot_nt(a, b):
    return lax.dot_general(a, b, (((1,), (1,)), ((), ())), preferred_element_type=F32)


def dot_tn(a, b):
    return lax.dot_general(a, b, (((0,), (0,)), ((), ())), preferred_element_type=F32)


def sds(shape, dtype):
    return jax.ShapeDtypeStruct(shape, dtype)


def place():
    band = lax.axis_index("band")
    batch = lax.axis_index("batch")
    return band >> 1, band & 1, batch >> 1, batch & 1


def one_hot_pack(pos, image):
    rows = lax.broadcasted_iota(jnp.int32, (PACK, SLOTS), 0).astype(F32)
    return jnp.where(rows == pos[image : image + 1, :], 1.0, 0.0).astype(BF)


def feature_pick():
    x, _, z, y = place()
    lane = lax.broadcasted_iota(jnp.int32, (D, HALF), 1)
    row = lax.broadcasted_iota(jnp.int32, (D, HALF), 0)
    want = jnp.zeros((D, HALF), jnp.int32)
    for q in range(8):
        dy, dz = q // 4, q % 4
        base = 96 * ((z ^ dz) * 2 + (y ^ dy)) + 48 * x - 48 * q
        want = jnp.where((lane >= 48 * q) & (lane < 48 * q + 48), lane + base, want)
    return jnp.where(row == want, 1.0, 0.0).astype(BF)


def statistics(values):
    center = values - jnp.mean(values, axis=-1, keepdims=True)
    rstd = lax.rsqrt(jnp.mean(center * center, axis=-1, keepdims=True) + NORM_EPS)
    return center * rstd, rstd


def norm_back(grad, z, rstd):
    return rstd * (
        grad
        - jnp.mean(grad, axis=-1, keepdims=True)
        - z * jnp.mean(grad * z, axis=-1, keepdims=True)
    )


def gather_bands(blocks, dst, sems):
    band = lax.axis_index("band")
    copies = []
    for k, block in enumerate(blocks):
        at = pl.multiple_of((band ^ k) * BAND, BAND)
        copy = pltpu.make_async_copy(block, dst.at[:, pl.ds(at, BAND), :], sems.at[k])
        copy.start()
        copies.append(copy)
    return copies


def head_probs(q2, k2, e, key_ok):
    lane = lax.broadcasted_iota(jnp.int32, (PACK, 128), 1)
    mine = (lane < HD) if e == 0 else (lane >= HD)
    qm = jnp.where(mine, q2, jnp.zeros_like(q2))
    scores = jnp.where(key_ok, dot_nt(qm, k2) * (1.0 / math.sqrt(HD)), -1e30)
    raised = jnp.exp(scores - jnp.max(scores, axis=-1, keepdims=True))
    return raised / jnp.sum(raised, axis=-1, keepdims=True)


def keys_shown(pos, image):
    shown = jnp.sum(jnp.where(pos[image : image + 1, :] >= 0, 1.0, 0.0), axis=-1, keepdims=True)
    return lax.broadcasted_iota(jnp.int32, (1, PACK), 1).astype(F32) < shown


def first_kernel(
    t0, t1, t2, t3, va, vb, gain, bias, wqkv, qvb,
    tok_o, norm_o, qkv_o, mix_o, pos_o,
    xs, w, sems,
):
    _, c, _, _ = place()
    copies = gather_bands((t0, t1, t2, t3), xs, sems)
    heads = pl.multiple_of(c * HALF, 128)
    loads = []
    for m in range(3):
        src = wqkv.at[:, pl.ds(pl.multiple_of(m * D + c * HALF, 128), HALF)]
        loads.append(pltpu.make_async_copy(src, w.at[m], sems.at[4 + m]))
        loads[-1].start()
    vis = va[...] + vb[...]
    upto = lax.broadcasted_iota(jnp.int32, (SLOTS, SLOTS), 0)
    slot = lax.broadcasted_iota(jnp.int32, (SLOTS, SLOTS), 1)
    before = jnp.where(upto < slot, 1.0, 0.0).astype(BF)
    pos = jnp.where(vis > 0, dot(vis.astype(BF), before), -1.0)
    pos_o[...] = pos
    for copy in copies:
        copy.wait()
    for i in range(IMGS):
        rows = slice(i * PACK, (i + 1) * PACK)
        tok = dot(one_hot_pack(pos, i), xs[i])
        tok_o[rows, :] = tok.astype(BF)
        z, _ = statistics(tok)
        norm_o[rows, :] = (z * gain[...] + bias[...]).astype(BF)
    normed = norm_o[...]
    for m in range(3):
        loads[m].wait()
        part = dot(normed, w[m])
        if m != 1:
            part = part + qvb[m // 2 : m // 2 + 1, pl.ds(heads, HALF)]
        qkv_o[m] = part.astype(BF)
    lane = lax.broadcasted_iota(jnp.int32, (PACK, 128), 1)
    for i in range(IMGS):
        rows = slice(i * PACK, (i + 1) * PACK)
        key_ok = keys_shown(pos, i)
        for hp in range(3):
            cols = slice(hp * 128, (hp + 1) * 128)
            q2, k2, v2 = (qkv_o[m, rows, cols] for m in range(3))
            outs = [dot(head_probs(q2, k2, e, key_ok).astype(BF), v2) for e in range(2)]
            mix_o[rows, cols] = jnp.where(lane < HD, outs[0], outs[1]).astype(BF)


def second_kernel(
    mix_a, mix_b, tok, c0, c1, c2, c3, pos_r, wp, bp, a_scale, gain, bias, we, be, wr, br, m_scale,
    res_o, one_o, pre_o, gb2_o, n2_o, mix_o, act_o, gh_o, gn2_o, bt2_o, small_o,
    xs, we_v, wr_v, act_v, sems,
):
    x, c, _, _ = place()
    mine, other = pl.multiple_of(c * HALF, 128), pl.multiple_of((1 - c) * HALF, 128)
    copy_a = pltpu.make_async_copy(mix_a, mix_o.at[:, pl.ds(mine, HALF)], sems.at[6])
    copy_b = pltpu.make_async_copy(mix_b, mix_o.at[:, pl.ds(other, HALF)], sems.at[7])
    copy_a.start()
    copy_b.start()
    copies = gather_bands((c0, c1, c2, c3), xs, sems)
    units = pl.multiple_of(c * FH, 128)
    load_e = pltpu.make_async_copy(we.at[:, pl.ds(units, FH)], we_v, sems.at[4])
    load_r = pltpu.make_async_copy(wr.at[pl.ds(units, FH), :], wr_v, sems.at[5])
    load_e.start()
    load_r.start()
    pos = pos_r[...]
    copy_a.wait()
    copy_b.wait()
    one = dot(mix_o[...], wp[...]) + bp[...]
    one_o[...] = one
    residual = tok[...].astype(F32) + a_scale[...] * one
    res_o[...] = residual
    z, _ = statistics(residual)
    n2_o[...] = (z * gain[...] + bias[...]).astype(BF)
    for copy in copies:
        copy.wait()
    for i in range(IMGS):
        rows = slice(i * PACK, (i + 1) * PACK)
        pre = dot(one_hot_pack(pos, i), xs[i])
        pre_o[rows, :] = pre.astype(BF)
        gb2_o[rows, :] = (m_scale[...] * pre).astype(BF)
    load_e.wait()
    load_r.wait()
    step = 256
    for f in range(FH // step):
        cols = slice(f * step, (f + 1) * step)
        shift = be[:, pl.ds(pl.multiple_of(c * FH + f * step, 128), step)]
        hidden = dot(n2_o[...], we_v[:, cols]) + shift
        phi = 0.5 * (1.0 + lax.erf(hidden * math.sqrt(0.5)))
        act_v[:, cols] = (hidden * phi).astype(BF)
        slope = phi + hidden * (jnp.exp(-0.5 * hidden * hidden) * (1.0 / math.sqrt(2.0 * math.pi)))
        back = dot_nt(gb2_o[...], wr_v[cols, :])
        gh_o[:, cols] = (back * slope).astype(BF)
    gn2_o[...] = dot_nt(gh_o[...], we_v[...]).astype(BF)
    act_o[...] = act_v[:, pl.ds(pl.multiple_of(x * D, 128), D)]
    two = dot(act_v[...], wr_v[...])
    bt2_o[...] = two.astype(BF)
    pre = pre_o[...].astype(F32)
    first = jnp.where(c == 0, 1.0, 0.0)
    small_o[...] = jnp.zeros_like(small_o)
    small_o[0:1, :] = first * jnp.sum(gb2_o[...].astype(F32), axis=0, keepdims=True)
    small_o[1:2, :] = jnp.sum(pre * (two + first * br[...]), axis=0, keepdims=True)


def mlp_grads_kernel(n2, gh, act, gb2, wr_send, wr_keep, we_send, we_keep, eb_o, full, sums):
    x, c, z, y = place()
    full[...] = dot_tn(act[...], gb2[...])
    for dy, out in ((1, wr_send), (0, wr_keep)):
        for dz in range(4):
            k = 4 * (y ^ dy) + (z ^ dz)
            out[dz] = full[pl.ds(pl.multiple_of(96 * k, 96), 96), :].astype(BF)
    picked = dot(n2[...], feature_pick()).astype(BF)
    for dy, out in ((1, we_send), (0, we_keep)):
        for dz in range(4):
            lo = 192 * dy + 48 * dz
            out[dz] = dot_tn(picked[:, lo : lo + 48], gh[...]).astype(BF)
    sums[...] = dot_tn(gh[...], jnp.ones((ROWS, 128), BF))
    lane = lax.broadcasted_iota(jnp.int32, (48, SMALL), 1)
    for q in range(8):
        b = (z ^ (q % 4)) * 2 + (y ^ (q // 4))
        here = (b >> 2) == c
        block = jnp.zeros((48, SMALL), F32)
        for k in range(4):
            at = pl.multiple_of(384 * (b & 3) + 192 * x + 48 * k, 48)
            block = jnp.where((lane == 10 + k) & here, sums[pl.ds(at, 48), :], block)
        eb_o[q] = block


def third_kernel(
    gn2_a, gn2_b, res, one, pre, tok, normed, qkv, mix, pos_r, small2, eb, wp, wqkv, a_scale, gain2, gain1,
    gres_o, gnp_o, send_o, keep_o,
    w, wp_v, gp, vecs, sems,
):
    x, c, z, y = place()
    heads = pl.multiple_of(c * HALF, 128)
    loads = []
    for m in range(3):
        src = wqkv.at[:, pl.ds(pl.multiple_of(m * D + c * HALF, 128), HALF)]
        loads.append(pltpu.make_async_copy(src, w.at[m], sems.at[m]))
        loads[-1].start()
    load_p = pltpu.make_async_copy(wp.at[pl.ds(heads, HALF), :], wp_v, sems.at[3])
    load_p.start()
    first = jnp.where(c == 0, 1.0, 0.0)

    def total(v):
        return jnp.sum(v, axis=0, keepdims=True)

    vecs[...] = jnp.zeros_like(vecs)
    gn2 = gn2_a[...].astype(F32) + gn2_b[...].astype(F32)
    z2, rstd2 = statistics(res[...])
    vecs[6:7, :] = first * total(gn2 * z2)
    vecs[7:8, :] = first * total(gn2)
    gres = pre[...].astype(F32) + norm_back(gn2 * gain2[...], z2, rstd2)
    gres_o[...] = gres
    vecs[5:6, :] = first * total(gres * one[...])
    gb1 = (a_scale[...] * gres).astype(BF)
    vecs[4:5, :] = first * total(gb1.astype(F32))
    vecs[8:10, :] = small2[0:2, :]
    load_p.wait()
    gm = dot_nt(gb1, wp_v[...]).astype(BF)
    pos = pos_r[...]
    lane = lax.broadcasted_iota(jnp.int32, (PACK, 128), 1)
    scale = 1.0 / math.sqrt(HD)
    for i in range(IMGS):
        rows = slice(i * PACK, (i + 1) * PACK)
        key_ok = keys_shown(pos, i)
        for hp in range(3):
            cols = slice(hp * 128, (hp + 1) * 128)
            q2, k2, v2 = (qkv[m, rows, cols] for m in range(3))
            g2 = gm[rows, cols]
            grads = []
            for e in range(2):
                probs = head_probs(q2, k2, e, key_ok)
                gmine = jnp.where((lane < HD) if e == 0 else (lane >= HD), g2, jnp.zeros_like(g2))
                gprob = dot_nt(gmine, v2)
                delta = jnp.sum(probs * gprob, axis=-1, keepdims=True)
                gscore = (probs * (gprob - delta)).astype(BF)
                grads.append(
                    (
                        dot(gscore, k2) * scale,
                        dot_tn(gscore, q2) * scale,
                        dot_tn(probs.astype(BF), g2),
                    )
                )
            for m in range(3):
                both = jnp.where(lane < HD, grads[0][m], grads[1][m])
                gp[rows, m * HALF + hp * 128 : m * HALF + (hp + 1) * 128] = both.astype(BF)
    gnp = jnp.zeros((ROWS, D), F32)
    for m in range(3):
        loads[m].wait()
        gnp = gnp + dot_nt(gp[:, m * HALF : (m + 1) * HALF], w[m])
    gnp_o[...] = gnp.astype(BF)
    z1, _ = statistics(tok[...].astype(F32))
    vecs[0:1, :] = total(gnp * z1)
    vecs[1:2, :] = total(gnp)
    vecs[2:3, pl.ds(heads, HALF)] = total(gp[:, 0:HALF].astype(F32))
    vecs[3:4, pl.ds(heads, HALF)] = total(gp[:, 2 * HALF : 3 * HALF].astype(F32))
    pick = feature_pick()
    picked = dot(normed[...], pick).astype(BF)
    rowl = lax.broadcasted_iota(jnp.int32, (D, 256), 0)
    colr = lax.broadcasted_iota(jnp.int32, (D, 256), 1)
    want = jnp.full((D, 256), -1, jnp.int32)
    for q in range(8):
        base = 96 * ((z ^ (q % 4)) * 2 + (y ^ (q // 4))) + 48 * x + 24 * c - 32 * q
        want = jnp.where((colr >= 32 * q) & (colr < 32 * q + 24), colr + base, want)
    pick_p = jnp.where(rowl == want, 1.0, 0.0).astype(BF)
    mixed = dot(mix[...], pick_p).astype(BF)
    vec_cols = lax.dot_general(
        pick, vecs[...].astype(BF), (((0,), (1,)), ((), ())), preferred_element_type=F32
    )
    for dy, out in ((1, send_o), (0, keep_o)):
        for dz in range(4):
            q = 4 * dy + dz
            lo = 48 * q
            out[dz, :, 0 : 3 * HALF] = dot_tn(picked[:, lo : lo + 48], gp[...]).astype(BF)
            out[dz, :, 3 * HALF : 3 * HALF + SMALL] = (vec_cols[lo : lo + 48] + eb[q]).astype(BF)
            proj = dot_tn(mixed[:, 32 * q : 32 * q + 32], gb1).astype(BF)
            out[dz, 0:32, 1280:1792] = proj[:, 0:512]
            out[dz, 32:48, 1280:1536] = proj[0:16, 512:768]
            out[dz, 32:48, 1536:1792] = proj[16:32, 512:768]


def last_kernel(gnp_a, gnp_b, tok, gres, bt2_a, bt2_b, res, pos_r, gain1, m_scale, br, out_o, gtok_o, wide):
    band = lax.axis_index("band")
    at = pl.multiple_of(band * BAND, BAND)
    pos = pos_r[...]
    for i in range(IMGS):
        rows = slice(i * PACK, (i + 1) * PACK)
        z1, rstd1 = statistics(tok[rows, :].astype(F32))
        gnp = gnp_a[rows, :].astype(F32) + gnp_b[rows, :].astype(F32)
        gtok = (gres[rows, :] + norm_back(gnp * gain1[...], z1, rstd1)).astype(BF)
        two = bt2_a[rows, :].astype(F32) + bt2_b[rows, :].astype(F32) + br[...]
        out = (res[rows, :] + m_scale[...] * two).astype(BF)
        pack = one_hot_pack(pos, i)
        for value, dst in ((gtok, gtok_o), (out, out_o)):
            wide[...] = dot_tn(pack, value)
            dst[i] = wide[pl.ds(at, BAND), :].astype(BF)


def call(kernel, outs, specs, scratch=(), flops=0, nbytes=0, vmem=40):
    return pl.pallas_call(
        kernel,
        out_shape=outs,
        in_specs=specs,
        out_specs=jax.tree.map(lambda _: VM, outs),
        scratch_shapes=list(scratch),
        compiler_params=pltpu.CompilerParams(vmem_limit_bytes=vmem * MIB),
        cost_estimate=pl.CostEstimate(flops=flops, bytes_accessed=nbytes, transcendentals=0),
    )


def by_core(value):
    return lax.ppermute(value, "band", [(i, i ^ 1) for i in range(4)])


def by_x(value):
    return lax.ppermute(value, "band", [(i, i ^ 2) for i in range(4)])


def by_y(value):
    return lax.ppermute(value, "batch", [(i, i ^ 1) for i in range(8)])


def by_z(value, dz):
    return lax.ppermute(value, "batch", [(i, i ^ (2 * dz)) for i in range(8)])


def reduce_shards(send, keep):
    arrived = by_y(send)
    both = keep.astype(F32) + arrived.astype(F32)
    parts = [by_z(both[dz].astype(BF), dz) for dz in (1, 2, 3)]
    return both[0] + parts[0].astype(F32) + parts[1].astype(F32) + parts[2].astype(F32)


def packed_body(
    tokens, cotangent, visible, first_gain, first_bias, qkv_weight, qv_bias, proj_weight, proj_bias,
    attn_scale, second_gain, second_bias, expand_weight, expand_bias, reduce_weight, reduce_bias, mlp_scale,
):
    band = lax.axis_index("band")
    core = band & 1
    row = lambda v: v.reshape(1, -1)
    g1, b1, g2, b2 = row(first_gain), row(first_bias), row(second_gain), row(second_bias)
    bp, asc, br, msc, be = row(proj_bias), row(attn_scale), row(reduce_bias), row(mlp_scale), row(expand_bias)

    tok_x = by_x(tokens)
    spread = lax.dynamic_update_slice(
        jnp.zeros((8, SLOTS), F32), visible.astype(F32), (jnp.int32(0), band * BAND)
    )
    vis_x = by_x(spread)
    cot_x = by_x(cotangent)
    tok_c = by_core(tokens)
    vis_chip = spread + vis_x
    vis_c = by_core(vis_chip)
    tok_d = by_core(tok_x)
    cot_c = by_core(cotangent)
    cot_d = by_core(cot_x)

    tok, normed, qkv, mix_own, pos = call(
        first_kernel,
        (
            sds((ROWS, D), BF),
            sds((ROWS, D), BF),
            sds((3, ROWS, HALF), BF),
            sds((ROWS, HALF), BF),
            sds((8, SLOTS), F32),
        ),
        [ANY] * 4 + [VM] * 4 + [ANY, VM],
        [
            pltpu.VMEM((IMGS, SLOTS, D), BF),
            pltpu.VMEM((3, D, HALF), BF),
            pltpu.SemaphoreType.DMA((7,)),
        ],
        flops=int(1.5e9),
        nbytes=int(6e6),
    )(tokens, tok_c, tok_x, tok_d, vis_chip, vis_c, g1, b1, qkv_weight, qv_bias)
    mix_other = by_core(mix_own)
    res, one, pre, gb2, n2, mix, act, gh, gn2, bt2, small2 = call(
        second_kernel,
        (
            sds((ROWS, D), F32),
            sds((ROWS, D), F32),
            sds((ROWS, D), BF),
            sds((ROWS, D), BF),
            sds((ROWS, D), BF),
            sds((ROWS, D), BF),
            sds((ROWS, D), BF),
            sds((ROWS, FH), BF),
            sds((ROWS, D), BF),
            sds((ROWS, D), BF),
            sds((8, D), F32),
        ),
        [ANY] * 2 + [VM] + [ANY] * 4 + [VM] * 6 + [ANY, VM, ANY] + [VM] * 2,
        [
            pltpu.VMEM((IMGS, SLOTS, D), BF),
            pltpu.VMEM((D, FH), BF),
            pltpu.VMEM((FH, D), BF),
            pltpu.VMEM((ROWS, FH), BF),
            pltpu.SemaphoreType.DMA((8,)),
        ],
        flops=int(5e9),
        nbytes=int(15e6),
    )(
        mix_own, mix_other, tok, cotangent, cot_c, cot_x, cot_d, pos, proj_weight, bp, asc, g2, b2,
        expand_weight, be, reduce_weight, br, msc,
    )
    gn2_other = by_core(gn2)
    wr_send, wr_keep, we_send, we_keep, eb = call(
        mlp_grads_kernel,
        (
            sds((4, 96, D), BF),
            sds((4, 96, D), BF),
            sds((4, 48, FH), BF),
            sds((4, 48, FH), BF),
            sds((8, 48, SMALL), F32),
        ),
        [VM] * 4,
        [pltpu.VMEM((D, D), F32), pltpu.VMEM((FH, 128), F32)],
        flops=int(2e9),
        nbytes=int(6e6),
    )(n2, gh, act, gb2)
    wr_sum = reduce_shards(wr_send, wr_keep)
    we_sum = reduce_shards(we_send, we_keep)
    gres, gnp, qp_send, qp_keep = call(
        third_kernel,
        (
            sds((ROWS, D), F32),
            sds((ROWS, D), BF),
            sds((4, 48, 1792), BF),
            sds((4, 48, 1792), BF),
        ),
        [VM] * 12 + [ANY] * 2 + [VM] * 3,
        [
            pltpu.VMEM((3, D, HALF), BF),
            pltpu.VMEM((HALF, D), BF),
            pltpu.VMEM((ROWS, 3 * HALF), BF),
            pltpu.VMEM((SMALL, D), F32),
            pltpu.SemaphoreType.DMA((4,)),
        ],
        flops=int(4e9),
        nbytes=int(12e6),
    )(
        gn2, gn2_other, res, one, pre, tok, normed, qkv, mix, pos, small2, eb, proj_weight, qkv_weight,
        asc, g2, g1,
    )
    qp_sum = reduce_shards(qp_send, qp_keep)
    bt2_other = by_core(bt2)
    gnp_other = by_core(gnp)
    layer_out, grad_tokens = call(
        last_kernel,
        (sds((IMGS, BAND, D), BF), sds((IMGS, BAND, D), BF)),
        [VM] * 11,
        [pltpu.VMEM((SLOTS, D), F32)],
        flops=int(1e9),
        nbytes=int(8e6),
    )(gnp, gnp_other, tok, gres, bt2, bt2_other, res, pos, g1, msc, br)

    moves = []
    for b in range(8):
        for g in range(4):
            z, y, x, c = b >> 1, b & 1, g >> 1, g & 1
            moves.append((b * 4 + g, ((2 * c + x) * 2 + y) * 4 + z))
    grad_reduce = lax.ppermute(wr_sum, ("batch", "band"), moves)

    def swap(mine):
        keep = jnp.where(core == 0, mine[0:24], mine[24:48])
        other = by_core(jnp.where(core == 0, mine[24:48], mine[0:24]))
        first = jnp.where(core == 0, keep, other)
        second = jnp.where(core == 0, other, keep)
        return first, second

    grad_expand = jnp.concatenate(swap(we_sum), axis=1)
    qkv_first, qkv_second = swap(qp_sum[:, 0 : 3 * HALF])
    pieces = []
    for m in range(3):
        cols = slice(m * HALF, (m + 1) * HALF)
        pieces += [qkv_first[:, cols], qkv_second[:, cols]]
    grad_qkv = jnp.concatenate(pieces, axis=1)
    vec = qp_sum[:, 3 * HALF : 3 * HALF + SMALL]
    vec = vec + by_core(vec)
    own = jnp.where(core == 0, vec[0:24], vec[24:48]).T
    grad_expand_bias = jnp.where(core == 0, vec[:, 10:12], vec[:, 12:14]).T.reshape(96)
    proj = jnp.concatenate(
        [
            qp_sum[0:32, 1280:1792],
            jnp.concatenate([qp_sum[32:48, 1280:1536], qp_sum[32:48, 1536:1792]], axis=0),
        ],
        axis=1,
    )[0:24]
    return (
        layer_out, grad_tokens, own[0], own[1], grad_qkv, own[2:4], proj, own[4], own[5], own[6], own[7],
        grad_expand, grad_expand_bias, grad_reduce, own[8], own[9],
    )


def layer_norm(values, norm_gain, norm_shift):
    center = values - jnp.mean(values, axis=-1, keepdims=True)
    spread = jnp.mean(center * center, axis=-1, keepdims=True)
    return center * lax.rsqrt(spread + NORM_EPS) * norm_gain + norm_shift


def gelu_exact(values):
    return jax.nn.gelu(values, approximate=False)


def split_rows(packed_rows, mask_rows):
    item_count = packed_rows.shape[0]
    slot_count = packed_rows.shape[1]
    heads_here = packed_rows.shape[4] // HD
    unpacked = packed_rows.reshape(item_count, slot_count, 3, heads_here, HD)
    queries = unpacked[:, :, 0]
    key_rows = unpacked[:, :, 1]
    value_rows = unpacked[:, :, 2]
    key_valid = mask_rows.reshape(item_count, slot_count) > 0
    score_scale = 1.0 / math.sqrt(HD)
    scores = (
        jnp.einsum("bqhe,bkhe->bhqk", queries, key_rows, preferred_element_type=jnp.float32)
        * score_scale
    )
    scores = jnp.where(key_valid[:, None, None, :], scores, -1e30)
    return (queries, key_rows, value_rows, scores)


def attend_plain(inputs):
    packed_rows, mask_rows = inputs
    queries, key_rows, value_rows, scores = split_rows(packed_rows, mask_rows)
    row_top = jnp.max(scores, axis=-1, keepdims=True)
    raised = jnp.exp(scores - row_top)
    row_total = jnp.sum(raised, axis=-1, keepdims=True)
    attn_prob = raised / row_total
    log_total = (row_top + jnp.log(row_total))[..., 0]
    mixed_rows = jnp.einsum(
        "bhqk,bkhe->bqhe",
        attn_prob.astype(jnp.bfloat16),
        value_rows,
        preferred_element_type=jnp.float32,
    ).astype(jnp.bfloat16)
    mixed_rows = mixed_rows.reshape(
        packed_rows.shape[0], packed_rows.shape[1], packed_rows.shape[4]
    )
    return (mixed_rows, log_total)


def backward_rows(score_parts, log_total, grad_rows):
    queries, key_rows, value_rows, scores = score_parts
    item_count, slot_count, heads_here, head_size = queries.shape
    score_scale = 1.0 / math.sqrt(HD)
    attn_prob = jnp.exp(scores - log_total[..., None])
    grad_heads = grad_rows.reshape(item_count, slot_count, heads_here, head_size)
    grad_prob = jnp.einsum(
        "bqhe,bkhe->bhqk", grad_heads, value_rows, preferred_element_type=jnp.float32
    )
    row_delta = jnp.sum(attn_prob * grad_prob, axis=-1, keepdims=True)
    grad_score = (attn_prob * (grad_prob - row_delta)).astype(jnp.bfloat16)
    grad_query = (
        jnp.einsum("bhqk,bkhe->bqhe", grad_score, key_rows, preferred_element_type=jnp.float32)
        * score_scale
    )
    grad_key = (
        jnp.einsum("bhqk,bqhe->bkhe", grad_score, queries, preferred_element_type=jnp.float32)
        * score_scale
    )
    grad_value = jnp.einsum(
        "bhqk,bqhe->bkhe",
        attn_prob.astype(jnp.bfloat16),
        grad_heads,
        preferred_element_type=jnp.float32,
    )
    stacked = jnp.stack([grad_query, grad_key, grad_value], axis=2)
    return stacked.reshape(item_count, slot_count, 3, 1, heads_here * head_size).astype(
        jnp.bfloat16
    )


def attend_again(inputs):
    packed_rows, mask_rows, grad_rows = inputs
    score_parts = split_rows(packed_rows, mask_rows)
    scores = score_parts[3]
    row_top = jnp.max(scores, axis=-1, keepdims=True)
    log_total = (row_top + jnp.log(jnp.sum(jnp.exp(scores - row_top), axis=-1, keepdims=True)))[
        ..., 0
    ]
    return backward_rows(score_parts, log_total, grad_rows)


def body(
    tokens,
    cotangent,
    visible,
    first_gain,
    first_bias,
    qkv_weight,
    qv_bias,
    proj_weight,
    proj_bias,
    attn_scale,
    second_gain,
    second_bias,
    expand_weight,
    expand_bias,
    reduce_weight,
    reduce_bias,
    mlp_scale,
):
    images, slot_count, model_width = tokens.shape
    groups = lax.axis_size("band")
    local_width = model_width // groups
    inputs_full = tokens.astype(jnp.float32)
    shown_mask = visible.astype(jnp.float32)
    normed, first_pull = jax.vjp(layer_norm, inputs_full, first_gain, first_bias)
    normed_low = normed.astype(jnp.bfloat16)
    qkv_bias = jnp.concatenate([qv_bias[0], jnp.zeros((model_width,), jnp.float32), qv_bias[1]])

    def project_qkv():
        product = jnp.einsum(
            "isd,de->ise", normed_low, qkv_weight, preferred_element_type=jnp.float32
        )
        return (
            (product + qkv_bias)
            .astype(jnp.bfloat16)
            .reshape(images, slot_count, 3, groups, local_width)
        )

    packed = project_qkv()
    mask_part = jnp.broadcast_to(
        shown_mask.astype(jnp.bfloat16)[:, :, None, None, None], (images, slot_count, 1, groups, 1)
    )
    results = attend_plain(
        (
            lax.all_to_all(packed, "band", split_axis=3, concat_axis=1, tiled=True),
            lax.all_to_all(mask_part, "band", split_axis=3, concat_axis=1, tiled=True),
        )
    )
    mixed_heads = results[0].reshape(images, groups * slot_count, 1, local_width)
    back_rows = lax.all_to_all(mixed_heads, "band", split_axis=1, concat_axis=2, tiled=True)
    mixed_rows = back_rows.reshape(images, slot_count, model_width)
    branch_one = (
        jnp.einsum("isd,de->ise", mixed_rows, proj_weight, preferred_element_type=jnp.float32)
        + proj_bias
    )
    residual = inputs_full + attn_scale * branch_one
    normed_two, second_pull = jax.vjp(layer_norm, residual, second_gain, second_bias)
    normed_two_low = normed_two.astype(jnp.bfloat16)
    hidden = (
        jnp.einsum("isd,df->isf", normed_two_low, expand_weight, preferred_element_type=jnp.float32)
        + expand_bias
    )
    activated, gelu_pull = jax.vjp(gelu_exact, hidden)
    activated_low = activated.astype(jnp.bfloat16)
    branch_two = (
        jnp.einsum("isf,fd->isd", activated_low, reduce_weight, preferred_element_type=jnp.float32)
        + reduce_bias
    )
    layer_out = (shown_mask[..., None] * (residual + mlp_scale * branch_two)).astype(jnp.bfloat16)
    grad_pre = shown_mask[..., None] * cotangent.astype(jnp.float32)
    grad_mlp_scale = jnp.sum(grad_pre * branch_two, axis=(0, 1))
    grad_branch_two = (mlp_scale * grad_pre).astype(jnp.bfloat16)
    grad_reduce_weight = jnp.einsum(
        "isf,isd->fd", activated_low, grad_branch_two, preferred_element_type=jnp.float32
    )
    grad_reduce_bias = jnp.sum(grad_branch_two.astype(jnp.float32), axis=(0, 1))
    grad_activated = jnp.einsum(
        "isd,fd->isf", grad_branch_two, reduce_weight, preferred_element_type=jnp.float32
    )
    grad_hidden = gelu_pull(grad_activated)[0].astype(jnp.bfloat16)
    grad_expand_weight = jnp.einsum(
        "isd,isf->df", normed_two_low, grad_hidden, preferred_element_type=jnp.float32
    )
    grad_expand_bias = jnp.sum(grad_hidden.astype(jnp.float32), axis=(0, 1))
    grad_normed_two = jnp.einsum(
        "isf,df->isd", grad_hidden, expand_weight, preferred_element_type=jnp.float32
    )
    grad_resid_norm, grad_second_gain, grad_second_bias = second_pull(grad_normed_two)
    grad_residual = grad_pre + grad_resid_norm
    grad_attn_scale = jnp.sum(grad_residual * branch_one, axis=(0, 1))
    grad_branch_one = (attn_scale * grad_residual).astype(jnp.bfloat16)
    grad_proj_weight = jnp.einsum(
        "isd,ise->de", mixed_rows, grad_branch_one, preferred_element_type=jnp.float32
    )
    grad_proj_bias = jnp.sum(grad_branch_one.astype(jnp.float32), axis=(0, 1))
    grad_mixed = jnp.einsum(
        "ise,de->isd", grad_branch_one, proj_weight, preferred_element_type=jnp.float32
    )
    grad_mixed = grad_mixed.astype(jnp.bfloat16).reshape(images, slot_count, 1, groups, local_width)
    repacked = project_qkv()
    grad_packed = attend_again(
        (
            lax.all_to_all(repacked, "band", split_axis=3, concat_axis=1, tiled=True),
            lax.all_to_all(mask_part, "band", split_axis=3, concat_axis=1, tiled=True),
            lax.all_to_all(grad_mixed, "band", split_axis=3, concat_axis=1, tiled=True),
        )
    )
    grad_bands = lax.all_to_all(grad_packed, "band", split_axis=1, concat_axis=3, tiled=True)
    grad_qkv = grad_bands.reshape(images, slot_count, 3 * model_width)
    grad_qkv_weight = jnp.einsum(
        "isd,ise->de", normed_low, grad_qkv, preferred_element_type=jnp.float32
    )
    column_sums = jnp.sum(grad_qkv.astype(jnp.float32), axis=(0, 1))
    grad_qv_bias = jnp.stack([column_sums[:model_width], column_sums[2 * model_width :]])
    grad_normed = jnp.einsum(
        "ise,de->isd", grad_qkv, qkv_weight, preferred_element_type=jnp.float32
    )
    grad_input_norm, grad_first_gain, grad_first_bias = first_pull(grad_normed)
    grad_tokens = (grad_residual + grad_input_norm).astype(jnp.bfloat16)
    all_sums = (
        lax.psum_scatter(grad_first_gain, ("batch", "band"), scatter_dimension=0, tiled=True),
        lax.psum_scatter(grad_first_bias, ("batch", "band"), scatter_dimension=0, tiled=True),
        lax.psum_scatter(grad_qkv_weight, ("batch", "band"), scatter_dimension=0, tiled=True),
        lax.psum_scatter(grad_qv_bias, ("batch", "band"), scatter_dimension=1, tiled=True),
        lax.psum_scatter(grad_proj_weight, ("batch", "band"), scatter_dimension=0, tiled=True),
        lax.psum_scatter(grad_proj_bias, ("batch", "band"), scatter_dimension=0, tiled=True),
        lax.psum_scatter(grad_attn_scale, ("batch", "band"), scatter_dimension=0, tiled=True),
        lax.psum_scatter(grad_second_gain, ("batch", "band"), scatter_dimension=0, tiled=True),
        lax.psum_scatter(grad_second_bias, ("batch", "band"), scatter_dimension=0, tiled=True),
        lax.psum_scatter(grad_expand_weight, ("batch", "band"), scatter_dimension=0, tiled=True),
        lax.psum_scatter(grad_expand_bias, ("batch", "band"), scatter_dimension=0, tiled=True),
        lax.psum_scatter(grad_reduce_weight, ("batch", "band"), scatter_dimension=0, tiled=True),
        lax.psum_scatter(grad_reduce_bias, ("batch", "band"), scatter_dimension=0, tiled=True),
        lax.psum_scatter(grad_mlp_scale, ("batch", "band"), scatter_dimension=0, tiled=True),
    )
    (
        sum_first_gain,
        sum_first_bias,
        sum_qkv_weight,
        sum_qv_bias,
        sum_proj_weight,
        sum_proj_bias,
        sum_attn_scale,
        sum_second_gain,
        sum_second_bias,
        sum_expand_weight,
        sum_expand_bias,
        sum_reduce_weight,
        sum_reduce_bias,
        sum_mlp_scale,
    ) = all_sums
    return (
        layer_out,
        grad_tokens,
        sum_first_gain,
        sum_first_bias,
        sum_qkv_weight,
        sum_qv_bias,
        sum_proj_weight,
        sum_proj_bias,
        sum_attn_scale,
        sum_second_gain,
        sum_second_bias,
        sum_expand_weight,
        sum_expand_bias,
        sum_reduce_weight,
        sum_reduce_bias,
        sum_mlp_scale,
    )


def solution(mesh):
    sizes = dict(mesh.shape)
    chosen = packed_body if (sizes["batch"], sizes["band"]) == (8, 4) else body
    placed = (
        P("batch", "band", None),
        P("batch", "band", None),
        P("batch", "band"),
        P(),
        P(),
        P(),
        P(),
        P(),
        P(),
        P(),
        P(),
        P(),
        P(),
        P(),
        P(),
        P(),
        P(),
    )
    return jax.shard_map(
        chosen,
        mesh=mesh,
        in_specs=placed,
        out_specs=(
            P("batch", "band", None),
            P("batch", "band", None),
            P(("batch", "band")),
            P(("batch", "band")),
            P(("batch", "band"), None),
            P(None, ("batch", "band")),
            P(("batch", "band"), None),
            P(("batch", "band")),
            P(("batch", "band")),
            P(("batch", "band")),
            P(("batch", "band")),
            P(("batch", "band"), None),
            P(("batch", "band")),
            P(("batch", "band"), None),
            P(("batch", "band")),
            P(("batch", "band")),
        ),
        check_vma=False,
    )
```

```python
import functools
import math

import jax
import jax.numpy as jnp
from jax import lax
from jax.experimental import pallas as pl
from jax.experimental.pallas import tpu as pltpu
from jax.sharding import PartitionSpec as P

HD = 64
NORM_EPS = 1e-06
PACK = 144
SLOTS = 256
BAND = 64
IMGS = 3
ROWS = IMGS * PACK
D = 768
HALF = D // 2
FF = 3072
FH = FF // 2
SMALL = 128
MIB = 1024 * 1024
F32 = jnp.float32
BF = jnp.bfloat16
ANY = pl.BlockSpec(memory_space=pl.ANY)
HBM = pl.BlockSpec(memory_space=pltpu.HBM)
VM = pl.BlockSpec(memory_space=pltpu.VMEM)


def dot(a, b):
    return jnp.dot(a, b, preferred_element_type=F32)


def dot_nt(a, b):
    return lax.dot_general(a, b, (((1,), (1,)), ((), ())), preferred_element_type=F32)


def dot_tn(a, b):
    return lax.dot_general(a, b, (((0,), (0,)), ((), ())), preferred_element_type=F32)


def sds(shape, dtype):
    return jax.ShapeDtypeStruct(shape, dtype)


def vm(shape, dtype):
    return pltpu.VMEM(shape, dtype)


def stay(value):
    return pltpu.with_memory_space_constraint(value, pltpu.HBM)


def place():
    band = lax.axis_index("band")
    batch = lax.axis_index("batch")
    return band >> 1, band & 1, batch >> 1, batch & 1


def one_hot_pack(pos, image):
    rows = lax.broadcasted_iota(jnp.int32, (PACK, SLOTS), 0).astype(F32)
    return jnp.where(rows == pos[image : image + 1, :], 1.0, 0.0).astype(BF)


def feature_pick():
    x, _, z, y = place()
    lane = lax.broadcasted_iota(jnp.int32, (D, HALF), 1)
    row = lax.broadcasted_iota(jnp.int32, (D, HALF), 0)
    want = jnp.zeros((D, HALF), jnp.int32)
    for q in range(8):
        dy, dz = q // 4, q % 4
        base = 96 * ((z ^ dz) * 2 + (y ^ dy)) + 48 * x - 48 * q
        want = jnp.where((lane >= 48 * q) & (lane < 48 * q + 48), lane + base, want)
    return jnp.where(row == want, 1.0, 0.0).astype(BF)


def statistics(values):
    center = values - jnp.mean(values, axis=-1, keepdims=True)
    rstd = lax.rsqrt(jnp.mean(center * center, axis=-1, keepdims=True) + NORM_EPS)
    return center * rstd, rstd


def norm_back(grad, z, rstd):
    return rstd * (
        grad
        - jnp.mean(grad, axis=-1, keepdims=True)
        - z * jnp.mean(grad * z, axis=-1, keepdims=True)
    )


def gather_bands(blocks, dst):
    band = lax.axis_index("band")
    for k, block in enumerate(blocks):
        at = pl.multiple_of((band ^ k) * BAND, BAND)
        for i in range(IMGS):
            dst[i, pl.ds(at, BAND), :] = block[i]


def two_heads(v):
    lane = lax.broadcasted_iota(jnp.int32, v.shape, 1)
    none = jnp.zeros_like(v)
    return jnp.concatenate([jnp.where(lane < HD, v, none), jnp.where(lane < HD, none, v)], axis=0)


def join_heads(v):
    lane = lax.broadcasted_iota(jnp.int32, (PACK, 128), 1)
    return jnp.where(lane < HD, v[:PACK], v[PACK:])


def keys_shown(pos, image):
    shown = jnp.sum(jnp.where(pos[image : image + 1, :] >= 0, 1.0, 0.0), axis=-1, keepdims=True)
    return lax.broadcasted_iota(jnp.int32, (1, PACK), 1).astype(F32) < shown


TICK = vm((8, 128), F32)
GAIN1, BIAS1, QB, VB, PB, ASC, GAIN2, BIAS2, RB, MSC = range(10)


def prepare_kernel(
    cot, gain1, bias1, qvb, bp, asc, gain2, bias2, br, msc, be, wqkv, wp, we, wr, vis, tok,
    cot_o, tok_o, par_o, be_o, wqkv_o, wp_o, we_o, wr_o, vis_o, sems,
):
    c = lax.axis_index("band") & 1
    units = pl.multiple_of(c * FH, 128)
    rows = (
        (GAIN1, gain1), (BIAS1, bias1), (QB, qvb.at[0]), (VB, qvb.at[1]), (PB, bp), (ASC, asc),
        (GAIN2, gain2), (BIAS2, bias2), (RB, br), (MSC, msc),
    )
    moves = [(cot, cot_o)] + [(v, par_o.at[r]) for r, v in rows]
    moves += [(be.at[pl.ds(units, FH)], be_o.at[0])]
    for m in range(3):
        moves.append((wqkv.at[:, pl.ds(pl.multiple_of(m * D + c * HALF, 128), HALF)], wqkv_o.at[m]))
    moves += [(wp, wp_o), (we.at[:, pl.ds(units, FH)], we_o), (wr.at[pl.ds(units, FH), :], wr_o)]
    moves += [(vis, vis_o), (tok, tok_o)]
    copies = [pltpu.make_async_copy(a, b, sems.at[i]) for i, (a, b) in enumerate(moves)]
    for copy in copies:
        copy.start()
    for copy in copies:
        copy.wait()


def hold_kernel(cot, tok, after_a, after_b, cot_o, tok_o):
    cot_o[...] = cot[...]
    tok_o[...] = tok[...]


def first_kernel(
    t0, t1, t2, t3, v0, v1, v2, v3, par, w,
    tok_o, norm_o, qkv_o, mix_o, pos_o, probs_o,
    xs, shown,
):
    band = lax.axis_index("band")
    c = band & 1
    gather_bands((t0, t1, t2, t3), xs)
    heads = pl.multiple_of(c * HALF, 128)
    to = lax.broadcasted_iota(jnp.int32, (BAND, SLOTS), 1) - lax.broadcasted_iota(jnp.int32, (BAND, SLOTS), 0)
    vis = jnp.zeros((16, SLOTS), F32)
    shown[...] = jnp.zeros_like(shown)
    for k, v in enumerate((v0, v1, v2, v3)):
        shown[0:IMGS, 0:BAND] = v[...].astype(F32)
        vis = vis + dot(shown[:, 0:BAND].astype(BF), jnp.where(to == (band ^ k) * BAND, 1.0, 0.0).astype(BF))
    upto = lax.broadcasted_iota(jnp.int32, (SLOTS, SLOTS), 0)
    slot = lax.broadcasted_iota(jnp.int32, (SLOTS, SLOTS), 1)
    before = jnp.where(upto < slot, 1.0, 0.0).astype(BF)
    pos = jnp.where(vis > 0, dot(vis.astype(BF), before), -1.0)
    pos_o[...] = pos[0:8]
    for i in range(IMGS):
        rows = slice(i * PACK, (i + 1) * PACK)
        tok = dot(one_hot_pack(pos, i), xs[i])
        tok_o[rows, :] = tok.astype(BF)
        z, _ = statistics(tok)
        norm_o[rows, :] = (z * par[GAIN1 : GAIN1 + 1, :] + par[BIAS1 : BIAS1 + 1, :]).astype(BF)
    normed = norm_o[...]
    for m in range(3):
        part = dot(normed, w[m])
        if m != 1:
            r = QB if m == 0 else VB
            part = part + par[r : r + 1, pl.ds(heads, HALF)]
        qkv_o[m] = part.astype(BF)
    for i in range(IMGS):
        rows = slice(i * PACK, (i + 1) * PACK)
        key_ok = keys_shown(pos, i)
        for hp in range(3):
            cols = slice(hp * 128, (hp + 1) * 128)
            q2, k2, v2 = (qkv_o[m, rows, cols] for m in range(3))
            scores = dot_nt(two_heads(q2), k2) * (1.0 / math.sqrt(HD))
            scores = jnp.where(key_ok, scores, -1e30)
            raised = jnp.exp(scores - jnp.max(scores, axis=-1, keepdims=True))
            probs = raised / jnp.sum(raised, axis=-1, keepdims=True)
            probs_o[i * 3 + hp] = probs
            mix_o[rows, cols] = join_heads(dot(probs.astype(BF), v2)).astype(BF)


def pick_kernel(normed, pick_o, pn_o):
    pick = feature_pick()
    pick_o[...] = pick
    pn_o[...] = dot(normed[...], pick).astype(BF)


def second_kernel(
    mix_a, mix_b, tok, c0, c1, c2, c3, pos_r, par, be, wp, we, wr, after,
    res_o, one_o, pre_o, gb2_o, n2_o, mix_o, act_o, gh_o, gn2_o, bt2_o, small_o,
    xs, act_v,
):
    x, c, _, _ = place()
    units = pl.multiple_of(c * FH, 128)
    mine, other = pl.multiple_of(c * HALF, 128), pl.multiple_of((1 - c) * HALF, 128)
    gather_bands((c0, c1, c2, c3), xs)
    mix_o[:, pl.ds(mine, HALF)] = mix_a[...]
    mix_o[:, pl.ds(other, HALF)] = mix_b[...]
    pos = pos_r[...]
    one = dot(mix_o[...], wp[...]) + par[PB : PB + 1, :]
    one_o[...] = one
    residual = tok[...].astype(F32) + par[ASC : ASC + 1, :] * one
    res_o[...] = residual
    z, _ = statistics(residual)
    n2_o[...] = (z * par[GAIN2 : GAIN2 + 1, :] + par[BIAS2 : BIAS2 + 1, :]).astype(BF)
    for i in range(IMGS):
        rows = slice(i * PACK, (i + 1) * PACK)
        pre = dot(one_hot_pack(pos, i), xs[i])
        pre_o[rows, :] = pre.astype(BF)
        gb2_o[rows, :] = (par[MSC : MSC + 1, :] * pre).astype(BF)
    step = 256
    for f in range(FH // step):
        cols = slice(f * step, (f + 1) * step)
        hidden = dot(n2_o[...], we[:, cols]) + be[0:1, cols]
        phi = 0.5 * (1.0 + lax.erf(hidden * math.sqrt(0.5)))
        act_v[:, cols] = (hidden * phi).astype(BF)
        slope = phi + hidden * (jnp.exp(-0.5 * hidden * hidden) * (1.0 / math.sqrt(2.0 * math.pi)))
        back = dot_nt(gb2_o[...], wr[cols, :])
        gh_o[:, cols] = (back * slope).astype(BF)
    gn2_o[...] = dot_nt(gh_o[...], we[...]).astype(BF)
    for j in range(4):
        lo, mid, hi = 384 * j, 384 * j + 192, 384 * j + 384
        act_o[:, 192 * j : 192 * j + 192] = jnp.where(x == 0, act_v[:, lo:mid], act_v[:, mid:hi])
    two = dot(act_v[...], wr[...])
    bt2_o[...] = two.astype(BF)
    pre = pre_o[...].astype(F32)
    first = jnp.where(c == 0, 1.0, 0.0)
    small_o[...] = jnp.zeros_like(small_o)
    small_o[0:1, :] = first * jnp.sum(gb2_o[...].astype(F32), axis=0, keepdims=True)
    small_o[1:2, :] = jnp.sum(pre * (two + first * par[RB : RB + 1, :]), axis=0, keepdims=True)


def mlp_grads_kernel(n2, gh, act, gb2, pick, wr_send, wr_keep, we_send, we_keep, eb_o, full, wide, sums):
    x, c, z, y = place()
    full[...] = dot_tn(act[...], gb2[...])
    for dy, out in ((1, wr_send), (0, wr_keep)):
        for dz in range(2):
            j = 2 * ((z & 1) ^ dz) + (y ^ dy)
            for to in range(2):
                at = pl.multiple_of(192 * j + 96 * to, 96)
                out[2 * dz + to] = full[pl.ds(at, 96), :].astype(BF)
    picked = dot(n2[...], pick[...]).astype(BF)
    wide[...] = dot_tn(picked, gh[...])
    for low, out in ((1, we_send), (0, we_keep)):
        for i in range(4):
            lo = 192 * (i & 1) + 48 * (low + 2 * (i >> 1))
            out[i] = wide[lo : lo + 48, :].astype(BF)
    sums[...] = dot_tn(gh[...], jnp.ones((ROWS, 128), BF))
    lane = lax.broadcasted_iota(jnp.int32, (48, SMALL), 1)
    for q in range(8):
        b = (z ^ (q % 4)) * 2 + (y ^ (q // 4))
        here = (b >> 2) == c
        block = jnp.zeros((48, SMALL), F32)
        for k in range(4):
            at = pl.multiple_of(384 * (b & 3) + 192 * x + 48 * k, 48)
            block = jnp.where((lane == 10 + k) & here, sums[pl.ds(at, 48), :], block)
        eb_o[q] = block


QC = 3 * HALF
QW = QC + SMALL + HALF


def third_kernel(
    gn2_a, gn2_b, res, one, pre, tok, qkv, probs_r, mix, pn, pick, small2, eb, wp, w, par,
    gres_o, gnp_o, send_o, keep_o, tick,
    gp, vecs, flat,
):
    x, c, z, y = place()
    tick[...] = jnp.zeros_like(tick)
    heads = pl.multiple_of(c * HALF, 128)
    first = jnp.where(c == 0, 1.0, 0.0)

    def total(v):
        return jnp.sum(v, axis=0, keepdims=True)

    vecs[...] = jnp.zeros_like(vecs)
    gn2 = gn2_a[...].astype(F32) + gn2_b[...].astype(F32)
    z2, rstd2 = statistics(res[...])
    vecs[6:7, :] = first * total(gn2 * z2)
    vecs[7:8, :] = first * total(gn2)
    gres = pre[...].astype(F32) + norm_back(gn2 * par[GAIN2 : GAIN2 + 1, :], z2, rstd2)
    gres_o[...] = gres
    vecs[5:6, :] = first * total(gres * one[...])
    gb1 = (par[ASC : ASC + 1, :] * gres).astype(BF)
    vecs[4:5, :] = first * total(gb1.astype(F32))
    vecs[8:10, :] = small2[0:2, :]
    gm = dot_nt(gb1, wp[pl.ds(heads, HALF), :]).astype(BF)
    scale = 1.0 / math.sqrt(HD)
    for i in range(IMGS):
        rows = slice(i * PACK, (i + 1) * PACK)
        for hp in range(3):
            cols = slice(hp * 128, (hp + 1) * 128)
            q2, k2, v2 = (qkv[m, rows, cols] for m in range(3))
            probs = probs_r[i * 3 + hp]
            g2 = two_heads(gm[rows, cols])
            gprob = dot_nt(g2, v2)
            delta = jnp.sum(probs * gprob, axis=-1, keepdims=True)
            gscore = (probs * (gprob - delta)).astype(BF)
            parts = (
                join_heads(dot(gscore, k2)) * scale,
                dot_tn(gscore, two_heads(q2)) * scale,
                dot_tn(probs.astype(BF), g2),
            )
            for m in range(3):
                gp[rows, m * HALF + hp * 128 : m * HALF + (hp + 1) * 128] = parts[m].astype(BF)
    gnp = jnp.zeros((ROWS, D), F32)
    for m in range(3):
        part = w[m]
        gnp = gnp + dot_nt(gp[:, m * HALF : (m + 1) * HALF], part)
    gnp_o[...] = gnp.astype(BF)
    z1, _ = statistics(tok[...].astype(F32))
    vecs[0:1, :] = total(gnp * z1)
    vecs[1:2, :] = total(gnp)
    vecs[2:3, pl.ds(heads, HALF)] = total(gp[:, 0:HALF].astype(F32))
    vecs[3:4, pl.ds(heads, HALF)] = total(gp[:, 2 * HALF : 3 * HALF].astype(F32))
    rowl = lax.broadcasted_iota(jnp.int32, (D, 192), 0)
    colr = lax.broadcasted_iota(jnp.int32, (D, 192), 1)
    want = jnp.zeros((D, 192), jnp.int32)
    for q in range(8):
        base = 96 * ((z ^ (q % 4)) * 2 + (y ^ (q // 4))) + 48 * x + 24 * c - 24 * q
        want = jnp.where((colr >= 24 * q) & (colr < 24 * q + 24), colr + base, want)
    pick_p = jnp.where(rowl == want, 1.0, 0.0).astype(BF)
    mixed = dot(mix[...], pick_p).astype(BF)
    proj = dot_tn(mixed, gb1)
    vec_cols = dot(vecs[...].astype(BF), pick[...]).T
    flat[...] = dot_tn(pn[...], gp[...])
    for dy, out in ((1, send_o), (0, keep_o)):
        for dz in range(4):
            q = 4 * dy + dz
            lo = 48 * q
            out[dz, :, 0:QC] = flat[lo : lo + 48, :].astype(BF)
            out[dz, :, QC : QC + SMALL] = (vec_cols[lo : lo + 48] + eb[q]).astype(BF)
            block = proj[24 * q : 24 * q + 24]
            out[dz, :, QC + SMALL :] = jnp.concatenate([block[:, :HALF], block[:, HALF:]], axis=0).astype(BF)


def last_kernel(gnp_a, gnp_b, tok, gres, bt2_a, bt2_b, res, pos_r, par, after, out_o, gtok_o, tick, wide):
    tick[...] = jnp.zeros_like(tick)
    band = lax.axis_index("band")
    at = pl.multiple_of(band * BAND, BAND)
    pos = pos_r[...]
    for i in range(IMGS):
        rows = slice(i * PACK, (i + 1) * PACK)
        z1, rstd1 = statistics(tok[rows, :].astype(F32))
        gnp = gnp_a[rows, :].astype(F32) + gnp_b[rows, :].astype(F32)
        gtok = (gres[rows, :] + norm_back(gnp * par[GAIN1 : GAIN1 + 1, :], z1, rstd1)).astype(BF)
        two = bt2_a[rows, :].astype(F32) + bt2_b[rows, :].astype(F32) + par[RB : RB + 1, :]
        out = (res[rows, :] + par[MSC : MSC + 1, :] * two).astype(BF)
        pack = one_hot_pack(pos, i)
        for value, dst in ((gtok, gtok_o), (out, out_o)):
            wide[...] = dot_tn(pack, value)
            dst[i] = wide[pl.ds(at, BAND), :].astype(BF)


def fold(keep, arrived, keep_o, send_o):
    count = keep.shape[0]
    for i in range(count):
        total = keep[i].astype(F32) + arrived[i].astype(F32)
        if i < count // 2:
            keep_o[i] = total
        else:
            send_o[i - count // 2] = total.astype(BF)


def fold_kernel(keep_a, arrived_a, keep_b, arrived_b, after, keep_ao, send_ao, keep_bo, send_bo, tick):
    fold(keep_a, arrived_a, keep_ao, send_ao)
    fold(keep_b, arrived_b, keep_bo, send_bo)
    tick[...] = jnp.zeros_like(tick)


def stage_kernel(
    keep, arrived, keep_a, arrived_a, keep_b, arrived_b, after,
    own_o, s1, s2, s3, keep_ao, send_ao, keep_bo, send_bo,
):
    own_o[...] = keep[0].astype(F32) + arrived[0].astype(F32)
    for dz, out in ((1, s1), (2, s2), (3, s3)):
        out[...] = (keep[dz].astype(F32) + arrived[dz].astype(F32)).astype(BF)
    for i in range(2):
        total = keep_a[i] + arrived_a[i].astype(F32)
        keep_ao[i] = total
        send_ao[i] = total.astype(BF)
    fold(keep_b, arrived_b, keep_bo, send_bo)


def finish_kernel(
    own, r1, r2, r3, wr_k, wr_a, we_k, we_a,
    qk_o, qs_o, vec_o, proj_o, wr_ko, wr_so, keep_o, send_o,
    sums, both,
):
    tail(own, r1, r2, r3, qk_o, qs_o, vec_o, proj_o, sums)
    c = lax.axis_index("band") & 1
    wr_ko[...] = wr_k[c] + wr_a[c].astype(F32)
    wr_so[...] = wr_k[1 - c] + wr_a[1 - c].astype(F32)
    both[...] = we_k[0] + we_a[0].astype(F32)
    keep_o[...] = both[pl.ds(pl.multiple_of(c * 24, 8), 24), :]
    send_o[...] = both[pl.ds(pl.multiple_of(24 - c * 24, 8), 24), :]


def tail(own, r1, r2, r3, keep_o, send_o, vec_o, proj_o, both):
    c = lax.axis_index("band") & 1
    both[...] = own[...] + r1[...].astype(F32) + r2[...].astype(F32) + r3[...].astype(F32)
    keep_o[...] = both[pl.ds(pl.multiple_of(c * 24, 8), 24), 0:QC]
    send_o[:, 0:QC] = both[pl.ds(pl.multiple_of(24 - c * 24, 8), 24), 0:QC]
    vec = both[:, QC : QC + SMALL]
    vec_o[...] = vec
    send_o[:, QC : QC + SMALL] = vec[0:24]
    send_o[:, QC + SMALL : QC + 2 * SMALL] = vec[24:48]
    proj_o[:, 0:HALF] = both[0:24, QC + SMALL :]
    proj_o[:, HALF:] = both[24:48, QC + SMALL :]


def out_kernel(
    keep, vec, arrived, we_keep, we_arrived, wr_keep, wr_arrived,
    qkv_o, first_o, bias_o, qv_o, bp_o, asc_o, gain2_o, bias2_o, br_o, msc_o, eb_o, we_o, wr_o, both,
):
    _, c, z, _ = place()
    wr_o[...] = jnp.where((z >> 1) == c, wr_keep[...], wr_arrived[...])
    we_o[:, pl.ds(pl.multiple_of(c * FH, 128), FH)] = we_keep[...]
    we_o[:, pl.ds(pl.multiple_of((1 - c) * FH, 128), FH)] = we_arrived[...]
    for m in range(3):
        mine = pl.multiple_of(m * D + c * HALF, 128)
        other = pl.multiple_of(m * D + (1 - c) * HALF, 128)
        qkv_o[:, pl.ds(mine, HALF)] = keep[:, m * HALF : (m + 1) * HALF]
        qkv_o[:, pl.ds(other, HALF)] = arrived[:, m * HALF : (m + 1) * HALF]
    both[0:24] = vec[0:24] + arrived[:, QC : QC + SMALL]
    both[24:48] = vec[24:48] + arrived[:, QC + SMALL : QC + 2 * SMALL]
    own = both[pl.ds(pl.multiple_of(c * 24, 8), 24), :].T
    outs = (first_o, bias_o, None, None, bp_o, asc_o, gain2_o, bias2_o, br_o, msc_o)
    for r, out in enumerate(outs):
        if out is not None:
            out[...] = own[r]
    qv_o[...] = own[2:4]
    units = both[...].T
    units = jnp.where(c == 0, units[10:12], units[12:14])
    eb_o[...] = jnp.concatenate([units[0:1], units[1:2]], axis=1).reshape(96)


def call(kernel, outs, specs, scratch=(), flops=0, nbytes=0, vmem=24, out_specs=None):
    return pl.pallas_call(
        kernel,
        out_shape=outs,
        in_specs=specs,
        out_specs=jax.tree.map(lambda _: VM, outs) if out_specs is None else out_specs,
        scratch_shapes=list(scratch),
        compiler_params=pltpu.CompilerParams(vmem_limit_bytes=vmem * MIB),
        cost_estimate=pl.CostEstimate(flops=flops, bytes_accessed=nbytes, transcendentals=0),
    )


def by_core(value):
    return lax.ppermute(value, "band", [(i, i ^ 1) for i in range(4)])


def by_x(value):
    return lax.ppermute(value, "band", [(i, i ^ 2) for i in range(4)])


def by_y(value):
    return lax.ppermute(value, "batch", [(i, i ^ 1) for i in range(8)])


def by_z(value, dz):
    return lax.ppermute(value, "batch", [(i, i ^ (2 * dz)) for i in range(8)])


def fold_pair(keep_a, arrived_a, keep_b, arrived_b, after):
    outs = []
    for keep in (keep_a, keep_b):
        half = (keep.shape[0] // 2,) + keep.shape[1:]
        outs += [vm(half, F32), vm(half, BF)]
    return call(fold_kernel, (*outs, TICK), [VM] * 4 + [ANY], nbytes=int(4e6))(
        keep_a, arrived_a, keep_b, arrived_b, after
    )


def packed_body(
    tokens, cotangent, visible, first_gain, first_bias, qkv_weight, qv_bias, proj_weight, proj_bias,
    attn_scale, second_gain, second_bias, expand_weight, expand_bias, reduce_weight, reduce_bias, mlp_scale,
):
    tok_x = by_x(tokens)
    tok_c = by_core(tokens)
    cot, tok_own, par, be, wqkv, wp, we, wr, vis = call(
        prepare_kernel,
        (
            vm(cotangent.shape, BF),
            vm(cotangent.shape, BF),
            vm((16, D), F32),
            vm((8, FH), F32),
            vm((3, D, HALF), BF),
            vm((D, D), BF),
            vm((D, FH), BF),
            vm((FH, D), BF),
            vm(visible.shape, visible.dtype),
        ),
        [ANY] * 17,
        [pltpu.SemaphoreType.DMA((20,))],
        nbytes=int(9e6),
    )(
        *map(
            stay,
            (
                cotangent, first_gain, first_bias, qv_bias, proj_bias, attn_scale, second_gain, second_bias,
                reduce_bias, mlp_scale, expand_bias, qkv_weight, proj_weight, expand_weight, reduce_weight, visible,
                tokens,
            ),
        )
    )
    vis_x = by_x(vis)
    vis_c = by_core(vis)
    cot_c = by_core(cot)
    block = vm(cotangent.shape, BF)
    cot, tok_x = call(hold_kernel, (block, block), [VM] * 2 + [ANY] * 2, nbytes=int(20e6))(cot, tok_x, vis_x, par)
    tok_d = by_core(tok_x)
    vis_d = by_core(vis_x)
    cot_x = by_x(cot)

    tok, normed, qkv, mix_own, pos, probs = call(
        first_kernel,
        (
            vm((ROWS, D), BF),
            vm((ROWS, D), BF),
            vm((3, ROWS, HALF), BF),
            vm((ROWS, HALF), BF),
            vm((8, SLOTS), F32),
            vm((9, 2 * PACK, PACK), F32),
        ),
        [VM] * 10,
        [
            pltpu.VMEM((IMGS, SLOTS, D), BF),
            pltpu.VMEM((16, 128), F32),
        ],
        flops=int(1.5e9),
        nbytes=int(6e6),
    )(tok_own, tok_c, tok_x, tok_d, vis, vis_c, vis_x, vis_d, par, wqkv)
    mix_other = by_core(mix_own)
    cot_d = by_core(cot_x)
    pick, pn = call(
        pick_kernel, (vm((D, HALF), BF), vm((ROWS, HALF), BF)), [VM], flops=int(5e8), nbytes=int(2e6)
    )(normed)
    res, one, pre, gb2, n2, mix, act, gh, gn2, bt2, small2 = call(
        second_kernel,
        (
            vm((ROWS, D), F32),
            vm((ROWS, D), F32),
            vm((ROWS, D), BF),
            vm((ROWS, D), BF),
            vm((ROWS, D), BF),
            vm((ROWS, D), BF),
            vm((ROWS, D), BF),
            vm((ROWS, FH), BF),
            vm((ROWS, D), BF),
            vm((ROWS, D), BF),
            vm((8, D), F32),
        ),
        [VM] * 13 + [ANY],
        [
            pltpu.VMEM((IMGS, SLOTS, D), BF),
            pltpu.VMEM((ROWS, FH), BF),
        ],
        flops=int(5e9),
        nbytes=int(15e6),
    )(mix_own, mix_other, tok, cot, cot_c, cot_x, cot_d, pos, par, be, wp, we, wr, pick)
    gn2_other = by_core(gn2)
    wr_send, wr_keep, we_send, we_keep, eb = call(
        mlp_grads_kernel,
        (
            vm((4, 96, D), BF),
            vm((4, 96, D), BF),
            vm((4, 48, FH), BF),
            vm((4, 48, FH), BF),
            vm((8, 48, SMALL), F32),
        ),
        [VM] * 5,
        [pltpu.VMEM((D, D), F32), pltpu.VMEM((HALF, FH), F32), pltpu.VMEM((FH, 128), F32)],
        flops=int(2e9),
        nbytes=int(6e6),
    )(n2, gh, act, gb2, pick)
    wr_y = by_y(wr_send)
    we_z = by_z(we_send, 1)
    gres, gnp, qp_send, qp_keep, tick = call(
        third_kernel,
        (
            vm((ROWS, D), F32),
            vm((ROWS, D), BF),
            vm((4, 48, QW), BF),
            vm((4, 48, QW), BF),
            TICK,
        ),
        [VM] * 16,
        [
            pltpu.VMEM((ROWS, QC), BF),
            pltpu.VMEM((SMALL, D), F32),
            pltpu.VMEM((HALF, QC), F32),
        ],
        flops=int(4e9),
        nbytes=int(12e6),
    )(gn2, gn2_other, res, one, pre, tok, qkv, probs, mix, pn, pick, small2, eb, wp, wqkv, par)
    qp_y = by_y(qp_send)
    wr_keep, wr_send, we_keep, we_send, tick = fold_pair(wr_keep, wr_y, we_keep, we_z, tick)
    wr_z = by_z(wr_send, 1)
    we_z = by_z(we_send, 2)
    bt2_other = by_core(bt2)
    gnp_other = by_core(gnp)
    layer_out, grad_tokens, tick = call(
        last_kernel,
        (sds((IMGS, BAND, D), BF), sds((IMGS, BAND, D), BF), TICK),
        [VM] * 9 + [ANY],
        [pltpu.VMEM((SLOTS, D), F32)],
        flops=int(1e9),
        nbytes=int(8e6),
    )(gnp, gnp_other, tok, gres, bt2, bt2_other, res, pos, par, tick)
    own, s1, s2, s3, wr_keep, wr_send, we_keep, we_send = call(
        stage_kernel,
        (vm((48, QW), F32),) + (vm((48, QW), BF),) * 3
        + (vm((2, 96, D), F32), vm((2, 96, D), BF), vm((1, 48, FH), F32), vm((1, 48, FH), BF)),
        [VM] * 6 + [ANY],
        nbytes=int(2e6),
    )(qp_keep, qp_y, wr_keep, wr_z, we_keep, we_z, tick)
    r1, r2, r3 = by_z(s1, 1), by_z(s2, 2), by_z(s3, 3)
    homeward = [(d, d ^ 16) for d in range(32) if (d >> 4) != (d & 1)]
    wr_z = lax.ppermute(wr_send, ("batch", "band"), homeward)
    we_y = by_y(we_send)

    qp_keep, qp_send, vec, proj, wr_keep, wr_send, we_keep, we_send = call(
        finish_kernel,
        (
            vm((24, QC), F32),
            vm((24, QC + 2 * SMALL), F32),
            vm((48, SMALL), F32),
            sds((24, D), F32),
            vm((96, D), F32),
            vm((96, D), F32),
            vm((24, FH), F32),
            vm((24, FH), F32),
        ),
        [VM] * 8,
        [pltpu.VMEM((48, QW), F32), pltpu.VMEM((48, FH), F32)],
        nbytes=int(1e6),
    )(own, r1, r2, r3, wr_keep, wr_z, we_keep, we_y)
    vector = sds((24,), F32)
    grad_qkv, gg1, gb1, gqv, gbp, gas, gg2, gb2, gbr, gms, geb, grad_expand, grad_reduce = call(
        out_kernel,
        (sds((24, 3 * D), F32), vector, vector, sds((2, 24), F32)) + (vector,) * 6
        + (sds((96,), F32), sds((24, FF), F32), sds((96, D), F32)),
        [VM] * 7,
        [pltpu.VMEM((48, SMALL), F32)],
        nbytes=int(1e6),
    )(qp_keep, vec, by_core(qp_send), we_keep, by_core(we_send), wr_keep, by_core(wr_send))
    return (
        layer_out, grad_tokens, gg1, gb1, grad_qkv, gqv, proj, gbp, gas, gg2, gb2, grad_expand, geb, grad_reduce,
        gbr, gms,
    )


def layer_norm(values, norm_gain, norm_shift):
    center = values - jnp.mean(values, axis=-1, keepdims=True)
    spread = jnp.mean(center * center, axis=-1, keepdims=True)
    return center * lax.rsqrt(spread + NORM_EPS) * norm_gain + norm_shift


def gelu_exact(values):
    return jax.nn.gelu(values, approximate=False)


def split_rows(packed_rows, mask_rows):
    item_count = packed_rows.shape[0]
    slot_count = packed_rows.shape[1]
    heads_here = packed_rows.shape[4] // HD
    unpacked = packed_rows.reshape(item_count, slot_count, 3, heads_here, HD)
    queries = unpacked[:, :, 0]
    key_rows = unpacked[:, :, 1]
    value_rows = unpacked[:, :, 2]
    key_valid = mask_rows.reshape(item_count, slot_count) > 0
    score_scale = 1.0 / math.sqrt(HD)
    scores = (
        jnp.einsum("bqhe,bkhe->bhqk", queries, key_rows, preferred_element_type=jnp.float32)
        * score_scale
    )
    scores = jnp.where(key_valid[:, None, None, :], scores, -1e30)
    return (queries, key_rows, value_rows, scores)


def attend_plain(inputs):
    packed_rows, mask_rows = inputs
    queries, key_rows, value_rows, scores = split_rows(packed_rows, mask_rows)
    row_top = jnp.max(scores, axis=-1, keepdims=True)
    raised = jnp.exp(scores - row_top)
    row_total = jnp.sum(raised, axis=-1, keepdims=True)
    attn_prob = raised / row_total
    log_total = (row_top + jnp.log(row_total))[..., 0]
    mixed_rows = jnp.einsum(
        "bhqk,bkhe->bqhe",
        attn_prob.astype(jnp.bfloat16),
        value_rows,
        preferred_element_type=jnp.float32,
    ).astype(jnp.bfloat16)
    mixed_rows = mixed_rows.reshape(
        packed_rows.shape[0], packed_rows.shape[1], packed_rows.shape[4]
    )
    return (mixed_rows, log_total)


def backward_rows(score_parts, log_total, grad_rows):
    queries, key_rows, value_rows, scores = score_parts
    item_count, slot_count, heads_here, head_size = queries.shape
    score_scale = 1.0 / math.sqrt(HD)
    attn_prob = jnp.exp(scores - log_total[..., None])
    grad_heads = grad_rows.reshape(item_count, slot_count, heads_here, head_size)
    grad_prob = jnp.einsum(
        "bqhe,bkhe->bhqk", grad_heads, value_rows, preferred_element_type=jnp.float32
    )
    row_delta = jnp.sum(attn_prob * grad_prob, axis=-1, keepdims=True)
    grad_score = (attn_prob * (grad_prob - row_delta)).astype(jnp.bfloat16)
    grad_query = (
        jnp.einsum("bhqk,bkhe->bqhe", grad_score, key_rows, preferred_element_type=jnp.float32)
        * score_scale
    )
    grad_key = (
        jnp.einsum("bhqk,bqhe->bkhe", grad_score, queries, preferred_element_type=jnp.float32)
        * score_scale
    )
    grad_value = jnp.einsum(
        "bhqk,bqhe->bkhe",
        attn_prob.astype(jnp.bfloat16),
        grad_heads,
        preferred_element_type=jnp.float32,
    )
    stacked = jnp.stack([grad_query, grad_key, grad_value], axis=2)
    return stacked.reshape(item_count, slot_count, 3, 1, heads_here * head_size).astype(
        jnp.bfloat16
    )


def attend_again(inputs):
    packed_rows, mask_rows, grad_rows = inputs
    score_parts = split_rows(packed_rows, mask_rows)
    scores = score_parts[3]
    row_top = jnp.max(scores, axis=-1, keepdims=True)
    log_total = (row_top + jnp.log(jnp.sum(jnp.exp(scores - row_top), axis=-1, keepdims=True)))[
        ..., 0
    ]
    return backward_rows(score_parts, log_total, grad_rows)


def body(
    tokens,
    cotangent,
    visible,
    first_gain,
    first_bias,
    qkv_weight,
    qv_bias,
    proj_weight,
    proj_bias,
    attn_scale,
    second_gain,
    second_bias,
    expand_weight,
    expand_bias,
    reduce_weight,
    reduce_bias,
    mlp_scale,
):
    images, slot_count, model_width = tokens.shape
    groups = lax.axis_size("band")
    local_width = model_width // groups
    inputs_full = tokens.astype(jnp.float32)
    shown_mask = visible.astype(jnp.float32)
    normed, first_pull = jax.vjp(layer_norm, inputs_full, first_gain, first_bias)
    normed_low = normed.astype(jnp.bfloat16)
    qkv_bias = jnp.concatenate([qv_bias[0], jnp.zeros((model_width,), jnp.float32), qv_bias[1]])

    def project_qkv():
        product = jnp.einsum(
            "isd,de->ise", normed_low, qkv_weight, preferred_element_type=jnp.float32
        )
        return (
            (product + qkv_bias)
            .astype(jnp.bfloat16)
            .reshape(images, slot_count, 3, groups, local_width)
        )

    packed = project_qkv()
    mask_part = jnp.broadcast_to(
        shown_mask.astype(jnp.bfloat16)[:, :, None, None, None], (images, slot_count, 1, groups, 1)
    )
    results = attend_plain(
        (
            lax.all_to_all(packed, "band", split_axis=3, concat_axis=1, tiled=True),
            lax.all_to_all(mask_part, "band", split_axis=3, concat_axis=1, tiled=True),
        )
    )
    mixed_heads = results[0].reshape(images, groups * slot_count, 1, local_width)
    back_rows = lax.all_to_all(mixed_heads, "band", split_axis=1, concat_axis=2, tiled=True)
    mixed_rows = back_rows.reshape(images, slot_count, model_width)
    branch_one = (
        jnp.einsum("isd,de->ise", mixed_rows, proj_weight, preferred_element_type=jnp.float32)
        + proj_bias
    )
    residual = inputs_full + attn_scale * branch_one
    normed_two, second_pull = jax.vjp(layer_norm, residual, second_gain, second_bias)
    normed_two_low = normed_two.astype(jnp.bfloat16)
    hidden = (
        jnp.einsum("isd,df->isf", normed_two_low, expand_weight, preferred_element_type=jnp.float32)
        + expand_bias
    )
    activated, gelu_pull = jax.vjp(gelu_exact, hidden)
    activated_low = activated.astype(jnp.bfloat16)
    branch_two = (
        jnp.einsum("isf,fd->isd", activated_low, reduce_weight, preferred_element_type=jnp.float32)
        + reduce_bias
    )
    layer_out = (shown_mask[..., None] * (residual + mlp_scale * branch_two)).astype(jnp.bfloat16)
    grad_pre = shown_mask[..., None] * cotangent.astype(jnp.float32)
    grad_mlp_scale = jnp.sum(grad_pre * branch_two, axis=(0, 1))
    grad_branch_two = (mlp_scale * grad_pre).astype(jnp.bfloat16)
    grad_reduce_weight = jnp.einsum(
        "isf,isd->fd", activated_low, grad_branch_two, preferred_element_type=jnp.float32
    )
    grad_reduce_bias = jnp.sum(grad_branch_two.astype(jnp.float32), axis=(0, 1))
    grad_activated = jnp.einsum(
        "isd,fd->isf", grad_branch_two, reduce_weight, preferred_element_type=jnp.float32
    )
    grad_hidden = gelu_pull(grad_activated)[0].astype(jnp.bfloat16)
    grad_expand_weight = jnp.einsum(
        "isd,isf->df", normed_two_low, grad_hidden, preferred_element_type=jnp.float32
    )
    grad_expand_bias = jnp.sum(grad_hidden.astype(jnp.float32), axis=(0, 1))
    grad_normed_two = jnp.einsum(
        "isf,df->isd", grad_hidden, expand_weight, preferred_element_type=jnp.float32
    )
    grad_resid_norm, grad_second_gain, grad_second_bias = second_pull(grad_normed_two)
    grad_residual = grad_pre + grad_resid_norm
    grad_attn_scale = jnp.sum(grad_residual * branch_one, axis=(0, 1))
    grad_branch_one = (attn_scale * grad_residual).astype(jnp.bfloat16)
    grad_proj_weight = jnp.einsum(
        "isd,ise->de", mixed_rows, grad_branch_one, preferred_element_type=jnp.float32
    )
    grad_proj_bias = jnp.sum(grad_branch_one.astype(jnp.float32), axis=(0, 1))
    grad_mixed = jnp.einsum(
        "ise,de->isd", grad_branch_one, proj_weight, preferred_element_type=jnp.float32
    )
    grad_mixed = grad_mixed.astype(jnp.bfloat16).reshape(images, slot_count, 1, groups, local_width)
    repacked = project_qkv()
    grad_packed = attend_again(
        (
            lax.all_to_all(repacked, "band", split_axis=3, concat_axis=1, tiled=True),
            lax.all_to_all(mask_part, "band", split_axis=3, concat_axis=1, tiled=True),
            lax.all_to_all(grad_mixed, "band", split_axis=3, concat_axis=1, tiled=True),
        )
    )
    grad_bands = lax.all_to_all(grad_packed, "band", split_axis=1, concat_axis=3, tiled=True)
    grad_qkv = grad_bands.reshape(images, slot_count, 3 * model_width)
    grad_qkv_weight = jnp.einsum(
        "isd,ise->de", normed_low, grad_qkv, preferred_element_type=jnp.float32
    )
    column_sums = jnp.sum(grad_qkv.astype(jnp.float32), axis=(0, 1))
    grad_qv_bias = jnp.stack([column_sums[:model_width], column_sums[2 * model_width :]])
    grad_normed = jnp.einsum(
        "ise,de->isd", grad_qkv, qkv_weight, preferred_element_type=jnp.float32
    )
    grad_input_norm, grad_first_gain, grad_first_bias = first_pull(grad_normed)
    grad_tokens = (grad_residual + grad_input_norm).astype(jnp.bfloat16)
    all_sums = (
        lax.psum_scatter(grad_first_gain, ("batch", "band"), scatter_dimension=0, tiled=True),
        lax.psum_scatter(grad_first_bias, ("batch", "band"), scatter_dimension=0, tiled=True),
        lax.psum_scatter(grad_qkv_weight, ("batch", "band"), scatter_dimension=0, tiled=True),
        lax.psum_scatter(grad_qv_bias, ("batch", "band"), scatter_dimension=1, tiled=True),
        lax.psum_scatter(grad_proj_weight, ("batch", "band"), scatter_dimension=0, tiled=True),
        lax.psum_scatter(grad_proj_bias, ("batch", "band"), scatter_dimension=0, tiled=True),
        lax.psum_scatter(grad_attn_scale, ("batch", "band"), scatter_dimension=0, tiled=True),
        lax.psum_scatter(grad_second_gain, ("batch", "band"), scatter_dimension=0, tiled=True),
        lax.psum_scatter(grad_second_bias, ("batch", "band"), scatter_dimension=0, tiled=True),
        lax.psum_scatter(grad_expand_weight, ("batch", "band"), scatter_dimension=0, tiled=True),
        lax.psum_scatter(grad_expand_bias, ("batch", "band"), scatter_dimension=0, tiled=True),
        lax.psum_scatter(grad_reduce_weight, ("batch", "band"), scatter_dimension=0, tiled=True),
        lax.psum_scatter(grad_reduce_bias, ("batch", "band"), scatter_dimension=0, tiled=True),
        lax.psum_scatter(grad_mlp_scale, ("batch", "band"), scatter_dimension=0, tiled=True),
    )
    (
        sum_first_gain,
        sum_first_bias,
        sum_qkv_weight,
        sum_qv_bias,
        sum_proj_weight,
        sum_proj_bias,
        sum_attn_scale,
        sum_second_gain,
        sum_second_bias,
        sum_expand_weight,
        sum_expand_bias,
        sum_reduce_weight,
        sum_reduce_bias,
        sum_mlp_scale,
    ) = all_sums
    return (
        layer_out,
        grad_tokens,
        sum_first_gain,
        sum_first_bias,
        sum_qkv_weight,
        sum_qv_bias,
        sum_proj_weight,
        sum_proj_bias,
        sum_attn_scale,
        sum_second_gain,
        sum_second_bias,
        sum_expand_weight,
        sum_expand_bias,
        sum_reduce_weight,
        sum_reduce_bias,
        sum_mlp_scale,
    )


def solution(mesh):
    sizes = dict(mesh.shape)
    chosen = packed_body if (sizes["batch"], sizes["band"]) == (8, 4) else body
    placed = (
        P("batch", "band", None),
        P("batch", "band", None),
        P("batch", "band"),
        P(),
        P(),
        P(),
        P(),
        P(),
        P(),
        P(),
        P(),
        P(),
        P(),
        P(),
        P(),
        P(),
        P(),
    )
    return jax.shard_map(
        chosen,
        mesh=mesh,
        in_specs=placed,
        out_specs=(
            P("batch", "band", None),
            P("batch", "band", None),
            P(("batch", "band")),
            P(("batch", "band")),
            P(("batch", "band"), None),
            P(None, ("batch", "band")),
            P(("batch", "band"), None),
            P(("batch", "band")),
            P(("batch", "band")),
            P(("batch", "band")),
            P(("batch", "band")),
            P(("batch", "band"), None),
            P(("batch", "band")),
            P(("batch", "band"), None),
            P(("batch", "band")),
            P(("batch", "band")),
        ),
        check_vma=False,
    )
```

```python
import math

import jax
import jax.numpy as jnp
from jax import lax
from jax.experimental import pallas as pl
from jax.experimental.pallas import tpu as pltpu
from jax.sharding import PartitionSpec as P

HD = 64
NORM_EPS = 1e-06
PACK = 144
SLOTS = 256
BAND = 64
IMGS = 3
ROWS = IMGS * PACK
D = 768
HALF = D // 2
FF = 3072
FH = FF // 2
SMALL = 128
MIB = 1024 * 1024
F32 = jnp.float32
BF = jnp.bfloat16
ANY = pl.BlockSpec(memory_space=pl.ANY)
HBM = pl.BlockSpec(memory_space=pltpu.HBM)
VM = pl.BlockSpec(memory_space=pltpu.VMEM)


def dot(a, b):
    return jnp.dot(a, b, preferred_element_type=F32)


def dot_nt(a, b):
    return lax.dot_general(a, b, (((1,), (1,)), ((), ())), preferred_element_type=F32)


def dot_tn(a, b):
    return lax.dot_general(a, b, (((0,), (0,)), ((), ())), preferred_element_type=F32)


def sds(shape, dtype):
    return jax.ShapeDtypeStruct(shape, dtype)


def vm(shape, dtype):
    return pltpu.VMEM(shape, dtype)


def stay(value):
    return pltpu.with_memory_space_constraint(value, pltpu.HBM)


def place():
    band = lax.axis_index("band")
    batch = lax.axis_index("batch")
    return band >> 1, band & 1, batch >> 1, batch & 1


def one_hot_pack(pos, image):
    rows = lax.broadcasted_iota(jnp.int32, (PACK, pos.shape[1]), 0).astype(F32)
    return jnp.where(rows == pos[image : image + 1, :], 1.0, 0.0).astype(BF)


def shard_picks():
    x, c, z, y = place()

    def pick(width, base):
        lane = lax.broadcasted_iota(jnp.int32, (1, 8 * width), 1)
        want = jnp.zeros((1, 8 * width), jnp.int32)
        for q in range(8):
            first = 96 * ((z ^ (q % 4)) * 2 + (y ^ (q // 4))) + base - width * q
            want = jnp.where((lane >= width * q) & (lane < width * (q + 1)), lane + first, want)
        row = lax.broadcasted_iota(jnp.int32, (D, 8 * width), 0)
        return jnp.where(row == want, 1.0, 0.0).astype(BF)

    return pick(48, 48 * x), pick(24, 48 * x + 24 * c)


def statistics(values):
    center = values - jnp.mean(values, axis=-1, keepdims=True)
    rstd = lax.rsqrt(jnp.mean(center * center, axis=-1, keepdims=True) + NORM_EPS)
    return center * rstd, rstd


def norm_back(grad, z, rstd):
    return rstd * (
        grad
        - jnp.mean(grad, axis=-1, keepdims=True)
        - z * jnp.mean(grad * z, axis=-1, keepdims=True)
    )


def gather_bands(blocks, dst):
    band = lax.axis_index("band")
    for k, block in enumerate(blocks):
        at = pl.multiple_of((band ^ k) * BAND, BAND)
        for i in range(IMGS):
            dst[i, pl.ds(at, BAND), :] = block[i]


def two_heads(v):
    lane = lax.broadcasted_iota(jnp.int32, v.shape, 1)
    none = jnp.zeros_like(v)
    return jnp.concatenate([jnp.where(lane < HD, v, none), jnp.where(lane < HD, none, v)], axis=0)


def join_heads(v):
    lane = lax.broadcasted_iota(jnp.int32, (PACK, 128), 1)
    return jnp.where(lane < HD, v[:PACK], v[PACK:])


def keys_shown(pos, image):
    shown = jnp.sum(jnp.where(pos[image : image + 1, :] >= 0, 1.0, 0.0), axis=-1, keepdims=True)
    return lax.broadcasted_iota(jnp.int32, (1, PACK), 1).astype(F32) < shown


TICK = vm((8, 128), F32)
GAIN1, BIAS1, QB, VB, PB, ASC, GAIN2, BIAS2, RB, MSC = range(10)


def prepare_kernel(
    cot, gain1, bias1, qvb, bp, asc, gain2, bias2, br, msc, be, wqkv, wp, we, wr, vis, tok,
    cot_o, tok_o, par_o, be_o, wqkv_o, wp_o, we_o, wr_o, vis_o, sems,
):
    c = lax.axis_index("band") & 1
    units = pl.multiple_of(c * FH, 128)
    rows = (
        (GAIN1, gain1), (BIAS1, bias1), (QB, qvb.at[0]), (VB, qvb.at[1]), (PB, bp), (ASC, asc),
        (GAIN2, gain2), (BIAS2, bias2), (RB, br), (MSC, msc),
    )
    moves = [(cot, cot_o)] + [(v, par_o.at[r]) for r, v in rows]
    moves += [(be.at[pl.ds(units, FH)], be_o.at[0])]
    for m in range(3):
        moves.append((wqkv.at[:, pl.ds(pl.multiple_of(m * D + c * HALF, 128), HALF)], wqkv_o.at[m]))
    moves += [(wp, wp_o), (we.at[:, pl.ds(units, FH)], we_o), (wr.at[pl.ds(units, FH), :], wr_o)]
    moves += [(vis, vis_o), (tok, tok_o)]
    copies = [pltpu.make_async_copy(a, b, sems.at[i]) for i, (a, b) in enumerate(moves)]
    for copy in copies:
        copy.start()
    for copy in copies:
        copy.wait()


def hold_kernel(cot, tok, after_a, after_b, cot_o, tok_o):
    cot_o[...] = cot[...]
    tok_o[...] = tok[...]


def first_kernel(
    t0, t1, t2, t3, v0, v1, v2, v3, par, w,
    tok_o, norm_o, qkv_o, mix_o, pos_o, probs_o, mine_o, theirs_o,
    xs, shown,
):
    band = lax.axis_index("band")
    c = band & 1
    gather_bands((t0, t1, t2, t3), xs)
    heads = pl.multiple_of(c * HALF, 128)
    to = lax.broadcasted_iota(jnp.int32, (BAND, SLOTS), 1) - lax.broadcasted_iota(jnp.int32, (BAND, SLOTS), 0)
    vis = jnp.zeros((16, SLOTS), F32)
    shown[...] = jnp.zeros_like(shown)
    for k, v in enumerate((v0, v1, v2, v3)):
        shown[0:IMGS, 0:BAND] = v[...].astype(F32)
        vis = vis + dot(shown[:, 0:BAND].astype(BF), jnp.where(to == (band ^ k) * BAND, 1.0, 0.0).astype(BF))
    upto = lax.broadcasted_iota(jnp.int32, (SLOTS, SLOTS), 0)
    slot = lax.broadcasted_iota(jnp.int32, (SLOTS, SLOTS), 1)
    before = jnp.where(upto < slot, 1.0, 0.0).astype(BF)
    pos = jnp.where(vis > 0, dot(vis.astype(BF), before), -1.0)
    pos_o[...] = pos[0:8]
    slot = lax.broadcasted_iota(jnp.int32, (SLOTS, BAND), 0) - lax.broadcasted_iota(jnp.int32, (SLOTS, BAND), 1)
    for out, b in ((mine_o, band), (theirs_o, band ^ 1)):
        out[...] = dot(pos.astype(BF), jnp.where(slot == b * BAND, 1.0, 0.0).astype(BF))
    for i in range(IMGS):
        rows = slice(i * PACK, (i + 1) * PACK)
        tok = dot(one_hot_pack(pos, i), xs[i])
        tok_o[rows, :] = tok.astype(BF)
        z, _ = statistics(tok)
        norm_o[rows, :] = (z * par[GAIN1 : GAIN1 + 1, :] + par[BIAS1 : BIAS1 + 1, :]).astype(BF)
    normed = norm_o[...]
    for m in range(3):
        part = dot(normed, w[m])
        if m != 1:
            r = QB if m == 0 else VB
            part = part + par[r : r + 1, pl.ds(heads, HALF)]
        qkv_o[m] = part.astype(BF)
    for i in range(IMGS):
        rows = slice(i * PACK, (i + 1) * PACK)
        key_ok = keys_shown(pos, i)
        for hp in range(3):
            cols = slice(hp * 128, (hp + 1) * 128)
            q2, k2, v2 = (qkv_o[m, rows, cols] for m in range(3))
            scores = dot_nt(two_heads(q2), k2) * (1.0 / math.sqrt(HD))
            scores = jnp.where(key_ok, scores, -1e30)
            raised = jnp.exp(scores - jnp.max(scores, axis=-1, keepdims=True))
            probs = raised / jnp.sum(raised, axis=-1, keepdims=True)
            probs_o[i * 3 + hp] = probs
            mix_o[rows, cols] = join_heads(dot(probs.astype(BF), v2)).astype(BF)


def pick_kernel(normed, pick_o, pick_p_o, pn_o):
    pick, pick_p = shard_picks()
    pick_o[...] = pick
    pick_p_o[...] = pick_p
    pn_o[...] = dot(normed[...], pick).astype(BF)


def hidden_kernel(mix_a, mix_b, tok, par, be, wp, we, after, res_o, one_o, n2_o, mix_o, act_o, slope_o):
    c = lax.axis_index("band") & 1
    mine, other = pl.multiple_of(c * HALF, 128), pl.multiple_of((1 - c) * HALF, 128)
    mix_o[:, pl.ds(mine, HALF)] = mix_a[...]
    mix_o[:, pl.ds(other, HALF)] = mix_b[...]
    one = dot(mix_o[...], wp[...]) + par[PB : PB + 1, :]
    one_o[...] = one
    residual = tok[...].astype(F32) + par[ASC : ASC + 1, :] * one
    res_o[...] = residual
    z, _ = statistics(residual)
    n2_o[...] = (z * par[GAIN2 : GAIN2 + 1, :] + par[BIAS2 : BIAS2 + 1, :]).astype(BF)
    step = 256
    for f in range(FH // step):
        cols = slice(f * step, (f + 1) * step)
        hidden = dot(n2_o[...], we[:, cols]) + be[0:1, cols]
        phi = 0.5 * (1.0 + lax.erf(hidden * math.sqrt(0.5)))
        act_o[:, cols] = (hidden * phi).astype(BF)
        slope_o[:, cols] = phi + hidden * (jnp.exp(-0.5 * hidden * hidden) * (1.0 / math.sqrt(2.0 * math.pi)))


def reduce_grad_kernel(c0, c1, c2, c3, pos_r, par, act, pre_o, gb2_o, send_o, keep_o, xs, act_x, full):
    x, c, z, y = place()
    gather_bands((c0, c1, c2, c3), xs)
    pos = pos_r[...]
    for i in range(IMGS):
        rows = slice(i * PACK, (i + 1) * PACK)
        pre = dot(one_hot_pack(pos, i), xs[i])
        pre_o[rows, :] = pre.astype(BF)
        gb2_o[rows, :] = (par[MSC : MSC + 1, :] * pre).astype(BF)
    for j in range(4):
        lo, mid, hi = 384 * j, 384 * j + 192, 384 * j + 384
        act_x[:, 192 * j : 192 * j + 192] = jnp.where(x == 0, act[:, lo:mid], act[:, mid:hi])
    full[...] = dot_tn(act_x[...], gb2_o[...])
    for dy, out in ((1, send_o), (0, keep_o)):
        for dz in range(2):
            j = 2 * ((z & 1) ^ dz) + (y ^ dy)
            for to in range(2):
                at = pl.multiple_of(192 * j + 96 * to, 96)
                out[2 * dz + to] = full[pl.ds(at, 96), :].astype(BF)


def back_kernel(gb2, wr, slope, we, gh_o, left_o, right_o):
    step = 256
    for f in range(FH // step):
        cols = slice(f * step, (f + 1) * step)
        back = dot_nt(gb2[...], wr[cols, :])
        gh_o[:, cols] = (back * slope[:, cols]).astype(BF)
    gn2 = dot_nt(gh_o[...], we[...]).astype(BF)
    left_o[...] = gn2[:, :HALF]
    right_o[...] = gn2[:, HALF:]


def expand_grad_kernel(n2, gh, pick, send_o, keep_o, tick, wide):
    tick[...] = jnp.zeros_like(tick)
    picked = dot(n2[...], pick[...]).astype(BF)
    wide[...] = dot_tn(picked, gh[...])
    for low, out in ((1, send_o), (0, keep_o)):
        for i in range(4):
            lo = 192 * (i & 1) + 48 * (low + 2 * (i >> 1))
            out[i] = wide[lo : lo + 48, :].astype(BF)


QC = 3 * HALF
QW = QC + HALF
QS = QW + SMALL


def both_halves(l_a, l_b, r_a, r_b):
    left = l_a[...].astype(F32) + l_b[...].astype(F32)
    right = r_a[...].astype(F32) + r_b[...].astype(F32)
    return jnp.concatenate([left, right], axis=1)


def attention_back_kernel(
    l_a, l_b, r_a, r_b, res, pre, qkv, probs_r, mix, pn, pick_p, wp, par, after,
    gres_o, gp, send_o, keep_o, tick,
    flat,
):
    tick[...] = jnp.zeros_like(tick)
    c = lax.axis_index("band") & 1
    heads = pl.multiple_of(c * HALF, 128)
    gn2 = both_halves(l_a, l_b, r_a, r_b)
    z2, rstd2 = statistics(res[...])
    gres = pre[...].astype(F32) + norm_back(gn2 * par[GAIN2 : GAIN2 + 1, :], z2, rstd2)
    gres_o[...] = gres
    gb1 = (par[ASC : ASC + 1, :] * gres).astype(BF)
    gm = dot_nt(gb1, wp[pl.ds(heads, HALF), :]).astype(BF)
    scale = 1.0 / math.sqrt(HD)
    for i in range(IMGS):
        rows = slice(i * PACK, (i + 1) * PACK)
        for hp in range(3):
            cols = slice(hp * 128, (hp + 1) * 128)
            q2, k2, v2 = (qkv[m, rows, cols] for m in range(3))
            probs = probs_r[i * 3 + hp]
            g2 = two_heads(gm[rows, cols])
            gprob = dot_nt(g2, v2)
            delta = jnp.sum(probs * gprob, axis=-1, keepdims=True)
            gscore = (probs * (gprob - delta)).astype(BF)
            parts = (
                join_heads(dot(gscore, k2)) * scale,
                dot_tn(gscore, two_heads(q2)) * scale,
                dot_tn(probs.astype(BF), g2),
            )
            for m in range(3):
                gp[rows, m * HALF + hp * 128 : m * HALF + (hp + 1) * 128] = parts[m].astype(BF)
    mixed = dot(mix[...], pick_p[...]).astype(BF)
    proj = dot_tn(mixed, gb1)
    flat[...] = dot_tn(pn[...], gp[...])
    for dy, out in ((1, send_o), (0, keep_o)):
        for i, dz in enumerate((0, 2, 1, 3)):
            q = 4 * dy + dz
            out[i, :, 0:QC] = flat[48 * q : 48 * q + 48, :].astype(BF)
            block = proj[24 * q : 24 * q + 24]
            out[i, :, QC:QW] = jnp.concatenate([block[:, :HALF], block[:, HALF:]], axis=0).astype(BF)


def vectors_kernel(
    l_a, l_b, r_a, r_b, res, one, gres, gp, w, act, wr, gb2, gh, pre, tok, pick, par, mine, theirs, after,
    gb_keep, gb_send, send_o, keep_o, tick,
    vecs, sums,
):
    tick[...] = jnp.zeros_like(tick)
    x, c, z, y = place()
    heads = pl.multiple_of(c * HALF, 128)
    first = jnp.where(c == 0, 1.0, 0.0)

    def total(v):
        return jnp.sum(v, axis=0, keepdims=True)

    vecs[...] = jnp.zeros_like(vecs)
    gnp = jnp.zeros((ROWS, D), F32)
    for m in range(3):
        gnp = gnp + dot_nt(gp[:, m * HALF : (m + 1) * HALF], w[m])
    z1, _ = statistics(tok[...].astype(F32))
    vecs[GAIN1 : GAIN1 + 1, :] = total(gnp * z1)
    vecs[BIAS1 : BIAS1 + 1, :] = total(gnp)
    vecs[QB : QB + 1, pl.ds(heads, HALF)] = total(gp[:, 0:HALF].astype(F32))
    vecs[VB : VB + 1, pl.ds(heads, HALF)] = total(gp[:, 2 * HALF : 3 * HALF].astype(F32))
    gb1 = (par[ASC : ASC + 1, :] * gres[...]).astype(BF)
    vecs[PB : PB + 1, :] = first * total(gb1.astype(F32))
    vecs[ASC : ASC + 1, :] = first * total(gres[...] * one[...])
    gn2 = both_halves(l_a, l_b, r_a, r_b)
    z2, _ = statistics(res[...])
    vecs[GAIN2 : GAIN2 + 1, :] = first * total(gn2 * z2)
    vecs[BIAS2 : BIAS2 + 1, :] = first * total(gn2)
    vecs[RB : RB + 1, :] = first * total(gb2[...].astype(F32))
    two = dot(act[...], wr[...])
    for m, value in enumerate((gnp.astype(BF), two.astype(BF))):
        for i in range(IMGS):
            rows = slice(i * PACK, (i + 1) * PACK)
            for at, out in ((mine, gb_keep), (theirs, gb_send)):
                out[m, i] = dot_tn(one_hot_pack(at[...], i), value[rows]).astype(BF)
    vecs[MSC : MSC + 1, :] = total(pre[...].astype(F32) * (two + first * par[RB : RB + 1, :]))
    cols = dot(vecs[...].astype(BF), pick[...]).T
    sums[...] = dot_tn(gh[...], jnp.ones((ROWS, SMALL), BF))
    lane = lax.broadcasted_iota(jnp.int32, (48, SMALL), 1)
    for dy, out in ((1, send_o), (0, keep_o)):
        for i, dz in enumerate((0, 2, 1, 3)):
            b = (z ^ dz) * 2 + (y ^ dy)
            q = 4 * dy + dz
            block = cols[48 * q : 48 * q + 48]
            for k in range(4):
                at = pl.multiple_of(384 * (b & 3) + 192 * x + 48 * k, 48)
                block = jnp.where((lane == 10 + k) & ((b >> 2) == c), sums[pl.ds(at, 48), :], block)
            out[i] = block.astype(BF)


def last_kernel(gb_a, gb_b, tok, gres, res, mine, par, after, out_o, gtok_o, tick):
    tick[...] = jnp.zeros_like(tick)

    def own_rows(pack, value):
        high = value.astype(BF)
        return dot_tn(pack, high) + dot_tn(pack, (value - high.astype(F32)).astype(BF))

    for i in range(IMGS):
        rows = slice(i * PACK, (i + 1) * PACK)
        pack = one_hot_pack(mine[...], i)
        z1, rstd1 = statistics(tok[i].astype(F32))
        gnp = gb_a[0, i].astype(F32) + gb_b[0, i].astype(F32)
        gtok = own_rows(pack, gres[rows, :]) + norm_back(gnp * par[GAIN1 : GAIN1 + 1, :], z1, rstd1)
        gtok_o[i] = gtok.astype(BF)
        ones = dot_tn(pack, jnp.ones((PACK, D), BF))
        two = gb_a[1, i].astype(F32) + gb_b[1, i].astype(F32) + ones * par[RB : RB + 1, :]
        out_o[i] = (own_rows(pack, res[rows, :]) + par[MSC : MSC + 1, :] * two).astype(BF)


def fold_kernel(keep, arrived, we_keep, we_arrived, after, keep_ao, send_ao, keep_bo, send_bo, tick):
    tick[...] = jnp.zeros_like(tick)
    fold(keep, arrived, keep_ao, send_ao)
    fold(we_keep, we_arrived, keep_bo, send_bo)


def fold(keep, arrived, keep_o, send_o):
    half = keep.shape[0] // 2
    for i in range(half):
        keep_o[i] = keep[i].astype(F32) + arrived[i].astype(F32)
        send_o[i] = (keep[half + i].astype(F32) + arrived[half + i].astype(F32)).astype(BF)


def second_fold_kernel(keep, arrived, we_keep, we_arrived, after, keep_o, send_o, we_keep_o, we_send_o, tick):
    tick[...] = jnp.zeros_like(tick)
    for i in range(2):
        total = keep[i] + arrived[i].astype(F32)
        keep_o[i] = total
        send_o[i] = total.astype(BF)
    fold(we_keep, we_arrived, we_keep_o, we_send_o)


def join_kernel(keep, arrived, vec_keep, vec_arrived, after, keep_o, send_o, tick):
    tick[...] = jnp.zeros_like(tick)
    fold(keep, arrived, keep_o.at[:, :, 0:QW], send_o.at[:, :, 0:QW])
    fold(vec_keep, vec_arrived, keep_o.at[:, :, QW:QS], send_o.at[:, :, QW:QS])


def third_fold_kernel(keep, arrived, after, keep_o, send_o, tick):
    tick[...] = jnp.zeros_like(tick)
    fold(keep, arrived, keep_o, send_o)


def finish_kernel(
    qp_k, qp_a, wr_k, wr_a, we_k, we_a, after,
    qk_o, qs_o, vec_o, proj_o, wr_ko, wr_so, keep_o, send_o,
    sums, both,
):
    c = lax.axis_index("band") & 1
    mine = pl.multiple_of(c * 24, 8)
    other = pl.multiple_of(24 - c * 24, 8)
    sums[...] = qp_k[0] + qp_a[0].astype(F32)
    qk_o[...] = sums[pl.ds(mine, 24), 0:QC]
    qs_o[:, 0:QC] = sums[pl.ds(other, 24), 0:QC]
    vec = sums[:, QW:QS]
    vec_o[...] = vec
    qs_o[:, QC : QC + SMALL] = vec[0:24]
    qs_o[:, QC + SMALL : QC + 2 * SMALL] = vec[24:48]
    proj_o[:, 0:HALF] = sums[0:24, QC:QW]
    proj_o[:, HALF:] = sums[24:48, QC:QW]
    for at, out in ((c, wr_ko), (1 - c, wr_so)):
        out[...] = wr_k[at] + wr_a[at].astype(F32)
    both[...] = we_k[0] + we_a[0].astype(F32)
    keep_o[...] = both[pl.ds(mine, 24), :]
    send_o[...] = both[pl.ds(other, 24), :]


def out_kernel(
    keep, vec, arrived, we_keep, we_arrived, wr_keep, wr_arrived,
    qkv_o, first_o, bias_o, qv_o, bp_o, asc_o, gain2_o, bias2_o, br_o, msc_o, eb_o, we_o, wr_o, both,
):
    _, c, z, _ = place()
    wr_o[...] = jnp.where((z >> 1) == c, wr_keep[...], wr_arrived[...])
    we_o[:, pl.ds(pl.multiple_of(c * FH, 128), FH)] = we_keep[...]
    we_o[:, pl.ds(pl.multiple_of((1 - c) * FH, 128), FH)] = we_arrived[...]
    for m in range(3):
        mine = pl.multiple_of(m * D + c * HALF, 128)
        other = pl.multiple_of(m * D + (1 - c) * HALF, 128)
        qkv_o[:, pl.ds(mine, HALF)] = keep[:, m * HALF : (m + 1) * HALF]
        qkv_o[:, pl.ds(other, HALF)] = arrived[:, m * HALF : (m + 1) * HALF]
    both[0:24] = vec[0:24] + arrived[:, QC : QC + SMALL]
    both[24:48] = vec[24:48] + arrived[:, QC + SMALL : QC + 2 * SMALL]
    own = both[pl.ds(pl.multiple_of(c * 24, 8), 24), :].T
    outs = (first_o, bias_o, None, None, bp_o, asc_o, gain2_o, bias2_o, br_o, msc_o)
    for r, out in enumerate(outs):
        if out is not None:
            out[...] = own[r]
    qv_o[...] = own[2:4]
    units = both[...].T
    units = jnp.where(c == 0, units[10:12], units[12:14])
    eb_o[...] = jnp.concatenate([units[0:1], units[1:2]], axis=1).reshape(96)


COSTS = {
    "first_kernel": (1500000000, 6000000),
    "pick_kernel": (500000000, 2000000),
    "hidden_kernel": (3000000000, 9000000),
    "reduce_grad_kernel": (1000000000, 4000000),
    "back_kernel": (2000000000, 6000000),
    "expand_grad_kernel": (1000000000, 4000000),
    "attention_back_kernel": (4000000000, 12000000),
    "vectors_kernel": (2000000000, 8000000),
    "fold_kernel": (0, 4000000),
    "second_fold_kernel": (0, 2000000),
    "last_kernel": (1000000000, 8000000),
    "spread_kernel": (0, 2000000),
    "finish_kernel": (0, 1000000),
    "out_kernel": (0, 1000000),
    "prepare_kernel": (0, 9000000),
    "hold_kernel": (0, 20000000),
}


def call(kernel, outs, specs, scratch=(), vmem=24):
    return pl.pallas_call(
        kernel,
        out_shape=outs,
        in_specs=specs,
        out_specs=jax.tree.map(lambda _: VM, outs),
        scratch_shapes=list(scratch),
        compiler_params=pltpu.CompilerParams(vmem_limit_bytes=vmem * MIB),
        cost_estimate=pl.CostEstimate(flops=COSTS.get(kernel.__name__, (0, 0))[0], bytes_accessed=COSTS.get(kernel.__name__, (0, 0))[1], transcendentals=0),
    )


def by_core(value):
    return lax.ppermute(value, "band", [(i, i ^ 1) for i in range(4)])


def by_x(value):
    return lax.ppermute(value, "band", [(i, i ^ 2) for i in range(4)])


def by_y(value):
    return lax.ppermute(value, "batch", [(i, i ^ 1) for i in range(8)])


def by_z(value, dz):
    return lax.ppermute(value, "batch", [(i, i ^ (2 * dz)) for i in range(8)])


def homeward(value, dz):
    pairs = [(d, d ^ (8 * dz)) for d in range(32) if ((d ^ (8 * dz)) >> 4) == (d & 1)]
    return lax.ppermute(value, ("batch", "band"), pairs)


def packed_body(
    tokens, cotangent, visible, first_gain, first_bias, qkv_weight, qv_bias, proj_weight, proj_bias,
    attn_scale, second_gain, second_bias, expand_weight, expand_bias, reduce_weight, reduce_bias, mlp_scale,
):
    block = vm(cotangent.shape, BF)
    rows_f, rows_b = vm((ROWS, D), F32), vm((ROWS, D), BF)
    tok_x = by_x(tokens)
    tok_c = by_core(tokens)
    cot, tok_own, par, be, wqkv, wp, we, wr, vis = call(
        prepare_kernel,
        (
            block,
            block,
            vm((16, D), F32),
            vm((8, FH), F32),
            vm((3, D, HALF), BF),
            vm((D, D), BF),
            vm((D, FH), BF),
            vm((FH, D), BF),
            vm(visible.shape, visible.dtype),
        ),
        [ANY] * 17,
        [pltpu.SemaphoreType.DMA((20,))]
    )(
        *map(
            stay,
            (
                cotangent, first_gain, first_bias, qv_bias, proj_bias, attn_scale, second_gain, second_bias,
                reduce_bias, mlp_scale, expand_bias, qkv_weight, proj_weight, expand_weight, reduce_weight, visible,
                tokens,
            ),
        )
    )
    vis_x = by_x(vis)
    vis_c = by_core(vis)
    cot_c = by_core(cot)
    cot, tok_x = call(hold_kernel, (block, block), [VM] * 2 + [ANY] * 2)(cot, tok_x, vis_x, par)
    tok_d = by_core(tok_x)
    vis_d = by_core(vis_x)
    cot_x = by_x(cot)
    tok, normed, qkv, mix_own, pos, probs, pos_mine, pos_theirs = call(
        first_kernel,
        (
            rows_b,
            rows_b,
            vm((3, ROWS, HALF), BF),
            vm((ROWS, HALF), BF),
            vm((8, SLOTS), F32),
            vm((9, 2 * PACK, PACK), F32),
            vm((16, BAND), F32),
            vm((16, BAND), F32),
        ),
        [VM] * 10,
        [pltpu.VMEM((IMGS, SLOTS, D), BF), pltpu.VMEM((16, 128), F32)],
    )(tok_own, tok_c, tok_x, tok_d, vis, vis_c, vis_x, vis_d, par, wqkv)
    mix_other = by_core(mix_own)
    cot_d = by_core(cot_x)
    pick, pick_p, pn = call(pick_kernel, (vm((D, HALF), BF), vm((D, 192), BF), vm((ROWS, HALF), BF)), [VM])(normed)
    res, one, n2, mix, act, slope = call(
        hidden_kernel,
        (rows_f, rows_f, rows_b, rows_b, vm((ROWS, FH), BF), vm((ROWS, FH), F32)),
        [VM] * 7 + [ANY],
    )(mix_own, mix_other, tok, par, be, wp, we, pick)
    pre, gb2, wr_send, wr_keep = call(
        reduce_grad_kernel,
        (rows_b, rows_b, vm((4, 96, D), BF), vm((4, 96, D), BF)),
        [VM] * 7,
        [pltpu.VMEM((IMGS, SLOTS, D), BF), pltpu.VMEM((ROWS, D), BF), pltpu.VMEM((D, D), F32)],
    )(cot, cot_c, cot_x, cot_d, pos, par, act)
    wr_y = by_y(wr_send)
    half_b = vm((ROWS, HALF), BF)
    gh, left, right = call(back_kernel, (vm((ROWS, FH), BF), half_b, half_b), [VM] * 4)(gb2, wr, slope, we)
    gn2 = (left, by_core(left), right, by_core(right))
    we_send, we_keep, tick = call(
        expand_grad_kernel,
        (vm((4, 48, FH), BF), vm((4, 48, FH), BF), TICK),
        [VM] * 3,
        [pltpu.VMEM((HALF, FH), F32)],
    )(n2, gh, pick)
    we_z = by_z(we_send, 1)
    gres, gp, qp_send, qp_keep, tick = call(
        attention_back_kernel,
        (rows_f, vm((ROWS, QC), BF), vm((4, 48, QW), BF), vm((4, 48, QW), BF), TICK),
        [VM] * 13 + [ANY],
        [pltpu.VMEM((HALF, QC), F32)],
    )(*gn2, res, pre, qkv, probs, mix, pn, pick_p, wp, par, tick)
    qp_y = by_y(qp_send)
    gb_keep, gb_send, vec_send, vec_keep, tick = call(
        vectors_kernel,
        (vm((2, *tokens.shape), BF), vm((2, *tokens.shape), BF), vm((4, 48, SMALL), BF), vm((4, 48, SMALL), BF), TICK),
        [VM] * 19 + [ANY],
        [pltpu.VMEM((SMALL, D), F32), pltpu.VMEM((FH, SMALL), F32)],
    )(*gn2, res, one, gres, gp, wqkv, act, wr, gb2, gh, pre, tok, pick, par, pos_mine, pos_theirs, tick)
    vec_y = by_y(vec_send)
    gb_other = by_core(gb_send)
    we_half = (2, 48, FH)
    wr_keep, wr_send, we_keep, we_send, tick = call(
        fold_kernel,
        (vm((2, 96, D), F32), vm((2, 96, D), BF), vm(we_half, F32), vm(we_half, BF), TICK),
        [VM] * 4 + [ANY],
    )(wr_keep, wr_y, we_keep, we_z, tick)
    wr_z = by_z(wr_send, 1)
    we_z = by_z(we_send, 2)
    qp_half = (2, 48, QS)
    qp_keep, qp_send, tick = call(
        join_kernel, (vm(qp_half, F32), vm(qp_half, BF), TICK), [VM] * 4 + [ANY]
    )(qp_keep, qp_y, vec_keep, vec_y, tick)
    qp_z = by_z(qp_send, 1)
    wr_keep, wr_send, we_keep, we_send, tick = call(
        second_fold_kernel,
        (vm((2, 96, D), F32), vm((2, 96, D), BF), vm((1, 48, FH), F32), vm((1, 48, FH), BF), TICK),
        [VM] * 4 + [ANY],
    )(wr_keep, wr_z, we_keep, we_z, tick)
    wr_z = homeward(wr_send, 2)
    we_y = by_y(we_send)
    layer_out, grad_tokens, tick = call(
        last_kernel,
        (sds(tokens.shape, BF), sds(tokens.shape, BF), TICK),
        [VM] * 7 + [ANY],
    )(gb_keep, gb_other, tok_own, gres, res, pos_mine, par, tick)
    qp_keep, qp_send, tick = call(
        third_fold_kernel, (vm((1, 48, QS), F32), vm((1, 48, QS), BF), TICK), [VM] * 2 + [ANY]
    )(qp_keep, qp_z, tick)
    qp_z = by_z(qp_send, 2)
    qp_keep, qp_send, vec, proj, wr_keep, wr_send, we_keep, we_send = call(
        finish_kernel,
        (
            vm((24, QC), F32),
            vm((24, QC + 2 * SMALL), F32),
            vm((48, SMALL), F32),
            sds((24, D), F32),
            vm((96, D), F32),
            vm((96, D), F32),
            vm((24, FH), F32),
            vm((24, FH), F32),
        ),
        [VM] * 6 + [ANY],
        [pltpu.VMEM((48, QS), F32), pltpu.VMEM((48, FH), F32)],
    )(qp_keep, qp_z, wr_keep, wr_z, we_keep, we_y, tick)
    vector = sds((24,), F32)
    grad_qkv, gg1, gb1, gqv, gbp, gas, gg2, gb2, gbr, gms, geb, grad_expand, grad_reduce = call(
        out_kernel,
        (
            sds((24, 3 * D), F32), vector, vector, sds((2, 24), F32), vector, vector, vector, vector, vector, vector,
            sds((96,), F32), sds((24, FF), F32), sds((96, D), F32),
        ),
        [VM] * 7,
        [pltpu.VMEM((48, SMALL), F32)],
    )(qp_keep, vec, by_core(qp_send), we_keep, by_core(we_send), wr_keep, by_core(wr_send))
    return (
        layer_out, grad_tokens, gg1, gb1, grad_qkv, gqv, proj, gbp, gas, gg2, gb2, grad_expand, geb, grad_reduce,
        gbr, gms,
    )


def layer_norm(values, norm_gain, norm_shift):
    center = values - jnp.mean(values, axis=-1, keepdims=True)
    spread = jnp.mean(center * center, axis=-1, keepdims=True)
    return center * lax.rsqrt(spread + NORM_EPS) * norm_gain + norm_shift


def gelu_exact(values):
    return jax.nn.gelu(values, approximate=False)


def split_rows(packed_rows, mask_rows):
    item_count = packed_rows.shape[0]
    slot_count = packed_rows.shape[1]
    heads_here = packed_rows.shape[4] // HD
    unpacked = packed_rows.reshape(item_count, slot_count, 3, heads_here, HD)
    queries = unpacked[:, :, 0]
    key_rows = unpacked[:, :, 1]
    value_rows = unpacked[:, :, 2]
    key_valid = mask_rows.reshape(item_count, slot_count) > 0
    score_scale = 1.0 / math.sqrt(HD)
    scores = (
        jnp.einsum("bqhe,bkhe->bhqk", queries, key_rows, preferred_element_type=jnp.float32)
        * score_scale
    )
    scores = jnp.where(key_valid[:, None, None, :], scores, -1e30)
    return (queries, key_rows, value_rows, scores)


def attend_plain(inputs):
    packed_rows, mask_rows = inputs
    queries, key_rows, value_rows, scores = split_rows(packed_rows, mask_rows)
    row_top = jnp.max(scores, axis=-1, keepdims=True)
    raised = jnp.exp(scores - row_top)
    row_total = jnp.sum(raised, axis=-1, keepdims=True)
    attn_prob = raised / row_total
    log_total = (row_top + jnp.log(row_total))[..., 0]
    mixed_rows = jnp.einsum(
        "bhqk,bkhe->bqhe",
        attn_prob.astype(jnp.bfloat16),
        value_rows,
        preferred_element_type=jnp.float32,
    ).astype(jnp.bfloat16)
    mixed_rows = mixed_rows.reshape(
        packed_rows.shape[0], packed_rows.shape[1], packed_rows.shape[4]
    )
    return (mixed_rows, log_total)


def backward_rows(score_parts, log_total, grad_rows):
    queries, key_rows, value_rows, scores = score_parts
    item_count, slot_count, heads_here, head_size = queries.shape
    score_scale = 1.0 / math.sqrt(HD)
    attn_prob = jnp.exp(scores - log_total[..., None])
    grad_heads = grad_rows.reshape(item_count, slot_count, heads_here, head_size)
    grad_prob = jnp.einsum(
        "bqhe,bkhe->bhqk", grad_heads, value_rows, preferred_element_type=jnp.float32
    )
    row_delta = jnp.sum(attn_prob * grad_prob, axis=-1, keepdims=True)
    grad_score = (attn_prob * (grad_prob - row_delta)).astype(jnp.bfloat16)
    grad_query = (
        jnp.einsum("bhqk,bkhe->bqhe", grad_score, key_rows, preferred_element_type=jnp.float32)
        * score_scale
    )
    grad_key = (
        jnp.einsum("bhqk,bqhe->bkhe", grad_score, queries, preferred_element_type=jnp.float32)
        * score_scale
    )
    grad_value = jnp.einsum(
        "bhqk,bqhe->bkhe",
        attn_prob.astype(jnp.bfloat16),
        grad_heads,
        preferred_element_type=jnp.float32,
    )
    stacked = jnp.stack([grad_query, grad_key, grad_value], axis=2)
    return stacked.reshape(item_count, slot_count, 3, 1, heads_here * head_size).astype(
        jnp.bfloat16
    )


def attend_again(inputs):
    packed_rows, mask_rows, grad_rows = inputs
    score_parts = split_rows(packed_rows, mask_rows)
    scores = score_parts[3]
    row_top = jnp.max(scores, axis=-1, keepdims=True)
    log_total = (row_top + jnp.log(jnp.sum(jnp.exp(scores - row_top), axis=-1, keepdims=True)))[
        ..., 0
    ]
    return backward_rows(score_parts, log_total, grad_rows)


def body(
    tokens,
    cotangent,
    visible,
    first_gain,
    first_bias,
    qkv_weight,
    qv_bias,
    proj_weight,
    proj_bias,
    attn_scale,
    second_gain,
    second_bias,
    expand_weight,
    expand_bias,
    reduce_weight,
    reduce_bias,
    mlp_scale,
):
    images, slot_count, model_width = tokens.shape
    groups = lax.axis_size("band")
    local_width = model_width // groups
    inputs_full = tokens.astype(jnp.float32)
    shown_mask = visible.astype(jnp.float32)
    normed, first_pull = jax.vjp(layer_norm, inputs_full, first_gain, first_bias)
    normed_low = normed.astype(jnp.bfloat16)
    qkv_bias = jnp.concatenate([qv_bias[0], jnp.zeros((model_width,), jnp.float32), qv_bias[1]])

    def project_qkv():
        product = jnp.einsum(
            "isd,de->ise", normed_low, qkv_weight, preferred_element_type=jnp.float32
        )
        return (
            (product + qkv_bias)
            .astype(jnp.bfloat16)
            .reshape(images, slot_count, 3, groups, local_width)
        )

    packed = project_qkv()
    mask_part = jnp.broadcast_to(
        shown_mask.astype(jnp.bfloat16)[:, :, None, None, None], (images, slot_count, 1, groups, 1)
    )
    results = attend_plain(
        (
            lax.all_to_all(packed, "band", split_axis=3, concat_axis=1, tiled=True),
            lax.all_to_all(mask_part, "band", split_axis=3, concat_axis=1, tiled=True),
        )
    )
    mixed_heads = results[0].reshape(images, groups * slot_count, 1, local_width)
    back_rows = lax.all_to_all(mixed_heads, "band", split_axis=1, concat_axis=2, tiled=True)
    mixed_rows = back_rows.reshape(images, slot_count, model_width)
    branch_one = (
        jnp.einsum("isd,de->ise", mixed_rows, proj_weight, preferred_element_type=jnp.float32)
        + proj_bias
    )
    residual = inputs_full + attn_scale * branch_one
    normed_two, second_pull = jax.vjp(layer_norm, residual, second_gain, second_bias)
    normed_two_low = normed_two.astype(jnp.bfloat16)
    hidden = (
        jnp.einsum("isd,df->isf", normed_two_low, expand_weight, preferred_element_type=jnp.float32)
        + expand_bias
    )
    activated, gelu_pull = jax.vjp(gelu_exact, hidden)
    activated_low = activated.astype(jnp.bfloat16)
    branch_two = (
        jnp.einsum("isf,fd->isd", activated_low, reduce_weight, preferred_element_type=jnp.float32)
        + reduce_bias
    )
    layer_out = (shown_mask[..., None] * (residual + mlp_scale * branch_two)).astype(jnp.bfloat16)
    grad_pre = shown_mask[..., None] * cotangent.astype(jnp.float32)
    grad_mlp_scale = jnp.sum(grad_pre * branch_two, axis=(0, 1))
    grad_branch_two = (mlp_scale * grad_pre).astype(jnp.bfloat16)
    grad_reduce_weight = jnp.einsum(
        "isf,isd->fd", activated_low, grad_branch_two, preferred_element_type=jnp.float32
    )
    grad_reduce_bias = jnp.sum(grad_branch_two.astype(jnp.float32), axis=(0, 1))
    grad_activated = jnp.einsum(
        "isd,fd->isf", grad_branch_two, reduce_weight, preferred_element_type=jnp.float32
    )
    grad_hidden = gelu_pull(grad_activated)[0].astype(jnp.bfloat16)
    grad_expand_weight = jnp.einsum(
        "isd,isf->df", normed_two_low, grad_hidden, preferred_element_type=jnp.float32
    )
    grad_expand_bias = jnp.sum(grad_hidden.astype(jnp.float32), axis=(0, 1))
    grad_normed_two = jnp.einsum(
        "isf,df->isd", grad_hidden, expand_weight, preferred_element_type=jnp.float32
    )
    grad_resid_norm, grad_second_gain, grad_second_bias = second_pull(grad_normed_two)
    grad_residual = grad_pre + grad_resid_norm
    grad_attn_scale = jnp.sum(grad_residual * branch_one, axis=(0, 1))
    grad_branch_one = (attn_scale * grad_residual).astype(jnp.bfloat16)
    grad_proj_weight = jnp.einsum(
        "isd,ise->de", mixed_rows, grad_branch_one, preferred_element_type=jnp.float32
    )
    grad_proj_bias = jnp.sum(grad_branch_one.astype(jnp.float32), axis=(0, 1))
    grad_mixed = jnp.einsum(
        "ise,de->isd", grad_branch_one, proj_weight, preferred_element_type=jnp.float32
    )
    grad_mixed = grad_mixed.astype(jnp.bfloat16).reshape(images, slot_count, 1, groups, local_width)
    repacked = project_qkv()
    grad_packed = attend_again(
        (
            lax.all_to_all(repacked, "band", split_axis=3, concat_axis=1, tiled=True),
            lax.all_to_all(mask_part, "band", split_axis=3, concat_axis=1, tiled=True),
            lax.all_to_all(grad_mixed, "band", split_axis=3, concat_axis=1, tiled=True),
        )
    )
    grad_bands = lax.all_to_all(grad_packed, "band", split_axis=1, concat_axis=3, tiled=True)
    grad_qkv = grad_bands.reshape(images, slot_count, 3 * model_width)
    grad_qkv_weight = jnp.einsum(
        "isd,ise->de", normed_low, grad_qkv, preferred_element_type=jnp.float32
    )
    column_sums = jnp.sum(grad_qkv.astype(jnp.float32), axis=(0, 1))
    grad_qv_bias = jnp.stack([column_sums[:model_width], column_sums[2 * model_width :]])
    grad_normed = jnp.einsum(
        "ise,de->isd", grad_qkv, qkv_weight, preferred_element_type=jnp.float32
    )
    grad_input_norm, grad_first_gain, grad_first_bias = first_pull(grad_normed)
    grad_tokens = (grad_residual + grad_input_norm).astype(jnp.bfloat16)
    all_sums = (
        lax.psum_scatter(grad_first_gain, ("batch", "band"), scatter_dimension=0, tiled=True),
        lax.psum_scatter(grad_first_bias, ("batch", "band"), scatter_dimension=0, tiled=True),
        lax.psum_scatter(grad_qkv_weight, ("batch", "band"), scatter_dimension=0, tiled=True),
        lax.psum_scatter(grad_qv_bias, ("batch", "band"), scatter_dimension=1, tiled=True),
        lax.psum_scatter(grad_proj_weight, ("batch", "band"), scatter_dimension=0, tiled=True),
        lax.psum_scatter(grad_proj_bias, ("batch", "band"), scatter_dimension=0, tiled=True),
        lax.psum_scatter(grad_attn_scale, ("batch", "band"), scatter_dimension=0, tiled=True),
        lax.psum_scatter(grad_second_gain, ("batch", "band"), scatter_dimension=0, tiled=True),
        lax.psum_scatter(grad_second_bias, ("batch", "band"), scatter_dimension=0, tiled=True),
        lax.psum_scatter(grad_expand_weight, ("batch", "band"), scatter_dimension=0, tiled=True),
        lax.psum_scatter(grad_expand_bias, ("batch", "band"), scatter_dimension=0, tiled=True),
        lax.psum_scatter(grad_reduce_weight, ("batch", "band"), scatter_dimension=0, tiled=True),
        lax.psum_scatter(grad_reduce_bias, ("batch", "band"), scatter_dimension=0, tiled=True),
        lax.psum_scatter(grad_mlp_scale, ("batch", "band"), scatter_dimension=0, tiled=True),
    )
    (
        sum_first_gain,
        sum_first_bias,
        sum_qkv_weight,
        sum_qv_bias,
        sum_proj_weight,
        sum_proj_bias,
        sum_attn_scale,
        sum_second_gain,
        sum_second_bias,
        sum_expand_weight,
        sum_expand_bias,
        sum_reduce_weight,
        sum_reduce_bias,
        sum_mlp_scale,
    ) = all_sums
    return (
        layer_out,
        grad_tokens,
        sum_first_gain,
        sum_first_bias,
        sum_qkv_weight,
        sum_qv_bias,
        sum_proj_weight,
        sum_proj_bias,
        sum_attn_scale,
        sum_second_gain,
        sum_second_bias,
        sum_expand_weight,
        sum_expand_bias,
        sum_reduce_weight,
        sum_reduce_bias,
        sum_mlp_scale,
    )


def solution(mesh):
    sizes = dict(mesh.shape)
    chosen = packed_body if (sizes["batch"], sizes["band"]) == (8, 4) else body
    placed = (
        P("batch", "band", None),
        P("batch", "band", None),
        P("batch", "band"),
        P(),
        P(),
        P(),
        P(),
        P(),
        P(),
        P(),
        P(),
        P(),
        P(),
        P(),
        P(),
        P(),
        P(),
    )
    return jax.shard_map(
        chosen,
        mesh=mesh,
        in_specs=placed,
        out_specs=(
            P("batch", "band", None),
            P("batch", "band", None),
            P(("batch", "band")),
            P(("batch", "band")),
            P(("batch", "band"), None),
            P(None, ("batch", "band")),
            P(("batch", "band"), None),
            P(("batch", "band")),
            P(("batch", "band")),
            P(("batch", "band")),
            P(("batch", "band")),
            P(("batch", "band"), None),
            P(("batch", "band")),
            P(("batch", "band"), None),
            P(("batch", "band")),
            P(("batch", "band")),
        ),
        check_vma=False,
    )
```

```python
import math

import jax
import jax.numpy as jnp
from jax import lax
from jax.experimental import pallas as pl
from jax.experimental.pallas import tpu as pltpu
from jax.sharding import PartitionSpec as P

HD = 64
NORM_EPS = 1e-06
PACK = 144
SLOTS = 256
BAND = 64
IMGS = 3
ROWS = IMGS * PACK
D = 768
HALF = D // 2
FF = 3072
FH = FF // 2
SMALL = 128
MIB = 1024 * 1024
F32 = jnp.float32
BF = jnp.bfloat16
ANY = pl.BlockSpec(memory_space=pl.ANY)
HBM = pl.BlockSpec(memory_space=pltpu.HBM)
VM = pl.BlockSpec(memory_space=pltpu.VMEM)


def dot(a, b):
    return jnp.dot(a, b, preferred_element_type=F32)


def dot_nt(a, b):
    return lax.dot_general(a, b, (((1,), (1,)), ((), ())), preferred_element_type=F32)


def dot_tn(a, b):
    return lax.dot_general(a, b, (((0,), (0,)), ((), ())), preferred_element_type=F32)


def sds(shape, dtype):
    return jax.ShapeDtypeStruct(shape, dtype)


def vm(shape, dtype):
    return pltpu.VMEM(shape, dtype)


def stay(value):
    return pltpu.with_memory_space_constraint(value, pltpu.HBM)


def place():
    band = lax.axis_index("band")
    batch = lax.axis_index("batch")
    return band >> 1, band & 1, batch >> 1, batch & 1


def one_hot_pack(pos, image):
    rows = lax.broadcasted_iota(jnp.int32, (PACK, pos.shape[1]), 0).astype(F32)
    return jnp.where(rows == pos[image : image + 1, :], 1.0, 0.0).astype(BF)


def shard_picks():
    x, c, z, y = place()

    def pick(width, base):
        lane = lax.broadcasted_iota(jnp.int32, (1, 8 * width), 1)
        want = jnp.zeros((1, 8 * width), jnp.int32)
        for q in range(8):
            first = 96 * ((z ^ (q % 4)) * 2 + (y ^ (q // 4))) + base - width * q
            want = jnp.where((lane >= width * q) & (lane < width * (q + 1)), lane + first, want)
        row = lax.broadcasted_iota(jnp.int32, (D, 8 * width), 0)
        return jnp.where(row == want, 1.0, 0.0).astype(BF)

    return pick(48, 48 * x), pick(24, 48 * x + 24 * c)


def statistics(values):
    center = values - jnp.mean(values, axis=-1, keepdims=True)
    rstd = lax.rsqrt(jnp.mean(center * center, axis=-1, keepdims=True) + NORM_EPS)
    return center * rstd, rstd


def norm_back(grad, z, rstd):
    return rstd * (
        grad
        - jnp.mean(grad, axis=-1, keepdims=True)
        - z * jnp.mean(grad * z, axis=-1, keepdims=True)
    )


def gather_bands(blocks, dst):
    band = lax.axis_index("band")
    for k, block in enumerate(blocks):
        at = pl.multiple_of((band ^ k) * BAND, BAND)
        for i in range(IMGS):
            dst[i, pl.ds(at, BAND), :] = block[i]


def two_heads(v):
    lane = lax.broadcasted_iota(jnp.int32, v.shape, 1)
    none = jnp.zeros_like(v)
    return jnp.concatenate([jnp.where(lane < HD, v, none), jnp.where(lane < HD, none, v)], axis=0)


def join_heads(v):
    lane = lax.broadcasted_iota(jnp.int32, (PACK, 128), 1)
    return jnp.where(lane < HD, v[:PACK], v[PACK:])


def keys_shown(pos, image):
    shown = jnp.sum(jnp.where(pos[image : image + 1, :] >= 0, 1.0, 0.0), axis=-1, keepdims=True)
    return lax.broadcasted_iota(jnp.int32, (1, PACK), 1).astype(F32) < shown


TICK = vm((8, 128), F32)
GAIN1, BIAS1, QB, VB, PB, ASC, GAIN2, BIAS2, RB, MSC = range(10)


def prepare_kernel(
    cot, gain1, bias1, qvb, bp, asc, gain2, bias2, br, msc, be, wqkv, wp, we, wr, vis, tok,
    cot_o, tok_o, par_o, be_o, wqkv_o, wp_o, we_o, wr_o, vis_o, sems,
):
    c = lax.axis_index("band") & 1
    units = pl.multiple_of(c * FH, 128)
    rows = (
        (GAIN1, gain1), (BIAS1, bias1), (QB, qvb.at[0]), (VB, qvb.at[1]), (PB, bp), (ASC, asc),
        (GAIN2, gain2), (BIAS2, bias2), (RB, br), (MSC, msc),
    )
    moves = [(cot, cot_o)] + [(v, par_o.at[r]) for r, v in rows]
    moves += [(be.at[pl.ds(units, FH)], be_o.at[0])]
    for m in range(3):
        moves.append((wqkv.at[:, pl.ds(pl.multiple_of(m * D + c * HALF, 128), HALF)], wqkv_o.at[m]))
    moves += [(wp, wp_o), (we.at[:, pl.ds(units, FH)], we_o), (wr.at[pl.ds(units, FH), :], wr_o)]
    moves += [(vis, vis_o), (tok, tok_o)]
    copies = [pltpu.make_async_copy(a, b, sems.at[i]) for i, (a, b) in enumerate(moves)]
    for copy in copies:
        copy.start()
    for copy in copies:
        copy.wait()


def hold_kernel(cot, tok, after_a, after_b, cot_o, tok_o):
    cot_o[...] = cot[...]
    tok_o[...] = tok[...]


def first_kernel(
    t0, t1, t2, t3, v0, v1, v2, v3, par, w,
    tok_o, norm_o, qkv_o, mix_o, mix2_o, pos_o, probs_o, mine_o, theirs_o,
    xs, shown,
):
    band = lax.axis_index("band")
    c = band & 1
    gather_bands((t0, t1, t2, t3), xs)
    heads = pl.multiple_of(c * HALF, 128)
    to = lax.broadcasted_iota(jnp.int32, (BAND, SLOTS), 1) - lax.broadcasted_iota(jnp.int32, (BAND, SLOTS), 0)
    vis = jnp.zeros((16, SLOTS), F32)
    shown[...] = jnp.zeros_like(shown)
    for k, v in enumerate((v0, v1, v2, v3)):
        shown[0:IMGS, 0:BAND] = v[...].astype(F32)
        vis = vis + dot(shown[:, 0:BAND].astype(BF), jnp.where(to == (band ^ k) * BAND, 1.0, 0.0).astype(BF))
    upto = lax.broadcasted_iota(jnp.int32, (SLOTS, SLOTS), 0)
    slot = lax.broadcasted_iota(jnp.int32, (SLOTS, SLOTS), 1)
    before = jnp.where(upto < slot, 1.0, 0.0).astype(BF)
    pos = jnp.where(vis > 0, dot(vis.astype(BF), before), -1.0)
    pos_o[...] = pos[0:8]
    slot = lax.broadcasted_iota(jnp.int32, (SLOTS, BAND), 0) - lax.broadcasted_iota(jnp.int32, (SLOTS, BAND), 1)
    for out, b in ((mine_o, band), (theirs_o, band ^ 1)):
        out[...] = dot(pos.astype(BF), jnp.where(slot == b * BAND, 1.0, 0.0).astype(BF))
    for i in range(IMGS):
        rows = slice(i * PACK, (i + 1) * PACK)
        tok = dot(one_hot_pack(pos, i), xs[i])
        tok_o[rows, :] = tok.astype(BF)
        z, _ = statistics(tok)
        norm_o[rows, :] = (z * par[GAIN1 : GAIN1 + 1, :] + par[BIAS1 : BIAS1 + 1, :]).astype(BF)
    normed = norm_o[...]
    for m in range(3):
        part = dot(normed, w[m])
        if m != 1:
            r = QB if m == 0 else VB
            part = part + par[r : r + 1, pl.ds(heads, HALF)]
        qkv_o[m] = part.astype(BF)
    for i in range(IMGS):
        rows = slice(i * PACK, (i + 1) * PACK)
        key_ok = keys_shown(pos, i)
        for hp in range(3):
            cols = slice(hp * 128, (hp + 1) * 128)
            q2, k2, v2 = (qkv_o[m, rows, cols] for m in range(3))
            scores = dot_nt(two_heads(q2), k2) * (1.0 / math.sqrt(HD))
            scores = jnp.where(key_ok, scores, -1e30)
            raised = jnp.exp(scores - jnp.max(scores, axis=-1, keepdims=True))
            probs = raised / jnp.sum(raised, axis=-1, keepdims=True)
            probs_o[i * 3 + hp] = probs
            mixed = join_heads(dot(probs.astype(BF), v2)).astype(BF)
            if hp < 2:
                mix_o[rows, cols] = mixed
            else:
                mix2_o[rows, :] = mixed


def pick_kernel(normed, pick_o, pick_p_o, pn_o):
    pick, pick_p = shard_picks()
    pick_o[...] = pick
    pick_p_o[...] = pick_p
    pn_o[...] = dot(normed[...], pick).astype(BF)


def hidden_units(n2, be, we, cols, act_o, slope_o):
    step = 256
    for f in range(cols // step):
        at = slice(f * step, (f + 1) * step)
        hidden = dot(n2[...], we[:, at]) + be[0:1, at]
        phi = 0.5 * (1.0 + lax.erf(hidden * math.sqrt(0.5)))
        act_o[:, at] = (hidden * phi).astype(BF)
        slope_o[:, at] = phi + hidden * (jnp.exp(-0.5 * hidden * hidden) * (1.0 / math.sqrt(2.0 * math.pi)))


def hidden_kernel(
    mix_a, mix_b, mix2_a, mix2_b, tok, par, be, wp, we, after, res_o, one_o, n2_o, mix_o, act_o, slope_o, tick
):
    tick[...] = jnp.zeros_like(tick)
    c = lax.axis_index("band") & 1
    mine, other = pl.multiple_of(c * HALF, 128), pl.multiple_of((1 - c) * HALF, 128)
    for at, first, second in ((mine, mix_a, mix2_a), (other, mix_b, mix2_b)):
        mix_o[:, pl.ds(at, 256)] = first[...]
        mix_o[:, pl.ds(pl.multiple_of(at + 256, 128), 128)] = second[...]
    one = dot(mix_o[...], wp[...]) + par[PB : PB + 1, :]
    one_o[...] = one
    residual = tok[...].astype(F32) + par[ASC : ASC + 1, :] * one
    res_o[...] = residual
    z, _ = statistics(residual)
    n2_o[...] = (z * par[GAIN2 : GAIN2 + 1, :] + par[BIAS2 : BIAS2 + 1, :]).astype(BF)
    hidden_units(n2_o, be, we, D, act_o, slope_o)


def more_hidden_kernel(n2, be, we, act_o, slope_o):
    hidden_units(n2, be.at[:, D:FH], we.at[:, D:FH], FH - D, act_o, slope_o)


def pass_kernel(v, after, out):
    out[...] = v[...]


def reduce_grad_kernel(c0, c1, c2, c3, pos_r, par, act_a, act_b, pre_o, gb2_o, send_o, keep_o, xs, act_x, full):
    x, c, z, y = place()
    gather_bands((c0, c1, c2, c3), xs)
    pos = pos_r[...]
    for i in range(IMGS):
        rows = slice(i * PACK, (i + 1) * PACK)
        pre = dot(one_hot_pack(pos, i), xs[i])
        pre_o[rows, :] = pre.astype(BF)
        gb2_o[rows, :] = (par[MSC : MSC + 1, :] * pre).astype(BF)
    for j in range(4):
        act = act_a if j < 2 else act_b
        lo = 384 * (j & 1)
        mid, hi = lo + 192, lo + 384
        act_x[:, 192 * j : 192 * j + 192] = jnp.where(x == 0, act[:, lo:mid], act[:, mid:hi])
    full[...] = dot_tn(act_x[...], gb2_o[...])
    for dy, out in ((1, send_o), (0, keep_o)):
        for dz in range(2):
            j = 2 * ((z & 1) ^ dz) + (y ^ dy)
            for to in range(2):
                at = pl.multiple_of(192 * j + 96 * to, 96)
                out[2 * dz + to] = full[pl.ds(at, 96), :].astype(BF)


def back_kernel(gb2, wr, slope_a, slope_b, we, gh_o, left_o, right_o):
    step = 256
    for f in range(FH // step):
        cols = slice(f * step, (f + 1) * step)
        back = dot_nt(gb2[...], wr[cols, :])
        slope = slope_a if f < 3 else slope_b
        at = slice((f % 3) * step, (f % 3 + 1) * step)
        gh_o[:, cols] = (back * slope[:, at]).astype(BF)
    gn2 = dot_nt(gh_o[...], we[...]).astype(BF)
    left_o[...] = gn2[:, :HALF]
    right_o[...] = gn2[:, HALF:]


def expand_grad_kernel(n2, gh, pick, send_o, keep_o, tick, wide):
    tick[...] = jnp.zeros_like(tick)
    picked = dot(n2[...], pick[...]).astype(BF)
    wide[...] = dot_tn(picked, gh[...])
    for low, out in ((1, send_o), (0, keep_o)):
        for i in range(4):
            lo = 192 * (i >> 1) + 48 * (low + 2 * (i & 1))
            out[i] = wide[lo : lo + 48, :].astype(BF)


QC = 3 * HALF
QW = QC + HALF
QS = QW + SMALL
FS = FH + 2 * SMALL


def both_halves(l_a, l_b, r_a, r_b):
    left = l_a[...].astype(F32) + l_b[...].astype(F32)
    right = r_a[...].astype(F32) + r_b[...].astype(F32)
    return jnp.concatenate([left, right], axis=1)


def attention_back_kernel(
    l_a, l_b, r_a, r_b, res, pre, qkv, probs_r, mix, pn, pick_p, wp, par, after,
    gres_o, gp, send_o, keep_o, tick,
    flat,
):
    tick[...] = jnp.zeros_like(tick)
    c = lax.axis_index("band") & 1
    heads = pl.multiple_of(c * HALF, 128)
    gn2 = both_halves(l_a, l_b, r_a, r_b)
    z2, rstd2 = statistics(res[...])
    gres = pre[...].astype(F32) + norm_back(gn2 * par[GAIN2 : GAIN2 + 1, :], z2, rstd2)
    gres_o[...] = gres
    gb1 = (par[ASC : ASC + 1, :] * gres).astype(BF)
    gm = dot_nt(gb1, wp[pl.ds(heads, HALF), :]).astype(BF)
    scale = 1.0 / math.sqrt(HD)
    for i in range(IMGS):
        rows = slice(i * PACK, (i + 1) * PACK)
        for hp in range(3):
            cols = slice(hp * 128, (hp + 1) * 128)
            q2, k2, v2 = (qkv[m, rows, cols] for m in range(3))
            probs = probs_r[i * 3 + hp]
            g2 = two_heads(gm[rows, cols])
            gprob = dot_nt(g2, v2)
            delta = jnp.sum(probs * gprob, axis=-1, keepdims=True)
            gscore = (probs * (gprob - delta)).astype(BF)
            parts = (
                join_heads(dot(gscore, k2)) * scale,
                dot_tn(gscore, two_heads(q2)) * scale,
                dot_tn(probs.astype(BF), g2),
            )
            for m in range(3):
                gp[rows, m * HALF + hp * 128 : m * HALF + (hp + 1) * 128] = parts[m].astype(BF)
    mixed = dot(mix[...], pick_p[...]).astype(BF)
    proj = dot_tn(mixed, gb1)
    flat[...] = dot_tn(pn[...], gp[...])
    for dy, out in ((1, send_o), (0, keep_o)):
        for i, dz in enumerate((0, 2, 1, 3)):
            q = 4 * dy + dz
            out[i, :, 0:QC] = flat[48 * q : 48 * q + 48, :].astype(BF)
            block = proj[24 * q : 24 * q + 24]
            out[i, :, QC:QW] = jnp.concatenate([block[:, :HALF], block[:, HALF:]], axis=0).astype(BF)


def vectors_kernel(
    l_a, l_b, r_a, r_b, res, one, gres, gp, w, act_a, act_b, wr, gb2, gh, pre, tok, pick, par, mine, theirs, after,
    gb_keep, gb_send, send_o, keep_o, tick,
    vecs, sums,
):
    tick[...] = jnp.zeros_like(tick)
    x, c, z, y = place()
    heads = pl.multiple_of(c * HALF, 128)
    first = jnp.where(c == 0, 1.0, 0.0)

    def total(v):
        return jnp.sum(v, axis=0, keepdims=True)

    vecs[...] = jnp.zeros_like(vecs)
    gnp = jnp.zeros((ROWS, D), F32)
    for m in range(3):
        gnp = gnp + dot_nt(gp[:, m * HALF : (m + 1) * HALF], w[m])
    z1, _ = statistics(tok[...].astype(F32))
    vecs[GAIN1 : GAIN1 + 1, :] = total(gnp * z1)
    vecs[BIAS1 : BIAS1 + 1, :] = total(gnp)
    vecs[QB : QB + 1, pl.ds(heads, HALF)] = total(gp[:, 0:HALF].astype(F32))
    vecs[VB : VB + 1, pl.ds(heads, HALF)] = total(gp[:, 2 * HALF : 3 * HALF].astype(F32))
    gb1 = (par[ASC : ASC + 1, :] * gres[...]).astype(BF)
    vecs[PB : PB + 1, :] = first * total(gb1.astype(F32))
    vecs[ASC : ASC + 1, :] = first * total(gres[...] * one[...])
    gn2 = both_halves(l_a, l_b, r_a, r_b)
    z2, _ = statistics(res[...])
    vecs[GAIN2 : GAIN2 + 1, :] = first * total(gn2 * z2)
    vecs[BIAS2 : BIAS2 + 1, :] = first * total(gn2)
    vecs[RB : RB + 1, :] = first * total(gb2[...].astype(F32))
    two = dot(act_a[...], wr[0:D, :]) + dot(act_b[...], wr[D:FH, :])
    for m, value in enumerate((gnp.astype(BF), two.astype(BF))):
        for i in range(IMGS):
            rows = slice(i * PACK, (i + 1) * PACK)
            for at, out in ((mine, gb_keep), (theirs, gb_send)):
                out[m, i] = dot_tn(one_hot_pack(at[...], i), value[rows]).astype(BF)
    vecs[MSC : MSC + 1, :] = total(pre[...].astype(F32) * (two + first * par[RB : RB + 1, :]))
    cols = dot(vecs[...].astype(BF), pick[...]).T
    sums[...] = dot_tn(gh[...], jnp.ones((ROWS, SMALL), BF))
    lane = lax.broadcasted_iota(jnp.int32, (48, SMALL), 1)
    for dy, out in ((1, send_o), (0, keep_o)):
        for dz in range(4):
            b = (z ^ dz) * 2 + (y ^ dy)
            q = 4 * dy + dz
            block = cols[48 * q : 48 * q + 48]
            for k in range(4):
                at = pl.multiple_of(384 * (b & 3) + 192 * x + 48 * k, 48)
                block = jnp.where((lane == 10 + k) & ((b >> 2) == c), sums[pl.ds(at, 48), :], block)
            out[dz >> 1, :, SMALL * (dz & 1) : SMALL * (dz & 1) + SMALL] = block.astype(BF)


def last_kernel(gb_a, gb_b, tok, gres, res, mine, par, after, out_o, gtok_o, tick):
    tick[...] = jnp.zeros_like(tick)

    def own_rows(pack, value):
        high = value.astype(BF)
        return dot_tn(pack, high) + dot_tn(pack, (value - high.astype(F32)).astype(BF))

    for i in range(IMGS):
        rows = slice(i * PACK, (i + 1) * PACK)
        pack = one_hot_pack(mine[...], i)
        z1, rstd1 = statistics(tok[i].astype(F32))
        gnp = gb_a[0, i].astype(F32) + gb_b[0, i].astype(F32)
        gtok = own_rows(pack, gres[rows, :]) + norm_back(gnp * par[GAIN1 : GAIN1 + 1, :], z1, rstd1)
        gtok_o[i] = gtok.astype(BF)
        ones = dot_tn(pack, jnp.ones((PACK, D), BF))
        two = gb_a[1, i].astype(F32) + gb_b[1, i].astype(F32) + ones * par[RB : RB + 1, :]
        out_o[i] = (own_rows(pack, res[rows, :]) + par[MSC : MSC + 1, :] * two).astype(BF)


def fold(keep, arrived, keep_o, send_o):
    half = keep.shape[0] // 2
    for i in range(half):
        keep_o[i] = keep[i].astype(F32) + arrived[i].astype(F32)
        send_o[i] = (keep[half + i].astype(F32) + arrived[half + i].astype(F32)).astype(BF)


def fold_kernel(keep, arrived, after, keep_o, send_o, tick):
    tick[...] = jnp.zeros_like(tick)
    fold(keep, arrived, keep_o, send_o)


def home_kernel(keep, arrived, after, keep_o, send_o, tick):
    tick[...] = jnp.zeros_like(tick)
    for i in range(4):
        total = keep[i].astype(F32) + arrived[i].astype(F32)
        keep_o[i] = total
        send_o[i] = total.astype(BF)


def fold(keep, arrived, keep_o, send_o):
    half = keep.shape[0] // 2
    for i in range(half):
        keep_o[i] = keep[i].astype(F32) + arrived[i].astype(F32)
        send_o[i] = (keep[half + i].astype(F32) + arrived[half + i].astype(F32)).astype(BF)


def fold_kernel(keep, arrived, after, keep_o, send_o, tick):
    tick[...] = jnp.zeros_like(tick)
    fold(keep, arrived, keep_o, send_o)


def second_fold_kernel(keep, arrived, we_keep, we_arrived, after, keep_o, send_o, we_keep_o, we_send_o, tick):
    tick[...] = jnp.zeros_like(tick)
    for i in range(2):
        total = keep[i] + arrived[i].astype(F32)
        keep_o[i] = total
        send_o[i] = total.astype(BF)
    fold(we_keep, we_arrived, we_keep_o, we_send_o)


def join_kernel(keep, arrived, vec_keep, vec_send, after, keep_o, send_o, tick):
    tick[...] = jnp.zeros_like(tick)
    fold(keep, arrived, keep_o.at[:, :, 0:FH], send_o.at[:, :, 0:FH])
    keep_o[:, :, FH:FS] = vec_keep[...].astype(F32)
    send_o[:, :, FH:FS] = vec_send[...]


def part_kernel(keep, arrived, after, keep_o, send_o, vec_ko, vec_so, tick):
    tick[...] = jnp.zeros_like(tick)
    fold(keep.at[:, :, 0:FH], arrived.at[:, :, 0:FH], keep_o, send_o)
    for hi in range(2):
        total = keep[hi, :, FH:FS] + arrived[hi, :, FH:FS].astype(F32)
        vec_ko[hi] = total[:, 0:SMALL]
        vec_so[hi] = total[:, SMALL:].astype(BF)


def rejoin_kernel(keep, arrived, vec_k, vec_a, after, keep_o, send_o, tick):
    tick[...] = jnp.zeros_like(tick)
    fold(keep, arrived, keep_o.at[:, :, 0:QW], send_o.at[:, :, 0:QW])
    fold(vec_k, vec_a, keep_o.at[:, :, QW:QS], send_o.at[:, :, QW:QS])


def settle_kernel(wr_k, wr_a, we_k, we_a, after, wr_ko, wr_so, we_ko, we_so, tick, both):
    tick[...] = jnp.zeros_like(tick)
    c = lax.axis_index("band") & 1
    for at, out in ((c, wr_ko), (1 - c, wr_so)):
        out[...] = wr_k[at] + wr_a[at].astype(F32)
    both[...] = we_k[0] + we_a[0].astype(F32)
    we_ko[...] = both[pl.ds(pl.multiple_of(c * 24, 8), 24), :]
    we_so[...] = both[pl.ds(pl.multiple_of(24 - c * 24, 8), 24), :]


def finish_kernel(qp_k, qp_a, after, keep_o, send_o, vec_o, proj_o, sums):
    c = lax.axis_index("band") & 1
    sums[...] = qp_k[0] + qp_a[0].astype(F32)
    keep_o[...] = sums[pl.ds(pl.multiple_of(c * 24, 8), 24), 0:QC]
    send_o[:, 0:QC] = sums[pl.ds(pl.multiple_of(24 - c * 24, 8), 24), 0:QC]
    vec = sums[:, QW:QS]
    vec_o[...] = vec
    send_o[:, QC : QC + SMALL] = vec[0:24]
    send_o[:, QC + SMALL :] = vec[24:48]
    proj_o[:, 0:HALF] = sums[0:24, QC:QW]
    proj_o[:, HALF:] = sums[24:48, QC:QW]


def out_kernel(
    keep, vec, arrived, we_keep, we_arrived, wr_keep, wr_arrived,
    qkv_o, first_o, bias_o, qv_o, bp_o, asc_o, gain2_o, bias2_o, br_o, msc_o, eb_o, we_o, wr_o, both,
):
    _, c, z, _ = place()
    wr_o[...] = jnp.where((z >> 1) == c, wr_keep[...], wr_arrived[...])
    we_o[:, pl.ds(pl.multiple_of(c * FH, 128), FH)] = we_keep[...]
    we_o[:, pl.ds(pl.multiple_of((1 - c) * FH, 128), FH)] = we_arrived[...]
    for m in range(3):
        mine = pl.multiple_of(m * D + c * HALF, 128)
        other = pl.multiple_of(m * D + (1 - c) * HALF, 128)
        qkv_o[:, pl.ds(mine, HALF)] = keep[:, m * HALF : (m + 1) * HALF]
        qkv_o[:, pl.ds(other, HALF)] = arrived[:, m * HALF : (m + 1) * HALF]
    both[0:24] = vec[0:24] + arrived[:, QC : QC + SMALL]
    both[24:48] = vec[24:48] + arrived[:, QC + SMALL :]
    own = both[pl.ds(pl.multiple_of(c * 24, 8), 24), :].T
    outs = (first_o, bias_o, None, None, bp_o, asc_o, gain2_o, bias2_o, br_o, msc_o)
    for r, out in enumerate(outs):
        if out is not None:
            out[...] = own[r]
    qv_o[...] = own[2:4]
    units = both[...].T
    units = jnp.where(c == 0, units[10:12], units[12:14])
    eb_o[...] = jnp.concatenate([units[0:1], units[1:2]], axis=1).reshape(96)


COSTS = {
    "first_kernel": (0, 0),
    "pick_kernel": (0, 0),
    "hidden_kernel": (0, 0),
    "reduce_grad_kernel": (1000000000, 4000000),
    "back_kernel": (0, 0),
    "expand_grad_kernel": (0, 0),
    "attention_back_kernel": (0, 0),
    "vectors_kernel": (8000000000, 20000000),
    "fold_kernel": (0, 0),
    "second_fold_kernel": (0, 2000000),
    "last_kernel": (0, 4000000),
    "spread_kernel": (0, 2000000),
    "finish_kernel": (0, 1000000),
    "out_kernel": (0, 1000000),
    "prepare_kernel": (0, 9000000),
    "hold_kernel": (0, 20000000),
    "home_kernel": (0, 0),
}


def call(kernel, outs, specs, scratch=(), vmem=24):
    return pl.pallas_call(
        kernel,
        out_shape=outs,
        in_specs=specs,
        out_specs=jax.tree.map(lambda _: VM, outs),
        scratch_shapes=list(scratch),
        compiler_params=pltpu.CompilerParams(vmem_limit_bytes=vmem * MIB),
        cost_estimate=pl.CostEstimate(flops=COSTS.get(kernel.__name__, (0, 0))[0], bytes_accessed=COSTS.get(kernel.__name__, (0, 0))[1], transcendentals=0),
    )


def fold_call(keep, arrived, after):
    half = (keep.shape[0] // 2, *keep.shape[1:])
    return call(fold_kernel, (vm(half, F32), vm(half, BF), TICK), [VM] * 2 + [ANY])(keep, arrived, after)


def by_core(value):
    return lax.ppermute(value, "band", [(i, i ^ 1) for i in range(4)])


def by_x(value):
    return lax.ppermute(value, "band", [(i, i ^ 2) for i in range(4)])


def by_y(value):
    return lax.ppermute(value, "batch", [(i, i ^ 1) for i in range(8)])


def by_z(value, dz):
    return lax.ppermute(value, "batch", [(i, i ^ (2 * dz)) for i in range(8)])


def homeward(value, dz):
    pairs = [(d, d ^ (8 * dz)) for d in range(32) if ((d ^ (8 * dz)) >> 4) == (d & 1)]
    return lax.ppermute(value, ("batch", "band"), pairs)


def packed_body(
    tokens, cotangent, visible, first_gain, first_bias, qkv_weight, qv_bias, proj_weight, proj_bias,
    attn_scale, second_gain, second_bias, expand_weight, expand_bias, reduce_weight, reduce_bias, mlp_scale,
):
    block = vm(cotangent.shape, BF)
    rows_f, rows_b = vm((ROWS, D), F32), vm((ROWS, D), BF)
    tok_x = by_x(tokens)
    tok_c = by_core(tokens)
    cot, tok_own, par, be, wqkv, wp, we, wr, vis = call(
        prepare_kernel,
        (
            block,
            block,
            vm((16, D), F32),
            vm((8, FH), F32),
            vm((3, D, HALF), BF),
            vm((D, D), BF),
            vm((D, FH), BF),
            vm((FH, D), BF),
            vm(visible.shape, visible.dtype),
        ),
        [ANY] * 17,
        [pltpu.SemaphoreType.DMA((20,))]
    )(
        *map(
            stay,
            (
                cotangent, first_gain, first_bias, qv_bias, proj_bias, attn_scale, second_gain, second_bias,
                reduce_bias, mlp_scale, expand_bias, qkv_weight, proj_weight, expand_weight, reduce_weight, visible,
                tokens,
            ),
        )
    )
    vis_x = by_x(vis)
    vis_c = by_core(vis)
    cot_c = by_core(cot)
    cot, tok_x = call(hold_kernel, (block, block), [VM] * 2 + [ANY] * 2)(cot, tok_x, vis_x, par)
    tok_d = by_core(tok_x)
    vis_d = by_core(vis_x)
    cot_x = by_x(cot)
    tok, normed, qkv, mix_own, mix2_own, pos, probs, pos_mine, pos_theirs = call(
        first_kernel,
        (
            rows_b,
            rows_b,
            vm((3, ROWS, HALF), BF),
            vm((ROWS, 256), BF),
            vm((ROWS, 128), BF),
            vm((8, SLOTS), F32),
            vm((9, 2 * PACK, PACK), F32),
            vm((16, BAND), F32),
            vm((16, BAND), F32),
        ),
        [VM] * 10,
        [pltpu.VMEM((IMGS, SLOTS, D), BF), pltpu.VMEM((16, 128), F32)],
    )(tok_own, tok_c, tok_x, tok_d, vis, vis_c, vis_x, vis_d, par, wqkv)
    mix_other, mix2_other = by_core(mix_own), by_core(mix2_own)
    pick, pick_p, pn = call(pick_kernel, (vm((D, HALF), BF), vm((D, 192), BF), vm((ROWS, HALF), BF)), [VM])(normed)
    res, one, n2, mix, act, slope, tick = call(
        hidden_kernel,
        (rows_f, rows_f, rows_b, rows_b, rows_b, rows_f, TICK),
        [VM] * 9 + [ANY],
    )(mix_own, mix_other, mix2_own, mix2_other, tok, par, be, wp, we, pick)
    cot_x = call(pass_kernel, block, [VM, ANY])(cot_x, tick)
    cot_d = by_core(cot_x)
    act_b, slope_b = call(more_hidden_kernel, (rows_b, rows_f), [VM] * 3)(n2, be, we)
    pre, gb2, wr_send, wr_keep = call(
        reduce_grad_kernel,
        (rows_b, rows_b, vm((4, 96, D), BF), vm((4, 96, D), BF)),
        [VM] * 8,
        [pltpu.VMEM((IMGS, SLOTS, D), BF), pltpu.VMEM((ROWS, D), BF), pltpu.VMEM((D, D), F32)],
    )(cot, cot_c, cot_x, cot_d, pos, par, act, act_b)
    wr_y = by_y(wr_send)
    half_b = vm((ROWS, HALF), BF)
    gh, left, right = call(back_kernel, (vm((ROWS, FH), BF), half_b, half_b), [VM] * 5)(gb2, wr, slope, slope_b, we)
    gn2 = (left, by_core(left), right, by_core(right))
    we_send, we_keep, tick = call(
        expand_grad_kernel,
        (vm((4, 48, FH), BF), vm((4, 48, FH), BF), TICK),
        [VM] * 3,
        [pltpu.VMEM((HALF, FH), F32)],
    )(n2, gh, pick)
    we_z = by_z(we_send, 1)
    gres, gp, qp_send, qp_keep, tick = call(
        attention_back_kernel,
        (rows_f, vm((ROWS, QC), BF), vm((4, 48, QW), BF), vm((4, 48, QW), BF), TICK),
        [VM] * 13 + [ANY],
        [pltpu.VMEM((HALF, QC), F32)],
    )(*gn2, res, pre, qkv, probs, mix, pn, pick_p, wp, par, tick)
    qp_y = by_y(qp_send)
    wr_keep, wr_send, tick = call(
        home_kernel, (vm((4, 96, D), F32), vm((4, 96, D), BF), TICK), [VM] * 2 + [ANY]
    )(wr_keep, wr_y, tick)
    wr_z = homeward(wr_send, 2)
    gb_keep, gb_send, vec_send, vec_keep, tick = call(
        vectors_kernel,
        (vm((2, *tokens.shape), BF), vm((2, *tokens.shape), BF), vm((2, 48, 2 * SMALL), BF), vm((2, 48, 2 * SMALL), BF), TICK),
        [VM] * 20 + [ANY],
        [pltpu.VMEM((SMALL, D), F32), pltpu.VMEM((FH, SMALL), F32)],
    )(*gn2, res, one, gres, gp, wqkv, act, act_b, wr, gb2, gh, pre, tok, pick, par, pos_mine, pos_theirs, tick)
    gb_other = by_core(gb_send)
    we_keep, we_send, tick = call(
        join_kernel, (vm((2, 48, FS), F32), vm((2, 48, FS), BF), TICK), [VM] * 4 + [ANY]
    )(we_keep, we_z, vec_keep, vec_send, tick)
    we_y = by_y(we_send)
    qp_keep, qp_send, tick = fold_call(qp_keep, qp_y, tick)
    qp_z = by_z(qp_send, 1)
    wr_keep, wr_send, tick = fold_call(wr_keep, wr_z, tick)
    wr_z = homeward(wr_send, 1)
    we_keep, we_send, vec_keep, vec_send, tick = call(
        part_kernel,
        (vm((1, 48, FH), F32), vm((1, 48, FH), BF), vm((2, 48, SMALL), F32), vm((2, 48, SMALL), BF), TICK),
        [VM] * 2 + [ANY],
    )(we_keep, we_y, tick)
    vec_z = by_z(vec_send, 1)
    we_z = by_z(we_send, 2)
    qp_keep, qp_send, tick = call(
        rejoin_kernel, (vm((1, 48, QS), F32), vm((1, 48, QS), BF), TICK), [VM] * 4 + [ANY]
    )(qp_keep, qp_z, vec_keep, vec_z, tick)
    qp_z = by_z(qp_send, 2)
    wr_keep, wr_send, we_keep, we_send, tick = call(
        settle_kernel,
        (vm((96, D), F32), vm((96, D), F32), vm((24, FH), F32), vm((24, FH), F32), TICK),
        [VM] * 4 + [ANY],
        [pltpu.VMEM((48, FH), F32)],
    )(wr_keep, wr_z, we_keep, we_z, tick)
    we_other, wr_other = by_core(we_send), by_core(wr_send)
    layer_out, grad_tokens, tick = call(
        last_kernel,
        (sds(tokens.shape, BF), sds(tokens.shape, BF), TICK),
        [VM] * 7 + [ANY],
    )(gb_keep, gb_other, tok_own, gres, res, pos_mine, par, tick)
    qp_keep, qp_send, vec, proj = call(
        finish_kernel,
        (vm((24, QC), F32), vm((24, QC + 2 * SMALL), F32), vm((48, SMALL), F32), sds((24, D), F32)),
        [VM] * 2 + [ANY],
        [pltpu.VMEM((48, QS), F32)],
    )(qp_keep, qp_z, tick)
    vector = sds((24,), F32)
    grad_qkv, gg1, gb1, gqv, gbp, gas, gg2, gb2, gbr, gms, geb, grad_expand, grad_reduce = call(
        out_kernel,
        (
            sds((24, 3 * D), F32), vector, vector, sds((2, 24), F32), vector, vector, vector, vector, vector, vector,
            sds((96,), F32), sds((24, FF), F32), sds((96, D), F32),
        ),
        [VM] * 7,
        [pltpu.VMEM((48, SMALL), F32)],
    )(qp_keep, vec, by_core(qp_send), we_keep, we_other, wr_keep, wr_other)
    return (
        layer_out, grad_tokens, gg1, gb1, grad_qkv, gqv, proj, gbp, gas, gg2, gb2, grad_expand, geb, grad_reduce,
        gbr, gms,
    )


def layer_norm(values, norm_gain, norm_shift):
    center = values - jnp.mean(values, axis=-1, keepdims=True)
    spread = jnp.mean(center * center, axis=-1, keepdims=True)
    return center * lax.rsqrt(spread + NORM_EPS) * norm_gain + norm_shift


def gelu_exact(values):
    return jax.nn.gelu(values, approximate=False)


def split_rows(packed_rows, mask_rows):
    item_count = packed_rows.shape[0]
    slot_count = packed_rows.shape[1]
    heads_here = packed_rows.shape[4] // HD
    unpacked = packed_rows.reshape(item_count, slot_count, 3, heads_here, HD)
    queries = unpacked[:, :, 0]
    key_rows = unpacked[:, :, 1]
    value_rows = unpacked[:, :, 2]
    key_valid = mask_rows.reshape(item_count, slot_count) > 0
    score_scale = 1.0 / math.sqrt(HD)
    scores = (
        jnp.einsum("bqhe,bkhe->bhqk", queries, key_rows, preferred_element_type=jnp.float32)
        * score_scale
    )
    scores = jnp.where(key_valid[:, None, None, :], scores, -1e30)
    return (queries, key_rows, value_rows, scores)


def attend_plain(inputs):
    packed_rows, mask_rows = inputs
    queries, key_rows, value_rows, scores = split_rows(packed_rows, mask_rows)
    row_top = jnp.max(scores, axis=-1, keepdims=True)
    raised = jnp.exp(scores - row_top)
    row_total = jnp.sum(raised, axis=-1, keepdims=True)
    attn_prob = raised / row_total
    log_total = (row_top + jnp.log(row_total))[..., 0]
    mixed_rows = jnp.einsum(
        "bhqk,bkhe->bqhe",
        attn_prob.astype(jnp.bfloat16),
        value_rows,
        preferred_element_type=jnp.float32,
    ).astype(jnp.bfloat16)
    mixed_rows = mixed_rows.reshape(
        packed_rows.shape[0], packed_rows.shape[1], packed_rows.shape[4]
    )
    return (mixed_rows, log_total)


def backward_rows(score_parts, log_total, grad_rows):
    queries, key_rows, value_rows, scores = score_parts
    item_count, slot_count, heads_here, head_size = queries.shape
    score_scale = 1.0 / math.sqrt(HD)
    attn_prob = jnp.exp(scores - log_total[..., None])
    grad_heads = grad_rows.reshape(item_count, slot_count, heads_here, head_size)
    grad_prob = jnp.einsum(
        "bqhe,bkhe->bhqk", grad_heads, value_rows, preferred_element_type=jnp.float32
    )
    row_delta = jnp.sum(attn_prob * grad_prob, axis=-1, keepdims=True)
    grad_score = (attn_prob * (grad_prob - row_delta)).astype(jnp.bfloat16)
    grad_query = (
        jnp.einsum("bhqk,bkhe->bqhe", grad_score, key_rows, preferred_element_type=jnp.float32)
        * score_scale
    )
    grad_key = (
        jnp.einsum("bhqk,bqhe->bkhe", grad_score, queries, preferred_element_type=jnp.float32)
        * score_scale
    )
    grad_value = jnp.einsum(
        "bhqk,bqhe->bkhe",
        attn_prob.astype(jnp.bfloat16),
        grad_heads,
        preferred_element_type=jnp.float32,
    )
    stacked = jnp.stack([grad_query, grad_key, grad_value], axis=2)
    return stacked.reshape(item_count, slot_count, 3, 1, heads_here * head_size).astype(
        jnp.bfloat16
    )


def attend_again(inputs):
    packed_rows, mask_rows, grad_rows = inputs
    score_parts = split_rows(packed_rows, mask_rows)
    scores = score_parts[3]
    row_top = jnp.max(scores, axis=-1, keepdims=True)
    log_total = (row_top + jnp.log(jnp.sum(jnp.exp(scores - row_top), axis=-1, keepdims=True)))[
        ..., 0
    ]
    return backward_rows(score_parts, log_total, grad_rows)


def body(
    tokens,
    cotangent,
    visible,
    first_gain,
    first_bias,
    qkv_weight,
    qv_bias,
    proj_weight,
    proj_bias,
    attn_scale,
    second_gain,
    second_bias,
    expand_weight,
    expand_bias,
    reduce_weight,
    reduce_bias,
    mlp_scale,
):
    images, slot_count, model_width = tokens.shape
    groups = lax.axis_size("band")
    local_width = model_width // groups
    inputs_full = tokens.astype(jnp.float32)
    shown_mask = visible.astype(jnp.float32)
    normed, first_pull = jax.vjp(layer_norm, inputs_full, first_gain, first_bias)
    normed_low = normed.astype(jnp.bfloat16)
    qkv_bias = jnp.concatenate([qv_bias[0], jnp.zeros((model_width,), jnp.float32), qv_bias[1]])

    def project_qkv():
        product = jnp.einsum(
            "isd,de->ise", normed_low, qkv_weight, preferred_element_type=jnp.float32
        )
        return (
            (product + qkv_bias)
            .astype(jnp.bfloat16)
            .reshape(images, slot_count, 3, groups, local_width)
        )

    packed = project_qkv()
    mask_part = jnp.broadcast_to(
        shown_mask.astype(jnp.bfloat16)[:, :, None, None, None], (images, slot_count, 1, groups, 1)
    )
    results = attend_plain(
        (
            lax.all_to_all(packed, "band", split_axis=3, concat_axis=1, tiled=True),
            lax.all_to_all(mask_part, "band", split_axis=3, concat_axis=1, tiled=True),
        )
    )
    mixed_heads = results[0].reshape(images, groups * slot_count, 1, local_width)
    back_rows = lax.all_to_all(mixed_heads, "band", split_axis=1, concat_axis=2, tiled=True)
    mixed_rows = back_rows.reshape(images, slot_count, model_width)
    branch_one = (
        jnp.einsum("isd,de->ise", mixed_rows, proj_weight, preferred_element_type=jnp.float32)
        + proj_bias
    )
    residual = inputs_full + attn_scale * branch_one
    normed_two, second_pull = jax.vjp(layer_norm, residual, second_gain, second_bias)
    normed_two_low = normed_two.astype(jnp.bfloat16)
    hidden = (
        jnp.einsum("isd,df->isf", normed_two_low, expand_weight, preferred_element_type=jnp.float32)
        + expand_bias
    )
    activated, gelu_pull = jax.vjp(gelu_exact, hidden)
    activated_low = activated.astype(jnp.bfloat16)
    branch_two = (
        jnp.einsum("isf,fd->isd", activated_low, reduce_weight, preferred_element_type=jnp.float32)
        + reduce_bias
    )
    layer_out = (shown_mask[..., None] * (residual + mlp_scale * branch_two)).astype(jnp.bfloat16)
    grad_pre = shown_mask[..., None] * cotangent.astype(jnp.float32)
    grad_mlp_scale = jnp.sum(grad_pre * branch_two, axis=(0, 1))
    grad_branch_two = (mlp_scale * grad_pre).astype(jnp.bfloat16)
    grad_reduce_weight = jnp.einsum(
        "isf,isd->fd", activated_low, grad_branch_two, preferred_element_type=jnp.float32
    )
    grad_reduce_bias = jnp.sum(grad_branch_two.astype(jnp.float32), axis=(0, 1))
    grad_activated = jnp.einsum(
        "isd,fd->isf", grad_branch_two, reduce_weight, preferred_element_type=jnp.float32
    )
    grad_hidden = gelu_pull(grad_activated)[0].astype(jnp.bfloat16)
    grad_expand_weight = jnp.einsum(
        "isd,isf->df", normed_two_low, grad_hidden, preferred_element_type=jnp.float32
    )
    grad_expand_bias = jnp.sum(grad_hidden.astype(jnp.float32), axis=(0, 1))
    grad_normed_two = jnp.einsum(
        "isf,df->isd", grad_hidden, expand_weight, preferred_element_type=jnp.float32
    )
    grad_resid_norm, grad_second_gain, grad_second_bias = second_pull(grad_normed_two)
    grad_residual = grad_pre + grad_resid_norm
    grad_attn_scale = jnp.sum(grad_residual * branch_one, axis=(0, 1))
    grad_branch_one = (attn_scale * grad_residual).astype(jnp.bfloat16)
    grad_proj_weight = jnp.einsum(
        "isd,ise->de", mixed_rows, grad_branch_one, preferred_element_type=jnp.float32
    )
    grad_proj_bias = jnp.sum(grad_branch_one.astype(jnp.float32), axis=(0, 1))
    grad_mixed = jnp.einsum(
        "ise,de->isd", grad_branch_one, proj_weight, preferred_element_type=jnp.float32
    )
    grad_mixed = grad_mixed.astype(jnp.bfloat16).reshape(images, slot_count, 1, groups, local_width)
    repacked = project_qkv()
    grad_packed = attend_again(
        (
            lax.all_to_all(repacked, "band", split_axis=3, concat_axis=1, tiled=True),
            lax.all_to_all(mask_part, "band", split_axis=3, concat_axis=1, tiled=True),
            lax.all_to_all(grad_mixed, "band", split_axis=3, concat_axis=1, tiled=True),
        )
    )
    grad_bands = lax.all_to_all(grad_packed, "band", split_axis=1, concat_axis=3, tiled=True)
    grad_qkv = grad_bands.reshape(images, slot_count, 3 * model_width)
    grad_qkv_weight = jnp.einsum(
        "isd,ise->de", normed_low, grad_qkv, preferred_element_type=jnp.float32
    )
    column_sums = jnp.sum(grad_qkv.astype(jnp.float32), axis=(0, 1))
    grad_qv_bias = jnp.stack([column_sums[:model_width], column_sums[2 * model_width :]])
    grad_normed = jnp.einsum(
        "ise,de->isd", grad_qkv, qkv_weight, preferred_element_type=jnp.float32
    )
    grad_input_norm, grad_first_gain, grad_first_bias = first_pull(grad_normed)
    grad_tokens = (grad_residual + grad_input_norm).astype(jnp.bfloat16)
    all_sums = (
        lax.psum_scatter(grad_first_gain, ("batch", "band"), scatter_dimension=0, tiled=True),
        lax.psum_scatter(grad_first_bias, ("batch", "band"), scatter_dimension=0, tiled=True),
        lax.psum_scatter(grad_qkv_weight, ("batch", "band"), scatter_dimension=0, tiled=True),
        lax.psum_scatter(grad_qv_bias, ("batch", "band"), scatter_dimension=1, tiled=True),
        lax.psum_scatter(grad_proj_weight, ("batch", "band"), scatter_dimension=0, tiled=True),
        lax.psum_scatter(grad_proj_bias, ("batch", "band"), scatter_dimension=0, tiled=True),
        lax.psum_scatter(grad_attn_scale, ("batch", "band"), scatter_dimension=0, tiled=True),
        lax.psum_scatter(grad_second_gain, ("batch", "band"), scatter_dimension=0, tiled=True),
        lax.psum_scatter(grad_second_bias, ("batch", "band"), scatter_dimension=0, tiled=True),
        lax.psum_scatter(grad_expand_weight, ("batch", "band"), scatter_dimension=0, tiled=True),
        lax.psum_scatter(grad_expand_bias, ("batch", "band"), scatter_dimension=0, tiled=True),
        lax.psum_scatter(grad_reduce_weight, ("batch", "band"), scatter_dimension=0, tiled=True),
        lax.psum_scatter(grad_reduce_bias, ("batch", "band"), scatter_dimension=0, tiled=True),
        lax.psum_scatter(grad_mlp_scale, ("batch", "band"), scatter_dimension=0, tiled=True),
    )
    (
        sum_first_gain,
        sum_first_bias,
        sum_qkv_weight,
        sum_qv_bias,
        sum_proj_weight,
        sum_proj_bias,
        sum_attn_scale,
        sum_second_gain,
        sum_second_bias,
        sum_expand_weight,
        sum_expand_bias,
        sum_reduce_weight,
        sum_reduce_bias,
        sum_mlp_scale,
    ) = all_sums
    return (
        layer_out,
        grad_tokens,
        sum_first_gain,
        sum_first_bias,
        sum_qkv_weight,
        sum_qv_bias,
        sum_proj_weight,
        sum_proj_bias,
        sum_attn_scale,
        sum_second_gain,
        sum_second_bias,
        sum_expand_weight,
        sum_expand_bias,
        sum_reduce_weight,
        sum_reduce_bias,
        sum_mlp_scale,
    )


def solution(mesh):
    sizes = dict(mesh.shape)
    chosen = packed_body if (sizes["batch"], sizes["band"]) == (8, 4) else body
    placed = (
        P("batch", "band", None),
        P("batch", "band", None),
        P("batch", "band"),
        P(),
        P(),
        P(),
        P(),
        P(),
        P(),
        P(),
        P(),
        P(),
        P(),
        P(),
        P(),
        P(),
        P(),
    )
    return jax.shard_map(
        chosen,
        mesh=mesh,
        in_specs=placed,
        out_specs=(
            P("batch", "band", None),
            P("batch", "band", None),
            P(("batch", "band")),
            P(("batch", "band")),
            P(("batch", "band"), None),
            P(None, ("batch", "band")),
            P(("batch", "band"), None),
            P(("batch", "band")),
            P(("batch", "band")),
            P(("batch", "band")),
            P(("batch", "band")),
            P(("batch", "band"), None),
            P(("batch", "band")),
            P(("batch", "band"), None),
            P(("batch", "band")),
            P(("batch", "band")),
        ),
        check_vma=False,
    )
```

```python
import math

import jax
import jax.numpy as jnp
from jax import lax
from jax.experimental import pallas as pl
from jax.experimental.pallas import tpu as pltpu
from jax.sharding import PartitionSpec as P

HD = 64
NORM_EPS = 1e-06
PACK = 144
SLOTS = 256
BAND = 64
IMGS = 3
ROWS = IMGS * PACK
D = 768
HALF = D // 2
FF = 3072
FH = FF // 2
SMALL = 128
MIB = 1024 * 1024
F32 = jnp.float32
BF = jnp.bfloat16
ANY = pl.BlockSpec(memory_space=pl.ANY)
HBM = pl.BlockSpec(memory_space=pltpu.HBM)
VM = pl.BlockSpec(memory_space=pltpu.VMEM)


def dot(a, b):
    return jnp.dot(a, b, preferred_element_type=F32)


def dot_nt(a, b):
    return lax.dot_general(a, b, (((1,), (1,)), ((), ())), preferred_element_type=F32)


def dot_tn(a, b):
    return lax.dot_general(a, b, (((0,), (0,)), ((), ())), preferred_element_type=F32)


def sds(shape, dtype):
    return jax.ShapeDtypeStruct(shape, dtype)


def vm(shape, dtype):
    return pltpu.VMEM(shape, dtype)


def stay(value):
    return pltpu.with_memory_space_constraint(value, pltpu.HBM)


def place():
    band = lax.axis_index("band")
    batch = lax.axis_index("batch")
    return band >> 1, band & 1, batch >> 1, batch & 1


def one_hot_pack(pos, image):
    rows = lax.broadcasted_iota(jnp.int32, (PACK, pos.shape[1]), 0).astype(F32)
    return jnp.where(rows == pos[image : image + 1, :], 1.0, 0.0).astype(BF)


def shard_picks():
    x, c, z, y = place()

    def pick(width, base):
        lane = lax.broadcasted_iota(jnp.int32, (1, 8 * width), 1)
        want = jnp.zeros((1, 8 * width), jnp.int32)
        for q in range(8):
            first = 96 * ((z ^ (q % 4)) * 2 + (y ^ (q // 4))) + base - width * q
            want = jnp.where((lane >= width * q) & (lane < width * (q + 1)), lane + first, want)
        row = lax.broadcasted_iota(jnp.int32, (D, 8 * width), 0)
        return jnp.where(row == want, 1.0, 0.0).astype(BF)

    return pick(48, 48 * x), pick(24, 48 * x + 24 * c)


def statistics(values):
    center = values - jnp.mean(values, axis=-1, keepdims=True)
    rstd = lax.rsqrt(jnp.mean(center * center, axis=-1, keepdims=True) + NORM_EPS)
    return center * rstd, rstd


def norm_back(grad, z, rstd):
    return rstd * (
        grad
        - jnp.mean(grad, axis=-1, keepdims=True)
        - z * jnp.mean(grad * z, axis=-1, keepdims=True)
    )


def gather_bands(blocks, dst):
    band = lax.axis_index("band")
    for k, block in enumerate(blocks):
        at = pl.multiple_of((band ^ k) * BAND, BAND)
        for i in range(IMGS):
            rows = block[i] if len(block.shape) == 3 else block[i * BAND : (i + 1) * BAND, :]
            dst[i, pl.ds(at, BAND), :] = rows


def two_heads(v):
    lane = lax.broadcasted_iota(jnp.int32, v.shape, 1)
    none = jnp.zeros_like(v)
    return jnp.concatenate([jnp.where(lane < HD, v, none), jnp.where(lane < HD, none, v)], axis=0)


def join_heads(v):
    lane = lax.broadcasted_iota(jnp.int32, (PACK, 128), 1)
    return jnp.where(lane < HD, v[:PACK], v[PACK:])


def keys_shown(pos, image):
    shown = jnp.sum(jnp.where(pos[image : image + 1, :] >= 0, 1.0, 0.0), axis=-1, keepdims=True)
    return lax.broadcasted_iota(jnp.int32, (1, PACK), 1).astype(F32) < shown


TICK = vm((8, 128), F32)
GAIN1, BIAS1, QB, VB, PB, ASC, GAIN2, BIAS2, RB, MSC = range(10)


OWN = IMGS * BAND


def prepare_kernel(
    cot, gain1, bias1, qvb, bp, asc, gain2, bias2, br, msc, be, wqkv, wp, we, wr, visible, tok,
    cot_o, own_o, par_o, be_o, wqkv_o, wp_o, we_o, wr_o, vis_o,
    vis, sems,
):
    c = lax.axis_index("band") & 1
    units = pl.multiple_of(c * FH, 128)
    rows = (
        (GAIN1, gain1), (BIAS1, bias1), (QB, qvb.at[0]), (VB, qvb.at[1]), (PB, bp), (ASC, asc),
        (GAIN2, gain2), (BIAS2, bias2), (RB, br), (MSC, msc),
    )
    moves = [(cot, cot_o)] + [(v, par_o.at[r]) for r, v in rows]
    moves += [(be.at[pl.ds(units, FH)], be_o.at[0])]
    for m in range(3):
        moves.append((wqkv.at[:, pl.ds(pl.multiple_of(m * D + c * HALF, 128), HALF)], wqkv_o.at[m]))
    moves += [(wp, wp_o), (we.at[:, pl.ds(units, FH)], we_o), (wr.at[pl.ds(units, FH), :], wr_o)]
    moves += [(tok.at[i], own_o.at[pl.ds(i * BAND, BAND), :]) for i in range(IMGS)]
    moves += [(visible, vis)]
    copies = [pltpu.make_async_copy(a, b, sems.at[i]) for i, (a, b) in enumerate(moves)]
    for copy in copies:
        copy.start()
    copies[-1].wait()
    seen = jnp.concatenate([vis[...].astype(F32), jnp.zeros((IMGS, 128 - BAND), F32)], axis=1)
    seen = jnp.concatenate([seen, jnp.zeros((16 - IMGS, 128), F32)], axis=0).astype(BF)
    vis_o[...] = seen
    own_o[OWN:, :] = jnp.zeros((16, D), BF)
    own_o[OWN:, 0:128] = seen
    for copy in copies[:-1]:
        copy.wait()


def hold_kernel(tok, vis, after, out):
    for i in range(IMGS):
        out[i * BAND : (i + 1) * BAND, :] = tok[i]
    out[OWN:, :] = jnp.zeros((16, D), BF)
    out[OWN:, 0:128] = vis[...]


def first_kernel(
    t0, t1, t2, t3, par, w,
    tok_o, norm_o, qkv_o, mix_o, mix2_o, pos_o, probs_o, mine_o, theirs_o,
    xs,
):
    band = lax.axis_index("band")
    c = band & 1
    gather_bands((t0, t1, t2, t3), xs)
    heads = pl.multiple_of(c * HALF, 128)
    to = lax.broadcasted_iota(jnp.int32, (BAND, SLOTS), 1) - lax.broadcasted_iota(jnp.int32, (BAND, SLOTS), 0)
    vis = jnp.zeros((16, SLOTS), F32)
    for k, t in enumerate((t0, t1, t2, t3)):
        vis = vis + dot(t[OWN:, 0:BAND], jnp.where(to == (band ^ k) * BAND, 1.0, 0.0).astype(BF))
    upto = lax.broadcasted_iota(jnp.int32, (SLOTS, SLOTS), 0)
    slot = lax.broadcasted_iota(jnp.int32, (SLOTS, SLOTS), 1)
    before = jnp.where(upto < slot, 1.0, 0.0).astype(BF)
    pos = jnp.where(vis > 0, dot(vis.astype(BF), before), -1.0)
    pos_o[...] = pos[0:8]
    slot = lax.broadcasted_iota(jnp.int32, (SLOTS, BAND), 0) - lax.broadcasted_iota(jnp.int32, (SLOTS, BAND), 1)
    for out, b in ((mine_o, band), (theirs_o, band ^ 1)):
        out[...] = dot(pos.astype(BF), jnp.where(slot == b * BAND, 1.0, 0.0).astype(BF))
    for i in range(IMGS):
        rows = slice(i * PACK, (i + 1) * PACK)
        tok = dot(one_hot_pack(pos, i), xs[i])
        tok_o[rows, :] = tok.astype(BF)
        z, _ = statistics(tok)
        norm_o[rows, :] = (z * par[GAIN1 : GAIN1 + 1, :] + par[BIAS1 : BIAS1 + 1, :]).astype(BF)
    normed = norm_o[...]
    for m in range(3):
        part = dot(normed, w[m])
        if m != 1:
            r = QB if m == 0 else VB
            part = part + par[r : r + 1, pl.ds(heads, HALF)]
        qkv_o[m] = part.astype(BF)
    for i in range(IMGS):
        rows = slice(i * PACK, (i + 1) * PACK)
        key_ok = keys_shown(pos, i)
        for hp in range(3):
            cols = slice(hp * 128, (hp + 1) * 128)
            q2, k2, v2 = (qkv_o[m, rows, cols] for m in range(3))
            scores = dot_nt(two_heads(q2), k2) * (1.0 / math.sqrt(HD))
            scores = jnp.where(key_ok, scores, -1e30)
            raised = jnp.exp(scores - jnp.max(scores, axis=-1, keepdims=True))
            probs = raised / jnp.sum(raised, axis=-1, keepdims=True)
            probs_o[i * 3 + hp] = probs
            mixed = join_heads(dot(probs.astype(BF), v2)).astype(BF)
            if hp < 2:
                mix_o[rows, cols] = mixed
            else:
                mix2_o[rows, :] = mixed


def pick_kernel(normed, pick_o, pick_p_o, pn_o):
    pick, pick_p = shard_picks()
    pick_o[...] = pick
    pick_p_o[...] = pick_p
    pn_o[...] = dot(normed[...], pick).astype(BF)


def hidden_units(n2, be, we, cols, act_o, slope_o):
    step = 256
    for f in range(cols // step):
        at = slice(f * step, (f + 1) * step)
        hidden = dot(n2[...], we[:, at]) + be[0:1, at]
        phi = 0.5 * (1.0 + lax.erf(hidden * math.sqrt(0.5)))
        act_o[:, at] = (hidden * phi).astype(BF)
        slope_o[:, at] = phi + hidden * (jnp.exp(-0.5 * hidden * hidden) * (1.0 / math.sqrt(2.0 * math.pi)))


def hidden_kernel(
    mix_a, mix_b, mix2_a, mix2_b, tok, par, be, wp, we, after, res_o, one_o, n2_o, mix_o, act_o, slope_o, tick
):
    tick[...] = jnp.zeros_like(tick)
    c = lax.axis_index("band") & 1
    mine, other = pl.multiple_of(c * HALF, 128), pl.multiple_of((1 - c) * HALF, 128)
    for at, first, second in ((mine, mix_a, mix2_a), (other, mix_b, mix2_b)):
        mix_o[:, pl.ds(at, 256)] = first[...]
        mix_o[:, pl.ds(pl.multiple_of(at + 256, 128), 128)] = second[...]
    one = dot(mix_o[...], wp[...]) + par[PB : PB + 1, :]
    one_o[...] = one
    residual = tok[...].astype(F32) + par[ASC : ASC + 1, :] * one
    res_o[...] = residual
    z, _ = statistics(residual)
    n2_o[...] = (z * par[GAIN2 : GAIN2 + 1, :] + par[BIAS2 : BIAS2 + 1, :]).astype(BF)
    hidden_units(n2_o, be, we, D, act_o, slope_o)


def more_hidden_kernel(n2, be, we, act_o, slope_o):
    hidden_units(n2, be.at[:, D:FH], we.at[:, D:FH], FH - D, act_o, slope_o)


def pass_kernel(v, after, out):
    out[...] = v[...]


def reduce_grad_kernel(c0, c1, c2, c3, pos_r, par, act_a, act_b, pre_o, gb2_o, send_o, keep_o, xs, act_x, full):
    x, c, z, y = place()
    gather_bands((c0, c1, c2, c3), xs)
    pos = pos_r[...]
    for i in range(IMGS):
        rows = slice(i * PACK, (i + 1) * PACK)
        pre = dot(one_hot_pack(pos, i), xs[i])
        pre_o[rows, :] = pre.astype(BF)
        gb2_o[rows, :] = (par[MSC : MSC + 1, :] * pre).astype(BF)
    for j in range(4):
        act = act_a if j < 2 else act_b
        lo = 384 * (j & 1)
        mid, hi = lo + 192, lo + 384
        act_x[:, 192 * j : 192 * j + 192] = jnp.where(x == 0, act[:, lo:mid], act[:, mid:hi])
    full[...] = dot_tn(act_x[...], gb2_o[...])
    for dy, out in ((1, send_o), (0, keep_o)):
        for dz in range(2):
            j = 2 * ((z & 1) ^ dz) + (y ^ dy)
            for to in range(2):
                at = pl.multiple_of(192 * j + 96 * to, 96)
                out[2 * dz + to] = full[pl.ds(at, 96), :].astype(BF)


def back_kernel(gb2, wr, slope_a, slope_b, we, gh_o, left_o, right_o):
    step = 256
    for f in range(FH // step):
        cols = slice(f * step, (f + 1) * step)
        back = dot_nt(gb2[...], wr[cols, :])
        slope = slope_a if f < 3 else slope_b
        at = slice((f % 3) * step, (f % 3 + 1) * step)
        gh_o[:, cols] = (back * slope[:, at]).astype(BF)
    gn2 = dot_nt(gh_o[...], we[...]).astype(BF)
    left_o[...] = gn2[:, :HALF]
    right_o[...] = gn2[:, HALF:]


def expand_grad_kernel(n2, gh, pick, send_o, keep_o, tick, wide):
    tick[...] = jnp.zeros_like(tick)
    picked = dot(n2[...], pick[...]).astype(BF)
    wide[...] = dot_tn(picked, gh[...])
    for low, out in ((1, send_o), (0, keep_o)):
        for i in range(4):
            lo = 192 * (i >> 1) + 48 * (low + 2 * (i & 1))
            out[i] = wide[lo : lo + 48, :].astype(BF)


QC = 3 * HALF
QW = QC + HALF
FS = FH + 2 * SMALL


def both_halves(l_a, l_b, r_a, r_b):
    left = l_a[...].astype(F32) + l_b[...].astype(F32)
    right = r_a[...].astype(F32) + r_b[...].astype(F32)
    return jnp.concatenate([left, right], axis=1)


def attention_back_kernel(
    l_a, l_b, r_a, r_b, res, pre, qkv, probs_r, mix, pn, pick_p, wp, par, after,
    gres_o, gp, send_o, keep_o, tick,
    flat,
):
    tick[...] = jnp.zeros_like(tick)
    c = lax.axis_index("band") & 1
    heads = pl.multiple_of(c * HALF, 128)
    gn2 = both_halves(l_a, l_b, r_a, r_b)
    z2, rstd2 = statistics(res[...])
    gres = pre[...].astype(F32) + norm_back(gn2 * par[GAIN2 : GAIN2 + 1, :], z2, rstd2)
    gres_o[...] = gres
    gb1 = (par[ASC : ASC + 1, :] * gres).astype(BF)
    gm = dot_nt(gb1, wp[pl.ds(heads, HALF), :]).astype(BF)
    scale = 1.0 / math.sqrt(HD)
    for i in range(IMGS):
        rows = slice(i * PACK, (i + 1) * PACK)
        for hp in range(3):
            cols = slice(hp * 128, (hp + 1) * 128)
            q2, k2, v2 = (qkv[m, rows, cols] for m in range(3))
            probs = probs_r[i * 3 + hp]
            g2 = two_heads(gm[rows, cols])
            gprob = dot_nt(g2, v2)
            delta = jnp.sum(probs * gprob, axis=-1, keepdims=True)
            gscore = (probs * (gprob - delta)).astype(BF)
            parts = (
                join_heads(dot(gscore, k2)) * scale,
                dot_tn(gscore, two_heads(q2)) * scale,
                dot_tn(probs.astype(BF), g2),
            )
            for m in range(3):
                gp[rows, m * HALF + hp * 128 : m * HALF + (hp + 1) * 128] = parts[m].astype(BF)
    mixed = dot(mix[...], pick_p[...]).astype(BF)
    proj = dot_tn(mixed, gb1)
    flat[...] = dot_tn(pn[...], gp[...])
    for dy, out in ((1, send_o), (0, keep_o)):
        for i, dz in enumerate((0, 2, 1, 3)):
            q = 4 * dy + dz
            out[i, :, 0:QC] = flat[48 * q : 48 * q + 48, :].astype(BF)
            block = proj[24 * q : 24 * q + 24]
            out[i, :, QC:QW] = jnp.concatenate([block[:, :HALF], block[:, HALF:]], axis=0).astype(BF)


def vectors_kernel(
    l_a, l_b, r_a, r_b, res, one, gres, gp, w, act_a, act_b, wr, gb2, gh, pre, tok, pick, par, mine, theirs, after,
    gb_keep, gb_send, send_o, keep_o, tick,
    vecs, sums,
):
    tick[...] = jnp.zeros_like(tick)
    x, c, z, y = place()
    heads = pl.multiple_of(c * HALF, 128)
    first = jnp.where(c == 0, 1.0, 0.0)

    def total(v):
        return jnp.sum(v, axis=0, keepdims=True)

    vecs[...] = jnp.zeros_like(vecs)
    gnp = jnp.zeros((ROWS, D), F32)
    for m in range(3):
        gnp = gnp + dot_nt(gp[:, m * HALF : (m + 1) * HALF], w[m])
    z1, _ = statistics(tok[...].astype(F32))
    vecs[GAIN1 : GAIN1 + 1, :] = total(gnp * z1)
    vecs[BIAS1 : BIAS1 + 1, :] = total(gnp)
    vecs[QB : QB + 1, pl.ds(heads, HALF)] = total(gp[:, 0:HALF].astype(F32))
    vecs[VB : VB + 1, pl.ds(heads, HALF)] = total(gp[:, 2 * HALF : 3 * HALF].astype(F32))
    gb1 = (par[ASC : ASC + 1, :] * gres[...]).astype(BF)
    vecs[PB : PB + 1, :] = first * total(gb1.astype(F32))
    vecs[ASC : ASC + 1, :] = first * total(gres[...] * one[...])
    gn2 = both_halves(l_a, l_b, r_a, r_b)
    z2, _ = statistics(res[...])
    vecs[GAIN2 : GAIN2 + 1, :] = first * total(gn2 * z2)
    vecs[BIAS2 : BIAS2 + 1, :] = first * total(gn2)
    vecs[RB : RB + 1, :] = first * total(gb2[...].astype(F32))
    two = dot(act_a[...], wr[0:D, :]) + dot(act_b[...], wr[D:FH, :])
    for m, value in enumerate((gnp.astype(BF), two.astype(BF))):
        for i in range(IMGS):
            rows = slice(i * PACK, (i + 1) * PACK)
            for at, out in ((mine, gb_keep), (theirs, gb_send)):
                out[m, i] = dot_tn(one_hot_pack(at[...], i), value[rows]).astype(BF)
    vecs[MSC : MSC + 1, :] = total(pre[...].astype(F32) * (two + first * par[RB : RB + 1, :]))
    cols = dot(vecs[...].astype(BF), pick[...]).T
    sums[...] = dot_tn(gh[...], jnp.ones((ROWS, SMALL), BF))
    lane = lax.broadcasted_iota(jnp.int32, (48, SMALL), 1)
    for dy, out in ((1, send_o), (0, keep_o)):
        for dz in range(4):
            b = (z ^ dz) * 2 + (y ^ dy)
            q = 4 * dy + dz
            block = cols[48 * q : 48 * q + 48]
            for k in range(4):
                at = pl.multiple_of(384 * (b & 3) + 192 * x + 48 * k, 48)
                block = jnp.where((lane == 10 + k) & ((b >> 2) == c), sums[pl.ds(at, 48), :], block)
            out[dz >> 1, :, SMALL * (dz & 1) : SMALL * (dz & 1) + SMALL] = block.astype(BF)


def last_kernel(gb_a, gb_b, tok, gres, res, mine, par, after, out_o, gtok_o, tick):
    tick[...] = jnp.zeros_like(tick)

    def own_rows(pack, value):
        high = value.astype(BF)
        return dot_tn(pack, high) + dot_tn(pack, (value - high.astype(F32)).astype(BF))

    for i in range(IMGS):
        rows = slice(i * PACK, (i + 1) * PACK)
        pack = one_hot_pack(mine[...], i)
        z1, rstd1 = statistics(tok[i * BAND : (i + 1) * BAND, :].astype(F32))
        gnp = gb_a[0, i].astype(F32) + gb_b[0, i].astype(F32)
        gtok = own_rows(pack, gres[rows, :]) + norm_back(gnp * par[GAIN1 : GAIN1 + 1, :], z1, rstd1)
        gtok_o[i] = gtok.astype(BF)
        ones = dot_tn(pack, jnp.ones((PACK, D), BF))
        two = gb_a[1, i].astype(F32) + gb_b[1, i].astype(F32) + ones * par[RB : RB + 1, :]
        out_o[i] = (own_rows(pack, res[rows, :]) + par[MSC : MSC + 1, :] * two).astype(BF)


def fold(keep, arrived, keep_o, send_o):
    half = keep.shape[0] // 2
    for i in range(half):
        keep_o[i] = keep[i].astype(F32) + arrived[i].astype(F32)
        send_o[i] = (keep[half + i].astype(F32) + arrived[half + i].astype(F32)).astype(BF)


def fold_kernel(keep, arrived, after, keep_o, send_o, tick):
    tick[...] = jnp.zeros_like(tick)
    fold(keep, arrived, keep_o, send_o)


def home_kernel(keep, arrived, after, keep_o, send_o, tick):
    tick[...] = jnp.zeros_like(tick)
    for i in range(4):
        total = keep[i].astype(F32) + arrived[i].astype(F32)
        keep_o[i] = total
        send_o[i] = total.astype(BF)


def fold(keep, arrived, keep_o, send_o):
    half = keep.shape[0] // 2
    for i in range(half):
        keep_o[i] = keep[i].astype(F32) + arrived[i].astype(F32)
        send_o[i] = (keep[half + i].astype(F32) + arrived[half + i].astype(F32)).astype(BF)


def fold_kernel(keep, arrived, after, keep_o, send_o, tick):
    tick[...] = jnp.zeros_like(tick)
    fold(keep, arrived, keep_o, send_o)


def second_fold_kernel(keep, arrived, we_keep, we_arrived, after, keep_o, send_o, we_keep_o, we_send_o, tick):
    tick[...] = jnp.zeros_like(tick)
    for i in range(2):
        total = keep[i] + arrived[i].astype(F32)
        keep_o[i] = total
        send_o[i] = total.astype(BF)
    fold(we_keep, we_arrived, we_keep_o, we_send_o)


def join_kernel(keep, arrived, vec_keep, vec_send, after, keep_o, send_o, tick):
    tick[...] = jnp.zeros_like(tick)
    fold(keep, arrived, keep_o.at[:, :, 0:FH], send_o.at[:, :, 0:FH])
    keep_o[:, :, FH:FS] = vec_keep[...].astype(F32)
    send_o[:, :, FH:FS] = vec_send[...]


def part_kernel(keep, arrived, after, keep_o, send_o, vec_ko, vec_so, tick):
    tick[...] = jnp.zeros_like(tick)
    fold(keep.at[:, :, 0:FH], arrived.at[:, :, 0:FH], keep_o, send_o)
    for hi in range(2):
        total = keep[hi, :, FH:FS] + arrived[hi, :, FH:FS].astype(F32)
        vec_ko[hi] = total[:, 0:SMALL]
        vec_so[hi] = total[:, SMALL:].astype(BF)


def settle_kernel(wr_k, wr_a, we_k, we_a, after, wr_ko, wr_so, we_ko, we_so, tick, both):
    tick[...] = jnp.zeros_like(tick)
    c = lax.axis_index("band") & 1
    for at, out in ((c, wr_ko), (1 - c, wr_so)):
        out[...] = (wr_k[at] + wr_a[at].astype(F32)).astype(out.dtype)
    both[...] = we_k[0] + we_a[0].astype(F32)
    we_ko[...] = both[pl.ds(pl.multiple_of(c * 24, 8), 24), :]
    we_so[...] = both[pl.ds(pl.multiple_of(24 - c * 24, 8), 24), :]


def finish_kernel(qp_k, qp_a, vec_k, vec_a, after, keep_o, send_o, vec_o, proj_o, sums):
    c = lax.axis_index("band") & 1
    sums[...] = qp_k[0] + qp_a[0].astype(F32)
    keep_o[...] = sums[pl.ds(pl.multiple_of(c * 24, 8), 24), 0:QC]
    send_o[:, 0:QC] = sums[pl.ds(pl.multiple_of(24 - c * 24, 8), 24), 0:QC]
    vec = vec_k[0] + vec_a[0].astype(F32)
    vec_o[...] = vec
    send_o[:, QC : QC + SMALL] = vec[0:24]
    send_o[:, QC + SMALL :] = vec[24:48]
    proj_o[:, 0:HALF] = sums[0:24, QC:QW]
    proj_o[:, HALF:] = sums[24:48, QC:QW]


def out_kernel(
    keep, vec, arrived, we_keep, we_arrived, wr_keep, wr_arrived,
    qkv_o, first_o, bias_o, qv_o, bp_o, asc_o, gain2_o, bias2_o, br_o, msc_o, eb_o, we_o, wr_o, both,
):
    _, c, z, _ = place()
    wr_o[...] = jnp.where((z >> 1) == c, wr_keep[...], wr_arrived[...].astype(F32))
    we_o[:, pl.ds(pl.multiple_of(c * FH, 128), FH)] = we_keep[...]
    we_o[:, pl.ds(pl.multiple_of((1 - c) * FH, 128), FH)] = we_arrived[...]
    for m in range(3):
        mine = pl.multiple_of(m * D + c * HALF, 128)
        other = pl.multiple_of(m * D + (1 - c) * HALF, 128)
        qkv_o[:, pl.ds(mine, HALF)] = keep[:, m * HALF : (m + 1) * HALF]
        qkv_o[:, pl.ds(other, HALF)] = arrived[:, m * HALF : (m + 1) * HALF]
    both[0:24] = vec[0:24] + arrived[:, QC : QC + SMALL]
    both[24:48] = vec[24:48] + arrived[:, QC + SMALL :]
    own = both[pl.ds(pl.multiple_of(c * 24, 8), 24), :].T
    outs = (first_o, bias_o, None, None, bp_o, asc_o, gain2_o, bias2_o, br_o, msc_o)
    for r, out in enumerate(outs):
        if out is not None:
            out[...] = own[r]
    qv_o[...] = own[2:4]
    units = both[...].T
    units = jnp.where(c == 0, units[10:12], units[12:14])
    eb_o[...] = jnp.concatenate([units[0:1], units[1:2]], axis=1).reshape(96)


COSTS = {
    "first_kernel": (0, 0),
    "pick_kernel": (0, 0),
    "hidden_kernel": (0, 0),
    "reduce_grad_kernel": (1000000000, 4000000),
    "back_kernel": (0, 0),
    "expand_grad_kernel": (0, 0),
    "attention_back_kernel": (0, 0),
    "vectors_kernel": (8000000000, 20000000),
    "fold_kernel": (0, 0),
    "second_fold_kernel": (0, 2000000),
    "last_kernel": (0, 1000000),
    "spread_kernel": (0, 2000000),
    "finish_kernel": (0, 1000000),
    "out_kernel": (0, 1000000),
    "prepare_kernel": (0, 9000000),
    "hold_kernel": (0, 20000000),
    "home_kernel": (0, 0),
}


def call(kernel, outs, specs, scratch=(), vmem=24):
    return pl.pallas_call(
        kernel,
        out_shape=outs,
        in_specs=specs,
        out_specs=jax.tree.map(lambda _: VM, outs),
        scratch_shapes=list(scratch),
        compiler_params=pltpu.CompilerParams(vmem_limit_bytes=vmem * MIB),
        cost_estimate=pl.CostEstimate(flops=COSTS.get(kernel.__name__, (0, 0))[0], bytes_accessed=COSTS.get(kernel.__name__, (0, 0))[1], transcendentals=0),
    )


def fold_call(keep, arrived, after):
    half = (keep.shape[0] // 2, *keep.shape[1:])
    return call(fold_kernel, (vm(half, F32), vm(half, BF), TICK), [VM] * 2 + [ANY])(keep, arrived, after)


def by_core(value):
    return lax.ppermute(value, "band", [(i, i ^ 1) for i in range(4)])


def by_x(value):
    return lax.ppermute(value, "band", [(i, i ^ 2) for i in range(4)])


def by_y(value):
    return lax.ppermute(value, "batch", [(i, i ^ 1) for i in range(8)])


def by_z(value, dz):
    return lax.ppermute(value, "batch", [(i, i ^ (2 * dz)) for i in range(8)])


def homeward(value, dz):
    pairs = [(d, d ^ (8 * dz)) for d in range(32) if ((d ^ (8 * dz)) >> 4) == (d & 1)]
    return lax.ppermute(value, ("batch", "band"), pairs)


def packed_body(
    tokens, cotangent, visible, first_gain, first_bias, qkv_weight, qv_bias, proj_weight, proj_bias,
    attn_scale, second_gain, second_bias, expand_weight, expand_bias, reduce_weight, reduce_bias, mlp_scale,
):
    block = vm(cotangent.shape, BF)
    rows_f, rows_b = vm((ROWS, D), F32), vm((ROWS, D), BF)
    tok_x = by_x(tokens)
    tok_block = vm((OWN + 16, D), BF)
    cot, tok_own, par, be, wqkv, wp, we, wr, vis = call(
        prepare_kernel,
        (
            block,
            tok_block,
            vm((16, D), F32),
            vm((8, FH), F32),
            vm((3, D, HALF), BF),
            vm((D, D), BF),
            vm((D, FH), BF),
            vm((FH, D), BF),
            vm((16, 128), BF),
        ),
        [ANY] * 17,
        [pltpu.VMEM(visible.shape, jnp.int32), pltpu.SemaphoreType.DMA((22,))],
    )(
        *map(
            stay,
            (
                cotangent, first_gain, first_bias, qv_bias, proj_bias, attn_scale, second_gain, second_bias,
                reduce_bias, mlp_scale, expand_bias, qkv_weight, proj_weight, expand_weight, reduce_weight, visible,
                tokens,
            ),
        )
    )
    vis_x = by_x(vis)
    tok_c = by_core(tok_own)
    cot_c = by_core(cot)
    tok_x = call(hold_kernel, tok_block, [VM] * 2 + [ANY])(tok_x, vis_x, par)
    tok_d = by_core(tok_x)
    cot_x = by_x(cot)
    tok, normed, qkv, mix_own, mix2_own, pos, probs, pos_mine, pos_theirs = call(
        first_kernel,
        (
            rows_b,
            rows_b,
            vm((3, ROWS, HALF), BF),
            vm((ROWS, 256), BF),
            vm((ROWS, 128), BF),
            vm((8, SLOTS), F32),
            vm((9, 2 * PACK, PACK), F32),
            vm((16, BAND), F32),
            vm((16, BAND), F32),
        ),
        [VM] * 6,
        [pltpu.VMEM((IMGS, SLOTS, D), BF)],
    )(tok_own, tok_c, tok_x, tok_d, par, wqkv)
    mix_other, mix2_other = by_core(mix_own), by_core(mix2_own)
    pick, pick_p, pn = call(pick_kernel, (vm((D, HALF), BF), vm((D, 192), BF), vm((ROWS, HALF), BF)), [VM])(normed)
    res, one, n2, mix, act, slope, tick = call(
        hidden_kernel,
        (rows_f, rows_f, rows_b, rows_b, rows_b, rows_f, TICK),
        [VM] * 9 + [ANY],
    )(mix_own, mix_other, mix2_own, mix2_other, tok, par, be, wp, we, pick)
    cot_x = call(pass_kernel, block, [VM, ANY])(cot_x, tick)
    cot_d = by_core(cot_x)
    act_b, slope_b = call(more_hidden_kernel, (rows_b, rows_f), [VM] * 3)(n2, be, we)
    pre, gb2, wr_send, wr_keep = call(
        reduce_grad_kernel,
        (rows_b, rows_b, vm((4, 96, D), BF), vm((4, 96, D), BF)),
        [VM] * 8,
        [pltpu.VMEM((IMGS, SLOTS, D), BF), pltpu.VMEM((ROWS, D), BF), pltpu.VMEM((D, D), F32)],
    )(cot, cot_c, cot_x, cot_d, pos, par, act, act_b)
    wr_y = by_y(wr_send)
    half_b = vm((ROWS, HALF), BF)
    gh, left, right = call(back_kernel, (vm((ROWS, FH), BF), half_b, half_b), [VM] * 5)(gb2, wr, slope, slope_b, we)
    gn2 = (left, by_core(left), right, by_core(right))
    we_send, we_keep, tick = call(
        expand_grad_kernel,
        (vm((4, 48, FH), BF), vm((4, 48, FH), BF), TICK),
        [VM] * 3,
        [pltpu.VMEM((HALF, FH), F32)],
    )(n2, gh, pick)
    we_z = by_z(we_send, 1)
    gres, gp, qp_send, qp_keep, tick = call(
        attention_back_kernel,
        (rows_f, vm((ROWS, QC), BF), vm((4, 48, QW), BF), vm((4, 48, QW), BF), TICK),
        [VM] * 13 + [ANY],
        [pltpu.VMEM((HALF, QC), F32)],
    )(*gn2, res, pre, qkv, probs, mix, pn, pick_p, wp, par, tick)
    qp_y = by_y(qp_send)
    wr_keep, wr_send, tick = call(
        home_kernel, (vm((4, 96, D), F32), vm((4, 96, D), BF), TICK), [VM] * 2 + [ANY]
    )(wr_keep, wr_y, tick)
    wr_z = homeward(wr_send, 2)
    gb_keep, gb_send, vec_send, vec_keep, tick = call(
        vectors_kernel,
        (vm((2, *tokens.shape), BF), vm((2, *tokens.shape), BF), vm((2, 48, 2 * SMALL), BF), vm((2, 48, 2 * SMALL), BF), TICK),
        [VM] * 20 + [ANY],
        [pltpu.VMEM((SMALL, D), F32), pltpu.VMEM((FH, SMALL), F32)],
    )(*gn2, res, one, gres, gp, wqkv, act, act_b, wr, gb2, gh, pre, tok, pick, par, pos_mine, pos_theirs, tick)
    gb_other = by_core(gb_send)
    we_keep, we_send, tick = call(
        join_kernel, (vm((2, 48, FS), F32), vm((2, 48, FS), BF), TICK), [VM] * 4 + [ANY]
    )(we_keep, we_z, vec_keep, vec_send, tick)
    we_y = by_y(we_send)
    qp_keep, qp_send, tick = fold_call(qp_keep, qp_y, tick)
    qp_z = by_z(qp_send, 1)
    wr_keep, wr_send, tick = fold_call(wr_keep, wr_z, tick)
    wr_z = homeward(wr_send, 1)
    we_keep, we_send, vec_keep, vec_send, tick = call(
        part_kernel,
        (vm((1, 48, FH), F32), vm((1, 48, FH), BF), vm((2, 48, SMALL), F32), vm((2, 48, SMALL), BF), TICK),
        [VM] * 2 + [ANY],
    )(we_keep, we_y, tick)
    vec_z = by_z(vec_send, 1)
    we_z = by_z(we_send, 2)
    layer_out, grad_tokens, tick = call(
        last_kernel,
        (sds(tokens.shape, BF), sds(tokens.shape, BF), TICK),
        [VM] * 7 + [ANY],
    )(gb_keep, gb_other, tok_own, gres, res, pos_mine, par, tick)
    qp_keep, qp_send, tick = fold_call(qp_keep, qp_z, tick)
    qp_z = by_z(qp_send, 2)
    vec_keep, vec_send, tick = fold_call(vec_keep, vec_z, tick)
    vec_z = by_z(vec_send, 2)
    wr_keep, wr_send, we_keep, we_send, tick = call(
        settle_kernel,
        (vm((96, D), F32), vm((96, D), BF), vm((24, FH), F32), vm((24, FH), F32), TICK),
        [VM] * 4 + [ANY],
        [pltpu.VMEM((48, FH), F32)],
    )(wr_keep, wr_z, we_keep, we_z, tick)
    we_other, wr_other = by_core(we_send), by_core(wr_send)
    qp_keep, qp_send, vec, proj = call(
        finish_kernel,
        (vm((24, QC), F32), vm((24, QC + 2 * SMALL), F32), vm((48, SMALL), F32), sds((24, D), F32)),
        [VM] * 4 + [ANY],
        [pltpu.VMEM((48, QW), F32)],
    )(qp_keep, qp_z, vec_keep, vec_z, tick)
    vector = sds((24,), F32)
    grad_qkv, gg1, gb1, gqv, gbp, gas, gg2, gb2, gbr, gms, geb, grad_expand, grad_reduce = call(
        out_kernel,
        (
            sds((24, 3 * D), F32), vector, vector, sds((2, 24), F32), vector, vector, vector, vector, vector, vector,
            sds((96,), F32), sds((24, FF), F32), sds((96, D), F32),
        ),
        [VM] * 7,
        [pltpu.VMEM((48, SMALL), F32)],
    )(qp_keep, vec, by_core(qp_send), we_keep, we_other, wr_keep, wr_other)
    return (
        layer_out, grad_tokens, gg1, gb1, grad_qkv, gqv, proj, gbp, gas, gg2, gb2, grad_expand, geb, grad_reduce,
        gbr, gms,
    )


def layer_norm(values, norm_gain, norm_shift):
    center = values - jnp.mean(values, axis=-1, keepdims=True)
    spread = jnp.mean(center * center, axis=-1, keepdims=True)
    return center * lax.rsqrt(spread + NORM_EPS) * norm_gain + norm_shift


def gelu_exact(values):
    return jax.nn.gelu(values, approximate=False)


def split_rows(packed_rows, mask_rows):
    item_count = packed_rows.shape[0]
    slot_count = packed_rows.shape[1]
    heads_here = packed_rows.shape[4] // HD
    unpacked = packed_rows.reshape(item_count, slot_count, 3, heads_here, HD)
    queries = unpacked[:, :, 0]
    key_rows = unpacked[:, :, 1]
    value_rows = unpacked[:, :, 2]
    key_valid = mask_rows.reshape(item_count, slot_count) > 0
    score_scale = 1.0 / math.sqrt(HD)
    scores = (
        jnp.einsum("bqhe,bkhe->bhqk", queries, key_rows, preferred_element_type=jnp.float32)
        * score_scale
    )
    scores = jnp.where(key_valid[:, None, None, :], scores, -1e30)
    return (queries, key_rows, value_rows, scores)


def attend_plain(inputs):
    packed_rows, mask_rows = inputs
    queries, key_rows, value_rows, scores = split_rows(packed_rows, mask_rows)
    row_top = jnp.max(scores, axis=-1, keepdims=True)
    raised = jnp.exp(scores - row_top)
    row_total = jnp.sum(raised, axis=-1, keepdims=True)
    attn_prob = raised / row_total
    log_total = (row_top + jnp.log(row_total))[..., 0]
    mixed_rows = jnp.einsum(
        "bhqk,bkhe->bqhe",
        attn_prob.astype(jnp.bfloat16),
        value_rows,
        preferred_element_type=jnp.float32,
    ).astype(jnp.bfloat16)
    mixed_rows = mixed_rows.reshape(
        packed_rows.shape[0], packed_rows.shape[1], packed_rows.shape[4]
    )
    return (mixed_rows, log_total)


def backward_rows(score_parts, log_total, grad_rows):
    queries, key_rows, value_rows, scores = score_parts
    item_count, slot_count, heads_here, head_size = queries.shape
    score_scale = 1.0 / math.sqrt(HD)
    attn_prob = jnp.exp(scores - log_total[..., None])
    grad_heads = grad_rows.reshape(item_count, slot_count, heads_here, head_size)
    grad_prob = jnp.einsum(
        "bqhe,bkhe->bhqk", grad_heads, value_rows, preferred_element_type=jnp.float32
    )
    row_delta = jnp.sum(attn_prob * grad_prob, axis=-1, keepdims=True)
    grad_score = (attn_prob * (grad_prob - row_delta)).astype(jnp.bfloat16)
    grad_query = (
        jnp.einsum("bhqk,bkhe->bqhe", grad_score, key_rows, preferred_element_type=jnp.float32)
        * score_scale
    )
    grad_key = (
        jnp.einsum("bhqk,bqhe->bkhe", grad_score, queries, preferred_element_type=jnp.float32)
        * score_scale
    )
    grad_value = jnp.einsum(
        "bhqk,bqhe->bkhe",
        attn_prob.astype(jnp.bfloat16),
        grad_heads,
        preferred_element_type=jnp.float32,
    )
    stacked = jnp.stack([grad_query, grad_key, grad_value], axis=2)
    return stacked.reshape(item_count, slot_count, 3, 1, heads_here * head_size).astype(
        jnp.bfloat16
    )


def attend_again(inputs):
    packed_rows, mask_rows, grad_rows = inputs
    score_parts = split_rows(packed_rows, mask_rows)
    scores = score_parts[3]
    row_top = jnp.max(scores, axis=-1, keepdims=True)
    log_total = (row_top + jnp.log(jnp.sum(jnp.exp(scores - row_top), axis=-1, keepdims=True)))[
        ..., 0
    ]
    return backward_rows(score_parts, log_total, grad_rows)


def body(
    tokens,
    cotangent,
    visible,
    first_gain,
    first_bias,
    qkv_weight,
    qv_bias,
    proj_weight,
    proj_bias,
    attn_scale,
    second_gain,
    second_bias,
    expand_weight,
    expand_bias,
    reduce_weight,
    reduce_bias,
    mlp_scale,
):
    images, slot_count, model_width = tokens.shape
    groups = lax.axis_size("band")
    local_width = model_width // groups
    inputs_full = tokens.astype(jnp.float32)
    shown_mask = visible.astype(jnp.float32)
    normed, first_pull = jax.vjp(layer_norm, inputs_full, first_gain, first_bias)
    normed_low = normed.astype(jnp.bfloat16)
    qkv_bias = jnp.concatenate([qv_bias[0], jnp.zeros((model_width,), jnp.float32), qv_bias[1]])

    def project_qkv():
        product = jnp.einsum(
            "isd,de->ise", normed_low, qkv_weight, preferred_element_type=jnp.float32
        )
        return (
            (product + qkv_bias)
            .astype(jnp.bfloat16)
            .reshape(images, slot_count, 3, groups, local_width)
        )

    packed = project_qkv()
    mask_part = jnp.broadcast_to(
        shown_mask.astype(jnp.bfloat16)[:, :, None, None, None], (images, slot_count, 1, groups, 1)
    )
    results = attend_plain(
        (
            lax.all_to_all(packed, "band", split_axis=3, concat_axis=1, tiled=True),
            lax.all_to_all(mask_part, "band", split_axis=3, concat_axis=1, tiled=True),
        )
    )
    mixed_heads = results[0].reshape(images, groups * slot_count, 1, local_width)
    back_rows = lax.all_to_all(mixed_heads, "band", split_axis=1, concat_axis=2, tiled=True)
    mixed_rows = back_rows.reshape(images, slot_count, model_width)
    branch_one = (
        jnp.einsum("isd,de->ise", mixed_rows, proj_weight, preferred_element_type=jnp.float32)
        + proj_bias
    )
    residual = inputs_full + attn_scale * branch_one
    normed_two, second_pull = jax.vjp(layer_norm, residual, second_gain, second_bias)
    normed_two_low = normed_two.astype(jnp.bfloat16)
    hidden = (
        jnp.einsum("isd,df->isf", normed_two_low, expand_weight, preferred_element_type=jnp.float32)
        + expand_bias
    )
    activated, gelu_pull = jax.vjp(gelu_exact, hidden)
    activated_low = activated.astype(jnp.bfloat16)
    branch_two = (
        jnp.einsum("isf,fd->isd", activated_low, reduce_weight, preferred_element_type=jnp.float32)
        + reduce_bias
    )
    layer_out = (shown_mask[..., None] * (residual + mlp_scale * branch_two)).astype(jnp.bfloat16)
    grad_pre = shown_mask[..., None] * cotangent.astype(jnp.float32)
    grad_mlp_scale = jnp.sum(grad_pre * branch_two, axis=(0, 1))
    grad_branch_two = (mlp_scale * grad_pre).astype(jnp.bfloat16)
    grad_reduce_weight = jnp.einsum(
        "isf,isd->fd", activated_low, grad_branch_two, preferred_element_type=jnp.float32
    )
    grad_reduce_bias = jnp.sum(grad_branch_two.astype(jnp.float32), axis=(0, 1))
    grad_activated = jnp.einsum(
        "isd,fd->isf", grad_branch_two, reduce_weight, preferred_element_type=jnp.float32
    )
    grad_hidden = gelu_pull(grad_activated)[0].astype(jnp.bfloat16)
    grad_expand_weight = jnp.einsum(
        "isd,isf->df", normed_two_low, grad_hidden, preferred_element_type=jnp.float32
    )
    grad_expand_bias = jnp.sum(grad_hidden.astype(jnp.float32), axis=(0, 1))
    grad_normed_two = jnp.einsum(
        "isf,df->isd", grad_hidden, expand_weight, preferred_element_type=jnp.float32
    )
    grad_resid_norm, grad_second_gain, grad_second_bias = second_pull(grad_normed_two)
    grad_residual = grad_pre + grad_resid_norm
    grad_attn_scale = jnp.sum(grad_residual * branch_one, axis=(0, 1))
    grad_branch_one = (attn_scale * grad_residual).astype(jnp.bfloat16)
    grad_proj_weight = jnp.einsum(
        "isd,ise->de", mixed_rows, grad_branch_one, preferred_element_type=jnp.float32
    )
    grad_proj_bias = jnp.sum(grad_branch_one.astype(jnp.float32), axis=(0, 1))
    grad_mixed = jnp.einsum(
        "ise,de->isd", grad_branch_one, proj_weight, preferred_element_type=jnp.float32
    )
    grad_mixed = grad_mixed.astype(jnp.bfloat16).reshape(images, slot_count, 1, groups, local_width)
    repacked = project_qkv()
    grad_packed = attend_again(
        (
            lax.all_to_all(repacked, "band", split_axis=3, concat_axis=1, tiled=True),
            lax.all_to_all(mask_part, "band", split_axis=3, concat_axis=1, tiled=True),
            lax.all_to_all(grad_mixed, "band", split_axis=3, concat_axis=1, tiled=True),
        )
    )
    grad_bands = lax.all_to_all(grad_packed, "band", split_axis=1, concat_axis=3, tiled=True)
    grad_qkv = grad_bands.reshape(images, slot_count, 3 * model_width)
    grad_qkv_weight = jnp.einsum(
        "isd,ise->de", normed_low, grad_qkv, preferred_element_type=jnp.float32
    )
    column_sums = jnp.sum(grad_qkv.astype(jnp.float32), axis=(0, 1))
    grad_qv_bias = jnp.stack([column_sums[:model_width], column_sums[2 * model_width :]])
    grad_normed = jnp.einsum(
        "ise,de->isd", grad_qkv, qkv_weight, preferred_element_type=jnp.float32
    )
    grad_input_norm, grad_first_gain, grad_first_bias = first_pull(grad_normed)
    grad_tokens = (grad_residual + grad_input_norm).astype(jnp.bfloat16)
    all_sums = (
        lax.psum_scatter(grad_first_gain, ("batch", "band"), scatter_dimension=0, tiled=True),
        lax.psum_scatter(grad_first_bias, ("batch", "band"), scatter_dimension=0, tiled=True),
        lax.psum_scatter(grad_qkv_weight, ("batch", "band"), scatter_dimension=0, tiled=True),
        lax.psum_scatter(grad_qv_bias, ("batch", "band"), scatter_dimension=1, tiled=True),
        lax.psum_scatter(grad_proj_weight, ("batch", "band"), scatter_dimension=0, tiled=True),
        lax.psum_scatter(grad_proj_bias, ("batch", "band"), scatter_dimension=0, tiled=True),
        lax.psum_scatter(grad_attn_scale, ("batch", "band"), scatter_dimension=0, tiled=True),
        lax.psum_scatter(grad_second_gain, ("batch", "band"), scatter_dimension=0, tiled=True),
        lax.psum_scatter(grad_second_bias, ("batch", "band"), scatter_dimension=0, tiled=True),
        lax.psum_scatter(grad_expand_weight, ("batch", "band"), scatter_dimension=0, tiled=True),
        lax.psum_scatter(grad_expand_bias, ("batch", "band"), scatter_dimension=0, tiled=True),
        lax.psum_scatter(grad_reduce_weight, ("batch", "band"), scatter_dimension=0, tiled=True),
        lax.psum_scatter(grad_reduce_bias, ("batch", "band"), scatter_dimension=0, tiled=True),
        lax.psum_scatter(grad_mlp_scale, ("batch", "band"), scatter_dimension=0, tiled=True),
    )
    (
        sum_first_gain,
        sum_first_bias,
        sum_qkv_weight,
        sum_qv_bias,
        sum_proj_weight,
        sum_proj_bias,
        sum_attn_scale,
        sum_second_gain,
        sum_second_bias,
        sum_expand_weight,
        sum_expand_bias,
        sum_reduce_weight,
        sum_reduce_bias,
        sum_mlp_scale,
    ) = all_sums
    return (
        layer_out,
        grad_tokens,
        sum_first_gain,
        sum_first_bias,
        sum_qkv_weight,
        sum_qv_bias,
        sum_proj_weight,
        sum_proj_bias,
        sum_attn_scale,
        sum_second_gain,
        sum_second_bias,
        sum_expand_weight,
        sum_expand_bias,
        sum_reduce_weight,
        sum_reduce_bias,
        sum_mlp_scale,
    )


def solution(mesh):
    sizes = dict(mesh.shape)
    chosen = packed_body if (sizes["batch"], sizes["band"]) == (8, 4) else body
    placed = (
        P("batch", "band", None),
        P("batch", "band", None),
        P("batch", "band"),
        P(),
        P(),
        P(),
        P(),
        P(),
        P(),
        P(),
        P(),
        P(),
        P(),
        P(),
        P(),
        P(),
        P(),
    )
    return jax.shard_map(
        chosen,
        mesh=mesh,
        in_specs=placed,
        out_specs=(
            P("batch", "band", None),
            P("batch", "band", None),
            P(("batch", "band")),
            P(("batch", "band")),
            P(("batch", "band"), None),
            P(None, ("batch", "band")),
            P(("batch", "band"), None),
            P(("batch", "band")),
            P(("batch", "band")),
            P(("batch", "band")),
            P(("batch", "band")),
            P(("batch", "band"), None),
            P(("batch", "band")),
            P(("batch", "band"), None),
            P(("batch", "band")),
            P(("batch", "band")),
        ),
        check_vma=False,
    )
```

```python
import math

import jax
import jax.numpy as jnp
from jax import lax
from jax.experimental import pallas as pl
from jax.experimental.pallas import tpu as pltpu
from jax.sharding import PartitionSpec as P

HD = 64
NORM_EPS = 1e-06
PACK = 144
SLOTS = 256
BAND = 64
IMGS = 3
ROWS = IMGS * PACK
D = 768
HALF = D // 2
FF = 3072
FH = FF // 2
SMALL = 128
MIB = 1024 * 1024
F32 = jnp.float32
BF = jnp.bfloat16
ANY = pl.BlockSpec(memory_space=pl.ANY)
HBM = pl.BlockSpec(memory_space=pltpu.HBM)
VM = pl.BlockSpec(memory_space=pltpu.VMEM)


def dot(a, b):
    return jnp.dot(a, b, preferred_element_type=F32)


def dot_nt(a, b):
    return lax.dot_general(a, b, (((1,), (1,)), ((), ())), preferred_element_type=F32)


def dot_tn(a, b):
    return lax.dot_general(a, b, (((0,), (0,)), ((), ())), preferred_element_type=F32)


def sds(shape, dtype):
    return jax.ShapeDtypeStruct(shape, dtype)


def vm(shape, dtype):
    return pltpu.VMEM(shape, dtype)


def stay(value):
    return pltpu.with_memory_space_constraint(value, pltpu.HBM)


def place():
    band = lax.axis_index("band")
    batch = lax.axis_index("batch")
    return band >> 1, band & 1, batch >> 1, batch & 1


def one_hot_pack(pos, image):
    rows = lax.broadcasted_iota(jnp.int32, (PACK, pos.shape[1]), 0).astype(F32)
    return jnp.where(rows == pos[image : image + 1, :], 1.0, 0.0).astype(BF)


def shard_picks():
    x, c, z, y = place()

    def pick(width, base):
        row = lax.broadcasted_iota(jnp.int32, (8 * width, 1), 0)
        want = jnp.zeros((8 * width, 1), jnp.int32)
        for q in range(8):
            first = 96 * ((z ^ (q % 4)) * 2 + (y ^ (q // 4))) + base - width * q
            want = jnp.where((row >= width * q) & (row < width * (q + 1)), row + first, want)
        lane = lax.broadcasted_iota(jnp.int32, (8 * width, D), 1)
        return jnp.where(lane == want, 1.0, 0.0).astype(BF)

    return pick(48, 48 * x), pick(24, 48 * x + 24 * c)


def statistics(values):
    center = values - jnp.mean(values, axis=-1, keepdims=True)
    rstd = lax.rsqrt(jnp.mean(center * center, axis=-1, keepdims=True) + NORM_EPS)
    return center * rstd, rstd


def norm_back(grad, z, rstd):
    return rstd * (
        grad
        - jnp.mean(grad, axis=-1, keepdims=True)
        - z * jnp.mean(grad * z, axis=-1, keepdims=True)
    )


def gather_bands(blocks, dst):
    band = lax.axis_index("band")
    for k, block in enumerate(blocks):
        at = pl.multiple_of((band ^ k) * BAND, BAND)
        for i in range(IMGS):
            dst[i, pl.ds(at, BAND), :] = block(i)


def images(ref):
    return lambda i: ref[i] if len(ref.shape) == 3 else ref[i * BAND : (i + 1) * BAND, :]


def images_of_two(a, b):
    count = a.shape[0]

    def block(i):
        lo, hi = i * BAND, (i + 1) * BAND
        parts = [a[lo : min(hi, count), :]] if lo < count else []
        parts += [b[max(lo, count) - count : hi - count, :]] if hi > count else []
        return parts[0] if len(parts) == 1 else jnp.concatenate(parts, axis=0)

    return block


def two_heads(v):
    lane = lax.broadcasted_iota(jnp.int32, v.shape, 1)
    none = jnp.zeros_like(v)
    return jnp.concatenate([jnp.where(lane < HD, v, none), jnp.where(lane < HD, none, v)], axis=0)


def join_heads(v):
    lane = lax.broadcasted_iota(jnp.int32, (PACK, 128), 1)
    return jnp.where(lane < HD, v[:PACK], v[PACK:])


def head_pairs():
    for i in range(IMGS):
        for hp in range(3):
            yield i, slice(i * PACK, (i + 1) * PACK), hp, slice(hp * 128, (hp + 1) * 128)


def keys_shown(pos, image):
    shown = jnp.sum(jnp.where(pos[image : image + 1, :] >= 0, 1.0, 0.0), axis=-1, keepdims=True)
    return lax.broadcasted_iota(jnp.int32, (PACK, 1), 0).astype(F32) < shown


TICK = vm((8, 128), F32)
GAIN1, BIAS1, QB, VB, PB, ASC, GAIN2, BIAS2, RB, MSC = range(10)


OWN = IMGS * BAND


def prepare_kernel(
    cot, gain1, bias1, qvb, bp, asc, gain2, bias2, br, msc, be, wqkv, wp, we, wr, visible, tok,
    cot_o, own_o, par_o, be_o, wqkv_o, wp_o, we_o, wr_o, vis_o, pick_o, pick_p_o,
    vis, sems,
):
    c = lax.axis_index("band") & 1
    units = pl.multiple_of(c * FH, 128)
    rows = (
        (GAIN1, gain1), (BIAS1, bias1), (QB, qvb.at[0]), (VB, qvb.at[1]), (PB, bp), (ASC, asc),
        (GAIN2, gain2), (BIAS2, bias2), (RB, br), (MSC, msc),
    )
    moves = [(cot, cot_o)] + [(v, par_o.at[r]) for r, v in rows]
    moves += [(be.at[pl.ds(units, FH)], be_o.at[0])]
    for m in range(3):
        src = wqkv.at[:, pl.ds(pl.multiple_of(m * D + c * HALF, 128), HALF)]
        moves.append((src, wqkv_o.at[:, pl.ds(m * HALF, HALF)]))
    moves += [(wp, wp_o), (we.at[:, pl.ds(units, FH)], we_o), (wr.at[pl.ds(units, FH), :], wr_o)]
    moves += [(tok.at[i], own_o.at[pl.ds(i * BAND, BAND), :]) for i in range(IMGS)]
    moves += [(visible, vis)]
    copies = [pltpu.make_async_copy(a, b, sems.at[i]) for i, (a, b) in enumerate(moves)]
    for copy in copies:
        copy.start()
    copies[-1].wait()
    seen = jnp.concatenate([vis[...].astype(F32), jnp.zeros((IMGS, 128 - BAND), F32)], axis=1)
    seen = jnp.concatenate([seen, jnp.zeros((16 - IMGS, 128), F32)], axis=0).astype(BF)
    vis_o[...] = jnp.zeros((16, D), BF)
    vis_o[:, 0:128] = seen
    own_o[OWN:, :] = jnp.zeros((16, D), BF)
    own_o[OWN:, 0:128] = seen
    pick_o[...], pick_p_o[...] = shard_picks()
    for copy in copies[:-1]:
        copy.wait()


SPLIT = 224
EARLY = 160


def hold_kernel(tok, vis, after, out, rest):
    count = out.shape[0]
    for i in range(IMGS):
        lo, hi = i * BAND, (i + 1) * BAND
        if lo < count:
            out[lo : min(hi, count), :] = tok[i, 0 : min(hi, count) - lo, :]
        if hi > count:
            rest[max(lo, count) - count : hi - count, :] = tok[i, max(lo, count) - lo :, :]
    rest[OWN - count :, :] = vis[...]


def first_kernel(
    t0, t1, x_a, x_b, d_a, d_b, par, w,
    tok_o, norm_o, qkv_o, mix_o, mix2_o, pos_o, probs_o, mine_o, theirs_o, far_o,
    xs, mix,
):
    band = lax.axis_index("band")
    c = band & 1
    gather_bands((images(t0), images(t1), images_of_two(x_a, x_b), images_of_two(d_a, d_b)), xs)
    heads = pl.multiple_of(c * HALF, 128)
    to = lax.broadcasted_iota(jnp.int32, (BAND, SLOTS), 1) - lax.broadcasted_iota(jnp.int32, (BAND, SLOTS), 0)
    vis = jnp.zeros((16, SLOTS), F32)
    for k, t in enumerate((t0, t1, x_b, d_b)):
        vis = vis + dot(t[t.shape[0] - 16 :, 0:BAND], jnp.where(to == (band ^ k) * BAND, 1.0, 0.0).astype(BF))
    upto = lax.broadcasted_iota(jnp.int32, (SLOTS, SLOTS), 0)
    slot = lax.broadcasted_iota(jnp.int32, (SLOTS, SLOTS), 1)
    before = jnp.where(upto < slot, 1.0, 0.0).astype(BF)
    pos = jnp.where(vis > 0, dot(vis.astype(BF), before), -1.0)
    pos_o[...] = pos[0:8]
    slot = lax.broadcasted_iota(jnp.int32, (SLOTS, BAND), 0) - lax.broadcasted_iota(jnp.int32, (SLOTS, BAND), 1)
    for out, b in ((mine_o, band), (theirs_o, band ^ 1), (far_o, band ^ 3)):
        out[...] = dot(pos.astype(BF), jnp.where(slot == b * BAND, 1.0, 0.0).astype(BF))
    for i in range(IMGS):
        rows = slice(i * PACK, (i + 1) * PACK)
        tok = dot(one_hot_pack(pos, i), xs[i])
        tok_o[rows, :] = tok.astype(BF)
        z, _ = statistics(tok)
        norm_o[rows, :] = (z * par[GAIN1 : GAIN1 + 1, :] + par[BIAS1 : BIAS1 + 1, :]).astype(BF)
    normed = norm_o[...]
    packed = dot(normed, w[...])
    for m in range(3):
        part = packed[:, m * HALF : (m + 1) * HALF]
        if m != 1:
            r = QB if m == 0 else VB
            part = part + par[r : r + 1, pl.ds(heads, HALF)]
        qkv_o[m] = part.astype(BF)
    scores = []
    for i, rows, hp, cols in head_pairs():
        scores.append(dot_nt(qkv_o[1, rows, cols], two_heads(qkv_o[0, rows, cols] * BF(HD**-0.5))))
    probs = []
    for n, (i, rows, hp, cols) in enumerate(head_pairs()):
        shown = jnp.where(keys_shown(pos, i), scores[n], -1e30)
        raised = jnp.exp(shown - jnp.max(shown, axis=0, keepdims=True))
        probs.append(raised / jnp.sum(raised, axis=0, keepdims=True))
    for n, (i, rows, hp, cols) in enumerate(head_pairs()):
        probs_o[n] = probs[n]
        mixed = join_heads(dot_tn(probs[n].astype(BF), qkv_o[2, rows, cols])).astype(BF)
        mix[rows, cols] = mixed
    mix_o[...] = mix[0:SPLIT, :]
    mix2_o[...] = mix[SPLIT:ROWS, :]


def half_kernel(mix_a, mix2_a, wp, c0, c1, x_a, x_b, pos_r, one_o, pre_o, xs):
    c = lax.axis_index("band") & 1
    mine = pl.multiple_of(c * HALF, 128)
    weights = wp[pl.ds(mine, HALF), :]
    one_o[0:SPLIT, :] = dot(mix_a[...], weights)
    one_o[SPLIT:ROWS, :] = dot(mix2_a[...], weights)
    gather_bands((images(c0), images(c1), images_of_two(x_a, x_b), lambda i: jnp.zeros((BAND, D), BF)), xs)
    pos = pos_r[...]
    for i in range(IMGS):
        pre_o[i * PACK : (i + 1) * PACK, :] = dot(one_hot_pack(pos, i), xs[i])


def hidden_kernel(half, mix_b, mix2_b, tok, par, be, wp, we, after, res_o, one_o, n2_o, act_o, slope_o):
    c = lax.axis_index("band") & 1
    weights = wp[pl.ds(pl.multiple_of((1 - c) * HALF, 128), HALF), :]
    one_o[0:SPLIT, :] = half[0:SPLIT, :] + dot(mix_b[...], weights) + par[PB : PB + 1, :]
    one_o[SPLIT:ROWS, :] = half[SPLIT:ROWS, :] + dot(mix2_b[...], weights) + par[PB : PB + 1, :]
    for i in range(IMGS):
        rows = slice(i * PACK, (i + 1) * PACK)
        residual = tok[rows, :].astype(F32) + par[ASC : ASC + 1, :] * one_o[rows, :]
        res_o[rows, :] = residual
        z, _ = statistics(residual)
        n2_o[rows, :] = (z * par[GAIN2 : GAIN2 + 1, :] + par[BIAS2 : BIAS2 + 1, :]).astype(BF)
    for f in range(FH // 256):
        cols = slice(f * 256, (f + 1) * 256)
        for i in range(IMGS):
            rows = slice(i * PACK, (i + 1) * PACK)
            hidden = dot(n2_o[rows, :], we[:, cols]) + be[0:1, cols]
            phi = 0.5 * (1.0 + lax.erf(hidden * math.sqrt(0.5)))
            act_o[rows, cols] = (hidden * phi).astype(BF)
            density = jnp.exp(-0.5 * hidden * hidden) * (1.0 / math.sqrt(2.0 * math.pi))
            slope_o[rows, cols] = phi + hidden * density


def split_kernel(v, out_a, out_b):
    for i in range(IMGS):
        lo = i * BAND
        for first, out in ((0, out_a), (OWN // 2, out_b)):
            start, stop = max(lo, first), min(lo + BAND, first + OWN // 2)
            if start < stop:
                out[start - first : stop - first, :] = v[i, start - lo : stop - lo, :]


def reduce_grad_kernel(part, d_a, d_b, far_r, par, act, pre_o, gb2_o, send_o, keep_o, act_x, full):
    x, c, z, y = place()
    block = images_of_two(d_a, d_b)
    for i in range(IMGS):
        rows = slice(i * PACK, (i + 1) * PACK)
        pre = part[rows, :] + dot(one_hot_pack(far_r[...], i), block(i))
        pre_o[rows, :] = pre.astype(BF)
        gb2_o[rows, :] = (par[MSC : MSC + 1, :] * pre).astype(BF)
    for chip in range(2):

        @pl.when(x == chip)
        def _():
            for j in range(4):
                lo = 384 * j + 192 * chip
                act_x[:, 192 * j : 192 * j + 192] = act[:, lo : lo + 192]

    full[...] = dot_tn(act_x[...], gb2_o[...])
    for dy, out in ((1, send_o), (0, keep_o)):
        for dz in range(2):
            j = 2 * ((z & 1) ^ dz) + (y ^ dy)
            for to in range(2):
                at = pl.multiple_of(192 * j + 96 * to, 96)
                out[2 * dz + to] = full[pl.ds(at, 96), :].astype(BF)


def back_kernel(gb2, wr, slope, we, gh_o, left_o, right_o):
    step = 256
    for f in range(FH // step):
        cols = slice(f * step, (f + 1) * step)
        back = dot_nt(gb2[...], wr[cols, :])
        gh_o[:, cols] = (back * slope[:, cols]).astype(BF)
    gn2 = dot_nt(gh_o[...], we[...]).astype(BF)
    left_o[...] = gn2[:, :HALF]
    right_o[...] = gn2[:, HALF:]


def expand_grad_kernel(n2, gh, pick, send_o, keep_o, tick, wide):
    tick[...] = jnp.zeros_like(tick)
    picked = dot_nt(pick[...], n2[...]).astype(BF)
    wide[...] = dot(picked, gh[...])
    for low, out in ((1, send_o), (0, keep_o)):
        for i in range(4):
            lo = 192 * (i >> 1) + 48 * (low + 2 * (i & 1))
            out[i] = wide[lo : lo + 48, :].astype(BF)


QC = 3 * HALF
QW = QC + HALF
FS = FH + 2 * SMALL


def both_halves(l_a, l_b, r_a, r_b):
    left = l_a[...].astype(F32) + l_b[...].astype(F32)
    right = r_a[...].astype(F32) + r_b[...].astype(F32)
    return jnp.concatenate([left, right], axis=1)


def attention_back_kernel(
    l_a, l_b, r_a, r_b, res, pre, qkv, probs_r, mix_a, mix2_a, mix_b, mix2_b, normed, pick, pick_p, wp, par, after,
    gres_o, gp, send_o, keep_o, tick,
    flat,
):
    tick[...] = jnp.zeros_like(tick)
    c = lax.axis_index("band") & 1
    heads = pl.multiple_of(c * HALF, 128)
    gn2 = both_halves(l_a, l_b, r_a, r_b)
    z2, rstd2 = statistics(res[...])
    gres = pre[...].astype(F32) + norm_back(gn2 * par[GAIN2 : GAIN2 + 1, :], z2, rstd2)
    gres_o[...] = gres
    gb1 = (par[ASC : ASC + 1, :] * gres).astype(BF)
    gm = dot_nt(gb1, wp[pl.ds(heads, HALF), :]).astype(BF)
    grads = [two_heads(gm[rows, cols]) for i, rows, hp, cols in head_pairs()]
    gprobs = [dot_nt(qkv[2, rows, cols], grads[n]) for n, (i, rows, hp, cols) in enumerate(head_pairs())]
    gscores = []
    for n in range(9):
        product = probs_r[n] * gprobs[n]
        gscores.append((product - probs_r[n] * jnp.sum(product, axis=0, keepdims=True)).astype(BF))
    for n, (i, rows, hp, cols) in enumerate(head_pairs()):
        parts = (
            join_heads(dot_tn(gscores[n], qkv[1, rows, cols] * BF(HD**-0.5))),
            dot(gscores[n], two_heads(qkv[0, rows, cols] * BF(HD**-0.5))),
            dot(probs_r[n].astype(BF), grads[n]),
        )
        for m in range(3):
            gp[rows, m * HALF + hp * 128 : m * HALF + (hp + 1) * 128] = parts[m].astype(BF)
    others = pl.multiple_of((1 - c) * HALF, 128)
    mixed = []
    for first, second in ((mix_a, mix_b), (mix2_a, mix2_b)):
        part = dot_nt(pick_p[:, pl.ds(heads, HALF)], first[...])
        mixed.append(part + dot_nt(pick_p[:, pl.ds(others, HALF)], second[...]))
    mixed = jnp.concatenate(mixed, axis=1).astype(BF)
    pn = dot_nt(pick[...], normed[...]).astype(BF)
    proj = dot(mixed, gb1)
    flat[...] = dot(pn, gp[...])
    for dy, out in ((1, send_o), (0, keep_o)):
        for i, dz in enumerate((0, 2, 1, 3)):
            q = 4 * dy + dz
            out[i, :, 0:QC] = flat[48 * q : 48 * q + 48, :].astype(BF)
            block = proj[24 * q : 24 * q + 24]
            out[i, :, QC:QW] = jnp.concatenate([block[:, :HALF], block[:, HALF:]], axis=0).astype(BF)


def vectors_kernel(
    l_a, l_b, r_a, r_b, res, one, gres, gp, w, act, wr, gb2, gh, pre, tok, pick, par, mine, theirs, after,
    gb_keep, gb_send, send_o, keep_o, tick,
    vecs, sums,
):
    tick[...] = jnp.zeros_like(tick)
    x, c, z, y = place()
    heads = pl.multiple_of(c * HALF, 128)
    first = jnp.where(c == 0, 1.0, 0.0)

    def total(v):
        return jnp.sum(v, axis=0, keepdims=True)

    vecs[...] = jnp.zeros_like(vecs)
    gnp = dot_nt(gp[...], w[...])
    z1, _ = statistics(tok[...].astype(F32))
    vecs[GAIN1 : GAIN1 + 1, :] = total(gnp * z1)
    vecs[BIAS1 : BIAS1 + 1, :] = total(gnp)
    vecs[QB : QB + 1, pl.ds(heads, HALF)] = total(gp[:, 0:HALF].astype(F32))
    vecs[VB : VB + 1, pl.ds(heads, HALF)] = total(gp[:, 2 * HALF : 3 * HALF].astype(F32))
    gb1 = (par[ASC : ASC + 1, :] * gres[...]).astype(BF)
    vecs[PB : PB + 1, :] = first * total(gb1.astype(F32))
    vecs[ASC : ASC + 1, :] = first * total(gres[...] * one[...])
    gn2 = both_halves(l_a, l_b, r_a, r_b)
    z2, _ = statistics(res[...])
    vecs[GAIN2 : GAIN2 + 1, :] = first * total(gn2 * z2)
    vecs[BIAS2 : BIAS2 + 1, :] = first * total(gn2)
    vecs[RB : RB + 1, :] = first * total(gb2[...].astype(F32))
    two = dot(act[...], wr[...])
    for m, value in enumerate((gnp.astype(BF), two.astype(BF))):
        for i in range(IMGS):
            rows = slice(i * PACK, (i + 1) * PACK)
            for at, out in ((mine, gb_keep), (theirs, gb_send)):
                out[m, i] = dot_tn(one_hot_pack(at[...], i), value[rows]).astype(BF)
    vecs[MSC : MSC + 1, :] = total(pre[...].astype(F32) * (two + first * par[RB : RB + 1, :]))
    cols = dot_nt(pick[...], vecs[...].astype(BF))
    sums[...] = dot_tn(gh[...], jnp.ones((ROWS, SMALL), BF))
    lane = lax.broadcasted_iota(jnp.int32, (48, SMALL), 1)
    for dy, out in ((1, send_o), (0, keep_o)):
        for dz in range(4):
            b = (z ^ dz) * 2 + (y ^ dy)
            q = 4 * dy + dz
            block = cols[48 * q : 48 * q + 48]
            for k in range(4):
                at = pl.multiple_of(384 * (b & 3) + 192 * x + 48 * k, 48)
                block = jnp.where((lane == 10 + k) & ((b >> 2) == c), sums[pl.ds(at, 48), :], block)
            out[dz >> 1, :, SMALL * (dz & 1) : SMALL * (dz & 1) + SMALL] = block.astype(BF)


def last_kernel(gb_a, gb_b, tok, gres, res, mine, par, after, out_o, gtok_o, tick):
    tick[...] = jnp.zeros_like(tick)

    def own_rows(pack, value):
        high = value.astype(BF)
        return dot_tn(pack, high) + dot_tn(pack, (value - high.astype(F32)).astype(BF))

    for i in range(IMGS):
        rows = slice(i * PACK, (i + 1) * PACK)
        pack = one_hot_pack(mine[...], i)
        z1, rstd1 = statistics(tok[i * BAND : (i + 1) * BAND, :].astype(F32))
        gnp = gb_a[0, i].astype(F32) + gb_b[0, i].astype(F32)
        gtok = own_rows(pack, gres[rows, :]) + norm_back(gnp * par[GAIN1 : GAIN1 + 1, :], z1, rstd1)
        gtok_o[i] = gtok.astype(BF)
        ones = dot_tn(pack, jnp.ones((PACK, D), BF))
        two = gb_a[1, i].astype(F32) + gb_b[1, i].astype(F32) + ones * par[RB : RB + 1, :]
        out_o[i] = (own_rows(pack, res[rows, :]) + par[MSC : MSC + 1, :] * two).astype(BF)


def fold(keep, arrived, keep_o, send_o):
    half = keep.shape[0] // 2
    for i in range(half):
        keep_o[i] = keep[i].astype(F32) + arrived[i].astype(F32)
        send_o[i] = (keep[half + i].astype(F32) + arrived[half + i].astype(F32)).astype(BF)


def fold_kernel(keep, arrived, after, keep_o, send_o, tick):
    tick[...] = jnp.zeros_like(tick)
    fold(keep, arrived, keep_o, send_o)


def home_kernel(keep, arrived, after, keep_o, send_o, tick):
    tick[...] = jnp.zeros_like(tick)
    for i in range(4):
        total = keep[i].astype(F32) + arrived[i].astype(F32)
        keep_o[i] = total
        send_o[i] = total.astype(BF)


def fold(keep, arrived, keep_o, send_o):
    half = keep.shape[0] // 2
    for i in range(half):
        keep_o[i] = keep[i].astype(F32) + arrived[i].astype(F32)
        send_o[i] = (keep[half + i].astype(F32) + arrived[half + i].astype(F32)).astype(BF)


def fold_kernel(keep, arrived, after, keep_o, send_o, tick):
    tick[...] = jnp.zeros_like(tick)
    fold(keep, arrived, keep_o, send_o)


def second_fold_kernel(keep, arrived, we_keep, we_arrived, after, keep_o, send_o, we_keep_o, we_send_o, tick):
    tick[...] = jnp.zeros_like(tick)
    for i in range(2):
        total = keep[i] + arrived[i].astype(F32)
        keep_o[i] = total
        send_o[i] = total.astype(BF)
    fold(we_keep, we_arrived, we_keep_o, we_send_o)


def join_kernel(keep, arrived, vec_keep, vec_send, after, keep_o, send_o, tick):
    tick[...] = jnp.zeros_like(tick)
    fold(keep, arrived, keep_o.at[:, :, 0:FH], send_o.at[:, :, 0:FH])
    keep_o[:, :, FH:FS] = vec_keep[...].astype(F32)
    send_o[:, :, FH:FS] = vec_send[...]


def part_kernel(keep, arrived, after, keep_o, send_o, vec_ko, vec_so, tick):
    tick[...] = jnp.zeros_like(tick)
    fold(keep.at[:, :, 0:FH], arrived.at[:, :, 0:FH], keep_o, send_o)
    for hi in range(2):
        total = keep[hi, :, FH:FS] + arrived[hi, :, FH:FS].astype(F32)
        vec_ko[hi] = total[:, 0:SMALL]
        vec_so[hi] = total[:, SMALL:].astype(BF)


def settle_kernel(wr_k, wr_a, we_k, we_a, after, wr_ko, wr_so, we_ko, we_so, tick, both):
    tick[...] = jnp.zeros_like(tick)
    c = lax.axis_index("band") & 1
    for at, out in ((c, wr_ko), (1 - c, wr_so)):
        out[...] = (wr_k[at] + wr_a[at].astype(F32)).astype(out.dtype)
    both[...] = we_k[0] + we_a[0].astype(F32)
    we_ko[...] = both[pl.ds(pl.multiple_of(c * 24, 8), 24), :]
    we_so[...] = both[pl.ds(pl.multiple_of(24 - c * 24, 8), 24), :]


def early_out_kernel(we_keep, we_arrived, wr_keep, wr_arrived, after, we_o, wr_o, tick):
    tick[...] = jnp.zeros_like(tick)
    _, c, z, _ = place()
    wr_o[...] = jnp.where((z >> 1) == c, wr_keep[...], wr_arrived[...].astype(F32))
    we_o[:, pl.ds(pl.multiple_of(c * FH, 128), FH)] = we_keep[...]
    we_o[:, pl.ds(pl.multiple_of((1 - c) * FH, 128), FH)] = we_arrived[...]


def finish_kernel(qp_k, qp_a, vec_k, vec_a, after, keep_o, send_o, vec_o, proj_o, tick, sums):
    tick[...] = jnp.zeros_like(tick)
    c = lax.axis_index("band") & 1
    sums[...] = qp_k[0] + qp_a[0].astype(F32)
    keep_o[...] = sums[pl.ds(pl.multiple_of(c * 24, 8), 24), 0:QC]
    send_o[:, 0:QC] = sums[pl.ds(pl.multiple_of(24 - c * 24, 8), 24), 0:QC]
    vec = vec_k[0] + vec_a[0].astype(F32)
    vec_o[...] = vec
    send_o[:, QC : QC + SMALL] = vec[0:24]
    send_o[:, QC + SMALL :] = vec[24:48]
    proj_o[:, 0:HALF] = sums[0:24, QC:QW]
    proj_o[:, HALF:] = sums[24:48, QC:QW]


def out_kernel(
    keep, vec, proj, arrived, after,
    qkv_o, first_o, bias_o, qv_o, bp_o, asc_o, gain2_o, bias2_o, br_o, msc_o, eb_o, proj_o, both,
):
    c = lax.axis_index("band") & 1
    proj_o[...] = proj[...]
    for m in range(3):
        mine = pl.multiple_of(m * D + c * HALF, 128)
        other = pl.multiple_of(m * D + (1 - c) * HALF, 128)
        qkv_o[:, pl.ds(mine, HALF)] = keep[:, m * HALF : (m + 1) * HALF]
        qkv_o[:, pl.ds(other, HALF)] = arrived[:, m * HALF : (m + 1) * HALF]
    both[0:24] = vec[0:24] + arrived[:, QC : QC + SMALL]
    both[24:48] = vec[24:48] + arrived[:, QC + SMALL :]
    own = both[pl.ds(pl.multiple_of(c * 24, 8), 24), :].T
    outs = (first_o, bias_o, None, None, bp_o, asc_o, gain2_o, bias2_o, br_o, msc_o)
    for r, out in enumerate(outs):
        if out is not None:
            out[...] = own[r]
    qv_o[...] = own[2:4]
    units = both[...].T
    units = jnp.where(c == 0, units[10:12], units[12:14])
    eb_o[...] = jnp.concatenate([units[0:1], units[1:2]], axis=1).reshape(96)


COSTS = {
    "first_kernel": (0, 0),
    "pick_kernel": (0, 0),
    "hidden_kernel": (0, 0),
    "reduce_grad_kernel": (0, 0),
    "back_kernel": (0, 0),
    "expand_grad_kernel": (0, 0),
    "attention_back_kernel": (0, 0),
    "vectors_kernel": (8000000000, 20000000),
    "fold_kernel": (0, 0),
    "second_fold_kernel": (0, 2000000),
    "last_kernel": (0, 1000000),
    "spread_kernel": (0, 2000000),
    "finish_kernel": (0, 1000000),
    "out_kernel": (0, 1000000),
    "prepare_kernel": (0, 9000000),
    "hold_kernel": (0, 0),
    "home_kernel": (0, 0),
    "half_kernel": (0, 0),
}


def call(kernel, outs, specs, scratch=(), vmem=24, cost=0):
    return pl.pallas_call(
        kernel,
        out_shape=outs,
        in_specs=specs,
        out_specs=jax.tree.map(lambda _: VM, outs),
        scratch_shapes=list(scratch),
        compiler_params=pltpu.CompilerParams(vmem_limit_bytes=vmem * MIB),
        cost_estimate=pl.CostEstimate(flops=COSTS.get(kernel.__name__, (0, 0))[0] + cost, bytes_accessed=COSTS.get(kernel.__name__, (0, 0))[1], transcendentals=0),
    )


def fold_call(keep, arrived, after, cost=0):
    half = (keep.shape[0] // 2, *keep.shape[1:])
    return call(fold_kernel, (vm(half, F32), vm(half, BF), TICK), [VM] * 2 + [ANY], cost=cost)(keep, arrived, after)


def by_core(value):
    return lax.ppermute(value, "band", [(i, i ^ 1) for i in range(4)])


def by_x(value):
    return lax.ppermute(value, "band", [(i, i ^ 2) for i in range(4)])


def by_y(value):
    return lax.ppermute(value, "batch", [(i, i ^ 1) for i in range(8)])


def by_z(value, dz):
    return lax.ppermute(value, "batch", [(i, i ^ (2 * dz)) for i in range(8)])


def homeward(value, dz):
    pairs = [(d, d ^ (8 * dz)) for d in range(32) if ((d ^ (8 * dz)) >> 4) == (d & 1)]
    return lax.ppermute(value, ("batch", "band"), pairs)


def packed_body(
    tokens, cotangent, visible, first_gain, first_bias, qkv_weight, qv_bias, proj_weight, proj_bias,
    attn_scale, second_gain, second_bias, expand_weight, expand_bias, reduce_weight, reduce_bias, mlp_scale,
):
    block = vm(cotangent.shape, BF)
    rows_f, rows_b = vm((ROWS, D), F32), vm((ROWS, D), BF)
    tok_x = by_x(tokens)
    tok_block = vm((OWN + 16, D), BF)
    cot, tok_own, par, be, wqkv, wp, we, wr, vis, pick, pick_p = call(
        prepare_kernel,
        (
            block,
            tok_block,
            vm((16, D), F32),
            vm((8, FH), F32),
            vm((D, QC), BF),
            vm((D, D), BF),
            vm((D, FH), BF),
            vm((FH, D), BF),
            vm((16, D), BF),
            vm((HALF, D), BF),
            vm((192, D), BF),
        ),
        [ANY] * 17,
        [pltpu.VMEM(visible.shape, jnp.int32), pltpu.SemaphoreType.DMA((22,))],
    )(
        *map(
            stay,
            (
                cotangent, first_gain, first_bias, qv_bias, proj_bias, attn_scale, second_gain, second_bias,
                reduce_bias, mlp_scale, expand_bias, qkv_weight, proj_weight, expand_weight, reduce_weight, visible,
                tokens,
            ),
        )
    )
    vis_x = by_x(vis)
    tok_c = by_core(tok_own)
    cot_c = by_core(cot)
    parts = (vm((EARLY, D), BF), vm((OWN + 16 - EARLY, D), BF))
    tok_x = call(hold_kernel, parts, [VM] * 2 + [ANY])(tok_x, vis_x, par)
    tok_d = [by_core(v) for v in tok_x]
    cot_x = call(split_kernel, (vm((OWN // 2, D), BF),) * 2, [VM])(by_x(cot))
    cot_d = [by_core(v) for v in cot_x]
    tok, normed, qkv, mix_own, mix2_own, pos, probs, pos_mine, pos_theirs, pos_far = call(
        first_kernel,
        (
            rows_b,
            rows_b,
            vm((3, ROWS, HALF), BF),
            vm((SPLIT, HALF), BF),
            vm((ROWS - SPLIT, HALF), BF),
            vm((8, SLOTS), F32),
            vm((9, PACK, 2 * PACK), F32),
            vm((16, BAND), F32),
            vm((16, BAND), F32),
            vm((16, BAND), F32),
        ),
        [VM] * 8,
        [pltpu.VMEM((IMGS, SLOTS, D), BF), pltpu.VMEM((ROWS, HALF), BF)],
    )(tok_own, tok_c, *tok_x, *tok_d, par, wqkv)
    mix_other, mix2_other = by_core(mix_own), by_core(mix2_own)
    half_one, half_pre = call(
        half_kernel, (rows_f, rows_f), [VM] * 8, [pltpu.VMEM((IMGS, SLOTS, D), BF)]
    )(mix_own, mix2_own, wp, cot, cot_c, *cot_x, pos)
    res, one, n2, act, slope = call(
        hidden_kernel,
        (rows_f, rows_f, rows_b, vm((ROWS, FH), BF), vm((ROWS, FH), F32)),
        [VM] * 8 + [ANY],
    )(half_one, mix_other, mix2_other, tok, par, be, wp, we, pick)
    pre, gb2, wr_send, wr_keep = call(
        reduce_grad_kernel,
        (rows_b, rows_b, vm((4, 96, D), BF), vm((4, 96, D), BF)),
        [VM] * 6,
        [pltpu.VMEM((ROWS, D), BF), pltpu.VMEM((D, D), F32)],
    )(half_pre, *cot_d, pos_far, par, act)
    wr_y = by_y(wr_send)
    half_b = vm((ROWS, HALF), BF)
    gh, left, right = call(back_kernel, (vm((ROWS, FH), BF), half_b, half_b), [VM] * 4)(gb2, wr, slope, we)
    gn2 = (left, by_core(left), right, by_core(right))
    we_send, we_keep, tick = call(
        expand_grad_kernel,
        (vm((4, 48, FH), BF), vm((4, 48, FH), BF), TICK),
        [VM] * 3,
        [pltpu.VMEM((HALF, FH), F32)],
    )(n2, gh, pick)
    we_z = by_z(we_send, 1)
    gres, gp, qp_send, qp_keep, tick = call(
        attention_back_kernel,
        (rows_f, vm((ROWS, QC), BF), vm((4, 48, QW), BF), vm((4, 48, QW), BF), TICK),
        [VM] * 17 + [ANY],
        [pltpu.VMEM((HALF, QC), F32)],
    )(*gn2, res, pre, qkv, probs, mix_own, mix2_own, mix_other, mix2_other, normed, pick, pick_p, wp, par, tick)
    qp_y = by_y(qp_send)
    wr_keep, wr_send, tick = call(
        home_kernel, (vm((4, 96, D), F32), vm((4, 96, D), BF), TICK), [VM] * 2 + [ANY]
    )(wr_keep, wr_y, tick)
    wr_z = homeward(wr_send, 2)
    gb_keep, gb_send, vec_send, vec_keep, tick = call(
        vectors_kernel,
        (vm((2, *tokens.shape), BF), vm((2, *tokens.shape), BF), vm((2, 48, 2 * SMALL), BF), vm((2, 48, 2 * SMALL), BF), TICK),
        [VM] * 19 + [ANY],
        [pltpu.VMEM((SMALL, D), F32), pltpu.VMEM((FH, SMALL), F32)],
    )(*gn2, res, one, gres, gp, wqkv, act, wr, gb2, gh, pre, tok, pick, par, pos_mine, pos_theirs, tick)
    gb_other = by_core(gb_send)
    we_keep, we_send, tick = call(
        join_kernel, (vm((2, 48, FS), F32), vm((2, 48, FS), BF), TICK), [VM] * 4 + [ANY]
    )(we_keep, we_z, vec_keep, vec_send, tick)
    we_y = by_y(we_send)
    qp_keep, qp_send, tick = fold_call(qp_keep, qp_y, tick)
    qp_z = by_z(qp_send, 1)
    wr_keep, wr_send, tick = fold_call(wr_keep, wr_z, tick)
    wr_z = homeward(wr_send, 1)
    we_keep, we_send, vec_keep, vec_send, tick = call(
        part_kernel,
        (vm((1, 48, FH), F32), vm((1, 48, FH), BF), vm((2, 48, SMALL), F32), vm((2, 48, SMALL), BF), TICK),
        [VM] * 2 + [ANY],
    )(we_keep, we_y, tick)
    vec_z = by_z(vec_send, 1)
    we_z = by_z(we_send, 2)
    layer_out, grad_tokens, tick = call(
        last_kernel,
        (sds(tokens.shape, BF), sds(tokens.shape, BF), TICK),
        [VM] * 7 + [ANY],
    )(gb_keep, gb_other, tok_own, gres, res, pos_mine, par, tick)
    qp_keep, qp_send, tick = fold_call(qp_keep, qp_z, tick)
    qp_z = by_z(qp_send, 2)
    vec_keep, vec_send, tick = fold_call(vec_keep, vec_z, tick, cost=4000000000)
    vec_z = by_z(vec_send, 2)
    wr_keep, wr_send, we_keep, we_send, tick = call(
        settle_kernel,
        (vm((96, D), F32), vm((96, D), BF), vm((24, FH), F32), vm((24, FH), F32), TICK),
        [VM] * 4 + [ANY],
        [pltpu.VMEM((48, FH), F32)],
    )(wr_keep, wr_z, we_keep, we_z, tick)
    we_other, wr_other = by_core(we_send), by_core(wr_send)
    qp_keep, qp_send, vec, proj, tick = call(
        finish_kernel,
        (vm((24, QC), F32), vm((24, QC + 2 * SMALL), F32), vm((48, SMALL), F32), vm((24, D), F32), TICK),
        [VM] * 4 + [ANY],
        [pltpu.VMEM((48, QW), F32)],
    )(qp_keep, qp_z, vec_keep, vec_z, tick)
    qp_other = by_core(qp_send)
    grad_expand, grad_reduce, tick = call(
        early_out_kernel, (sds((24, FF), F32), sds((96, D), F32), TICK), [VM] * 4 + [ANY]
    )(we_keep, we_other, wr_keep, wr_other, tick)
    vector = sds((24,), F32)
    grad_qkv, gg1, gb1, gqv, gbp, gas, gg2, gb2, gbr, gms, geb, grad_proj = call(
        out_kernel,
        (
            sds((24, 3 * D), F32), vector, vector, sds((2, 24), F32), vector, vector, vector, vector, vector, vector,
            sds((96,), F32), sds((24, D), F32),
        ),
        [VM] * 4 + [ANY],
        [pltpu.VMEM((48, SMALL), F32)],
    )(qp_keep, vec, proj, qp_other, tick)
    return (
        layer_out, grad_tokens, gg1, gb1, grad_qkv, gqv, grad_proj, gbp, gas, gg2, gb2, grad_expand, geb, grad_reduce,
        gbr, gms,
    )


def layer_norm(values, norm_gain, norm_shift):
    center = values - jnp.mean(values, axis=-1, keepdims=True)
    spread = jnp.mean(center * center, axis=-1, keepdims=True)
    return center * lax.rsqrt(spread + NORM_EPS) * norm_gain + norm_shift


def gelu_exact(values):
    return jax.nn.gelu(values, approximate=False)


def split_rows(packed_rows, mask_rows):
    item_count = packed_rows.shape[0]
    slot_count = packed_rows.shape[1]
    heads_here = packed_rows.shape[4] // HD
    unpacked = packed_rows.reshape(item_count, slot_count, 3, heads_here, HD)
    queries = unpacked[:, :, 0]
    key_rows = unpacked[:, :, 1]
    value_rows = unpacked[:, :, 2]
    key_valid = mask_rows.reshape(item_count, slot_count) > 0
    score_scale = 1.0 / math.sqrt(HD)
    scores = (
        jnp.einsum("bqhe,bkhe->bhqk", queries, key_rows, preferred_element_type=jnp.float32)
        * score_scale
    )
    scores = jnp.where(key_valid[:, None, None, :], scores, -1e30)
    return (queries, key_rows, value_rows, scores)


def attend_plain(inputs):
    packed_rows, mask_rows = inputs
    queries, key_rows, value_rows, scores = split_rows(packed_rows, mask_rows)
    row_top = jnp.max(scores, axis=-1, keepdims=True)
    raised = jnp.exp(scores - row_top)
    row_total = jnp.sum(raised, axis=-1, keepdims=True)
    attn_prob = raised / row_total
    log_total = (row_top + jnp.log(row_total))[..., 0]
    mixed_rows = jnp.einsum(
        "bhqk,bkhe->bqhe",
        attn_prob.astype(jnp.bfloat16),
        value_rows,
        preferred_element_type=jnp.float32,
    ).astype(jnp.bfloat16)
    mixed_rows = mixed_rows.reshape(
        packed_rows.shape[0], packed_rows.shape[1], packed_rows.shape[4]
    )
    return (mixed_rows, log_total)


def backward_rows(score_parts, log_total, grad_rows):
    queries, key_rows, value_rows, scores = score_parts
    item_count, slot_count, heads_here, head_size = queries.shape
    score_scale = 1.0 / math.sqrt(HD)
    attn_prob = jnp.exp(scores - log_total[..., None])
    grad_heads = grad_rows.reshape(item_count, slot_count, heads_here, head_size)
    grad_prob = jnp.einsum(
        "bqhe,bkhe->bhqk", grad_heads, value_rows, preferred_element_type=jnp.float32
    )
    row_delta = jnp.sum(attn_prob * grad_prob, axis=-1, keepdims=True)
    grad_score = (attn_prob * (grad_prob - row_delta)).astype(jnp.bfloat16)
    grad_query = (
        jnp.einsum("bhqk,bkhe->bqhe", grad_score, key_rows, preferred_element_type=jnp.float32)
        * score_scale
    )
    grad_key = (
        jnp.einsum("bhqk,bqhe->bkhe", grad_score, queries, preferred_element_type=jnp.float32)
        * score_scale
    )
    grad_value = jnp.einsum(
        "bhqk,bqhe->bkhe",
        attn_prob.astype(jnp.bfloat16),
        grad_heads,
        preferred_element_type=jnp.float32,
    )
    stacked = jnp.stack([grad_query, grad_key, grad_value], axis=2)
    return stacked.reshape(item_count, slot_count, 3, 1, heads_here * head_size).astype(
        jnp.bfloat16
    )


def attend_again(inputs):
    packed_rows, mask_rows, grad_rows = inputs
    score_parts = split_rows(packed_rows, mask_rows)
    scores = score_parts[3]
    row_top = jnp.max(scores, axis=-1, keepdims=True)
    log_total = (row_top + jnp.log(jnp.sum(jnp.exp(scores - row_top), axis=-1, keepdims=True)))[
        ..., 0
    ]
    return backward_rows(score_parts, log_total, grad_rows)


def body(
    tokens,
    cotangent,
    visible,
    first_gain,
    first_bias,
    qkv_weight,
    qv_bias,
    proj_weight,
    proj_bias,
    attn_scale,
    second_gain,
    second_bias,
    expand_weight,
    expand_bias,
    reduce_weight,
    reduce_bias,
    mlp_scale,
):
    images, slot_count, model_width = tokens.shape
    groups = lax.axis_size("band")
    local_width = model_width // groups
    inputs_full = tokens.astype(jnp.float32)
    shown_mask = visible.astype(jnp.float32)
    normed, first_pull = jax.vjp(layer_norm, inputs_full, first_gain, first_bias)
    normed_low = normed.astype(jnp.bfloat16)
    qkv_bias = jnp.concatenate([qv_bias[0], jnp.zeros((model_width,), jnp.float32), qv_bias[1]])

    def project_qkv():
        product = jnp.einsum(
            "isd,de->ise", normed_low, qkv_weight, preferred_element_type=jnp.float32
        )
        return (
            (product + qkv_bias)
            .astype(jnp.bfloat16)
            .reshape(images, slot_count, 3, groups, local_width)
        )

    packed = project_qkv()
    mask_part = jnp.broadcast_to(
        shown_mask.astype(jnp.bfloat16)[:, :, None, None, None], (images, slot_count, 1, groups, 1)
    )
    results = attend_plain(
        (
            lax.all_to_all(packed, "band", split_axis=3, concat_axis=1, tiled=True),
            lax.all_to_all(mask_part, "band", split_axis=3, concat_axis=1, tiled=True),
        )
    )
    mixed_heads = results[0].reshape(images, groups * slot_count, 1, local_width)
    back_rows = lax.all_to_all(mixed_heads, "band", split_axis=1, concat_axis=2, tiled=True)
    mixed_rows = back_rows.reshape(images, slot_count, model_width)
    branch_one = (
        jnp.einsum("isd,de->ise", mixed_rows, proj_weight, preferred_element_type=jnp.float32)
        + proj_bias
    )
    residual = inputs_full + attn_scale * branch_one
    normed_two, second_pull = jax.vjp(layer_norm, residual, second_gain, second_bias)
    normed_two_low = normed_two.astype(jnp.bfloat16)
    hidden = (
        jnp.einsum("isd,df->isf", normed_two_low, expand_weight, preferred_element_type=jnp.float32)
        + expand_bias
    )
    activated, gelu_pull = jax.vjp(gelu_exact, hidden)
    activated_low = activated.astype(jnp.bfloat16)
    branch_two = (
        jnp.einsum("isf,fd->isd", activated_low, reduce_weight, preferred_element_type=jnp.float32)
        + reduce_bias
    )
    layer_out = (shown_mask[..., None] * (residual + mlp_scale * branch_two)).astype(jnp.bfloat16)
    grad_pre = shown_mask[..., None] * cotangent.astype(jnp.float32)
    grad_mlp_scale = jnp.sum(grad_pre * branch_two, axis=(0, 1))
    grad_branch_two = (mlp_scale * grad_pre).astype(jnp.bfloat16)
    grad_reduce_weight = jnp.einsum(
        "isf,isd->fd", activated_low, grad_branch_two, preferred_element_type=jnp.float32
    )
    grad_reduce_bias = jnp.sum(grad_branch_two.astype(jnp.float32), axis=(0, 1))
    grad_activated = jnp.einsum(
        "isd,fd->isf", grad_branch_two, reduce_weight, preferred_element_type=jnp.float32
    )
    grad_hidden = gelu_pull(grad_activated)[0].astype(jnp.bfloat16)
    grad_expand_weight = jnp.einsum(
        "isd,isf->df", normed_two_low, grad_hidden, preferred_element_type=jnp.float32
    )
    grad_expand_bias = jnp.sum(grad_hidden.astype(jnp.float32), axis=(0, 1))
    grad_normed_two = jnp.einsum(
        "isf,df->isd", grad_hidden, expand_weight, preferred_element_type=jnp.float32
    )
    grad_resid_norm, grad_second_gain, grad_second_bias = second_pull(grad_normed_two)
    grad_residual = grad_pre + grad_resid_norm
    grad_attn_scale = jnp.sum(grad_residual * branch_one, axis=(0, 1))
    grad_branch_one = (attn_scale * grad_residual).astype(jnp.bfloat16)
    grad_proj_weight = jnp.einsum(
        "isd,ise->de", mixed_rows, grad_branch_one, preferred_element_type=jnp.float32
    )
    grad_proj_bias = jnp.sum(grad_branch_one.astype(jnp.float32), axis=(0, 1))
    grad_mixed = jnp.einsum(
        "ise,de->isd", grad_branch_one, proj_weight, preferred_element_type=jnp.float32
    )
    grad_mixed = grad_mixed.astype(jnp.bfloat16).reshape(images, slot_count, 1, groups, local_width)
    repacked = project_qkv()
    grad_packed = attend_again(
        (
            lax.all_to_all(repacked, "band", split_axis=3, concat_axis=1, tiled=True),
            lax.all_to_all(mask_part, "band", split_axis=3, concat_axis=1, tiled=True),
            lax.all_to_all(grad_mixed, "band", split_axis=3, concat_axis=1, tiled=True),
        )
    )
    grad_bands = lax.all_to_all(grad_packed, "band", split_axis=1, concat_axis=3, tiled=True)
    grad_qkv = grad_bands.reshape(images, slot_count, 3 * model_width)
    grad_qkv_weight = jnp.einsum(
        "isd,ise->de", normed_low, grad_qkv, preferred_element_type=jnp.float32
    )
    column_sums = jnp.sum(grad_qkv.astype(jnp.float32), axis=(0, 1))
    grad_qv_bias = jnp.stack([column_sums[:model_width], column_sums[2 * model_width :]])
    grad_normed = jnp.einsum(
        "ise,de->isd", grad_qkv, qkv_weight, preferred_element_type=jnp.float32
    )
    grad_input_norm, grad_first_gain, grad_first_bias = first_pull(grad_normed)
    grad_tokens = (grad_residual + grad_input_norm).astype(jnp.bfloat16)
    all_sums = (
        lax.psum_scatter(grad_first_gain, ("batch", "band"), scatter_dimension=0, tiled=True),
        lax.psum_scatter(grad_first_bias, ("batch", "band"), scatter_dimension=0, tiled=True),
        lax.psum_scatter(grad_qkv_weight, ("batch", "band"), scatter_dimension=0, tiled=True),
        lax.psum_scatter(grad_qv_bias, ("batch", "band"), scatter_dimension=1, tiled=True),
        lax.psum_scatter(grad_proj_weight, ("batch", "band"), scatter_dimension=0, tiled=True),
        lax.psum_scatter(grad_proj_bias, ("batch", "band"), scatter_dimension=0, tiled=True),
        lax.psum_scatter(grad_attn_scale, ("batch", "band"), scatter_dimension=0, tiled=True),
        lax.psum_scatter(grad_second_gain, ("batch", "band"), scatter_dimension=0, tiled=True),
        lax.psum_scatter(grad_second_bias, ("batch", "band"), scatter_dimension=0, tiled=True),
        lax.psum_scatter(grad_expand_weight, ("batch", "band"), scatter_dimension=0, tiled=True),
        lax.psum_scatter(grad_expand_bias, ("batch", "band"), scatter_dimension=0, tiled=True),
        lax.psum_scatter(grad_reduce_weight, ("batch", "band"), scatter_dimension=0, tiled=True),
        lax.psum_scatter(grad_reduce_bias, ("batch", "band"), scatter_dimension=0, tiled=True),
        lax.psum_scatter(grad_mlp_scale, ("batch", "band"), scatter_dimension=0, tiled=True),
    )
    (
        sum_first_gain,
        sum_first_bias,
        sum_qkv_weight,
        sum_qv_bias,
        sum_proj_weight,
        sum_proj_bias,
        sum_attn_scale,
        sum_second_gain,
        sum_second_bias,
        sum_expand_weight,
        sum_expand_bias,
        sum_reduce_weight,
        sum_reduce_bias,
        sum_mlp_scale,
    ) = all_sums
    return (
        layer_out,
        grad_tokens,
        sum_first_gain,
        sum_first_bias,
        sum_qkv_weight,
        sum_qv_bias,
        sum_proj_weight,
        sum_proj_bias,
        sum_attn_scale,
        sum_second_gain,
        sum_second_bias,
        sum_expand_weight,
        sum_expand_bias,
        sum_reduce_weight,
        sum_reduce_bias,
        sum_mlp_scale,
    )


def solution(mesh):
    sizes = dict(mesh.shape)
    chosen = packed_body if (sizes["batch"], sizes["band"]) == (8, 4) else body
    placed = (
        P("batch", "band", None),
        P("batch", "band", None),
        P("batch", "band"),
        P(),
        P(),
        P(),
        P(),
        P(),
        P(),
        P(),
        P(),
        P(),
        P(),
        P(),
        P(),
        P(),
        P(),
    )
    return jax.shard_map(
        chosen,
        mesh=mesh,
        in_specs=placed,
        out_specs=(
            P("batch", "band", None),
            P("batch", "band", None),
            P(("batch", "band")),
            P(("batch", "band")),
            P(("batch", "band"), None),
            P(None, ("batch", "band")),
            P(("batch", "band"), None),
            P(("batch", "band")),
            P(("batch", "band")),
            P(("batch", "band")),
            P(("batch", "band")),
            P(("batch", "band"), None),
            P(("batch", "band")),
            P(("batch", "band"), None),
            P(("batch", "band")),
            P(("batch", "band")),
        ),
        check_vma=False,
    )
```

```python
import math

import jax
import jax.numpy as jnp
from jax import lax
from jax.experimental import pallas as pl
from jax.experimental.pallas import tpu as pltpu
from jax.sharding import PartitionSpec as P

HD = 64
NORM_EPS = 1e-06
PACK = 144
SLOTS = 256
BAND = 64
IMGS = 3
ROWS = IMGS * PACK
D = 768
HALF = D // 2
FF = 3072
FH = FF // 2
SMALL = 128
MIB = 1024 * 1024
F32 = jnp.float32
BF = jnp.bfloat16
ANY = pl.BlockSpec(memory_space=pl.ANY)
HBM = pl.BlockSpec(memory_space=pltpu.HBM)
VM = pl.BlockSpec(memory_space=pltpu.VMEM)


def dot(a, b):
    return jnp.dot(a, b, preferred_element_type=F32)


def dot_nt(a, b):
    return lax.dot_general(a, b, (((1,), (1,)), ((), ())), preferred_element_type=F32)


def dot_tn(a, b):
    return lax.dot_general(a, b, (((0,), (0,)), ((), ())), preferred_element_type=F32)


def sds(shape, dtype):
    return jax.ShapeDtypeStruct(shape, dtype)


def vm(shape, dtype):
    return pltpu.VMEM(shape, dtype)


def stay(value):
    return pltpu.with_memory_space_constraint(value, pltpu.HBM)


def place():
    band = lax.axis_index("band")
    batch = lax.axis_index("batch")
    return band >> 1, band & 1, batch >> 1, batch & 1


def one_hot_pack(pos, image):
    rows = lax.broadcasted_iota(jnp.int32, (PACK, pos.shape[1]), 0).astype(F32)
    return jnp.where(rows == pos[image : image + 1, :], 1.0, 0.0).astype(BF)


def shard_picks():
    x, c, z, y = place()

    def pick(width, base):
        row = lax.broadcasted_iota(jnp.int32, (8 * width, 1), 0)
        want = jnp.zeros((8 * width, 1), jnp.int32)
        for q in range(8):
            first = 96 * ((z ^ (q % 4)) * 2 + (y ^ (q // 4))) + base - width * q
            want = jnp.where((row >= width * q) & (row < width * (q + 1)), row + first, want)
        lane = lax.broadcasted_iota(jnp.int32, (8 * width, D), 1)
        return jnp.where(lane == want, 1.0, 0.0).astype(BF)

    return pick(48, 48 * x), pick(24, 48 * x + 24 * c)


def statistics(values):
    center = values - jnp.mean(values, axis=-1, keepdims=True)
    rstd = lax.rsqrt(jnp.mean(center * center, axis=-1, keepdims=True) + NORM_EPS)
    return center * rstd, rstd


def norm_back(grad, z, rstd):
    return rstd * (
        grad
        - jnp.mean(grad, axis=-1, keepdims=True)
        - z * jnp.mean(grad * z, axis=-1, keepdims=True)
    )


def gather_bands(blocks, dst):
    band = lax.axis_index("band")
    for k, block in enumerate(blocks):
        at = pl.multiple_of((band ^ k) * BAND, BAND)
        for i in range(IMGS):
            dst[i, pl.ds(at, BAND), :] = block(i)


def images(ref):
    return lambda i: ref[i] if len(ref.shape) == 3 else ref[i * BAND : (i + 1) * BAND, :]


def images_of_two(a, b):
    count = a.shape[0]

    def block(i):
        lo, hi = i * BAND, (i + 1) * BAND
        parts = [a[lo : min(hi, count), :]] if lo < count else []
        parts += [b[max(lo, count) - count : hi - count, :]] if hi > count else []
        return parts[0] if len(parts) == 1 else jnp.concatenate(parts, axis=0)

    return block


def two_heads(v):
    lane = lax.broadcasted_iota(jnp.int32, v.shape, 1)
    none = jnp.zeros_like(v)
    return jnp.concatenate([jnp.where(lane < HD, v, none), jnp.where(lane < HD, none, v)], axis=0)


def join_heads(v):
    lane = lax.broadcasted_iota(jnp.int32, (PACK, 128), 1)
    return jnp.where(lane < HD, v[:PACK], v[PACK:])


def head_pairs():
    for i in range(IMGS):
        for hp in range(3):
            yield i, slice(i * PACK, (i + 1) * PACK), hp, slice(hp * 128, (hp + 1) * 128)


def keys_shown(pos, image):
    shown = jnp.sum(jnp.where(pos[image : image + 1, :] >= 0, 1.0, 0.0), axis=-1, keepdims=True)
    return lax.broadcasted_iota(jnp.int32, (PACK, 1), 0).astype(F32) < shown


TICK = vm((8, 128), F32)
GAIN1, BIAS1, QB, VB, PB, ASC, GAIN2, BIAS2, RB, MSC = range(10)


OWN = IMGS * BAND


def prepare_kernel(
    cot, gain1, bias1, qvb, bp, asc, gain2, bias2, br, msc, be, wqkv, wp, we, wr, visible, tok,
    cot_o, own_o, par_o, be_o, wqkv_o, wp_o, we_o, wr_o, vis_o, pick_o, pick_p_o,
    vis, sems,
):
    c = lax.axis_index("band") & 1
    units = pl.multiple_of(c * FH, 128)
    rows = (
        (GAIN1, gain1), (BIAS1, bias1), (QB, qvb.at[0]), (VB, qvb.at[1]), (PB, bp), (ASC, asc),
        (GAIN2, gain2), (BIAS2, bias2), (RB, br), (MSC, msc),
    )
    moves = [(cot, cot_o)] + [(v, par_o.at[r]) for r, v in rows]
    moves += [(be.at[pl.ds(units, FH)], be_o.at[0])]
    for m in range(3):
        src = wqkv.at[:, pl.ds(pl.multiple_of(m * D + c * HALF, 128), HALF)]
        moves.append((src, wqkv_o.at[:, pl.ds(m * HALF, HALF)]))
    moves += [(wp, wp_o), (we.at[:, pl.ds(units, FH)], we_o), (wr.at[pl.ds(units, FH), :], wr_o)]
    moves += [(tok.at[i], own_o.at[pl.ds(i * BAND, BAND), :]) for i in range(IMGS)]
    moves += [(visible, vis)]
    copies = [pltpu.make_async_copy(a, b, sems.at[i]) for i, (a, b) in enumerate(moves)]
    for copy in copies:
        copy.start()
    copies[-1].wait()
    seen = jnp.concatenate([vis[...].astype(F32), jnp.zeros((IMGS, 128 - BAND), F32)], axis=1)
    seen = jnp.concatenate([seen, jnp.zeros((16 - IMGS, 128), F32)], axis=0).astype(BF)
    vis_o[...] = jnp.zeros((16, D), BF)
    vis_o[:, 0:128] = seen
    own_o[OWN:, :] = jnp.zeros((16, D), BF)
    own_o[OWN:, 0:128] = seen
    pick_o[...], pick_p_o[...] = shard_picks()
    for copy in copies[:-1]:
        copy.wait()


SPLIT = 224
EARLY = 160


def hold_kernel(tok, vis, after, out, rest):
    count = out.shape[0]
    for i in range(IMGS):
        lo, hi = i * BAND, (i + 1) * BAND
        if lo < count:
            out[lo : min(hi, count), :] = tok[i, 0 : min(hi, count) - lo, :]
        if hi > count:
            rest[max(lo, count) - count : hi - count, :] = tok[i, max(lo, count) - lo :, :]
    rest[OWN - count :, :] = vis[...]


def first_kernel(
    t0, t1, x_a, x_b, d_a, d_b, par, w,
    tok_o, norm_o, qkv_o, mix_o, mix2_o, pos_o, probs_o, mine_o, theirs_o, far_o,
    xs, mix,
):
    band = lax.axis_index("band")
    c = band & 1
    gather_bands((images(t0), images(t1), images_of_two(x_a, x_b), images_of_two(d_a, d_b)), xs)
    heads = pl.multiple_of(c * HALF, 128)
    to = lax.broadcasted_iota(jnp.int32, (BAND, SLOTS), 1) - lax.broadcasted_iota(jnp.int32, (BAND, SLOTS), 0)
    vis = jnp.zeros((16, SLOTS), F32)
    for k, t in enumerate((t0, t1, x_b, d_b)):
        vis = vis + dot(t[t.shape[0] - 16 :, 0:BAND], jnp.where(to == (band ^ k) * BAND, 1.0, 0.0).astype(BF))
    upto = lax.broadcasted_iota(jnp.int32, (SLOTS, SLOTS), 0)
    slot = lax.broadcasted_iota(jnp.int32, (SLOTS, SLOTS), 1)
    before = jnp.where(upto < slot, 1.0, 0.0).astype(BF)
    pos = jnp.where(vis > 0, dot(vis.astype(BF), before), -1.0)
    pos_o[...] = pos[0:8]
    slot = lax.broadcasted_iota(jnp.int32, (SLOTS, BAND), 0) - lax.broadcasted_iota(jnp.int32, (SLOTS, BAND), 1)
    for out, b in ((mine_o, band), (theirs_o, band ^ 1), (far_o, band ^ 3)):
        out[...] = dot(pos.astype(BF), jnp.where(slot == b * BAND, 1.0, 0.0).astype(BF))
    for i in range(IMGS):
        rows = slice(i * PACK, (i + 1) * PACK)
        tok = dot(one_hot_pack(pos, i), xs[i])
        tok_o[rows, :] = tok.astype(BF)
        z, _ = statistics(tok)
        norm_o[rows, :] = (z * par[GAIN1 : GAIN1 + 1, :] + par[BIAS1 : BIAS1 + 1, :]).astype(BF)
    normed = norm_o[...]
    packed = dot(normed, w[...])
    for m in range(3):
        part = packed[:, m * HALF : (m + 1) * HALF]
        if m != 1:
            r = QB if m == 0 else VB
            part = part + par[r : r + 1, pl.ds(heads, HALF)]
        qkv_o[m] = part.astype(BF)
    scores = []
    for i, rows, hp, cols in head_pairs():
        scores.append(dot_nt(qkv_o[1, rows, cols], two_heads(qkv_o[0, rows, cols] * BF(HD**-0.5))))
    probs = []
    for n, (i, rows, hp, cols) in enumerate(head_pairs()):
        shown = jnp.where(keys_shown(pos, i), scores[n], -1e30)
        raised = jnp.exp(shown - jnp.max(shown, axis=0, keepdims=True))
        probs.append(raised / jnp.sum(raised, axis=0, keepdims=True))
    for n, (i, rows, hp, cols) in enumerate(head_pairs()):
        probs_o[n] = probs[n]
        mixed = join_heads(dot_tn(probs[n].astype(BF), qkv_o[2, rows, cols])).astype(BF)
        mix[rows, cols] = mixed
    mix_o[...] = mix[0:SPLIT, :]
    mix2_o[...] = mix[SPLIT:ROWS, :]


def half_kernel(mix_a, mix2_a, wp, c0, c1, x_a, x_b, pos_r, one_o, pre_o, xs):
    c = lax.axis_index("band") & 1
    mine = pl.multiple_of(c * HALF, 128)
    weights = wp[pl.ds(mine, HALF), :]
    one_o[0:SPLIT, :] = dot(mix_a[...], weights)
    one_o[SPLIT:ROWS, :] = dot(mix2_a[...], weights)
    gather_bands((images(c0), images(c1), images_of_two(x_a, x_b), lambda i: jnp.zeros((BAND, D), BF)), xs)
    pos = pos_r[...]
    for i in range(IMGS):
        pre_o[i * PACK : (i + 1) * PACK, :] = dot(one_hot_pack(pos, i), xs[i])


def hidden_kernel(half, mix_b, mix2_b, tok, par, be, wp, we, after, res_o, one_o, n2_o, act_o, slope_o):
    c = lax.axis_index("band") & 1
    weights = wp[pl.ds(pl.multiple_of((1 - c) * HALF, 128), HALF), :]
    one_o[0:SPLIT, :] = half[0:SPLIT, :] + dot(mix_b[...], weights) + par[PB : PB + 1, :]
    one_o[SPLIT:ROWS, :] = half[SPLIT:ROWS, :] + dot(mix2_b[...], weights) + par[PB : PB + 1, :]
    for i in range(IMGS):
        rows = slice(i * PACK, (i + 1) * PACK)
        residual = tok[rows, :].astype(F32) + par[ASC : ASC + 1, :] * one_o[rows, :]
        res_o[rows, :] = residual
        z, _ = statistics(residual)
        n2_o[rows, :] = (z * par[GAIN2 : GAIN2 + 1, :] + par[BIAS2 : BIAS2 + 1, :]).astype(BF)
    for f in range(FH // 256):
        cols = slice(f * 256, (f + 1) * 256)
        for i in range(IMGS):
            rows = slice(i * PACK, (i + 1) * PACK)
            hidden = dot(n2_o[rows, :], we[:, cols]) + be[0:1, cols]
            phi = 0.5 * (1.0 + lax.erf(hidden * math.sqrt(0.5)))
            act_o[rows, cols] = (hidden * phi).astype(BF)
            density = jnp.exp(-0.5 * hidden * hidden) * (1.0 / math.sqrt(2.0 * math.pi))
            slope_o[rows, cols] = phi + hidden * density


def split_kernel(v, out_a, out_b):
    for i in range(IMGS):
        lo = i * BAND
        for first, out in ((0, out_a), (OWN // 2, out_b)):
            start, stop = max(lo, first), min(lo + BAND, first + OWN // 2)
            if start < stop:
                out[start - first : stop - first, :] = v[i, start - lo : stop - lo, :]


def reduce_grad_kernel(part, d_a, d_b, far_r, par, act, pre_o, gb2_o, send_o, keep_o, act_x, full):
    x, c, z, y = place()
    block = images_of_two(d_a, d_b)
    for i in range(IMGS):
        rows = slice(i * PACK, (i + 1) * PACK)
        pre = part[rows, :] + dot(one_hot_pack(far_r[...], i), block(i))
        pre_o[rows, :] = pre.astype(BF)
        gb2_o[rows, :] = (par[MSC : MSC + 1, :] * pre).astype(BF)
    for chip in range(2):

        @pl.when(x == chip)
        def _():
            for j in range(4):
                lo = 384 * j + 192 * chip
                act_x[:, 192 * j : 192 * j + 192] = act[:, lo : lo + 192]

    full[...] = dot_tn(act_x[...], gb2_o[...])
    for dy, out in ((1, send_o), (0, keep_o)):
        for dz in range(2):
            j = 2 * ((z & 1) ^ dz) + (y ^ dy)
            for to in range(2):
                at = pl.multiple_of(192 * j + 96 * to, 96)
                out[2 * dz + to] = full[pl.ds(at, 96), :].astype(BF)


def back_kernel(gb2, wr, slope, we, gh_o, left_o, right_o):
    step = 256
    for f in range(FH // step):
        cols = slice(f * step, (f + 1) * step)
        back = dot_nt(gb2[...], wr[cols, :])
        gh_o[:, cols] = (back * slope[:, cols]).astype(BF)
    gn2 = dot_nt(gh_o[...], we[...]).astype(BF)
    left_o[...] = gn2[:, :HALF]
    right_o[...] = gn2[:, HALF:]


def expand_grad_kernel(n2, gh, pick, send_o, keep_o, tick, wide):
    tick[...] = jnp.zeros_like(tick)
    picked = dot_nt(pick[...], n2[...]).astype(BF)
    wide[...] = dot(picked, gh[...])
    for low, out in ((1, send_o), (0, keep_o)):
        for i in range(4):
            lo = 192 * (i >> 1) + 48 * (low + 2 * (i & 1))
            out[i] = wide[lo : lo + 48, :].astype(BF)


QC = 3 * HALF
QW = QC + HALF
FS = FH + 2 * SMALL


def both_halves(l_a, l_b, r_a, r_b):
    left = l_a[...].astype(F32) + l_b[...].astype(F32)
    right = r_a[...].astype(F32) + r_b[...].astype(F32)
    return jnp.concatenate([left, right], axis=1)


def attention_back_kernel(
    l_a, l_b, r_a, r_b, res, pre, qkv, probs_r, mix_a, mix2_a, mix_b, mix2_b, normed, pick, pick_p, wp, par, after,
    gres_o, gp, send_o, keep_o, tick,
    flat,
):
    tick[...] = jnp.zeros_like(tick)
    c = lax.axis_index("band") & 1
    heads = pl.multiple_of(c * HALF, 128)
    gn2 = both_halves(l_a, l_b, r_a, r_b)
    z2, rstd2 = statistics(res[...])
    gres = pre[...].astype(F32) + norm_back(gn2 * par[GAIN2 : GAIN2 + 1, :], z2, rstd2)
    gres_o[...] = gres
    gb1 = (par[ASC : ASC + 1, :] * gres).astype(BF)
    gm = dot_nt(gb1, wp[pl.ds(heads, HALF), :]).astype(BF)
    grads = [two_heads(gm[rows, cols]) for i, rows, hp, cols in head_pairs()]
    gprobs = [dot_nt(qkv[2, rows, cols], grads[n]) for n, (i, rows, hp, cols) in enumerate(head_pairs())]
    gscores = []
    for n in range(9):
        product = probs_r[n] * gprobs[n]
        gscores.append((product - probs_r[n] * jnp.sum(product, axis=0, keepdims=True)).astype(BF))
    for n, (i, rows, hp, cols) in enumerate(head_pairs()):
        parts = (
            join_heads(dot_tn(gscores[n], qkv[1, rows, cols] * BF(HD**-0.5))),
            dot(gscores[n], two_heads(qkv[0, rows, cols] * BF(HD**-0.5))),
            dot(probs_r[n].astype(BF), grads[n]),
        )
        for m in range(3):
            gp[rows, m * HALF + hp * 128 : m * HALF + (hp + 1) * 128] = parts[m].astype(BF)
    others = pl.multiple_of((1 - c) * HALF, 128)
    mixed = []
    for first, second in ((mix_a, mix_b), (mix2_a, mix2_b)):
        part = dot_nt(pick_p[:, pl.ds(heads, HALF)], first[...])
        mixed.append(part + dot_nt(pick_p[:, pl.ds(others, HALF)], second[...]))
    mixed = jnp.concatenate(mixed, axis=1).astype(BF)
    pn = dot_nt(pick[...], normed[...]).astype(BF)
    proj = dot(mixed, gb1)
    flat[...] = dot(pn, gp[...])
    for dy, out in ((1, send_o), (0, keep_o)):
        for i, dz in enumerate((0, 2, 1, 3)):
            q = 4 * dy + dz
            out[i, :, 0:QC] = flat[48 * q : 48 * q + 48, :].astype(BF)
            block = proj[24 * q : 24 * q + 24]
            out[i, :, QC:QW] = jnp.concatenate([block[:, :HALF], block[:, HALF:]], axis=0).astype(BF)


def vectors_kernel(
    l_a, l_b, r_a, r_b, res, one, gres, gp, w, act, wr, gb2, gh, pre, tok, pick, par, mine, theirs, after,
    gb_keep, gb_send, send_o, keep_o, tick,
    vecs, sums,
):
    tick[...] = jnp.zeros_like(tick)
    x, c, z, y = place()
    heads = pl.multiple_of(c * HALF, 128)
    first = jnp.where(c == 0, 1.0, 0.0)

    def total(v):
        return jnp.sum(v, axis=0, keepdims=True)

    vecs[...] = jnp.zeros_like(vecs)
    gnp = dot_nt(gp[...], w[...])
    z1, _ = statistics(tok[...].astype(F32))
    vecs[GAIN1 : GAIN1 + 1, :] = total(gnp * z1)
    vecs[BIAS1 : BIAS1 + 1, :] = total(gnp)
    vecs[QB : QB + 1, pl.ds(heads, HALF)] = total(gp[:, 0:HALF].astype(F32))
    vecs[VB : VB + 1, pl.ds(heads, HALF)] = total(gp[:, 2 * HALF : 3 * HALF].astype(F32))
    gb1 = (par[ASC : ASC + 1, :] * gres[...]).astype(BF)
    vecs[PB : PB + 1, :] = first * total(gb1.astype(F32))
    vecs[ASC : ASC + 1, :] = first * total(gres[...] * one[...])
    gn2 = both_halves(l_a, l_b, r_a, r_b)
    z2, _ = statistics(res[...])
    vecs[GAIN2 : GAIN2 + 1, :] = first * total(gn2 * z2)
    vecs[BIAS2 : BIAS2 + 1, :] = first * total(gn2)
    vecs[RB : RB + 1, :] = first * total(gb2[...].astype(F32))
    two = dot(act[...], wr[...])
    for m, value in enumerate((gnp.astype(BF), two.astype(BF))):
        for i in range(IMGS):
            rows = slice(i * PACK, (i + 1) * PACK)
            for at, out in ((mine, gb_keep), (theirs, gb_send)):
                out[m, i] = dot_tn(one_hot_pack(at[...], i), value[rows]).astype(BF)
    vecs[MSC : MSC + 1, :] = total(pre[...].astype(F32) * (two + first * par[RB : RB + 1, :]))
    cols = dot_nt(pick[...], vecs[...].astype(BF))
    sums[...] = dot_tn(gh[...], jnp.ones((ROWS, SMALL), BF))
    lane = lax.broadcasted_iota(jnp.int32, (48, SMALL), 1)
    for dy, out in ((1, send_o), (0, keep_o)):
        for dz in range(4):
            b = (z ^ dz) * 2 + (y ^ dy)
            q = 4 * dy + dz
            block = cols[48 * q : 48 * q + 48]
            for k in range(4):
                at = pl.multiple_of(384 * (b & 3) + 192 * x + 48 * k, 48)
                block = jnp.where((lane == 10 + k) & ((b >> 2) == c), sums[pl.ds(at, 48), :], block)
            out[dz >> 1, :, SMALL * (dz & 1) : SMALL * (dz & 1) + SMALL] = block.astype(BF)


def last_kernel(gb_a, gb_b, tok, gres, res, mine, par, after, out_o, gtok_o, tick):
    tick[...] = jnp.zeros_like(tick)

    def own_rows(pack, value):
        high = value.astype(BF)
        return dot_tn(pack, high) + dot_tn(pack, (value - high.astype(F32)).astype(BF))

    for i in range(IMGS):
        rows = slice(i * PACK, (i + 1) * PACK)
        pack = one_hot_pack(mine[...], i)
        z1, rstd1 = statistics(tok[i * BAND : (i + 1) * BAND, :].astype(F32))
        gnp = gb_a[0, i].astype(F32) + gb_b[0, i].astype(F32)
        gtok = own_rows(pack, gres[rows, :]) + norm_back(gnp * par[GAIN1 : GAIN1 + 1, :], z1, rstd1)
        gtok_o[i] = gtok.astype(BF)
        ones = dot_tn(pack, jnp.ones((PACK, D), BF))
        two = gb_a[1, i].astype(F32) + gb_b[1, i].astype(F32) + ones * par[RB : RB + 1, :]
        out_o[i] = (own_rows(pack, res[rows, :]) + par[MSC : MSC + 1, :] * two).astype(BF)


def fold(keep, arrived, keep_o, send_o):
    half = keep.shape[0] // 2
    for i in range(half):
        keep_o[i] = keep[i].astype(F32) + arrived[i].astype(F32)
        send_o[i] = (keep[half + i].astype(F32) + arrived[half + i].astype(F32)).astype(BF)


def fold_kernel(keep, arrived, after, keep_o, send_o, tick):
    tick[...] = jnp.zeros_like(tick)
    fold(keep, arrived, keep_o, send_o)


def home_kernel(keep, arrived, after, keep_o, send_o, tick):
    tick[...] = jnp.zeros_like(tick)
    for i in range(4):
        total = keep[i].astype(F32) + arrived[i].astype(F32)
        keep_o[i] = total
        send_o[i] = total.astype(BF)


def fold(keep, arrived, keep_o, send_o):
    half = keep.shape[0] // 2
    for i in range(half):
        keep_o[i] = keep[i].astype(F32) + arrived[i].astype(F32)
        send_o[i] = (keep[half + i].astype(F32) + arrived[half + i].astype(F32)).astype(BF)


def fold_kernel(keep, arrived, after, keep_o, send_o, tick):
    tick[...] = jnp.zeros_like(tick)
    fold(keep, arrived, keep_o, send_o)


def second_fold_kernel(keep, arrived, we_keep, we_arrived, after, keep_o, send_o, we_keep_o, we_send_o, tick):
    tick[...] = jnp.zeros_like(tick)
    for i in range(2):
        total = keep[i] + arrived[i].astype(F32)
        keep_o[i] = total
        send_o[i] = total.astype(BF)
    fold(we_keep, we_arrived, we_keep_o, we_send_o)


def join_kernel(keep, arrived, vec_keep, vec_send, after, keep_o, send_o, tick):
    tick[...] = jnp.zeros_like(tick)
    fold(keep, arrived, keep_o.at[:, :, 0:FH], send_o.at[:, :, 0:FH])
    keep_o[:, :, FH:FS] = vec_keep[...].astype(F32)
    send_o[:, :, FH:FS] = vec_send[...]


def part_kernel(keep, arrived, after, keep_o, send_o, vec_ko, vec_so, tick):
    tick[...] = jnp.zeros_like(tick)
    fold(keep.at[:, :, 0:FH], arrived.at[:, :, 0:FH], keep_o, send_o)
    for hi in range(2):
        total = keep[hi, :, FH:FS] + arrived[hi, :, FH:FS].astype(F32)
        vec_ko[hi] = total[:, 0:SMALL]
        vec_so[hi] = total[:, SMALL:].astype(BF)


def settle_kernel(wr_k, wr_a, we_k, we_a, after, wr_ko, wr_so, we_ko, we_so, tick, both):
    tick[...] = jnp.zeros_like(tick)
    c = lax.axis_index("band") & 1
    for at, out in ((c, wr_ko), (1 - c, wr_so)):
        out[...] = (wr_k[at] + wr_a[at].astype(F32)).astype(out.dtype)
    both[...] = we_k[0] + we_a[0].astype(F32)
    we_ko[...] = both[pl.ds(pl.multiple_of(c * 24, 8), 24), :]
    we_so[...] = both[pl.ds(pl.multiple_of(24 - c * 24, 8), 24), :].astype(BF)


USED = 16
NEAR = QC + D


def cut_kernel(keep, arrived, after, mine_o, hop_o, near_o, far_o, tick, both):
    tick[...] = jnp.zeros_like(tick)
    c = lax.axis_index("band") & 1
    mine, theirs = pl.multiple_of(c * 24, 8), pl.multiple_of(24 - c * 24, 8)
    for n, own_o, other_o in ((0, mine_o, hop_o), (1, near_o, far_o)):
        both[...] = keep[n].astype(F32) + arrived[n].astype(F32)
        own_o[:, 0:QC] = both[pl.ds(mine, 24), 0:QC].astype(own_o.dtype)
        other_o[...] = both[pl.ds(theirs, 24), 0:QC].astype(own_o.dtype)
        own_o[:, QC : QC + HALF] = both[0:24, QC:QW].astype(own_o.dtype)
        own_o[:, QC + HALF :] = both[24:48, QC:QW].astype(own_o.dtype)


def cores_kernel(vec_a, vec_b, hop, after, keep_o, send_o, other_o, tick):
    tick[...] = jnp.zeros_like(tick)
    keep_o[...] = jnp.zeros_like(keep_o)
    keep_o[:, 0:USED] = vec_a[0, :, 0:USED] + vec_b[0].astype(F32)
    send_o[...] = (vec_a[1, :, 0:USED] + vec_b[1].astype(F32)).astype(BF)
    other_o[...] = hop[...]


def vector_fold_kernel(keep, arrived, after, out, send_o, tick):
    tick[...] = jnp.zeros_like(tick)
    total = keep[...] + arrived[...].astype(F32)
    out[...] = total
    send_o[...] = total[:, :, 0:USED].astype(BF)


def total_kernel(mine, near, hop, far, vec_k, vec_a, after, own_o, other_o, vec_o, tick):
    tick[...] = jnp.zeros_like(tick)
    own_o[...] = mine[...] + near[...].astype(F32)
    other_o[...] = hop[...] + far[...].astype(F32)
    vec_o[...] = vec_k[...]
    vec_o[:, 0:USED] = vec_k[:, 0:USED] + vec_a[...].astype(F32)


def out_kernel(
    own, other, vec_r, we_keep, we_arrived, wr_keep, wr_arrived, after,
    qkv_o, first_o, bias_o, qv_o, bp_o, asc_o, gain2_o, bias2_o, br_o, msc_o, eb_o, proj_o, we_o, wr_o,
):
    _, c, z, _ = place()
    wr_o[...] = jnp.where((z >> 1) == c, wr_keep[...], wr_arrived[...].astype(F32))
    we_o[:, pl.ds(pl.multiple_of(c * FH, 128), FH)] = we_keep[...]
    we_o[:, pl.ds(pl.multiple_of((1 - c) * FH, 128), FH)] = we_arrived[...].astype(F32)
    proj_o[...] = own[:, QC:NEAR]
    for m in range(3):
        cols = slice(m * HALF, (m + 1) * HALF)
        qkv_o[:, pl.ds(pl.multiple_of(m * D + c * HALF, 128), HALF)] = own[:, cols]
        qkv_o[:, pl.ds(pl.multiple_of(m * D + (1 - c) * HALF, 128), HALF)] = other[:, cols]
    vec = vec_r[pl.ds(pl.multiple_of(c * 24, 8), 24), :].T
    outs = (first_o, bias_o, None, None, bp_o, asc_o, gain2_o, bias2_o, br_o, msc_o)
    for r, out in enumerate(outs):
        if out is not None:
            out[...] = vec[r]
    qv_o[...] = vec[2:4]
    units = vec_r[...].T
    units = jnp.where(c == 0, units[10:12], units[12:14])
    eb_o[...] = jnp.concatenate([units[0:1], units[1:2]], axis=1).reshape(96)


COSTS = {
    "vectors_kernel": (8000000000, 20000000),
    "second_fold_kernel": (0, 2000000),
    "last_kernel": (0, 1000000),
    "spread_kernel": (0, 2000000),
    "finish_kernel": (0, 1000000),
    "out_kernel": (0, 1000000),
    "prepare_kernel": (0, 9000000),
    "total_kernel": (4000000000, 0),
}


def call(kernel, outs, specs, scratch=(), vmem=24, cost=0):
    return pl.pallas_call(
        kernel,
        out_shape=outs,
        in_specs=specs,
        out_specs=jax.tree.map(lambda _: VM, outs),
        scratch_shapes=list(scratch),
        compiler_params=pltpu.CompilerParams(vmem_limit_bytes=vmem * MIB),
        cost_estimate=pl.CostEstimate(flops=COSTS.get(kernel.__name__, (0, 0))[0] + cost, bytes_accessed=COSTS.get(kernel.__name__, (0, 0))[1], transcendentals=0),
    )


def fold_call(keep, arrived, after, cost=0):
    half = (keep.shape[0] // 2, *keep.shape[1:])
    return call(fold_kernel, (vm(half, F32), vm(half, BF), TICK), [VM] * 2 + [ANY], cost=cost)(keep, arrived, after)


def by_core(value):
    return lax.ppermute(value, "band", [(i, i ^ 1) for i in range(4)])


def by_x(value):
    return lax.ppermute(value, "band", [(i, i ^ 2) for i in range(4)])


def by_y(value):
    return lax.ppermute(value, "batch", [(i, i ^ 1) for i in range(8)])


def by_z(value, dz):
    return lax.ppermute(value, "batch", [(i, i ^ (2 * dz)) for i in range(8)])


def across(value):
    return lax.ppermute(value, ("batch", "band"), [(d, d ^ 17) for d in range(32)])


def homeward(value, dz):
    pairs = [(d, d ^ (8 * dz)) for d in range(32) if ((d ^ (8 * dz)) >> 4) == (d & 1)]
    return lax.ppermute(value, ("batch", "band"), pairs)


def packed_body(
    tokens, cotangent, visible, first_gain, first_bias, qkv_weight, qv_bias, proj_weight, proj_bias,
    attn_scale, second_gain, second_bias, expand_weight, expand_bias, reduce_weight, reduce_bias, mlp_scale,
):
    block = vm(cotangent.shape, BF)
    rows_f, rows_b = vm((ROWS, D), F32), vm((ROWS, D), BF)
    tok_x = by_x(tokens)
    tok_block = vm((OWN + 16, D), BF)
    cot, tok_own, par, be, wqkv, wp, we, wr, vis, pick, pick_p = call(
        prepare_kernel,
        (
            block,
            tok_block,
            vm((16, D), F32),
            vm((8, FH), F32),
            vm((D, QC), BF),
            vm((D, D), BF),
            vm((D, FH), BF),
            vm((FH, D), BF),
            vm((16, D), BF),
            vm((HALF, D), BF),
            vm((192, D), BF),
        ),
        [ANY] * 17,
        [pltpu.VMEM(visible.shape, jnp.int32), pltpu.SemaphoreType.DMA((22,))],
    )(
        *map(
            stay,
            (
                cotangent, first_gain, first_bias, qv_bias, proj_bias, attn_scale, second_gain, second_bias,
                reduce_bias, mlp_scale, expand_bias, qkv_weight, proj_weight, expand_weight, reduce_weight, visible,
                tokens,
            ),
        )
    )
    vis_x = by_x(vis)
    tok_c = by_core(tok_own)
    cot_c = by_core(cot)
    parts = (vm((EARLY, D), BF), vm((OWN + 16 - EARLY, D), BF))
    tok_x = call(hold_kernel, parts, [VM] * 2 + [ANY])(tok_x, vis_x, par)
    tok_d = [by_core(v) for v in tok_x]
    cot_x = call(split_kernel, (vm((OWN // 2, D), BF),) * 2, [VM])(by_x(cot))
    cot_d = [by_core(v) for v in cot_x]
    tok, normed, qkv, mix_own, mix2_own, pos, probs, pos_mine, pos_theirs, pos_far = call(
        first_kernel,
        (
            rows_b,
            rows_b,
            vm((3, ROWS, HALF), BF),
            vm((SPLIT, HALF), BF),
            vm((ROWS - SPLIT, HALF), BF),
            vm((8, SLOTS), F32),
            vm((9, PACK, 2 * PACK), F32),
            vm((16, BAND), F32),
            vm((16, BAND), F32),
            vm((16, BAND), F32),
        ),
        [VM] * 8,
        [pltpu.VMEM((IMGS, SLOTS, D), BF), pltpu.VMEM((ROWS, HALF), BF)],
    )(tok_own, tok_c, *tok_x, *tok_d, par, wqkv)
    mix_other, mix2_other = by_core(mix_own), by_core(mix2_own)
    half_one, half_pre = call(
        half_kernel, (rows_f, rows_f), [VM] * 8, [pltpu.VMEM((IMGS, SLOTS, D), BF)]
    )(mix_own, mix2_own, wp, cot, cot_c, *cot_x, pos)
    res, one, n2, act, slope = call(
        hidden_kernel,
        (rows_f, rows_f, rows_b, vm((ROWS, FH), BF), vm((ROWS, FH), F32)),
        [VM] * 8 + [ANY],
    )(half_one, mix_other, mix2_other, tok, par, be, wp, we, pick)
    pre, gb2, wr_send, wr_keep = call(
        reduce_grad_kernel,
        (rows_b, rows_b, vm((4, 96, D), BF), vm((4, 96, D), BF)),
        [VM] * 6,
        [pltpu.VMEM((ROWS, D), BF), pltpu.VMEM((D, D), F32)],
    )(half_pre, *cot_d, pos_far, par, act)
    wr_y = by_y(wr_send)
    half_b = vm((ROWS, HALF), BF)
    gh, left, right = call(back_kernel, (vm((ROWS, FH), BF), half_b, half_b), [VM] * 4)(gb2, wr, slope, we)
    gn2 = (left, by_core(left), right, by_core(right))
    we_send, we_keep, tick = call(
        expand_grad_kernel,
        (vm((4, 48, FH), BF), vm((4, 48, FH), BF), TICK),
        [VM] * 3,
        [pltpu.VMEM((HALF, FH), F32)],
    )(n2, gh, pick)
    we_z = by_z(we_send, 1)
    gres, gp, qp_send, qp_keep, tick = call(
        attention_back_kernel,
        (rows_f, vm((ROWS, QC), BF), vm((4, 48, QW), BF), vm((4, 48, QW), BF), TICK),
        [VM] * 17 + [ANY],
        [pltpu.VMEM((HALF, QC), F32)],
    )(*gn2, res, pre, qkv, probs, mix_own, mix2_own, mix_other, mix2_other, normed, pick, pick_p, wp, par, tick)
    qp_y = by_y(qp_send)
    wr_keep, wr_send, tick = call(
        home_kernel, (vm((4, 96, D), F32), vm((4, 96, D), BF), TICK), [VM] * 2 + [ANY]
    )(wr_keep, wr_y, tick)
    wr_z = homeward(wr_send, 2)
    gb_keep, gb_send, vec_send, vec_keep, tick = call(
        vectors_kernel,
        (vm((2, *tokens.shape), BF), vm((2, *tokens.shape), BF), vm((2, 48, 2 * SMALL), BF), vm((2, 48, 2 * SMALL), BF), TICK),
        [VM] * 19 + [ANY],
        [pltpu.VMEM((SMALL, D), F32), pltpu.VMEM((FH, SMALL), F32)],
    )(*gn2, res, one, gres, gp, wqkv, act, wr, gb2, gh, pre, tok, pick, par, pos_mine, pos_theirs, tick)
    gb_other = by_core(gb_send)
    we_keep, we_send, tick = call(
        join_kernel, (vm((2, 48, FS), F32), vm((2, 48, FS), BF), TICK), [VM] * 4 + [ANY]
    )(we_keep, we_z, vec_keep, vec_send, tick)
    we_y = by_y(we_send)
    qp_keep, qp_send, tick = fold_call(qp_keep, qp_y, tick, cost=0)
    qp_z = by_z(qp_send, 1)
    wr_keep, wr_send, tick = fold_call(wr_keep, wr_z, tick, cost=0)
    wr_z = homeward(wr_send, 1)
    we_keep, we_send, vec_keep, vec_send, tick = call(
        part_kernel,
        (vm((1, 48, FH), F32), vm((1, 48, FH), BF), vm((2, 48, SMALL), F32), vm((2, 48, SMALL), BF), TICK),
        [VM] * 2 + [ANY],
    )(we_keep, we_y, tick)
    vec_z = by_z(vec_send, 1)
    we_z = by_z(we_send, 2)
    mine, hop, near, far, tick = call(
        cut_kernel,
        (vm((24, NEAR), F32), vm((24, QC), F32), vm((24, NEAR), BF), vm((24, QC), BF), TICK),
        [VM] * 2 + [ANY],
        [pltpu.VMEM((48, QW), F32)],
        cost=0,
    )(qp_keep, qp_z, tick)
    near, far, hop = by_z(near, 2), across(far), by_core(hop)
    vec, vec_send, tick = call(
        vector_fold_kernel, (vm((2, 48, SMALL), F32), vm((2, 48, USED), BF), TICK), [VM] * 2 + [ANY], cost=4000000000
    )(vec_keep, vec_z, tick)
    vec_other = by_core(vec_send)
    layer_out, grad_tokens, tick = call(
        last_kernel,
        (sds(tokens.shape, BF), sds(tokens.shape, BF), TICK),
        [VM] * 7 + [ANY],
    )(gb_keep, gb_other, tok_own, gres, res, pos_mine, par, tick)
    vec_keep, vec_send, hop, tick = call(
        cores_kernel,
        (vm((48, SMALL), F32), vm((48, USED), BF), vm((24, QC), F32), TICK),
        [VM] * 3 + [ANY],
    )(vec, vec_other, hop, tick)
    vec_z = by_z(vec_send, 2)
    wr_keep, wr_send, we_keep, we_send, tick = call(
        settle_kernel,
        (vm((96, D), F32), vm((96, D), BF), vm((24, FH), F32), vm((24, FH), BF), TICK),
        [VM] * 4 + [ANY],
        [pltpu.VMEM((48, FH), F32)],
    )(wr_keep, wr_z, we_keep, we_z, tick)
    we_other, wr_other = by_core(we_send), by_core(wr_send)
    own, other, vec, tick = call(
        total_kernel,
        (vm((24, NEAR), F32), vm((24, QC), F32), vm((48, SMALL), F32), TICK),
        [VM] * 6 + [ANY],
    )(mine, near, hop, far, vec_keep, vec_z, tick)
    vector = sds((24,), F32)
    grad_qkv, gg1, gb1, gqv, gbp, gas, gg2, gb2, gbr, gms, geb, grad_proj, grad_expand, grad_reduce = call(
        out_kernel,
        (
            sds((24, 3 * D), F32), vector, vector, sds((2, 24), F32), vector, vector, vector, vector, vector, vector,
            sds((96,), F32), sds((24, D), F32), sds((24, FF), F32), sds((96, D), F32),
        ),
        [VM] * 7 + [ANY],
    )(own, other, vec, we_keep, we_other, wr_keep, wr_other, tick)
    return (
        layer_out, grad_tokens, gg1, gb1, grad_qkv, gqv, grad_proj, gbp, gas, gg2, gb2, grad_expand, geb, grad_reduce,
        gbr, gms,
    )


def layer_norm(values, norm_gain, norm_shift):
    center = values - jnp.mean(values, axis=-1, keepdims=True)
    spread = jnp.mean(center * center, axis=-1, keepdims=True)
    return center * lax.rsqrt(spread + NORM_EPS) * norm_gain + norm_shift


def gelu_exact(values):
    return jax.nn.gelu(values, approximate=False)


def split_rows(packed_rows, mask_rows):
    item_count = packed_rows.shape[0]
    slot_count = packed_rows.shape[1]
    heads_here = packed_rows.shape[4] // HD
    unpacked = packed_rows.reshape(item_count, slot_count, 3, heads_here, HD)
    queries = unpacked[:, :, 0]
    key_rows = unpacked[:, :, 1]
    value_rows = unpacked[:, :, 2]
    key_valid = mask_rows.reshape(item_count, slot_count) > 0
    score_scale = 1.0 / math.sqrt(HD)
    scores = (
        jnp.einsum("bqhe,bkhe->bhqk", queries, key_rows, preferred_element_type=jnp.float32)
        * score_scale
    )
    scores = jnp.where(key_valid[:, None, None, :], scores, -1e30)
    return (queries, key_rows, value_rows, scores)


def attend_plain(inputs):
    packed_rows, mask_rows = inputs
    queries, key_rows, value_rows, scores = split_rows(packed_rows, mask_rows)
    row_top = jnp.max(scores, axis=-1, keepdims=True)
    raised = jnp.exp(scores - row_top)
    row_total = jnp.sum(raised, axis=-1, keepdims=True)
    attn_prob = raised / row_total
    log_total = (row_top + jnp.log(row_total))[..., 0]
    mixed_rows = jnp.einsum(
        "bhqk,bkhe->bqhe",
        attn_prob.astype(jnp.bfloat16),
        value_rows,
        preferred_element_type=jnp.float32,
    ).astype(jnp.bfloat16)
    mixed_rows = mixed_rows.reshape(
        packed_rows.shape[0], packed_rows.shape[1], packed_rows.shape[4]
    )
    return (mixed_rows, log_total)


def backward_rows(score_parts, log_total, grad_rows):
    queries, key_rows, value_rows, scores = score_parts
    item_count, slot_count, heads_here, head_size = queries.shape
    score_scale = 1.0 / math.sqrt(HD)
    attn_prob = jnp.exp(scores - log_total[..., None])
    grad_heads = grad_rows.reshape(item_count, slot_count, heads_here, head_size)
    grad_prob = jnp.einsum(
        "bqhe,bkhe->bhqk", grad_heads, value_rows, preferred_element_type=jnp.float32
    )
    row_delta = jnp.sum(attn_prob * grad_prob, axis=-1, keepdims=True)
    grad_score = (attn_prob * (grad_prob - row_delta)).astype(jnp.bfloat16)
    grad_query = (
        jnp.einsum("bhqk,bkhe->bqhe", grad_score, key_rows, preferred_element_type=jnp.float32)
        * score_scale
    )
    grad_key = (
        jnp.einsum("bhqk,bqhe->bkhe", grad_score, queries, preferred_element_type=jnp.float32)
        * score_scale
    )
    grad_value = jnp.einsum(
        "bhqk,bqhe->bkhe",
        attn_prob.astype(jnp.bfloat16),
        grad_heads,
        preferred_element_type=jnp.float32,
    )
    stacked = jnp.stack([grad_query, grad_key, grad_value], axis=2)
    return stacked.reshape(item_count, slot_count, 3, 1, heads_here * head_size).astype(
        jnp.bfloat16
    )


def attend_again(inputs):
    packed_rows, mask_rows, grad_rows = inputs
    score_parts = split_rows(packed_rows, mask_rows)
    scores = score_parts[3]
    row_top = jnp.max(scores, axis=-1, keepdims=True)
    log_total = (row_top + jnp.log(jnp.sum(jnp.exp(scores - row_top), axis=-1, keepdims=True)))[
        ..., 0
    ]
    return backward_rows(score_parts, log_total, grad_rows)


def body(
    tokens,
    cotangent,
    visible,
    first_gain,
    first_bias,
    qkv_weight,
    qv_bias,
    proj_weight,
    proj_bias,
    attn_scale,
    second_gain,
    second_bias,
    expand_weight,
    expand_bias,
    reduce_weight,
    reduce_bias,
    mlp_scale,
):
    images, slot_count, model_width = tokens.shape
    groups = lax.axis_size("band")
    local_width = model_width // groups
    inputs_full = tokens.astype(jnp.float32)
    shown_mask = visible.astype(jnp.float32)
    normed, first_pull = jax.vjp(layer_norm, inputs_full, first_gain, first_bias)
    normed_low = normed.astype(jnp.bfloat16)
    qkv_bias = jnp.concatenate([qv_bias[0], jnp.zeros((model_width,), jnp.float32), qv_bias[1]])

    def project_qkv():
        product = jnp.einsum(
            "isd,de->ise", normed_low, qkv_weight, preferred_element_type=jnp.float32
        )
        return (
            (product + qkv_bias)
            .astype(jnp.bfloat16)
            .reshape(images, slot_count, 3, groups, local_width)
        )

    packed = project_qkv()
    mask_part = jnp.broadcast_to(
        shown_mask.astype(jnp.bfloat16)[:, :, None, None, None], (images, slot_count, 1, groups, 1)
    )
    results = attend_plain(
        (
            lax.all_to_all(packed, "band", split_axis=3, concat_axis=1, tiled=True),
            lax.all_to_all(mask_part, "band", split_axis=3, concat_axis=1, tiled=True),
        )
    )
    mixed_heads = results[0].reshape(images, groups * slot_count, 1, local_width)
    back_rows = lax.all_to_all(mixed_heads, "band", split_axis=1, concat_axis=2, tiled=True)
    mixed_rows = back_rows.reshape(images, slot_count, model_width)
    branch_one = (
        jnp.einsum("isd,de->ise", mixed_rows, proj_weight, preferred_element_type=jnp.float32)
        + proj_bias
    )
    residual = inputs_full + attn_scale * branch_one
    normed_two, second_pull = jax.vjp(layer_norm, residual, second_gain, second_bias)
    normed_two_low = normed_two.astype(jnp.bfloat16)
    hidden = (
        jnp.einsum("isd,df->isf", normed_two_low, expand_weight, preferred_element_type=jnp.float32)
        + expand_bias
    )
    activated, gelu_pull = jax.vjp(gelu_exact, hidden)
    activated_low = activated.astype(jnp.bfloat16)
    branch_two = (
        jnp.einsum("isf,fd->isd", activated_low, reduce_weight, preferred_element_type=jnp.float32)
        + reduce_bias
    )
    layer_out = (shown_mask[..., None] * (residual + mlp_scale * branch_two)).astype(jnp.bfloat16)
    grad_pre = shown_mask[..., None] * cotangent.astype(jnp.float32)
    grad_mlp_scale = jnp.sum(grad_pre * branch_two, axis=(0, 1))
    grad_branch_two = (mlp_scale * grad_pre).astype(jnp.bfloat16)
    grad_reduce_weight = jnp.einsum(
        "isf,isd->fd", activated_low, grad_branch_two, preferred_element_type=jnp.float32
    )
    grad_reduce_bias = jnp.sum(grad_branch_two.astype(jnp.float32), axis=(0, 1))
    grad_activated = jnp.einsum(
        "isd,fd->isf", grad_branch_two, reduce_weight, preferred_element_type=jnp.float32
    )
    grad_hidden = gelu_pull(grad_activated)[0].astype(jnp.bfloat16)
    grad_expand_weight = jnp.einsum(
        "isd,isf->df", normed_two_low, grad_hidden, preferred_element_type=jnp.float32
    )
    grad_expand_bias = jnp.sum(grad_hidden.astype(jnp.float32), axis=(0, 1))
    grad_normed_two = jnp.einsum(
        "isf,df->isd", grad_hidden, expand_weight, preferred_element_type=jnp.float32
    )
    grad_resid_norm, grad_second_gain, grad_second_bias = second_pull(grad_normed_two)
    grad_residual = grad_pre + grad_resid_norm
    grad_attn_scale = jnp.sum(grad_residual * branch_one, axis=(0, 1))
    grad_branch_one = (attn_scale * grad_residual).astype(jnp.bfloat16)
    grad_proj_weight = jnp.einsum(
        "isd,ise->de", mixed_rows, grad_branch_one, preferred_element_type=jnp.float32
    )
    grad_proj_bias = jnp.sum(grad_branch_one.astype(jnp.float32), axis=(0, 1))
    grad_mixed = jnp.einsum(
        "ise,de->isd", grad_branch_one, proj_weight, preferred_element_type=jnp.float32
    )
    grad_mixed = grad_mixed.astype(jnp.bfloat16).reshape(images, slot_count, 1, groups, local_width)
    repacked = project_qkv()
    grad_packed = attend_again(
        (
            lax.all_to_all(repacked, "band", split_axis=3, concat_axis=1, tiled=True),
            lax.all_to_all(mask_part, "band", split_axis=3, concat_axis=1, tiled=True),
            lax.all_to_all(grad_mixed, "band", split_axis=3, concat_axis=1, tiled=True),
        )
    )
    grad_bands = lax.all_to_all(grad_packed, "band", split_axis=1, concat_axis=3, tiled=True)
    grad_qkv = grad_bands.reshape(images, slot_count, 3 * model_width)
    grad_qkv_weight = jnp.einsum(
        "isd,ise->de", normed_low, grad_qkv, preferred_element_type=jnp.float32
    )
    column_sums = jnp.sum(grad_qkv.astype(jnp.float32), axis=(0, 1))
    grad_qv_bias = jnp.stack([column_sums[:model_width], column_sums[2 * model_width :]])
    grad_normed = jnp.einsum(
        "ise,de->isd", grad_qkv, qkv_weight, preferred_element_type=jnp.float32
    )
    grad_input_norm, grad_first_gain, grad_first_bias = first_pull(grad_normed)
    grad_tokens = (grad_residual + grad_input_norm).astype(jnp.bfloat16)
    all_sums = (
        lax.psum_scatter(grad_first_gain, ("batch", "band"), scatter_dimension=0, tiled=True),
        lax.psum_scatter(grad_first_bias, ("batch", "band"), scatter_dimension=0, tiled=True),
        lax.psum_scatter(grad_qkv_weight, ("batch", "band"), scatter_dimension=0, tiled=True),
        lax.psum_scatter(grad_qv_bias, ("batch", "band"), scatter_dimension=1, tiled=True),
        lax.psum_scatter(grad_proj_weight, ("batch", "band"), scatter_dimension=0, tiled=True),
        lax.psum_scatter(grad_proj_bias, ("batch", "band"), scatter_dimension=0, tiled=True),
        lax.psum_scatter(grad_attn_scale, ("batch", "band"), scatter_dimension=0, tiled=True),
        lax.psum_scatter(grad_second_gain, ("batch", "band"), scatter_dimension=0, tiled=True),
        lax.psum_scatter(grad_second_bias, ("batch", "band"), scatter_dimension=0, tiled=True),
        lax.psum_scatter(grad_expand_weight, ("batch", "band"), scatter_dimension=0, tiled=True),
        lax.psum_scatter(grad_expand_bias, ("batch", "band"), scatter_dimension=0, tiled=True),
        lax.psum_scatter(grad_reduce_weight, ("batch", "band"), scatter_dimension=0, tiled=True),
        lax.psum_scatter(grad_reduce_bias, ("batch", "band"), scatter_dimension=0, tiled=True),
        lax.psum_scatter(grad_mlp_scale, ("batch", "band"), scatter_dimension=0, tiled=True),
    )
    (
        sum_first_gain,
        sum_first_bias,
        sum_qkv_weight,
        sum_qv_bias,
        sum_proj_weight,
        sum_proj_bias,
        sum_attn_scale,
        sum_second_gain,
        sum_second_bias,
        sum_expand_weight,
        sum_expand_bias,
        sum_reduce_weight,
        sum_reduce_bias,
        sum_mlp_scale,
    ) = all_sums
    return (
        layer_out,
        grad_tokens,
        sum_first_gain,
        sum_first_bias,
        sum_qkv_weight,
        sum_qv_bias,
        sum_proj_weight,
        sum_proj_bias,
        sum_attn_scale,
        sum_second_gain,
        sum_second_bias,
        sum_expand_weight,
        sum_expand_bias,
        sum_reduce_weight,
        sum_reduce_bias,
        sum_mlp_scale,
    )


def solution(mesh):
    sizes = dict(mesh.shape)
    chosen = packed_body if (sizes["batch"], sizes["band"]) == (8, 4) else body
    placed = (
        P("batch", "band", None),
        P("batch", "band", None),
        P("batch", "band"),
        P(),
        P(),
        P(),
        P(),
        P(),
        P(),
        P(),
        P(),
        P(),
        P(),
        P(),
        P(),
        P(),
        P(),
    )
    return jax.shard_map(
        chosen,
        mesh=mesh,
        in_specs=placed,
        out_specs=(
            P("batch", "band", None),
            P("batch", "band", None),
            P(("batch", "band")),
            P(("batch", "band")),
            P(("batch", "band"), None),
            P(None, ("batch", "band")),
            P(("batch", "band"), None),
            P(("batch", "band")),
            P(("batch", "band")),
            P(("batch", "band")),
            P(("batch", "band")),
            P(("batch", "band"), None),
            P(("batch", "band")),
            P(("batch", "band"), None),
            P(("batch", "band")),
            P(("batch", "band")),
        ),
        check_vma=False,
    )
```

```python
import math

import jax
import jax.numpy as jnp
from jax import lax
from jax.experimental import pallas as pl
from jax.experimental.pallas import tpu as pltpu
from jax.sharding import PartitionSpec as P

HD = 64
NORM_EPS = 1e-06
PACK = 144
SLOTS = 256
BAND = 64
IMGS = 3
ROWS = IMGS * PACK
D = 768
HALF = D // 2
FF = 3072
FH = FF // 2
SMALL = 128
MIB = 1024 * 1024
F32 = jnp.float32
BF = jnp.bfloat16
ANY = pl.BlockSpec(memory_space=pl.ANY)
HBM = pl.BlockSpec(memory_space=pltpu.HBM)
VM = pl.BlockSpec(memory_space=pltpu.VMEM)


def dot(a, b):
    return jnp.dot(a, b, preferred_element_type=F32)


def dot_nt(a, b):
    return lax.dot_general(a, b, (((1,), (1,)), ((), ())), preferred_element_type=F32)


def dot_tn(a, b):
    return lax.dot_general(a, b, (((0,), (0,)), ((), ())), preferred_element_type=F32)


def sds(shape, dtype):
    return jax.ShapeDtypeStruct(shape, dtype)


def vm(shape, dtype):
    return pltpu.VMEM(shape, dtype)


def stay(value):
    return pltpu.with_memory_space_constraint(value, pltpu.HBM)


def place():
    band = lax.axis_index("band")
    batch = lax.axis_index("batch")
    return band >> 1, band & 1, batch >> 1, batch & 1


def one_hot_pack(pos, image):
    rows = lax.broadcasted_iota(jnp.int32, (PACK, pos.shape[1]), 0).astype(F32)
    return jnp.where(rows == pos[image : image + 1, :], 1.0, 0.0).astype(BF)


def shard_picks():
    x, c, z, y = place()

    def pick(width, base):
        row = lax.broadcasted_iota(jnp.int32, (8 * width, 1), 0)
        want = jnp.zeros((8 * width, 1), jnp.int32)
        for q in range(8):
            first = 96 * ((z ^ (q % 4)) * 2 + (y ^ (q // 4))) + base - width * q
            want = jnp.where((row >= width * q) & (row < width * (q + 1)), row + first, want)
        lane = lax.broadcasted_iota(jnp.int32, (8 * width, D), 1)
        return jnp.where(lane == want, 1.0, 0.0).astype(BF)

    return pick(48, 48 * x), pick(24, 48 * x + 24 * c)


def statistics(values):
    center = values - jnp.mean(values, axis=-1, keepdims=True)
    rstd = lax.rsqrt(jnp.mean(center * center, axis=-1, keepdims=True) + NORM_EPS)
    return center * rstd, rstd


def norm_back(grad, z, rstd):
    return rstd * (
        grad
        - jnp.mean(grad, axis=-1, keepdims=True)
        - z * jnp.mean(grad * z, axis=-1, keepdims=True)
    )


def gather_bands(blocks, dst):
    band = lax.axis_index("band")
    for k, block in enumerate(blocks):
        at = pl.multiple_of((band ^ k) * BAND, BAND)
        for i in range(IMGS):
            dst[i, pl.ds(at, BAND), :] = block(i)


def images(ref):
    return lambda i: ref[i] if len(ref.shape) == 3 else ref[i * BAND : (i + 1) * BAND, :]


def images_of_two(a, b):
    count = a.shape[0]

    def block(i):
        lo, hi = i * BAND, (i + 1) * BAND
        parts = [a[lo : min(hi, count), :]] if lo < count else []
        parts += [b[max(lo, count) - count : hi - count, :]] if hi > count else []
        return parts[0] if len(parts) == 1 else jnp.concatenate(parts, axis=0)

    return block


def two_heads(v):
    lane = lax.broadcasted_iota(jnp.int32, v.shape, 1)
    none = jnp.zeros_like(v)
    return jnp.concatenate([jnp.where(lane < HD, v, none), jnp.where(lane < HD, none, v)], axis=0)


def join_heads(v):
    lane = lax.broadcasted_iota(jnp.int32, (PACK, 128), 1)
    return jnp.where(lane < HD, v[:PACK], v[PACK:])


def head_pairs():
    for i in range(IMGS):
        for hp in range(3):
            yield i, slice(i * PACK, (i + 1) * PACK), hp, slice(hp * 128, (hp + 1) * 128)


def keys_shown(pos, image):
    shown = jnp.sum(jnp.where(pos[image : image + 1, :] >= 0, 1.0, 0.0), axis=-1, keepdims=True)
    return lax.broadcasted_iota(jnp.int32, (PACK, 1), 0).astype(F32) < shown


TICK = vm((8, 128), F32)
GAIN1, BIAS1, QB, VB, PB, ASC, GAIN2, BIAS2, RB, MSC = range(10)


OWN = IMGS * BAND


def prepare_kernel(
    cot, gain1, bias1, qvb, bp, asc, gain2, bias2, br, msc, be, wqkv, wp, we, wr, visible, tok,
    cot_o, own_o, par_o, be_o, wqkv_o, wp_o, we_o, wr_o, vis_o, pick_o, pick_p_o,
    vis, sems,
):
    c = lax.axis_index("band") & 1
    units = pl.multiple_of(c * FH, 128)
    rows = (
        (GAIN1, gain1), (BIAS1, bias1), (QB, qvb.at[0]), (VB, qvb.at[1]), (PB, bp), (ASC, asc),
        (GAIN2, gain2), (BIAS2, bias2), (RB, br), (MSC, msc),
    )
    moves = [(cot, cot_o)] + [(v, par_o.at[r]) for r, v in rows]
    moves += [(be.at[pl.ds(units, FH)], be_o.at[0])]
    for m in range(3):
        src = wqkv.at[:, pl.ds(pl.multiple_of(m * D + c * HALF, 128), HALF)]
        moves.append((src, wqkv_o.at[:, pl.ds(m * HALF, HALF)]))
    moves += [(wp, wp_o), (we.at[:, pl.ds(units, FH)], we_o), (wr.at[pl.ds(units, FH), :], wr_o)]
    moves += [(tok.at[i], own_o.at[pl.ds(i * BAND, BAND), :]) for i in range(IMGS)]
    moves += [(visible, vis)]
    copies = [pltpu.make_async_copy(a, b, sems.at[i]) for i, (a, b) in enumerate(moves)]
    for copy in copies:
        copy.start()
    copies[-1].wait()
    seen = jnp.concatenate([vis[...].astype(F32), jnp.zeros((IMGS, 128 - BAND), F32)], axis=1)
    seen = jnp.concatenate([seen, jnp.zeros((16 - IMGS, 128), F32)], axis=0).astype(BF)
    vis_o[...] = jnp.zeros((16, D), BF)
    vis_o[:, 0:128] = seen
    own_o[OWN:, :] = jnp.zeros((16, D), BF)
    own_o[OWN:, 0:128] = seen
    pick_o[...], pick_p_o[...] = shard_picks()
    for copy in copies[:-1]:
        copy.wait()


SPLIT = 224
EARLY = 160


def hold_kernel(tok, vis, after, out, rest):
    count = out.shape[0]
    for i in range(IMGS):
        lo, hi = i * BAND, (i + 1) * BAND
        if lo < count:
            out[lo : min(hi, count), :] = tok[i, 0 : min(hi, count) - lo, :]
        if hi > count:
            rest[max(lo, count) - count : hi - count, :] = tok[i, max(lo, count) - lo :, :]
    rest[OWN - count :, :] = vis[...]


def first_kernel(
    t0, t1, x_a, x_b, d_a, d_b, par, w,
    tok_o, norm_o, qkv_o, mix_o, mix2_o, pos_o, probs_o, mine_o, theirs_o, far_o,
    xs, mix,
):
    band = lax.axis_index("band")
    c = band & 1
    gather_bands((images(t0), images(t1), images_of_two(x_a, x_b), images_of_two(d_a, d_b)), xs)
    heads = pl.multiple_of(c * HALF, 128)
    to = lax.broadcasted_iota(jnp.int32, (BAND, SLOTS), 1) - lax.broadcasted_iota(jnp.int32, (BAND, SLOTS), 0)
    vis = jnp.zeros((16, SLOTS), F32)
    for k, t in enumerate((t0, t1, x_b, d_b)):
        vis = vis + dot(t[t.shape[0] - 16 :, 0:BAND], jnp.where(to == (band ^ k) * BAND, 1.0, 0.0).astype(BF))
    upto = lax.broadcasted_iota(jnp.int32, (SLOTS, SLOTS), 0)
    slot = lax.broadcasted_iota(jnp.int32, (SLOTS, SLOTS), 1)
    before = jnp.where(upto < slot, 1.0, 0.0).astype(BF)
    pos = jnp.where(vis > 0, dot(vis.astype(BF), before), -1.0)
    pos_o[...] = pos[0:8]
    slot = lax.broadcasted_iota(jnp.int32, (SLOTS, BAND), 0) - lax.broadcasted_iota(jnp.int32, (SLOTS, BAND), 1)
    for out, b in ((mine_o, band), (theirs_o, band ^ 1), (far_o, band ^ 3)):
        out[...] = dot(pos.astype(BF), jnp.where(slot == b * BAND, 1.0, 0.0).astype(BF))
    for i in range(IMGS):
        rows = slice(i * PACK, (i + 1) * PACK)
        tok = dot(one_hot_pack(pos, i), xs[i])
        tok_o[rows, :] = tok.astype(BF)
        z, _ = statistics(tok)
        norm_o[rows, :] = (z * par[GAIN1 : GAIN1 + 1, :] + par[BIAS1 : BIAS1 + 1, :]).astype(BF)
    normed = norm_o[...]
    packed = dot(normed, w[...])
    for m in range(3):
        part = packed[:, m * HALF : (m + 1) * HALF]
        if m != 1:
            r = QB if m == 0 else VB
            part = part + par[r : r + 1, pl.ds(heads, HALF)]
        qkv_o[m] = part.astype(BF)
    scores = []
    for i, rows, hp, cols in head_pairs():
        scores.append(dot_nt(qkv_o[1, rows, cols], two_heads(qkv_o[0, rows, cols] * BF(HD**-0.5))))
    probs = []
    for n, (i, rows, hp, cols) in enumerate(head_pairs()):
        shown = jnp.where(keys_shown(pos, i), scores[n], -1e30)
        raised = jnp.exp(shown - jnp.max(shown, axis=0, keepdims=True))
        probs.append(raised / jnp.sum(raised, axis=0, keepdims=True))
    for n, (i, rows, hp, cols) in enumerate(head_pairs()):
        probs_o[n] = probs[n]
        mixed = join_heads(dot_tn(probs[n].astype(BF), qkv_o[2, rows, cols])).astype(BF)
        mix[rows, cols] = mixed
    mix_o[...] = mix[0:SPLIT, :]
    mix2_o[...] = mix[SPLIT:ROWS, :]


def half_kernel(mix_a, mix2_a, wp, c0, c1, x_a, x_b, pos_r, one_o, pre_o, xs):
    c = lax.axis_index("band") & 1
    mine = pl.multiple_of(c * HALF, 128)
    weights = wp[pl.ds(mine, HALF), :]
    one_o[0:SPLIT, :] = dot(mix_a[...], weights)
    one_o[SPLIT:ROWS, :] = dot(mix2_a[...], weights)
    gather_bands((images(c0), images(c1), images_of_two(x_a, x_b), lambda i: jnp.zeros((BAND, D), BF)), xs)
    pos = pos_r[...]
    for i in range(IMGS):
        pre_o[i * PACK : (i + 1) * PACK, :] = dot(one_hot_pack(pos, i), xs[i])


def hidden_kernel(half, mix_b, mix2_b, tok, par, be, wp, we, after, res_o, one_o, n2_o, act_o, slope_o):
    c = lax.axis_index("band") & 1
    weights = wp[pl.ds(pl.multiple_of((1 - c) * HALF, 128), HALF), :]
    one_o[0:SPLIT, :] = half[0:SPLIT, :] + dot(mix_b[...], weights) + par[PB : PB + 1, :]
    one_o[SPLIT:ROWS, :] = half[SPLIT:ROWS, :] + dot(mix2_b[...], weights) + par[PB : PB + 1, :]
    for i in range(IMGS):
        rows = slice(i * PACK, (i + 1) * PACK)
        residual = tok[rows, :].astype(F32) + par[ASC : ASC + 1, :] * one_o[rows, :]
        res_o[rows, :] = residual
        z, _ = statistics(residual)
        n2_o[rows, :] = (z * par[GAIN2 : GAIN2 + 1, :] + par[BIAS2 : BIAS2 + 1, :]).astype(BF)
    for f in range(FH // 256):
        cols = slice(f * 256, (f + 1) * 256)
        for i in range(IMGS):
            rows = slice(i * PACK, (i + 1) * PACK)
            hidden = dot(n2_o[rows, :], we[:, cols]) + be[0:1, cols]
            phi = 0.5 * (1.0 + lax.erf(hidden * math.sqrt(0.5)))
            act_o[rows, cols] = (hidden * phi).astype(BF)
            density = jnp.exp(-0.5 * hidden * hidden) * (1.0 / math.sqrt(2.0 * math.pi))
            slope_o[rows, cols] = phi + hidden * density


def split_kernel(v, out_a, out_b):
    for i in range(IMGS):
        lo = i * BAND
        for first, out in ((0, out_a), (OWN // 2, out_b)):
            start, stop = max(lo, first), min(lo + BAND, first + OWN // 2)
            if start < stop:
                out[start - first : stop - first, :] = v[i, start - lo : stop - lo, :]


def reduce_grad_kernel(part, d_a, d_b, far_r, par, act, pre_o, gb2_o, send_o, keep_o, act_x, full):
    x, c, z, y = place()
    block = images_of_two(d_a, d_b)
    for i in range(IMGS):
        rows = slice(i * PACK, (i + 1) * PACK)
        pre = part[rows, :] + dot(one_hot_pack(far_r[...], i), block(i))
        pre_o[rows, :] = pre.astype(BF)
        gb2_o[rows, :] = (par[MSC : MSC + 1, :] * pre).astype(BF)
    for chip in range(2):

        @pl.when(x == chip)
        def _():
            for j in range(4):
                lo = 384 * j + 192 * chip
                act_x[:, 192 * j : 192 * j + 192] = act[:, lo : lo + 192]

    full[...] = dot_tn(act_x[...], gb2_o[...])
    for dy, out in ((1, send_o), (0, keep_o)):
        for dz in range(2):
            j = 2 * ((z & 1) ^ dz) + (y ^ dy)
            for to in range(2):
                at = pl.multiple_of(192 * j + 96 * to, 96)
                out[2 * dz + to] = full[pl.ds(at, 96), :].astype(BF)


def back_kernel(gb2, wr, slope, we, gh_o, left_o, right_o):
    step = 256
    for f in range(FH // step):
        cols = slice(f * step, (f + 1) * step)
        back = dot_nt(gb2[...], wr[cols, :])
        gh_o[:, cols] = (back * slope[:, cols]).astype(BF)
    gn2 = dot_nt(gh_o[...], we[...]).astype(BF)
    left_o[...] = gn2[:, :HALF]
    right_o[...] = gn2[:, HALF:]


def expand_grad_kernel(n2, gh, pick, send_o, keep_o, tick, wide):
    tick[...] = jnp.zeros_like(tick)
    picked = dot_nt(pick[...], n2[...]).astype(BF)
    wide[...] = dot(picked, gh[...])
    for low, out in ((1, send_o), (0, keep_o)):
        for i in range(4):
            lo = 192 * (i >> 1) + 48 * (low + 2 * (i & 1))
            out[i] = wide[lo : lo + 48, :].astype(BF)


QC = 3 * HALF
QW = QC + HALF
FS = FH + 2 * SMALL


def both_halves(l_a, l_b, r_a, r_b):
    left = l_a[...].astype(F32) + l_b[...].astype(F32)
    right = r_a[...].astype(F32) + r_b[...].astype(F32)
    return jnp.concatenate([left, right], axis=1)


def attention_back_kernel(
    l_a, l_b, r_a, r_b, res, pre, qkv, probs_r, mix_a, mix2_a, mix_b, mix2_b, normed, pick, pick_p, wp, par, after,
    gres_o, gp, send_o, keep_o, tick,
    flat,
):
    tick[...] = jnp.zeros_like(tick)
    c = lax.axis_index("band") & 1
    heads = pl.multiple_of(c * HALF, 128)
    gn2 = both_halves(l_a, l_b, r_a, r_b)
    z2, rstd2 = statistics(res[...])
    gres = pre[...].astype(F32) + norm_back(gn2 * par[GAIN2 : GAIN2 + 1, :], z2, rstd2)
    gres_o[...] = gres
    gb1 = (par[ASC : ASC + 1, :] * gres).astype(BF)
    gm = dot_nt(gb1, wp[pl.ds(heads, HALF), :]).astype(BF)
    grads = [two_heads(gm[rows, cols]) for i, rows, hp, cols in head_pairs()]
    gprobs = [dot_nt(qkv[2, rows, cols], grads[n]) for n, (i, rows, hp, cols) in enumerate(head_pairs())]
    gscores = []
    for n in range(9):
        product = probs_r[n] * gprobs[n]
        gscores.append((product - probs_r[n] * jnp.sum(product, axis=0, keepdims=True)).astype(BF))
    for n, (i, rows, hp, cols) in enumerate(head_pairs()):
        parts = (
            join_heads(dot_tn(gscores[n], qkv[1, rows, cols] * BF(HD**-0.5))),
            dot(gscores[n], two_heads(qkv[0, rows, cols] * BF(HD**-0.5))),
            dot(probs_r[n].astype(BF), grads[n]),
        )
        for m in range(3):
            gp[rows, m * HALF + hp * 128 : m * HALF + (hp + 1) * 128] = parts[m].astype(BF)
    others = pl.multiple_of((1 - c) * HALF, 128)
    mixed = []
    for first, second in ((mix_a, mix_b), (mix2_a, mix2_b)):
        part = dot_nt(pick_p[:, pl.ds(heads, HALF)], first[...])
        mixed.append(part + dot_nt(pick_p[:, pl.ds(others, HALF)], second[...]))
    mixed = jnp.concatenate(mixed, axis=1).astype(BF)
    pn = dot_nt(pick[...], normed[...]).astype(BF)
    proj = dot(mixed, gb1)
    flat[...] = dot(pn, gp[...])
    for dy, out in ((1, send_o), (0, keep_o)):
        for i, dz in enumerate((0, 2, 1, 3)):
            q = 4 * dy + dz
            out[i, :, 0:QC] = flat[48 * q : 48 * q + 48, :].astype(BF)
            block = proj[24 * q : 24 * q + 24]
            out[i, :, QC:QW] = jnp.concatenate([block[:, :HALF], block[:, HALF:]], axis=0).astype(BF)


def vectors_kernel(
    l_a, l_b, r_a, r_b, res, one, gres, gp, w, act, wr, gb2, gh, pre, tok, pick, par, mine, theirs, after,
    gb_keep, gb_send, send_o, keep_o, tick,
    vecs, sums,
):
    tick[...] = jnp.zeros_like(tick)
    x, c, z, y = place()
    heads = pl.multiple_of(c * HALF, 128)
    first = jnp.where(c == 0, 1.0, 0.0)

    def total(v):
        return jnp.sum(v, axis=0, keepdims=True)

    vecs[...] = jnp.zeros_like(vecs)
    gnp = dot_nt(gp[...], w[...])
    z1, _ = statistics(tok[...].astype(F32))
    vecs[GAIN1 : GAIN1 + 1, :] = total(gnp * z1)
    vecs[BIAS1 : BIAS1 + 1, :] = total(gnp)
    vecs[QB : QB + 1, pl.ds(heads, HALF)] = total(gp[:, 0:HALF].astype(F32))
    vecs[VB : VB + 1, pl.ds(heads, HALF)] = total(gp[:, 2 * HALF : 3 * HALF].astype(F32))
    gb1 = (par[ASC : ASC + 1, :] * gres[...]).astype(BF)
    vecs[PB : PB + 1, :] = first * total(gb1.astype(F32))
    vecs[ASC : ASC + 1, :] = first * total(gres[...] * one[...])
    gn2 = both_halves(l_a, l_b, r_a, r_b)
    z2, _ = statistics(res[...])
    vecs[GAIN2 : GAIN2 + 1, :] = first * total(gn2 * z2)
    vecs[BIAS2 : BIAS2 + 1, :] = first * total(gn2)
    vecs[RB : RB + 1, :] = first * total(gb2[...].astype(F32))
    two = dot(act[...], wr[...])
    for m, value in enumerate((gnp.astype(BF), two.astype(BF))):
        for i in range(IMGS):
            rows = slice(i * PACK, (i + 1) * PACK)
            for at, out in ((mine, gb_keep), (theirs, gb_send)):
                out[m, i] = dot_tn(one_hot_pack(at[...], i), value[rows]).astype(BF)
    vecs[MSC : MSC + 1, :] = total(pre[...].astype(F32) * (two + first * par[RB : RB + 1, :]))
    cols = dot_nt(pick[...], vecs[...].astype(BF))
    sums[...] = dot_tn(gh[...], jnp.ones((ROWS, SMALL), BF))
    lane = lax.broadcasted_iota(jnp.int32, (48, SMALL), 1)
    for dy, out in ((1, send_o), (0, keep_o)):
        for dz in range(4):
            b = (z ^ dz) * 2 + (y ^ dy)
            q = 4 * dy + dz
            block = cols[48 * q : 48 * q + 48]
            for k in range(4):
                at = pl.multiple_of(384 * (b & 3) + 192 * x + 48 * k, 48)
                block = jnp.where((lane == 10 + k) & ((b >> 2) == c), sums[pl.ds(at, 48), :], block)
            out[dz >> 1, :, SMALL * (dz & 1) : SMALL * (dz & 1) + SMALL] = block.astype(BF)


def own_rows(pack, value):
    high = value.astype(BF)
    return dot_tn(pack, high) + dot_tn(pack, (value - high.astype(F32)).astype(BF))


def token_grad_kernel(gb_a, gb_b, tok, gres, mine, par, after, gtok_o, tick):
    tick[...] = jnp.zeros_like(tick)
    for i in range(IMGS):
        rows = slice(i * PACK, (i + 1) * PACK)
        pack = one_hot_pack(mine[...], i)
        z1, rstd1 = statistics(tok[i * BAND : (i + 1) * BAND, :].astype(F32))
        gnp = gb_a[0, i].astype(F32) + gb_b[0, i].astype(F32)
        gtok = own_rows(pack, gres[rows, :]) + norm_back(gnp * par[GAIN1 : GAIN1 + 1, :], z1, rstd1)
        gtok_o[i] = gtok.astype(BF)


def layer_out_kernel(gb_a, gb_b, res, mine, par, after, out_o, tick):
    tick[...] = jnp.zeros_like(tick)
    for i in range(IMGS):
        rows = slice(i * PACK, (i + 1) * PACK)
        pack = one_hot_pack(mine[...], i)
        ones = dot_tn(pack, jnp.ones((PACK, D), BF))
        two = gb_a[1, i].astype(F32) + gb_b[1, i].astype(F32) + ones * par[RB : RB + 1, :]
        out_o[i] = (own_rows(pack, res[rows, :]) + par[MSC : MSC + 1, :] * two).astype(BF)


def fold(keep, arrived, keep_o, send_o):
    half = keep.shape[0] // 2
    for i in range(half):
        keep_o[i] = keep[i].astype(F32) + arrived[i].astype(F32)
        send_o[i] = (keep[half + i].astype(F32) + arrived[half + i].astype(F32)).astype(BF)


def fold_kernel(keep, arrived, after, keep_o, send_o, tick):
    tick[...] = jnp.zeros_like(tick)
    fold(keep, arrived, keep_o, send_o)


def home_kernel(keep, arrived, after, keep_o, send_o, tick):
    tick[...] = jnp.zeros_like(tick)
    for i in range(4):
        total = keep[i].astype(F32) + arrived[i].astype(F32)
        keep_o[i] = total
        send_o[i] = total.astype(BF)


def fold(keep, arrived, keep_o, send_o):
    half = keep.shape[0] // 2
    for i in range(half):
        keep_o[i] = keep[i].astype(F32) + arrived[i].astype(F32)
        send_o[i] = (keep[half + i].astype(F32) + arrived[half + i].astype(F32)).astype(BF)


def fold_kernel(keep, arrived, after, keep_o, send_o, tick):
    tick[...] = jnp.zeros_like(tick)
    fold(keep, arrived, keep_o, send_o)


def second_fold_kernel(keep, arrived, we_keep, we_arrived, after, keep_o, send_o, we_keep_o, we_send_o, tick):
    tick[...] = jnp.zeros_like(tick)
    for i in range(2):
        total = keep[i] + arrived[i].astype(F32)
        keep_o[i] = total
        send_o[i] = total.astype(BF)
    fold(we_keep, we_arrived, we_keep_o, we_send_o)


def join_kernel(keep, arrived, vec_keep, vec_send, after, keep_o, send_o, tick):
    tick[...] = jnp.zeros_like(tick)
    fold(keep, arrived, keep_o.at[:, :, 0:FH], send_o.at[:, :, 0:FH])
    keep_o[:, :, FH:FS] = vec_keep[...].astype(F32)
    send_o[:, :, FH:FS] = vec_send[...]


def part_kernel(keep, arrived, after, keep_o, send_o, vec_ko, vec_so, tick):
    tick[...] = jnp.zeros_like(tick)
    fold(keep.at[:, :, 0:FH], arrived.at[:, :, 0:FH], keep_o, send_o)
    for hi in range(2):
        total = keep[hi, :, FH:FS] + arrived[hi, :, FH:FS].astype(F32)
        vec_ko[hi] = total[:, 0:SMALL]
        vec_so[hi] = total[:, SMALL:].astype(BF)


def settle_kernel(wr_k, wr_a, we_k, we_a, after, wr_ko, wr_so, we_ko, we_so, tick, both):
    tick[...] = jnp.zeros_like(tick)
    c = lax.axis_index("band") & 1
    for at, out in ((c, wr_ko), (1 - c, wr_so)):
        out[...] = (wr_k[at] + wr_a[at].astype(F32)).astype(out.dtype)
    both[...] = we_k[0] + we_a[0].astype(F32)
    we_ko[...] = both[pl.ds(pl.multiple_of(c * 24, 8), 24), :]
    we_so[...] = both[pl.ds(pl.multiple_of(24 - c * 24, 8), 24), :].astype(BF)


USED = 16
NEAR = QC + D


def cut_kernel(keep, arrived, after, mine_o, hop_o, near_o, far_o, tick, both):
    tick[...] = jnp.zeros_like(tick)
    c = lax.axis_index("band") & 1
    mine, theirs = pl.multiple_of(c * 24, 8), pl.multiple_of(24 - c * 24, 8)
    for n, own_o, other_o in ((0, mine_o, hop_o), (1, near_o, far_o)):
        both[...] = keep[n].astype(F32) + arrived[n].astype(F32)
        own_o[:, 0:QC] = both[pl.ds(mine, 24), 0:QC].astype(own_o.dtype)
        other_o[...] = both[pl.ds(theirs, 24), 0:QC].astype(own_o.dtype)
        own_o[:, QC : QC + HALF] = both[0:24, QC:QW].astype(own_o.dtype)
        own_o[:, QC + HALF :] = both[24:48, QC:QW].astype(own_o.dtype)


def cores_kernel(vec_a, vec_b, hop, after, keep_o, send_o, other_o, tick):
    tick[...] = jnp.zeros_like(tick)
    keep_o[...] = jnp.zeros_like(keep_o)
    keep_o[:, 0:USED] = vec_a[0, :, 0:USED] + vec_b[0].astype(F32)
    send_o[...] = (vec_a[1, :, 0:USED] + vec_b[1].astype(F32)).astype(BF)
    other_o[...] = hop[...]


def vector_fold_kernel(keep, arrived, after, out, send_o, tick):
    tick[...] = jnp.zeros_like(tick)
    total = keep[...] + arrived[...].astype(F32)
    out[...] = total
    send_o[...] = total[:, :, 0:USED].astype(BF)


def total_kernel(mine, near, hop, far, vec_k, vec_a, after, own_o, other_o, vec_o, tick):
    tick[...] = jnp.zeros_like(tick)
    own_o[...] = mine[...] + near[...].astype(F32)
    other_o[...] = hop[...] + far[...].astype(F32)
    vec_o[...] = vec_k[...]
    vec_o[:, 0:USED] = vec_k[:, 0:USED] + vec_a[...].astype(F32)


def out_kernel(
    own, other, vec_r, we_keep, we_arrived, wr_keep, wr_arrived, after,
    qkv_o, first_o, bias_o, qv_o, bp_o, asc_o, gain2_o, bias2_o, br_o, msc_o, eb_o, proj_o, we_o, wr_o,
):
    _, c, z, _ = place()
    wr_o[...] = jnp.where((z >> 1) == c, wr_keep[...], wr_arrived[...].astype(F32))
    we_o[:, pl.ds(pl.multiple_of(c * FH, 128), FH)] = we_keep[...]
    we_o[:, pl.ds(pl.multiple_of((1 - c) * FH, 128), FH)] = we_arrived[...].astype(F32)
    proj_o[...] = own[:, QC:NEAR]
    for m in range(3):
        cols = slice(m * HALF, (m + 1) * HALF)
        qkv_o[:, pl.ds(pl.multiple_of(m * D + c * HALF, 128), HALF)] = own[:, cols]
        qkv_o[:, pl.ds(pl.multiple_of(m * D + (1 - c) * HALF, 128), HALF)] = other[:, cols]
    vec = vec_r[pl.ds(pl.multiple_of(c * 24, 8), 24), :].T
    outs = (first_o, bias_o, None, None, bp_o, asc_o, gain2_o, bias2_o, br_o, msc_o)
    for r, out in enumerate(outs):
        if out is not None:
            out[...] = vec[r]
    qv_o[...] = vec[2:4]
    units = vec_r[...].T
    units = jnp.where(c == 0, units[10:12], units[12:14])
    eb_o[...] = jnp.concatenate([units[0:1], units[1:2]], axis=1).reshape(96)


COSTS = {
    "vectors_kernel": (8000000000, 20000000),
    "second_fold_kernel": (0, 2000000),
    "last_kernel": (0, 1000000),
    "spread_kernel": (0, 2000000),
    "finish_kernel": (0, 1000000),
    "out_kernel": (0, 1000000),
    "prepare_kernel": (0, 9000000),
    "total_kernel": (4000000000, 0),
}


def call(kernel, outs, specs, scratch=(), vmem=24, cost=0):
    return pl.pallas_call(
        kernel,
        out_shape=outs,
        in_specs=specs,
        out_specs=jax.tree.map(lambda _: VM, outs),
        scratch_shapes=list(scratch),
        compiler_params=pltpu.CompilerParams(vmem_limit_bytes=vmem * MIB),
        cost_estimate=pl.CostEstimate(flops=COSTS.get(kernel.__name__, (0, 0))[0] + cost, bytes_accessed=COSTS.get(kernel.__name__, (0, 0))[1], transcendentals=0),
    )


def fold_call(keep, arrived, after, cost=0):
    half = (keep.shape[0] // 2, *keep.shape[1:])
    return call(fold_kernel, (vm(half, F32), vm(half, BF), TICK), [VM] * 2 + [ANY], cost=cost)(keep, arrived, after)


def by_core(value):
    return lax.ppermute(value, "band", [(i, i ^ 1) for i in range(4)])


def by_x(value):
    return lax.ppermute(value, "band", [(i, i ^ 2) for i in range(4)])


def by_y(value):
    return lax.ppermute(value, "batch", [(i, i ^ 1) for i in range(8)])


def by_z(value, dz):
    return lax.ppermute(value, "batch", [(i, i ^ (2 * dz)) for i in range(8)])


def across(value):
    return lax.ppermute(value, ("batch", "band"), [(d, d ^ 17) for d in range(32)])


def homeward(value, dz):
    pairs = [(d, d ^ (8 * dz)) for d in range(32) if ((d ^ (8 * dz)) >> 4) == (d & 1)]
    return lax.ppermute(value, ("batch", "band"), pairs)


def packed_body(
    tokens, cotangent, visible, first_gain, first_bias, qkv_weight, qv_bias, proj_weight, proj_bias,
    attn_scale, second_gain, second_bias, expand_weight, expand_bias, reduce_weight, reduce_bias, mlp_scale,
):
    block = vm(cotangent.shape, BF)
    rows_f, rows_b = vm((ROWS, D), F32), vm((ROWS, D), BF)
    tok_x = by_x(tokens)
    tok_block = vm((OWN + 16, D), BF)
    cot, tok_own, par, be, wqkv, wp, we, wr, vis, pick, pick_p = call(
        prepare_kernel,
        (
            block,
            tok_block,
            vm((16, D), F32),
            vm((8, FH), F32),
            vm((D, QC), BF),
            vm((D, D), BF),
            vm((D, FH), BF),
            vm((FH, D), BF),
            vm((16, D), BF),
            vm((HALF, D), BF),
            vm((192, D), BF),
        ),
        [ANY] * 17,
        [pltpu.VMEM(visible.shape, jnp.int32), pltpu.SemaphoreType.DMA((22,))],
    )(
        *map(
            stay,
            (
                cotangent, first_gain, first_bias, qv_bias, proj_bias, attn_scale, second_gain, second_bias,
                reduce_bias, mlp_scale, expand_bias, qkv_weight, proj_weight, expand_weight, reduce_weight, visible,
                tokens,
            ),
        )
    )
    vis_x = by_x(vis)
    tok_c = by_core(tok_own)
    cot_c = by_core(cot)
    parts = (vm((EARLY, D), BF), vm((OWN + 16 - EARLY, D), BF))
    tok_x = call(hold_kernel, parts, [VM] * 2 + [ANY])(tok_x, vis_x, par)
    tok_d = [by_core(v) for v in tok_x]
    cot_x = call(split_kernel, (vm((OWN // 2, D), BF),) * 2, [VM])(by_x(cot))
    cot_d = [by_core(v) for v in cot_x]
    tok, normed, qkv, mix_own, mix2_own, pos, probs, pos_mine, pos_theirs, pos_far = call(
        first_kernel,
        (
            rows_b,
            rows_b,
            vm((3, ROWS, HALF), BF),
            vm((SPLIT, HALF), BF),
            vm((ROWS - SPLIT, HALF), BF),
            vm((8, SLOTS), F32),
            vm((9, PACK, 2 * PACK), F32),
            vm((16, BAND), F32),
            vm((16, BAND), F32),
            vm((16, BAND), F32),
        ),
        [VM] * 8,
        [pltpu.VMEM((IMGS, SLOTS, D), BF), pltpu.VMEM((ROWS, HALF), BF)],
    )(tok_own, tok_c, *tok_x, *tok_d, par, wqkv)
    mix_other, mix2_other = by_core(mix_own), by_core(mix2_own)
    half_one, half_pre = call(
        half_kernel, (rows_f, rows_f), [VM] * 8, [pltpu.VMEM((IMGS, SLOTS, D), BF)]
    )(mix_own, mix2_own, wp, cot, cot_c, *cot_x, pos)
    res, one, n2, act, slope = call(
        hidden_kernel,
        (rows_f, rows_f, rows_b, vm((ROWS, FH), BF), vm((ROWS, FH), F32)),
        [VM] * 8 + [ANY],
    )(half_one, mix_other, mix2_other, tok, par, be, wp, we, pick)
    pre, gb2, wr_send, wr_keep = call(
        reduce_grad_kernel,
        (rows_b, rows_b, vm((4, 96, D), BF), vm((4, 96, D), BF)),
        [VM] * 6,
        [pltpu.VMEM((ROWS, D), BF), pltpu.VMEM((D, D), F32)],
    )(half_pre, *cot_d, pos_far, par, act)
    wr_y = by_y(wr_send)
    half_b = vm((ROWS, HALF), BF)
    gh, left, right = call(back_kernel, (vm((ROWS, FH), BF), half_b, half_b), [VM] * 4)(gb2, wr, slope, we)
    gn2 = (left, by_core(left), right, by_core(right))
    we_send, we_keep, tick = call(
        expand_grad_kernel,
        (vm((4, 48, FH), BF), vm((4, 48, FH), BF), TICK),
        [VM] * 3,
        [pltpu.VMEM((HALF, FH), F32)],
    )(n2, gh, pick)
    we_z = by_z(we_send, 1)
    gres, gp, qp_send, qp_keep, tick = call(
        attention_back_kernel,
        (rows_f, vm((ROWS, QC), BF), vm((4, 48, QW), BF), vm((4, 48, QW), BF), TICK),
        [VM] * 17 + [ANY],
        [pltpu.VMEM((HALF, QC), F32)],
    )(*gn2, res, pre, qkv, probs, mix_own, mix2_own, mix_other, mix2_other, normed, pick, pick_p, wp, par, tick)
    qp_y = by_y(qp_send)
    wr_keep, wr_send, tick = call(
        home_kernel, (vm((4, 96, D), F32), vm((4, 96, D), BF), TICK), [VM] * 2 + [ANY]
    )(wr_keep, wr_y, tick)
    wr_z = homeward(wr_send, 2)
    gb_keep, gb_send, vec_send, vec_keep, tick = call(
        vectors_kernel,
        (vm((2, *tokens.shape), BF), vm((2, *tokens.shape), BF), vm((2, 48, 2 * SMALL), BF), vm((2, 48, 2 * SMALL), BF), TICK),
        [VM] * 19 + [ANY],
        [pltpu.VMEM((SMALL, D), F32), pltpu.VMEM((FH, SMALL), F32)],
    )(*gn2, res, one, gres, gp, wqkv, act, wr, gb2, gh, pre, tok, pick, par, pos_mine, pos_theirs, tick)
    gb_other = by_core(gb_send)
    we_keep, we_send, tick = call(
        join_kernel, (vm((2, 48, FS), F32), vm((2, 48, FS), BF), TICK), [VM] * 4 + [ANY]
    )(we_keep, we_z, vec_keep, vec_send, tick)
    we_y = by_y(we_send)
    qp_keep, qp_send, tick = fold_call(qp_keep, qp_y, tick, cost=0)
    qp_z = by_z(qp_send, 1)
    wr_keep, wr_send, tick = fold_call(wr_keep, wr_z, tick, cost=0)
    wr_z = homeward(wr_send, 1)
    we_keep, we_send, vec_keep, vec_send, tick = call(
        part_kernel,
        (vm((1, 48, FH), F32), vm((1, 48, FH), BF), vm((2, 48, SMALL), F32), vm((2, 48, SMALL), BF), TICK),
        [VM] * 2 + [ANY],
    )(we_keep, we_y, tick)
    vec_z = by_z(vec_send, 1)
    we_z = by_z(we_send, 2)
    mine, hop, near, far, tick = call(
        cut_kernel,
        (vm((24, NEAR), F32), vm((24, QC), F32), vm((24, NEAR), BF), vm((24, QC), BF), TICK),
        [VM] * 2 + [ANY],
        [pltpu.VMEM((48, QW), F32)],
        cost=0,
    )(qp_keep, qp_z, tick)
    near, far, hop = by_z(near, 2), across(far), by_core(hop)
    vec, vec_send, tick = call(
        vector_fold_kernel, (vm((2, 48, SMALL), F32), vm((2, 48, USED), BF), TICK), [VM] * 2 + [ANY], cost=4000000000
    )(vec_keep, vec_z, tick)
    vec_other = by_core(vec_send)
    layer_out, tick = call(layer_out_kernel, (sds(tokens.shape, BF), TICK), [VM] * 5 + [ANY])(
        gb_keep, gb_other, res, pos_mine, par, tick
    )
    vec_keep, vec_send, hop, tick = call(
        cores_kernel,
        (vm((48, SMALL), F32), vm((48, USED), BF), vm((24, QC), F32), TICK),
        [VM] * 3 + [ANY],
    )(vec, vec_other, hop, tick)
    vec_z = by_z(vec_send, 2)
    grad_tokens, tick = call(token_grad_kernel, (sds(tokens.shape, BF), TICK), [VM] * 6 + [ANY])(
        gb_keep, gb_other, tok_own, gres, pos_mine, par, tick
    )
    wr_keep, wr_send, we_keep, we_send, tick = call(
        settle_kernel,
        (vm((96, D), F32), vm((96, D), BF), vm((24, FH), F32), vm((24, FH), BF), TICK),
        [VM] * 4 + [ANY],
        [pltpu.VMEM((48, FH), F32)],
    )(wr_keep, wr_z, we_keep, we_z, tick)
    we_other, wr_other = by_core(we_send), by_core(wr_send)
    own, other, vec, tick = call(
        total_kernel,
        (vm((24, NEAR), F32), vm((24, QC), F32), vm((48, SMALL), F32), TICK),
        [VM] * 6 + [ANY],
    )(mine, near, hop, far, vec_keep, vec_z, tick)
    vector = sds((24,), F32)
    grad_qkv, gg1, gb1, gqv, gbp, gas, gg2, gb2, gbr, gms, geb, grad_proj, grad_expand, grad_reduce = call(
        out_kernel,
        (
            sds((24, 3 * D), F32), vector, vector, sds((2, 24), F32), vector, vector, vector, vector, vector, vector,
            sds((96,), F32), sds((24, D), F32), sds((24, FF), F32), sds((96, D), F32),
        ),
        [VM] * 7 + [ANY],
    )(own, other, vec, we_keep, we_other, wr_keep, wr_other, tick)
    return (
        layer_out, grad_tokens, gg1, gb1, grad_qkv, gqv, grad_proj, gbp, gas, gg2, gb2, grad_expand, geb, grad_reduce,
        gbr, gms,
    )


def layer_norm(values, norm_gain, norm_shift):
    center = values - jnp.mean(values, axis=-1, keepdims=True)
    spread = jnp.mean(center * center, axis=-1, keepdims=True)
    return center * lax.rsqrt(spread + NORM_EPS) * norm_gain + norm_shift


def gelu_exact(values):
    return jax.nn.gelu(values, approximate=False)


def split_rows(packed_rows, mask_rows):
    item_count = packed_rows.shape[0]
    slot_count = packed_rows.shape[1]
    heads_here = packed_rows.shape[4] // HD
    unpacked = packed_rows.reshape(item_count, slot_count, 3, heads_here, HD)
    queries = unpacked[:, :, 0]
    key_rows = unpacked[:, :, 1]
    value_rows = unpacked[:, :, 2]
    key_valid = mask_rows.reshape(item_count, slot_count) > 0
    score_scale = 1.0 / math.sqrt(HD)
    scores = (
        jnp.einsum("bqhe,bkhe->bhqk", queries, key_rows, preferred_element_type=jnp.float32)
        * score_scale
    )
    scores = jnp.where(key_valid[:, None, None, :], scores, -1e30)
    return (queries, key_rows, value_rows, scores)


def attend_plain(inputs):
    packed_rows, mask_rows = inputs
    queries, key_rows, value_rows, scores = split_rows(packed_rows, mask_rows)
    row_top = jnp.max(scores, axis=-1, keepdims=True)
    raised = jnp.exp(scores - row_top)
    row_total = jnp.sum(raised, axis=-1, keepdims=True)
    attn_prob = raised / row_total
    log_total = (row_top + jnp.log(row_total))[..., 0]
    mixed_rows = jnp.einsum(
        "bhqk,bkhe->bqhe",
        attn_prob.astype(jnp.bfloat16),
        value_rows,
        preferred_element_type=jnp.float32,
    ).astype(jnp.bfloat16)
    mixed_rows = mixed_rows.reshape(
        packed_rows.shape[0], packed_rows.shape[1], packed_rows.shape[4]
    )
    return (mixed_rows, log_total)


def backward_rows(score_parts, log_total, grad_rows):
    queries, key_rows, value_rows, scores = score_parts
    item_count, slot_count, heads_here, head_size = queries.shape
    score_scale = 1.0 / math.sqrt(HD)
    attn_prob = jnp.exp(scores - log_total[..., None])
    grad_heads = grad_rows.reshape(item_count, slot_count, heads_here, head_size)
    grad_prob = jnp.einsum(
        "bqhe,bkhe->bhqk", grad_heads, value_rows, preferred_element_type=jnp.float32
    )
    row_delta = jnp.sum(attn_prob * grad_prob, axis=-1, keepdims=True)
    grad_score = (attn_prob * (grad_prob - row_delta)).astype(jnp.bfloat16)
    grad_query = (
        jnp.einsum("bhqk,bkhe->bqhe", grad_score, key_rows, preferred_element_type=jnp.float32)
        * score_scale
    )
    grad_key = (
        jnp.einsum("bhqk,bqhe->bkhe", grad_score, queries, preferred_element_type=jnp.float32)
        * score_scale
    )
    grad_value = jnp.einsum(
        "bhqk,bqhe->bkhe",
        attn_prob.astype(jnp.bfloat16),
        grad_heads,
        preferred_element_type=jnp.float32,
    )
    stacked = jnp.stack([grad_query, grad_key, grad_value], axis=2)
    return stacked.reshape(item_count, slot_count, 3, 1, heads_here * head_size).astype(
        jnp.bfloat16
    )


def attend_again(inputs):
    packed_rows, mask_rows, grad_rows = inputs
    score_parts = split_rows(packed_rows, mask_rows)
    scores = score_parts[3]
    row_top = jnp.max(scores, axis=-1, keepdims=True)
    log_total = (row_top + jnp.log(jnp.sum(jnp.exp(scores - row_top), axis=-1, keepdims=True)))[
        ..., 0
    ]
    return backward_rows(score_parts, log_total, grad_rows)


def body(
    tokens,
    cotangent,
    visible,
    first_gain,
    first_bias,
    qkv_weight,
    qv_bias,
    proj_weight,
    proj_bias,
    attn_scale,
    second_gain,
    second_bias,
    expand_weight,
    expand_bias,
    reduce_weight,
    reduce_bias,
    mlp_scale,
):
    images, slot_count, model_width = tokens.shape
    groups = lax.axis_size("band")
    local_width = model_width // groups
    inputs_full = tokens.astype(jnp.float32)
    shown_mask = visible.astype(jnp.float32)
    normed, first_pull = jax.vjp(layer_norm, inputs_full, first_gain, first_bias)
    normed_low = normed.astype(jnp.bfloat16)
    qkv_bias = jnp.concatenate([qv_bias[0], jnp.zeros((model_width,), jnp.float32), qv_bias[1]])

    def project_qkv():
        product = jnp.einsum(
            "isd,de->ise", normed_low, qkv_weight, preferred_element_type=jnp.float32
        )
        return (
            (product + qkv_bias)
            .astype(jnp.bfloat16)
            .reshape(images, slot_count, 3, groups, local_width)
        )

    packed = project_qkv()
    mask_part = jnp.broadcast_to(
        shown_mask.astype(jnp.bfloat16)[:, :, None, None, None], (images, slot_count, 1, groups, 1)
    )
    results = attend_plain(
        (
            lax.all_to_all(packed, "band", split_axis=3, concat_axis=1, tiled=True),
            lax.all_to_all(mask_part, "band", split_axis=3, concat_axis=1, tiled=True),
        )
    )
    mixed_heads = results[0].reshape(images, groups * slot_count, 1, local_width)
    back_rows = lax.all_to_all(mixed_heads, "band", split_axis=1, concat_axis=2, tiled=True)
    mixed_rows = back_rows.reshape(images, slot_count, model_width)
    branch_one = (
        jnp.einsum("isd,de->ise", mixed_rows, proj_weight, preferred_element_type=jnp.float32)
        + proj_bias
    )
    residual = inputs_full + attn_scale * branch_one
    normed_two, second_pull = jax.vjp(layer_norm, residual, second_gain, second_bias)
    normed_two_low = normed_two.astype(jnp.bfloat16)
    hidden = (
        jnp.einsum("isd,df->isf", normed_two_low, expand_weight, preferred_element_type=jnp.float32)
        + expand_bias
    )
    activated, gelu_pull = jax.vjp(gelu_exact, hidden)
    activated_low = activated.astype(jnp.bfloat16)
    branch_two = (
        jnp.einsum("isf,fd->isd", activated_low, reduce_weight, preferred_element_type=jnp.float32)
        + reduce_bias
    )
    layer_out = (shown_mask[..., None] * (residual + mlp_scale * branch_two)).astype(jnp.bfloat16)
    grad_pre = shown_mask[..., None] * cotangent.astype(jnp.float32)
    grad_mlp_scale = jnp.sum(grad_pre * branch_two, axis=(0, 1))
    grad_branch_two = (mlp_scale * grad_pre).astype(jnp.bfloat16)
    grad_reduce_weight = jnp.einsum(
        "isf,isd->fd", activated_low, grad_branch_two, preferred_element_type=jnp.float32
    )
    grad_reduce_bias = jnp.sum(grad_branch_two.astype(jnp.float32), axis=(0, 1))
    grad_activated = jnp.einsum(
        "isd,fd->isf", grad_branch_two, reduce_weight, preferred_element_type=jnp.float32
    )
    grad_hidden = gelu_pull(grad_activated)[0].astype(jnp.bfloat16)
    grad_expand_weight = jnp.einsum(
        "isd,isf->df", normed_two_low, grad_hidden, preferred_element_type=jnp.float32
    )
    grad_expand_bias = jnp.sum(grad_hidden.astype(jnp.float32), axis=(0, 1))
    grad_normed_two = jnp.einsum(
        "isf,df->isd", grad_hidden, expand_weight, preferred_element_type=jnp.float32
    )
    grad_resid_norm, grad_second_gain, grad_second_bias = second_pull(grad_normed_two)
    grad_residual = grad_pre + grad_resid_norm
    grad_attn_scale = jnp.sum(grad_residual * branch_one, axis=(0, 1))
    grad_branch_one = (attn_scale * grad_residual).astype(jnp.bfloat16)
    grad_proj_weight = jnp.einsum(
        "isd,ise->de", mixed_rows, grad_branch_one, preferred_element_type=jnp.float32
    )
    grad_proj_bias = jnp.sum(grad_branch_one.astype(jnp.float32), axis=(0, 1))
    grad_mixed = jnp.einsum(
        "ise,de->isd", grad_branch_one, proj_weight, preferred_element_type=jnp.float32
    )
    grad_mixed = grad_mixed.astype(jnp.bfloat16).reshape(images, slot_count, 1, groups, local_width)
    repacked = project_qkv()
    grad_packed = attend_again(
        (
            lax.all_to_all(repacked, "band", split_axis=3, concat_axis=1, tiled=True),
            lax.all_to_all(mask_part, "band", split_axis=3, concat_axis=1, tiled=True),
            lax.all_to_all(grad_mixed, "band", split_axis=3, concat_axis=1, tiled=True),
        )
    )
    grad_bands = lax.all_to_all(grad_packed, "band", split_axis=1, concat_axis=3, tiled=True)
    grad_qkv = grad_bands.reshape(images, slot_count, 3 * model_width)
    grad_qkv_weight = jnp.einsum(
        "isd,ise->de", normed_low, grad_qkv, preferred_element_type=jnp.float32
    )
    column_sums = jnp.sum(grad_qkv.astype(jnp.float32), axis=(0, 1))
    grad_qv_bias = jnp.stack([column_sums[:model_width], column_sums[2 * model_width :]])
    grad_normed = jnp.einsum(
        "ise,de->isd", grad_qkv, qkv_weight, preferred_element_type=jnp.float32
    )
    grad_input_norm, grad_first_gain, grad_first_bias = first_pull(grad_normed)
    grad_tokens = (grad_residual + grad_input_norm).astype(jnp.bfloat16)
    all_sums = (
        lax.psum_scatter(grad_first_gain, ("batch", "band"), scatter_dimension=0, tiled=True),
        lax.psum_scatter(grad_first_bias, ("batch", "band"), scatter_dimension=0, tiled=True),
        lax.psum_scatter(grad_qkv_weight, ("batch", "band"), scatter_dimension=0, tiled=True),
        lax.psum_scatter(grad_qv_bias, ("batch", "band"), scatter_dimension=1, tiled=True),
        lax.psum_scatter(grad_proj_weight, ("batch", "band"), scatter_dimension=0, tiled=True),
        lax.psum_scatter(grad_proj_bias, ("batch", "band"), scatter_dimension=0, tiled=True),
        lax.psum_scatter(grad_attn_scale, ("batch", "band"), scatter_dimension=0, tiled=True),
        lax.psum_scatter(grad_second_gain, ("batch", "band"), scatter_dimension=0, tiled=True),
        lax.psum_scatter(grad_second_bias, ("batch", "band"), scatter_dimension=0, tiled=True),
        lax.psum_scatter(grad_expand_weight, ("batch", "band"), scatter_dimension=0, tiled=True),
        lax.psum_scatter(grad_expand_bias, ("batch", "band"), scatter_dimension=0, tiled=True),
        lax.psum_scatter(grad_reduce_weight, ("batch", "band"), scatter_dimension=0, tiled=True),
        lax.psum_scatter(grad_reduce_bias, ("batch", "band"), scatter_dimension=0, tiled=True),
        lax.psum_scatter(grad_mlp_scale, ("batch", "band"), scatter_dimension=0, tiled=True),
    )
    (
        sum_first_gain,
        sum_first_bias,
        sum_qkv_weight,
        sum_qv_bias,
        sum_proj_weight,
        sum_proj_bias,
        sum_attn_scale,
        sum_second_gain,
        sum_second_bias,
        sum_expand_weight,
        sum_expand_bias,
        sum_reduce_weight,
        sum_reduce_bias,
        sum_mlp_scale,
    ) = all_sums
    return (
        layer_out,
        grad_tokens,
        sum_first_gain,
        sum_first_bias,
        sum_qkv_weight,
        sum_qv_bias,
        sum_proj_weight,
        sum_proj_bias,
        sum_attn_scale,
        sum_second_gain,
        sum_second_bias,
        sum_expand_weight,
        sum_expand_bias,
        sum_reduce_weight,
        sum_reduce_bias,
        sum_mlp_scale,
    )


def solution(mesh):
    sizes = dict(mesh.shape)
    chosen = packed_body if (sizes["batch"], sizes["band"]) == (8, 4) else body
    placed = (
        P("batch", "band", None),
        P("batch", "band", None),
        P("batch", "band"),
        P(),
        P(),
        P(),
        P(),
        P(),
        P(),
        P(),
        P(),
        P(),
        P(),
        P(),
        P(),
        P(),
        P(),
    )
    return jax.shard_map(
        chosen,
        mesh=mesh,
        in_specs=placed,
        out_specs=(
            P("batch", "band", None),
            P("batch", "band", None),
            P(("batch", "band")),
            P(("batch", "band")),
            P(("batch", "band"), None),
            P(None, ("batch", "band")),
            P(("batch", "band"), None),
            P(("batch", "band")),
            P(("batch", "band")),
            P(("batch", "band")),
            P(("batch", "band")),
            P(("batch", "band"), None),
            P(("batch", "band")),
            P(("batch", "band"), None),
            P(("batch", "band")),
            P(("batch", "band")),
        ),
        check_vma=False,
    )
```

```python
import math

import jax
import jax.numpy as jnp
from jax import lax
from jax.experimental import pallas as pl
from jax.experimental.pallas import tpu as pltpu
from jax.sharding import PartitionSpec as P

HD = 64
NORM_EPS = 1e-06
PACK = 144
SLOTS = 256
BAND = 64
IMGS = 3
ROWS = IMGS * PACK
D = 768
HALF = D // 2
FF = 3072
FH = FF // 2
SMALL = 128
MIB = 1024 * 1024
F32 = jnp.float32
BF = jnp.bfloat16
ANY = pl.BlockSpec(memory_space=pl.ANY)
HBM = pl.BlockSpec(memory_space=pltpu.HBM)
VM = pl.BlockSpec(memory_space=pltpu.VMEM)


def dot(a, b):
    return jnp.dot(a, b, preferred_element_type=F32)


def dot_nt(a, b):
    return lax.dot_general(a, b, (((1,), (1,)), ((), ())), preferred_element_type=F32)


def dot_tn(a, b):
    return lax.dot_general(a, b, (((0,), (0,)), ((), ())), preferred_element_type=F32)


def sds(shape, dtype):
    return jax.ShapeDtypeStruct(shape, dtype)


def vm(shape, dtype):
    return pltpu.VMEM(shape, dtype)


def stay(value):
    return pltpu.with_memory_space_constraint(value, pltpu.HBM)


def place():
    band = lax.axis_index("band")
    batch = lax.axis_index("batch")
    return band >> 1, band & 1, batch >> 1, batch & 1


def one_hot_pack(pos, image):
    rows = lax.broadcasted_iota(jnp.int32, (PACK, pos.shape[1]), 0).astype(F32)
    return jnp.where(rows == pos[image : image + 1, :], 1.0, 0.0).astype(BF)


def shard_picks():
    x, c, z, y = place()

    def pick(width, base):
        row = lax.broadcasted_iota(jnp.int32, (8 * width, 1), 0)
        want = jnp.zeros((8 * width, 1), jnp.int32)
        for q in range(8):
            first = 96 * ((z ^ (q % 4)) * 2 + (y ^ (q // 4))) + base - width * q
            want = jnp.where((row >= width * q) & (row < width * (q + 1)), row + first, want)
        lane = lax.broadcasted_iota(jnp.int32, (8 * width, D), 1)
        return jnp.where(lane == want, 1.0, 0.0).astype(BF)

    return pick(48, 48 * x), pick(24, 48 * x + 24 * c)


def statistics(values):
    center = values - jnp.mean(values, axis=-1, keepdims=True)
    rstd = lax.rsqrt(jnp.mean(center * center, axis=-1, keepdims=True) + NORM_EPS)
    return center * rstd, rstd


def norm_back(grad, z, rstd):
    return rstd * (
        grad
        - jnp.mean(grad, axis=-1, keepdims=True)
        - z * jnp.mean(grad * z, axis=-1, keepdims=True)
    )


def gather_bands(blocks, dst):
    band = lax.axis_index("band")
    for k, block in enumerate(blocks):
        at = pl.multiple_of((band ^ k) * BAND, BAND)
        for i in range(IMGS):
            dst[i, pl.ds(at, BAND), :] = block(i)


def images(ref):
    return lambda i: ref[i] if len(ref.shape) == 3 else ref[i * BAND : (i + 1) * BAND, :]


def images_of_two(a, b):
    count = a.shape[0]

    def block(i):
        lo, hi = i * BAND, (i + 1) * BAND
        parts = [a[lo : min(hi, count), :]] if lo < count else []
        parts += [b[max(lo, count) - count : hi - count, :]] if hi > count else []
        return parts[0] if len(parts) == 1 else jnp.concatenate(parts, axis=0)

    return block


def two_heads(v):
    lane = lax.broadcasted_iota(jnp.int32, v.shape, 1)
    none = jnp.zeros_like(v)
    return jnp.concatenate([jnp.where(lane < HD, v, none), jnp.where(lane < HD, none, v)], axis=0)


def join_heads(v):
    lane = lax.broadcasted_iota(jnp.int32, (PACK, 128), 1)
    return jnp.where(lane < HD, v[:PACK], v[PACK:])


def head_pairs():
    for i in range(IMGS):
        for hp in range(3):
            yield i, slice(i * PACK, (i + 1) * PACK), hp, slice(hp * 128, (hp + 1) * 128)


def keys_shown(pos, image):
    shown = jnp.sum(jnp.where(pos[image : image + 1, :] >= 0, 1.0, 0.0), axis=-1, keepdims=True)
    return lax.broadcasted_iota(jnp.int32, (PACK, 1), 0).astype(F32) < shown


TICK = vm((8, 128), F32)
GAIN1, BIAS1, QB, VB, PB, ASC, GAIN2, BIAS2, RB, MSC = range(10)


OWN = IMGS * BAND


def prepare_kernel(
    cot, gain1, bias1, qvb, bp, asc, gain2, bias2, br, msc, be, wqkv, wp, we, wr, visible, tok,
    cot_o, own_o, par_o, be_o, wqkv_o, wp_o, we_o, wr_o, vis_o, pick_o, pick_p_o,
    vis, sems,
):
    c = lax.axis_index("band") & 1
    units = pl.multiple_of(c * FH, 128)
    rows = (
        (GAIN1, gain1), (BIAS1, bias1), (QB, qvb.at[0]), (VB, qvb.at[1]), (PB, bp), (ASC, asc),
        (GAIN2, gain2), (BIAS2, bias2), (RB, br), (MSC, msc),
    )
    moves = [(cot, cot_o)] + [(v, par_o.at[r]) for r, v in rows]
    moves += [(be.at[pl.ds(units, FH)], be_o.at[0])]
    for m in range(3):
        src = wqkv.at[:, pl.ds(pl.multiple_of(m * D + c * HALF, 128), HALF)]
        moves.append((src, wqkv_o.at[:, pl.ds(m * HALF, HALF)]))
    moves += [(wp, wp_o), (we.at[:, pl.ds(units, FH)], we_o), (wr.at[pl.ds(units, FH), :], wr_o)]
    moves += [(tok.at[i], own_o.at[pl.ds(i * BAND, BAND), :]) for i in range(IMGS)]
    moves += [(visible, vis)]
    copies = [pltpu.make_async_copy(a, b, sems.at[i]) for i, (a, b) in enumerate(moves)]
    for copy in copies:
        copy.start()
    copies[-1].wait()
    seen = jnp.concatenate([vis[...].astype(F32), jnp.zeros((IMGS, 128 - BAND), F32)], axis=1)
    seen = jnp.concatenate([seen, jnp.zeros((16 - IMGS, 128), F32)], axis=0).astype(BF)
    vis_o[...] = jnp.zeros((16, D), BF)
    vis_o[:, 0:128] = seen
    own_o[OWN:, :] = jnp.zeros((16, D), BF)
    own_o[OWN:, 0:128] = seen
    pick_o[...], pick_p_o[...] = shard_picks()
    for copy in copies[:-1]:
        copy.wait()


SPLIT = 224
EARLY = 160


def hold_kernel(tok, vis, after, out, rest):
    count = out.shape[0]
    for i in range(IMGS):
        lo, hi = i * BAND, (i + 1) * BAND
        if lo < count:
            out[lo : min(hi, count), :] = tok[i, 0 : min(hi, count) - lo, :]
        if hi > count:
            rest[max(lo, count) - count : hi - count, :] = tok[i, max(lo, count) - lo :, :]
    rest[OWN - count :, :] = vis[...]


def first_kernel(
    t0, t1, x_a, x_b, d_a, d_b, par, w,
    tok_o, norm_o, qkv_o, mix_o, mix2_o, pos_o, probs_o, mine_o, theirs_o, far_o,
    xs, mix,
):
    band = lax.axis_index("band")
    c = band & 1
    gather_bands((images(t0), images(t1), images_of_two(x_a, x_b), images_of_two(d_a, d_b)), xs)
    heads = pl.multiple_of(c * HALF, 128)
    to = lax.broadcasted_iota(jnp.int32, (BAND, SLOTS), 1) - lax.broadcasted_iota(jnp.int32, (BAND, SLOTS), 0)
    vis = jnp.zeros((16, SLOTS), F32)
    for k, t in enumerate((t0, t1, x_b, d_b)):
        vis = vis + dot(t[t.shape[0] - 16 :, 0:BAND], jnp.where(to == (band ^ k) * BAND, 1.0, 0.0).astype(BF))
    upto = lax.broadcasted_iota(jnp.int32, (SLOTS, SLOTS), 0)
    slot = lax.broadcasted_iota(jnp.int32, (SLOTS, SLOTS), 1)
    before = jnp.where(upto < slot, 1.0, 0.0).astype(BF)
    pos = jnp.where(vis > 0, dot(vis.astype(BF), before), -1.0)
    pos_o[...] = pos[0:8]
    slot = lax.broadcasted_iota(jnp.int32, (SLOTS, BAND), 0) - lax.broadcasted_iota(jnp.int32, (SLOTS, BAND), 1)
    for out, b in ((mine_o, band), (theirs_o, band ^ 1), (far_o, band ^ 3)):
        out[...] = dot(pos.astype(BF), jnp.where(slot == b * BAND, 1.0, 0.0).astype(BF))
    for i in range(IMGS):
        rows = slice(i * PACK, (i + 1) * PACK)
        tok = dot(one_hot_pack(pos, i), xs[i])
        tok_o[rows, :] = tok.astype(BF)
        z, _ = statistics(tok)
        norm_o[rows, :] = (z * par[GAIN1 : GAIN1 + 1, :] + par[BIAS1 : BIAS1 + 1, :]).astype(BF)
    normed = norm_o[...]
    packed = dot(normed, w[...])
    for m in range(3):
        part = packed[:, m * HALF : (m + 1) * HALF]
        if m != 1:
            r = QB if m == 0 else VB
            part = part + par[r : r + 1, pl.ds(heads, HALF)]
        qkv_o[m] = part.astype(BF)
    scores = []
    for i, rows, hp, cols in head_pairs():
        scores.append(dot_nt(qkv_o[1, rows, cols], two_heads(qkv_o[0, rows, cols] * BF(HD**-0.5))))
    probs = []
    for n, (i, rows, hp, cols) in enumerate(head_pairs()):
        shown = jnp.where(keys_shown(pos, i), scores[n], -1e30)
        raised = jnp.exp(shown - jnp.max(shown, axis=0, keepdims=True))
        probs.append(raised / jnp.sum(raised, axis=0, keepdims=True))
    for n, (i, rows, hp, cols) in enumerate(head_pairs()):
        probs_o[n] = probs[n]
        mixed = join_heads(dot_tn(probs[n].astype(BF), qkv_o[2, rows, cols])).astype(BF)
        mix[rows, cols] = mixed
    mix_o[...] = mix[0:SPLIT, :]
    mix2_o[...] = mix[SPLIT:ROWS, :]


def half_kernel(mix_a, mix2_a, wp, c0, c1, x_a, x_b, pos_r, one_o, pre_o, xs):
    c = lax.axis_index("band") & 1
    mine = pl.multiple_of(c * HALF, 128)
    weights = wp[pl.ds(mine, HALF), :]
    one_o[0:SPLIT, :] = dot(mix_a[...], weights)
    one_o[SPLIT:ROWS, :] = dot(mix2_a[...], weights)
    gather_bands((images(c0), images(c1), images_of_two(x_a, x_b), lambda i: jnp.zeros((BAND, D), BF)), xs)
    pos = pos_r[...]
    for i in range(IMGS):
        pre_o[i * PACK : (i + 1) * PACK, :] = dot(one_hot_pack(pos, i), xs[i])


def hidden_kernel(half, mix_b, mix2_b, tok, par, be, wp, we, after, res_o, one_o, n2_o, act_o, slope_o):
    c = lax.axis_index("band") & 1
    weights = wp[pl.ds(pl.multiple_of((1 - c) * HALF, 128), HALF), :]
    one_o[0:SPLIT, :] = half[0:SPLIT, :] + dot(mix_b[...], weights) + par[PB : PB + 1, :]
    one_o[SPLIT:ROWS, :] = half[SPLIT:ROWS, :] + dot(mix2_b[...], weights) + par[PB : PB + 1, :]
    for i in range(IMGS):
        rows = slice(i * PACK, (i + 1) * PACK)
        residual = tok[rows, :].astype(F32) + par[ASC : ASC + 1, :] * one_o[rows, :]
        res_o[rows, :] = residual
        z, _ = statistics(residual)
        n2_o[rows, :] = (z * par[GAIN2 : GAIN2 + 1, :] + par[BIAS2 : BIAS2 + 1, :]).astype(BF)
    for f in range(FH // 256):
        cols = slice(f * 256, (f + 1) * 256)
        for i in range(IMGS):
            rows = slice(i * PACK, (i + 1) * PACK)
            hidden = dot(n2_o[rows, :], we[:, cols]) + be[0:1, cols]
            phi = 0.5 * (1.0 + lax.erf(hidden * math.sqrt(0.5)))
            act_o[rows, cols] = (hidden * phi).astype(BF)
            density = jnp.exp(-0.5 * hidden * hidden) * (1.0 / math.sqrt(2.0 * math.pi))
            slope_o[rows, cols] = phi + hidden * density


def split_kernel(v, out_a, out_b):
    for i in range(IMGS):
        lo = i * BAND
        for first, out in ((0, out_a), (OWN // 2, out_b)):
            start, stop = max(lo, first), min(lo + BAND, first + OWN // 2)
            if start < stop:
                out[start - first : stop - first, :] = v[i, start - lo : stop - lo, :]


def reduce_grad_kernel(part, d_a, d_b, far_r, par, act, pre_o, gb2_o, send_o, keep_o, act_x, full):
    x, c, z, y = place()
    block = images_of_two(d_a, d_b)
    for i in range(IMGS):
        rows = slice(i * PACK, (i + 1) * PACK)
        pre = part[rows, :] + dot(one_hot_pack(far_r[...], i), block(i))
        pre_o[rows, :] = pre.astype(BF)
        gb2_o[rows, :] = (par[MSC : MSC + 1, :] * pre).astype(BF)
    for chip in range(2):

        @pl.when(x == chip)
        def _():
            for j in range(4):
                lo = 384 * j + 192 * chip
                act_x[:, 192 * j : 192 * j + 192] = act[:, lo : lo + 192]

    full[...] = dot_tn(act_x[...], gb2_o[...])
    for dy, out in ((1, send_o), (0, keep_o)):
        for dz in range(2):
            j = 2 * ((z & 1) ^ dz) + (y ^ dy)
            for to in range(2):
                at = pl.multiple_of(192 * j + 96 * to, 96)
                out[2 * dz + to] = full[pl.ds(at, 96), :].astype(BF)


def back_kernel(gb2, wr, slope, we, gh_o, left_o, right_o):
    step = 256
    for f in range(FH // step):
        cols = slice(f * step, (f + 1) * step)
        back = dot_nt(gb2[...], wr[cols, :])
        gh_o[:, cols] = (back * slope[:, cols]).astype(BF)
    gn2 = dot_nt(gh_o[...], we[...]).astype(BF)
    left_o[...] = gn2[:, :HALF]
    right_o[...] = gn2[:, HALF:]


def expand_grad_kernel(n2, gh, pick, send_o, keep_o, tick, wide):
    tick[...] = jnp.zeros_like(tick)
    picked = dot_nt(pick[...], n2[...]).astype(BF)
    wide[...] = dot(picked, gh[...])
    for low, out in ((1, send_o), (0, keep_o)):
        for i in range(4):
            lo = 192 * (i >> 1) + 48 * (low + 2 * (i & 1))
            out[i] = wide[lo : lo + 48, :].astype(BF)


QC = 3 * HALF
QW = QC + HALF
FS = FH + 2 * SMALL


def both_halves(l_a, l_b, r_a, r_b):
    left = l_a[...].astype(F32) + l_b[...].astype(F32)
    right = r_a[...].astype(F32) + r_b[...].astype(F32)
    return jnp.concatenate([left, right], axis=1)


def attention_back_kernel(
    l_a, l_b, r_a, r_b, res, pre, qkv, probs_r, mix_a, mix2_a, mix_b, mix2_b, normed, pick, pick_p, wp, par, after,
    gres_o, gp, send_o, keep_o, tick,
    flat,
):
    tick[...] = jnp.zeros_like(tick)
    c = lax.axis_index("band") & 1
    heads = pl.multiple_of(c * HALF, 128)
    gn2 = both_halves(l_a, l_b, r_a, r_b)
    z2, rstd2 = statistics(res[...])
    gres = pre[...].astype(F32) + norm_back(gn2 * par[GAIN2 : GAIN2 + 1, :], z2, rstd2)
    gres_o[...] = gres
    gb1 = (par[ASC : ASC + 1, :] * gres).astype(BF)
    gm = dot_nt(gb1, wp[pl.ds(heads, HALF), :]).astype(BF)
    grads = [two_heads(gm[rows, cols]) for i, rows, hp, cols in head_pairs()]
    gprobs = [dot_nt(qkv[2, rows, cols], grads[n]) for n, (i, rows, hp, cols) in enumerate(head_pairs())]
    gscores = []
    for n in range(9):
        product = probs_r[n] * gprobs[n]
        gscores.append((product - probs_r[n] * jnp.sum(product, axis=0, keepdims=True)).astype(BF))
    for n, (i, rows, hp, cols) in enumerate(head_pairs()):
        parts = (
            join_heads(dot_tn(gscores[n], qkv[1, rows, cols] * BF(HD**-0.5))),
            dot(gscores[n], two_heads(qkv[0, rows, cols] * BF(HD**-0.5))),
            dot(probs_r[n].astype(BF), grads[n]),
        )
        for m in range(3):
            gp[rows, m * HALF + hp * 128 : m * HALF + (hp + 1) * 128] = parts[m].astype(BF)
    others = pl.multiple_of((1 - c) * HALF, 128)
    mixed = []
    for first, second in ((mix_a, mix_b), (mix2_a, mix2_b)):
        part = dot_nt(pick_p[:, pl.ds(heads, HALF)], first[...])
        mixed.append(part + dot_nt(pick_p[:, pl.ds(others, HALF)], second[...]))
    mixed = jnp.concatenate(mixed, axis=1).astype(BF)
    pn = dot_nt(pick[...], normed[...]).astype(BF)
    proj = dot(mixed, gb1)
    flat[...] = dot(pn, gp[...])
    for dy, out in ((1, send_o), (0, keep_o)):
        for i, dz in enumerate((0, 2, 1, 3)):
            q = 4 * dy + dz
            out[i, :, 0:QC] = flat[48 * q : 48 * q + 48, :].astype(BF)
            block = proj[24 * q : 24 * q + 24]
            out[i, :, QC:QW] = jnp.concatenate([block[:, :HALF], block[:, HALF:]], axis=0).astype(BF)


def vectors_kernel(
    l_a, l_b, r_a, r_b, res, one, gres, gp, w, act, wr, gb2, gh, pre, tok, pick, par, mine, theirs, after,
    gb_keep, gb_send, send_o, keep_o, tick,
    vecs, sums,
):
    tick[...] = jnp.zeros_like(tick)
    x, c, z, y = place()
    heads = pl.multiple_of(c * HALF, 128)
    first = jnp.where(c == 0, 1.0, 0.0)

    def total(v):
        return jnp.sum(v, axis=0, keepdims=True)

    vecs[...] = jnp.zeros_like(vecs)
    gnp = dot_nt(gp[...], w[...])
    z1, _ = statistics(tok[...].astype(F32))
    vecs[GAIN1 : GAIN1 + 1, :] = total(gnp * z1)
    vecs[BIAS1 : BIAS1 + 1, :] = total(gnp)
    vecs[QB : QB + 1, pl.ds(heads, HALF)] = total(gp[:, 0:HALF].astype(F32))
    vecs[VB : VB + 1, pl.ds(heads, HALF)] = total(gp[:, 2 * HALF : 3 * HALF].astype(F32))
    gb1 = (par[ASC : ASC + 1, :] * gres[...]).astype(BF)
    vecs[PB : PB + 1, :] = first * total(gb1.astype(F32))
    vecs[ASC : ASC + 1, :] = first * total(gres[...] * one[...])
    gn2 = both_halves(l_a, l_b, r_a, r_b)
    z2, _ = statistics(res[...])
    vecs[GAIN2 : GAIN2 + 1, :] = first * total(gn2 * z2)
    vecs[BIAS2 : BIAS2 + 1, :] = first * total(gn2)
    vecs[RB : RB + 1, :] = first * total(gb2[...].astype(F32))
    two = dot(act[...], wr[...])
    for m, value in enumerate((gnp.astype(BF), two.astype(BF))):
        for i in range(IMGS):
            rows = slice(i * PACK, (i + 1) * PACK)
            for at, out in ((mine, gb_keep), (theirs, gb_send)):
                out[m, i] = dot_tn(one_hot_pack(at[...], i), value[rows]).astype(BF)
    vecs[MSC : MSC + 1, :] = total(pre[...].astype(F32) * (two + first * par[RB : RB + 1, :]))
    cols = dot_nt(pick[...], vecs[...].astype(BF))
    sums[...] = dot_tn(gh[...], jnp.ones((ROWS, SMALL), BF))
    lane = lax.broadcasted_iota(jnp.int32, (48, SMALL), 1)
    for dy, out in ((1, send_o), (0, keep_o)):
        for dz in range(4):
            b = (z ^ dz) * 2 + (y ^ dy)
            q = 4 * dy + dz
            block = cols[48 * q : 48 * q + 48]
            for k in range(4):
                at = pl.multiple_of(384 * (b & 3) + 192 * x + 48 * k, 48)
                block = jnp.where((lane == 10 + k) & ((b >> 2) == c), sums[pl.ds(at, 48), :], block)
            out[dz >> 1, :, SMALL * (dz & 1) : SMALL * (dz & 1) + SMALL] = block.astype(BF)


def own_rows(pack, value):
    high = value.astype(BF)
    return dot_tn(pack, high) + dot_tn(pack, (value - high.astype(F32)).astype(BF))


def token_grad_kernel(gb_a, gb_b, tok, gres, mine, par, after, gtok_o, tick):
    tick[...] = jnp.zeros_like(tick)
    for i in range(IMGS):
        rows = slice(i * PACK, (i + 1) * PACK)
        pack = one_hot_pack(mine[...], i)
        z1, rstd1 = statistics(tok[i * BAND : (i + 1) * BAND, :].astype(F32))
        gnp = gb_a[0, i].astype(F32) + gb_b[0, i].astype(F32)
        gtok = own_rows(pack, gres[rows, :]) + norm_back(gnp * par[GAIN1 : GAIN1 + 1, :], z1, rstd1)
        gtok_o[i] = gtok.astype(BF)


def layer_out_kernel(gb_a, gb_b, res, mine, par, after, out_o, tick):
    tick[...] = jnp.zeros_like(tick)
    for i in range(IMGS):
        rows = slice(i * PACK, (i + 1) * PACK)
        pack = one_hot_pack(mine[...], i)
        ones = dot_tn(pack, jnp.ones((PACK, D), BF))
        two = gb_a[1, i].astype(F32) + gb_b[1, i].astype(F32) + ones * par[RB : RB + 1, :]
        out_o[i] = (own_rows(pack, res[rows, :]) + par[MSC : MSC + 1, :] * two).astype(BF)


def fold(keep, arrived, keep_o, send_o):
    half = keep.shape[0] // 2
    for i in range(half):
        keep_o[i] = keep[i].astype(F32) + arrived[i].astype(F32)
        send_o[i] = (keep[half + i].astype(F32) + arrived[half + i].astype(F32)).astype(BF)


def fold_kernel(keep, arrived, after, keep_o, send_o, tick):
    tick[...] = jnp.zeros_like(tick)
    fold(keep, arrived, keep_o, send_o)


def home_kernel(keep, arrived, after, keep_o, send_o, tick):
    tick[...] = jnp.zeros_like(tick)
    for i in range(4):
        total = keep[i].astype(F32) + arrived[i].astype(F32)
        keep_o[i] = total
        send_o[i] = total.astype(BF)


def fold(keep, arrived, keep_o, send_o):
    half = keep.shape[0] // 2
    for i in range(half):
        keep_o[i] = keep[i].astype(F32) + arrived[i].astype(F32)
        send_o[i] = (keep[half + i].astype(F32) + arrived[half + i].astype(F32)).astype(BF)


def fold_kernel(keep, arrived, after, keep_o, send_o, tick):
    tick[...] = jnp.zeros_like(tick)
    fold(keep, arrived, keep_o, send_o)


def second_fold_kernel(keep, arrived, we_keep, we_arrived, after, keep_o, send_o, we_keep_o, we_send_o, tick):
    tick[...] = jnp.zeros_like(tick)
    for i in range(2):
        total = keep[i] + arrived[i].astype(F32)
        keep_o[i] = total
        send_o[i] = total.astype(BF)
    fold(we_keep, we_arrived, we_keep_o, we_send_o)


def join_kernel(keep, arrived, vec_keep, vec_send, after, keep_o, send_o, tick):
    tick[...] = jnp.zeros_like(tick)
    fold(keep, arrived, keep_o.at[:, :, 0:FH], send_o.at[:, :, 0:FH])
    keep_o[:, :, FH:FS] = vec_keep[...].astype(F32)
    send_o[:, :, FH:FS] = vec_send[...]


def part_kernel(keep, arrived, after, keep_o, send_o, vec_ko, vec_so, tick):
    tick[...] = jnp.zeros_like(tick)
    fold(keep.at[:, :, 0:FH], arrived.at[:, :, 0:FH], keep_o, send_o)
    for hi in range(2):
        total = keep[hi, :, FH:FS] + arrived[hi, :, FH:FS].astype(F32)
        vec_ko[hi] = total[:, 0:SMALL]
        vec_so[hi] = total[:, SMALL:].astype(BF)


def settle_kernel(wr_k, wr_a, we_k, we_a, after, wr_ko, wr_so, we_ko, we_so, tick, both):
    tick[...] = jnp.zeros_like(tick)
    c = lax.axis_index("band") & 1
    for at, out in ((c, wr_ko), (1 - c, wr_so)):
        out[...] = (wr_k[at] + wr_a[at].astype(F32)).astype(out.dtype)
    both[...] = we_k[0] + we_a[0].astype(F32)
    we_ko[...] = both[pl.ds(pl.multiple_of(c * 24, 8), 24), :]
    we_so[...] = both[pl.ds(pl.multiple_of(24 - c * 24, 8), 24), :].astype(BF)


USED = 16
NEAR = QC + D


def cut_kernel(keep, arrived, after, mine_o, hop_o, near_o, far_o, tick, both):
    tick[...] = jnp.zeros_like(tick)
    c = lax.axis_index("band") & 1
    mine, theirs = pl.multiple_of(c * 24, 8), pl.multiple_of(24 - c * 24, 8)
    for n, own_o, other_o in ((0, mine_o, hop_o), (1, near_o, far_o)):
        both[...] = keep[n].astype(F32) + arrived[n].astype(F32)
        own_o[:, 0:QC] = both[pl.ds(mine, 24), 0:QC].astype(own_o.dtype)
        other_o[...] = both[pl.ds(theirs, 24), 0:QC].astype(own_o.dtype)
        own_o[:, QC : QC + HALF] = both[0:24, QC:QW].astype(own_o.dtype)
        own_o[:, QC + HALF :] = both[24:48, QC:QW].astype(own_o.dtype)


def cores_kernel(vec_a, vec_b, hop, after, keep_o, send_o, other_o, tick):
    tick[...] = jnp.zeros_like(tick)
    keep_o[...] = jnp.zeros_like(keep_o)
    keep_o[:, 0:USED] = vec_a[0, :, 0:USED] + vec_b[0].astype(F32)
    send_o[...] = (vec_a[1, :, 0:USED] + vec_b[1].astype(F32)).astype(BF)
    other_o[...] = hop[...]


def vector_fold_kernel(keep, arrived, after, out, send_o, tick):
    tick[...] = jnp.zeros_like(tick)
    total = keep[...] + arrived[...].astype(F32)
    out[...] = total
    send_o[...] = total[:, :, 0:USED].astype(BF)


def total_kernel(mine, near, hop, far, vec_k, vec_a, after, own_o, other_o, vec_o, tick):
    tick[...] = jnp.zeros_like(tick)
    own_o[...] = mine[...] + near[...].astype(F32)
    other_o[...] = hop[...] + far[...].astype(F32)
    vec_o[...] = vec_k[...]
    vec_o[:, 0:USED] = vec_k[:, 0:USED] + vec_a[...].astype(F32)


def out_kernel(
    own, other, vec_r, we_keep, we_arrived, wr_keep, wr_arrived, after,
    qkv_o, first_o, bias_o, qv_o, bp_o, asc_o, gain2_o, bias2_o, br_o, msc_o, eb_o, proj_o, we_o, wr_o,
):
    _, c, z, _ = place()
    wr_o[...] = jnp.where((z >> 1) == c, wr_keep[...], wr_arrived[...].astype(F32))
    we_o[:, pl.ds(pl.multiple_of(c * FH, 128), FH)] = we_keep[...]
    we_o[:, pl.ds(pl.multiple_of((1 - c) * FH, 128), FH)] = we_arrived[...].astype(F32)
    proj_o[...] = own[:, QC:NEAR]
    for m in range(3):
        cols = slice(m * HALF, (m + 1) * HALF)
        qkv_o[:, pl.ds(pl.multiple_of(m * D + c * HALF, 128), HALF)] = own[:, cols]
        qkv_o[:, pl.ds(pl.multiple_of(m * D + (1 - c) * HALF, 128), HALF)] = other[:, cols]
    vec = vec_r[pl.ds(pl.multiple_of(c * 24, 8), 24), :].T
    outs = (first_o, bias_o, None, None, bp_o, asc_o, gain2_o, bias2_o, br_o, msc_o)
    for r, out in enumerate(outs):
        if out is not None:
            out[...] = vec[r]
    qv_o[...] = vec[2:4]
    units = vec_r[...].T
    units = jnp.where(c == 0, units[10:12], units[12:14])
    eb_o[...] = jnp.concatenate([units[0:1], units[1:2]], axis=1).reshape(96)


COSTS = {
    "back_kernel": (2000000000, 0),
    "expand_grad_kernel": (1000000000, 0),
    "vectors_kernel": (8000000000, 20000000),
    "second_fold_kernel": (0, 2000000),
    "last_kernel": (0, 1000000),
    "spread_kernel": (0, 2000000),
    "finish_kernel": (0, 1000000),
    "out_kernel": (0, 1000000),
    "prepare_kernel": (0, 9000000),
    "total_kernel": (4000000000, 0),
}


def call(kernel, outs, specs, scratch=(), vmem=24, cost=0):
    return pl.pallas_call(
        kernel,
        out_shape=outs,
        in_specs=specs,
        out_specs=jax.tree.map(lambda _: VM, outs),
        scratch_shapes=list(scratch),
        compiler_params=pltpu.CompilerParams(vmem_limit_bytes=vmem * MIB),
        cost_estimate=pl.CostEstimate(flops=COSTS.get(kernel.__name__, (0, 0))[0] + cost, bytes_accessed=COSTS.get(kernel.__name__, (0, 0))[1], transcendentals=0),
    )


def fold_call(keep, arrived, after, cost=0):
    half = (keep.shape[0] // 2, *keep.shape[1:])
    return call(fold_kernel, (vm(half, F32), vm(half, BF), TICK), [VM] * 2 + [ANY], cost=cost)(keep, arrived, after)


def by_core(value):
    return lax.ppermute(value, "band", [(i, i ^ 1) for i in range(4)])


def by_x(value):
    return lax.ppermute(value, "band", [(i, i ^ 2) for i in range(4)])


def by_y(value):
    return lax.ppermute(value, "batch", [(i, i ^ 1) for i in range(8)])


def by_z(value, dz):
    return lax.ppermute(value, "batch", [(i, i ^ (2 * dz)) for i in range(8)])


def across(value):
    return lax.ppermute(value, ("batch", "band"), [(d, d ^ 17) for d in range(32)])


def homeward(value, dz):
    pairs = [(d, d ^ (8 * dz)) for d in range(32) if ((d ^ (8 * dz)) >> 4) == (d & 1)]
    return lax.ppermute(value, ("batch", "band"), pairs)


def packed_body(
    tokens, cotangent, visible, first_gain, first_bias, qkv_weight, qv_bias, proj_weight, proj_bias,
    attn_scale, second_gain, second_bias, expand_weight, expand_bias, reduce_weight, reduce_bias, mlp_scale,
):
    block = vm(cotangent.shape, BF)
    rows_f, rows_b = vm((ROWS, D), F32), vm((ROWS, D), BF)
    tok_x = by_x(tokens)
    tok_block = vm((OWN + 16, D), BF)
    cot, tok_own, par, be, wqkv, wp, we, wr, vis, pick, pick_p = call(
        prepare_kernel,
        (
            block,
            tok_block,
            vm((16, D), F32),
            vm((8, FH), F32),
            vm((D, QC), BF),
            vm((D, D), BF),
            vm((D, FH), BF),
            vm((FH, D), BF),
            vm((16, D), BF),
            vm((HALF, D), BF),
            vm((192, D), BF),
        ),
        [ANY] * 17,
        [pltpu.VMEM(visible.shape, jnp.int32), pltpu.SemaphoreType.DMA((22,))],
    )(
        *map(
            stay,
            (
                cotangent, first_gain, first_bias, qv_bias, proj_bias, attn_scale, second_gain, second_bias,
                reduce_bias, mlp_scale, expand_bias, qkv_weight, proj_weight, expand_weight, reduce_weight, visible,
                tokens,
            ),
        )
    )
    vis_x = by_x(vis)
    tok_c = by_core(tok_own)
    cot_c = by_core(cot)
    parts = (vm((EARLY, D), BF), vm((OWN + 16 - EARLY, D), BF))
    tok_x = call(hold_kernel, parts, [VM] * 2 + [ANY])(tok_x, vis_x, par)
    tok_d = [by_core(v) for v in tok_x]
    cot_x = call(split_kernel, (vm((OWN // 2, D), BF),) * 2, [VM])(by_x(cot))
    cot_d = [by_core(v) for v in cot_x]
    tok, normed, qkv, mix_own, mix2_own, pos, probs, pos_mine, pos_theirs, pos_far = call(
        first_kernel,
        (
            rows_b,
            rows_b,
            vm((3, ROWS, HALF), BF),
            vm((SPLIT, HALF), BF),
            vm((ROWS - SPLIT, HALF), BF),
            vm((8, SLOTS), F32),
            vm((9, PACK, 2 * PACK), F32),
            vm((16, BAND), F32),
            vm((16, BAND), F32),
            vm((16, BAND), F32),
        ),
        [VM] * 8,
        [pltpu.VMEM((IMGS, SLOTS, D), BF), pltpu.VMEM((ROWS, HALF), BF)],
    )(tok_own, tok_c, *tok_x, *tok_d, par, wqkv)
    mix_other, mix2_other = by_core(mix_own), by_core(mix2_own)
    half_one, half_pre = call(
        half_kernel, (rows_f, rows_f), [VM] * 8, [pltpu.VMEM((IMGS, SLOTS, D), BF)]
    )(mix_own, mix2_own, wp, cot, cot_c, *cot_x, pos)
    res, one, n2, act, slope = call(
        hidden_kernel,
        (rows_f, rows_f, rows_b, vm((ROWS, FH), BF), vm((ROWS, FH), F32)),
        [VM] * 8 + [ANY],
    )(half_one, mix_other, mix2_other, tok, par, be, wp, we, pick)
    pre, gb2, wr_send, wr_keep = call(
        reduce_grad_kernel,
        (rows_b, rows_b, vm((4, 96, D), BF), vm((4, 96, D), BF)),
        [VM] * 6,
        [pltpu.VMEM((ROWS, D), BF), pltpu.VMEM((D, D), F32)],
    )(half_pre, *cot_d, pos_far, par, act)
    wr_y = by_y(wr_send)
    half_b = vm((ROWS, HALF), BF)
    gh, left, right = call(back_kernel, (vm((ROWS, FH), BF), half_b, half_b), [VM] * 4)(gb2, wr, slope, we)
    gn2 = (left, by_core(left), right, by_core(right))
    we_send, we_keep, tick = call(
        expand_grad_kernel,
        (vm((4, 48, FH), BF), vm((4, 48, FH), BF), TICK),
        [VM] * 3,
        [pltpu.VMEM((HALF, FH), F32)],
    )(n2, gh, pick)
    we_z = by_z(we_send, 1)
    gres, gp, qp_send, qp_keep, tick = call(
        attention_back_kernel,
        (rows_f, vm((ROWS, QC), BF), vm((4, 48, QW), BF), vm((4, 48, QW), BF), TICK),
        [VM] * 17 + [ANY],
        [pltpu.VMEM((HALF, QC), F32)],
    )(*gn2, res, pre, qkv, probs, mix_own, mix2_own, mix_other, mix2_other, normed, pick, pick_p, wp, par, tick)
    qp_y = by_y(qp_send)
    wr_keep, wr_send, tick = call(
        home_kernel, (vm((4, 96, D), F32), vm((4, 96, D), BF), TICK), [VM] * 2 + [ANY]
    )(wr_keep, wr_y, tick)
    wr_z = homeward(wr_send, 2)
    gb_keep, gb_send, vec_send, vec_keep, tick = call(
        vectors_kernel,
        (vm((2, *tokens.shape), BF), vm((2, *tokens.shape), BF), vm((2, 48, 2 * SMALL), BF), vm((2, 48, 2 * SMALL), BF), TICK),
        [VM] * 19 + [ANY],
        [pltpu.VMEM((SMALL, D), F32), pltpu.VMEM((FH, SMALL), F32)],
    )(*gn2, res, one, gres, gp, wqkv, act, wr, gb2, gh, pre, tok, pick, par, pos_mine, pos_theirs, tick)
    gb_other = by_core(gb_send)
    we_keep, we_send, tick = call(
        join_kernel, (vm((2, 48, FS), F32), vm((2, 48, FS), BF), TICK), [VM] * 4 + [ANY]
    )(we_keep, we_z, vec_keep, vec_send, tick)
    we_y = by_y(we_send)
    qp_keep, qp_send, tick = fold_call(qp_keep, qp_y, tick, cost=0)
    qp_z = by_z(qp_send, 1)
    wr_keep, wr_send, tick = fold_call(wr_keep, wr_z, tick, cost=0)
    wr_z = homeward(wr_send, 1)
    we_keep, we_send, vec_keep, vec_send, tick = call(
        part_kernel,
        (vm((1, 48, FH), F32), vm((1, 48, FH), BF), vm((2, 48, SMALL), F32), vm((2, 48, SMALL), BF), TICK),
        [VM] * 2 + [ANY],
    )(we_keep, we_y, tick)
    vec_z = by_z(vec_send, 1)
    we_z = by_z(we_send, 2)
    mine, hop, near, far, tick = call(
        cut_kernel,
        (vm((24, NEAR), F32), vm((24, QC), F32), vm((24, NEAR), BF), vm((24, QC), BF), TICK),
        [VM] * 2 + [ANY],
        [pltpu.VMEM((48, QW), F32)],
        cost=0,
    )(qp_keep, qp_z, tick)
    near, far, hop = by_z(near, 2), across(far), by_core(hop)
    vec, vec_send, tick = call(
        vector_fold_kernel, (vm((2, 48, SMALL), F32), vm((2, 48, USED), BF), TICK), [VM] * 2 + [ANY], cost=4000000000
    )(vec_keep, vec_z, tick)
    vec_other = by_core(vec_send)
    layer_out, tick = call(layer_out_kernel, (sds(tokens.shape, BF), TICK), [VM] * 5 + [ANY])(
        gb_keep, gb_other, res, pos_mine, par, tick
    )
    vec_keep, vec_send, hop, tick = call(
        cores_kernel,
        (vm((48, SMALL), F32), vm((48, USED), BF), vm((24, QC), F32), TICK),
        [VM] * 3 + [ANY],
    )(vec, vec_other, hop, tick)
    vec_z = by_z(vec_send, 2)
    grad_tokens, tick = call(token_grad_kernel, (sds(tokens.shape, BF), TICK), [VM] * 6 + [ANY])(
        gb_keep, gb_other, tok_own, gres, pos_mine, par, tick
    )
    wr_keep, wr_send, we_keep, we_send, tick = call(
        settle_kernel,
        (vm((96, D), F32), vm((96, D), BF), vm((24, FH), F32), vm((24, FH), BF), TICK),
        [VM] * 4 + [ANY],
        [pltpu.VMEM((48, FH), F32)],
    )(wr_keep, wr_z, we_keep, we_z, tick)
    we_other, wr_other = by_core(we_send), by_core(wr_send)
    own, other, vec, tick = call(
        total_kernel,
        (vm((24, NEAR), F32), vm((24, QC), F32), vm((48, SMALL), F32), TICK),
        [VM] * 6 + [ANY],
    )(mine, near, hop, far, vec_keep, vec_z, tick)
    vector = sds((24,), F32)
    grad_qkv, gg1, gb1, gqv, gbp, gas, gg2, gb2, gbr, gms, geb, grad_proj, grad_expand, grad_reduce = call(
        out_kernel,
        (
            sds((24, 3 * D), F32), vector, vector, sds((2, 24), F32), vector, vector, vector, vector, vector, vector,
            sds((96,), F32), sds((24, D), F32), sds((24, FF), F32), sds((96, D), F32),
        ),
        [VM] * 7 + [ANY],
    )(own, other, vec, we_keep, we_other, wr_keep, wr_other, tick)
    return (
        layer_out, grad_tokens, gg1, gb1, grad_qkv, gqv, grad_proj, gbp, gas, gg2, gb2, grad_expand, geb, grad_reduce,
        gbr, gms,
    )


def layer_norm(values, norm_gain, norm_shift):
    center = values - jnp.mean(values, axis=-1, keepdims=True)
    spread = jnp.mean(center * center, axis=-1, keepdims=True)
    return center * lax.rsqrt(spread + NORM_EPS) * norm_gain + norm_shift


def gelu_exact(values):
    return jax.nn.gelu(values, approximate=False)


def split_rows(packed_rows, mask_rows):
    item_count = packed_rows.shape[0]
    slot_count = packed_rows.shape[1]
    heads_here = packed_rows.shape[4] // HD
    unpacked = packed_rows.reshape(item_count, slot_count, 3, heads_here, HD)
    queries = unpacked[:, :, 0]
    key_rows = unpacked[:, :, 1]
    value_rows = unpacked[:, :, 2]
    key_valid = mask_rows.reshape(item_count, slot_count) > 0
    score_scale = 1.0 / math.sqrt(HD)
    scores = (
        jnp.einsum("bqhe,bkhe->bhqk", queries, key_rows, preferred_element_type=jnp.float32)
        * score_scale
    )
    scores = jnp.where(key_valid[:, None, None, :], scores, -1e30)
    return (queries, key_rows, value_rows, scores)


def attend_plain(inputs):
    packed_rows, mask_rows = inputs
    queries, key_rows, value_rows, scores = split_rows(packed_rows, mask_rows)
    row_top = jnp.max(scores, axis=-1, keepdims=True)
    raised = jnp.exp(scores - row_top)
    row_total = jnp.sum(raised, axis=-1, keepdims=True)
    attn_prob = raised / row_total
    log_total = (row_top + jnp.log(row_total))[..., 0]
    mixed_rows = jnp.einsum(
        "bhqk,bkhe->bqhe",
        attn_prob.astype(jnp.bfloat16),
        value_rows,
        preferred_element_type=jnp.float32,
    ).astype(jnp.bfloat16)
    mixed_rows = mixed_rows.reshape(
        packed_rows.shape[0], packed_rows.shape[1], packed_rows.shape[4]
    )
    return (mixed_rows, log_total)


def backward_rows(score_parts, log_total, grad_rows):
    queries, key_rows, value_rows, scores = score_parts
    item_count, slot_count, heads_here, head_size = queries.shape
    score_scale = 1.0 / math.sqrt(HD)
    attn_prob = jnp.exp(scores - log_total[..., None])
    grad_heads = grad_rows.reshape(item_count, slot_count, heads_here, head_size)
    grad_prob = jnp.einsum(
        "bqhe,bkhe->bhqk", grad_heads, value_rows, preferred_element_type=jnp.float32
    )
    row_delta = jnp.sum(attn_prob * grad_prob, axis=-1, keepdims=True)
    grad_score = (attn_prob * (grad_prob - row_delta)).astype(jnp.bfloat16)
    grad_query = (
        jnp.einsum("bhqk,bkhe->bqhe", grad_score, key_rows, preferred_element_type=jnp.float32)
        * score_scale
    )
    grad_key = (
        jnp.einsum("bhqk,bqhe->bkhe", grad_score, queries, preferred_element_type=jnp.float32)
        * score_scale
    )
    grad_value = jnp.einsum(
        "bhqk,bqhe->bkhe",
        attn_prob.astype(jnp.bfloat16),
        grad_heads,
        preferred_element_type=jnp.float32,
    )
    stacked = jnp.stack([grad_query, grad_key, grad_value], axis=2)
    return stacked.reshape(item_count, slot_count, 3, 1, heads_here * head_size).astype(
        jnp.bfloat16
    )


def attend_again(inputs):
    packed_rows, mask_rows, grad_rows = inputs
    score_parts = split_rows(packed_rows, mask_rows)
    scores = score_parts[3]
    row_top = jnp.max(scores, axis=-1, keepdims=True)
    log_total = (row_top + jnp.log(jnp.sum(jnp.exp(scores - row_top), axis=-1, keepdims=True)))[
        ..., 0
    ]
    return backward_rows(score_parts, log_total, grad_rows)


def body(
    tokens,
    cotangent,
    visible,
    first_gain,
    first_bias,
    qkv_weight,
    qv_bias,
    proj_weight,
    proj_bias,
    attn_scale,
    second_gain,
    second_bias,
    expand_weight,
    expand_bias,
    reduce_weight,
    reduce_bias,
    mlp_scale,
):
    images, slot_count, model_width = tokens.shape
    groups = lax.axis_size("band")
    local_width = model_width // groups
    inputs_full = tokens.astype(jnp.float32)
    shown_mask = visible.astype(jnp.float32)
    normed, first_pull = jax.vjp(layer_norm, inputs_full, first_gain, first_bias)
    normed_low = normed.astype(jnp.bfloat16)
    qkv_bias = jnp.concatenate([qv_bias[0], jnp.zeros((model_width,), jnp.float32), qv_bias[1]])

    def project_qkv():
        product = jnp.einsum(
            "isd,de->ise", normed_low, qkv_weight, preferred_element_type=jnp.float32
        )
        return (
            (product + qkv_bias)
            .astype(jnp.bfloat16)
            .reshape(images, slot_count, 3, groups, local_width)
        )

    packed = project_qkv()
    mask_part = jnp.broadcast_to(
        shown_mask.astype(jnp.bfloat16)[:, :, None, None, None], (images, slot_count, 1, groups, 1)
    )
    results = attend_plain(
        (
            lax.all_to_all(packed, "band", split_axis=3, concat_axis=1, tiled=True),
            lax.all_to_all(mask_part, "band", split_axis=3, concat_axis=1, tiled=True),
        )
    )
    mixed_heads = results[0].reshape(images, groups * slot_count, 1, local_width)
    back_rows = lax.all_to_all(mixed_heads, "band", split_axis=1, concat_axis=2, tiled=True)
    mixed_rows = back_rows.reshape(images, slot_count, model_width)
    branch_one = (
        jnp.einsum("isd,de->ise", mixed_rows, proj_weight, preferred_element_type=jnp.float32)
        + proj_bias
    )
    residual = inputs_full + attn_scale * branch_one
    normed_two, second_pull = jax.vjp(layer_norm, residual, second_gain, second_bias)
    normed_two_low = normed_two.astype(jnp.bfloat16)
    hidden = (
        jnp.einsum("isd,df->isf", normed_two_low, expand_weight, preferred_element_type=jnp.float32)
        + expand_bias
    )
    activated, gelu_pull = jax.vjp(gelu_exact, hidden)
    activated_low = activated.astype(jnp.bfloat16)
    branch_two = (
        jnp.einsum("isf,fd->isd", activated_low, reduce_weight, preferred_element_type=jnp.float32)
        + reduce_bias
    )
    layer_out = (shown_mask[..., None] * (residual + mlp_scale * branch_two)).astype(jnp.bfloat16)
    grad_pre = shown_mask[..., None] * cotangent.astype(jnp.float32)
    grad_mlp_scale = jnp.sum(grad_pre * branch_two, axis=(0, 1))
    grad_branch_two = (mlp_scale * grad_pre).astype(jnp.bfloat16)
    grad_reduce_weight = jnp.einsum(
        "isf,isd->fd", activated_low, grad_branch_two, preferred_element_type=jnp.float32
    )
    grad_reduce_bias = jnp.sum(grad_branch_two.astype(jnp.float32), axis=(0, 1))
    grad_activated = jnp.einsum(
        "isd,fd->isf", grad_branch_two, reduce_weight, preferred_element_type=jnp.float32
    )
    grad_hidden = gelu_pull(grad_activated)[0].astype(jnp.bfloat16)
    grad_expand_weight = jnp.einsum(
        "isd,isf->df", normed_two_low, grad_hidden, preferred_element_type=jnp.float32
    )
    grad_expand_bias = jnp.sum(grad_hidden.astype(jnp.float32), axis=(0, 1))
    grad_normed_two = jnp.einsum(
        "isf,df->isd", grad_hidden, expand_weight, preferred_element_type=jnp.float32
    )
    grad_resid_norm, grad_second_gain, grad_second_bias = second_pull(grad_normed_two)
    grad_residual = grad_pre + grad_resid_norm
    grad_attn_scale = jnp.sum(grad_residual * branch_one, axis=(0, 1))
    grad_branch_one = (attn_scale * grad_residual).astype(jnp.bfloat16)
    grad_proj_weight = jnp.einsum(
        "isd,ise->de", mixed_rows, grad_branch_one, preferred_element_type=jnp.float32
    )
    grad_proj_bias = jnp.sum(grad_branch_one.astype(jnp.float32), axis=(0, 1))
    grad_mixed = jnp.einsum(
        "ise,de->isd", grad_branch_one, proj_weight, preferred_element_type=jnp.float32
    )
    grad_mixed = grad_mixed.astype(jnp.bfloat16).reshape(images, slot_count, 1, groups, local_width)
    repacked = project_qkv()
    grad_packed = attend_again(
        (
            lax.all_to_all(repacked, "band", split_axis=3, concat_axis=1, tiled=True),
            lax.all_to_all(mask_part, "band", split_axis=3, concat_axis=1, tiled=True),
            lax.all_to_all(grad_mixed, "band", split_axis=3, concat_axis=1, tiled=True),
        )
    )
    grad_bands = lax.all_to_all(grad_packed, "band", split_axis=1, concat_axis=3, tiled=True)
    grad_qkv = grad_bands.reshape(images, slot_count, 3 * model_width)
    grad_qkv_weight = jnp.einsum(
        "isd,ise->de", normed_low, grad_qkv, preferred_element_type=jnp.float32
    )
    column_sums = jnp.sum(grad_qkv.astype(jnp.float32), axis=(0, 1))
    grad_qv_bias = jnp.stack([column_sums[:model_width], column_sums[2 * model_width :]])
    grad_normed = jnp.einsum(
        "ise,de->isd", grad_qkv, qkv_weight, preferred_element_type=jnp.float32
    )
    grad_input_norm, grad_first_gain, grad_first_bias = first_pull(grad_normed)
    grad_tokens = (grad_residual + grad_input_norm).astype(jnp.bfloat16)
    all_sums = (
        lax.psum_scatter(grad_first_gain, ("batch", "band"), scatter_dimension=0, tiled=True),
        lax.psum_scatter(grad_first_bias, ("batch", "band"), scatter_dimension=0, tiled=True),
        lax.psum_scatter(grad_qkv_weight, ("batch", "band"), scatter_dimension=0, tiled=True),
        lax.psum_scatter(grad_qv_bias, ("batch", "band"), scatter_dimension=1, tiled=True),
        lax.psum_scatter(grad_proj_weight, ("batch", "band"), scatter_dimension=0, tiled=True),
        lax.psum_scatter(grad_proj_bias, ("batch", "band"), scatter_dimension=0, tiled=True),
        lax.psum_scatter(grad_attn_scale, ("batch", "band"), scatter_dimension=0, tiled=True),
        lax.psum_scatter(grad_second_gain, ("batch", "band"), scatter_dimension=0, tiled=True),
        lax.psum_scatter(grad_second_bias, ("batch", "band"), scatter_dimension=0, tiled=True),
        lax.psum_scatter(grad_expand_weight, ("batch", "band"), scatter_dimension=0, tiled=True),
        lax.psum_scatter(grad_expand_bias, ("batch", "band"), scatter_dimension=0, tiled=True),
        lax.psum_scatter(grad_reduce_weight, ("batch", "band"), scatter_dimension=0, tiled=True),
        lax.psum_scatter(grad_reduce_bias, ("batch", "band"), scatter_dimension=0, tiled=True),
        lax.psum_scatter(grad_mlp_scale, ("batch", "band"), scatter_dimension=0, tiled=True),
    )
    (
        sum_first_gain,
        sum_first_bias,
        sum_qkv_weight,
        sum_qv_bias,
        sum_proj_weight,
        sum_proj_bias,
        sum_attn_scale,
        sum_second_gain,
        sum_second_bias,
        sum_expand_weight,
        sum_expand_bias,
        sum_reduce_weight,
        sum_reduce_bias,
        sum_mlp_scale,
    ) = all_sums
    return (
        layer_out,
        grad_tokens,
        sum_first_gain,
        sum_first_bias,
        sum_qkv_weight,
        sum_qv_bias,
        sum_proj_weight,
        sum_proj_bias,
        sum_attn_scale,
        sum_second_gain,
        sum_second_bias,
        sum_expand_weight,
        sum_expand_bias,
        sum_reduce_weight,
        sum_reduce_bias,
        sum_mlp_scale,
    )


def solution(mesh):
    sizes = dict(mesh.shape)
    chosen = packed_body if (sizes["batch"], sizes["band"]) == (8, 4) else body
    placed = (
        P("batch", "band", None),
        P("batch", "band", None),
        P("batch", "band"),
        P(),
        P(),
        P(),
        P(),
        P(),
        P(),
        P(),
        P(),
        P(),
        P(),
        P(),
        P(),
        P(),
        P(),
    )
    return jax.shard_map(
        chosen,
        mesh=mesh,
        in_specs=placed,
        out_specs=(
            P("batch", "band", None),
            P("batch", "band", None),
            P(("batch", "band")),
            P(("batch", "band")),
            P(("batch", "band"), None),
            P(None, ("batch", "band")),
            P(("batch", "band"), None),
            P(("batch", "band")),
            P(("batch", "band")),
            P(("batch", "band")),
            P(("batch", "band")),
            P(("batch", "band"), None),
            P(("batch", "band")),
            P(("batch", "band"), None),
            P(("batch", "band")),
            P(("batch", "band")),
        ),
        check_vma=False,
    )
```
